32 devices in a mesh: role: 4 (over x, core), ctx: 4 (over z), tp: 2 (over y).
Axes of the slice: x: 2, y: 2, z: 4, core: 2. Of those that a mesh axis runs over, the one named last changes fastest.
Arguments:
- prefill_q: bfloat16 [4, 1024, 64, 128], P('role', 'ctx', 'tp'), may hold values from -6 to 6
- prefill_k: bfloat16 [4, 1024, 8, 128], P('role', 'ctx', 'tp'), may hold values from -6 to 6
- prefill_v: bfloat16 [4, 1024, 8, 128], P('role', 'ctx', 'tp'), may hold values from -6 to 6
- decode_q: bfloat16 [512, 4, 64, 128], P(('role', 'ctx'), None, 'tp'), may hold values from -6 to 6
- decode_k: bfloat16 [512, 4, 8, 128], P(('role', 'ctx'), None, 'tp'), may hold values from -6 to 6
- decode_v: bfloat16 [512, 4, 8, 128], P(('role', 'ctx'), None, 'tp'), may hold values from -6 to 6
- cache_k: bfloat16 [512, 128, 8, 128], P(('role', 'ctx'), None, 'tp'), may hold values from -6 to 6
- cache_v: bfloat16 [512, 128, 8, 128], P(('role', 'ctx'), None, 'tp'), may hold values from -6 to 6
- cache_len: int32 [512], P(('role', 'ctx')), may hold values from 1 to 128
- page_list: int32 [512, 4], P(('role', 'ctx')), may hold values from 0 to 31, as said below
Outputs:
- prefill_out: bfloat16 [4, 1024, 64, 128], P('role', 'ctx', 'tp')
- decode_out: bfloat16 [512, 4, 8192], P(('role', 'ctx', 'tp'))
The draws below stay inside these ranges and needn't reach their ends.
Inputs may be any that keep to these rules, and one draw needn't show every extreme that they name: `page_list`: each request names 4 pages of 4 different owners, where the owner of page p is p // 2. Among the requests of one device (aligned blocks of 32 rows), all pages named from one owner are the same page.
All inputs are finite; a program needn't handle non-finite values.
Results may differ from the reference program's by a relative error of at most 0.0033.
Values may be sent and summed in bfloat16 or wider, within the bound.
No kernel may reach another device: no remote copies, remote signals or barrier semaphores. Data moves between devices by JAX's collectives and lax.ppermute only.
A program may use at most 192 MiB of HBM per device.

```python
import math
import jax
import jax.numpy as jnp
from jax import lax

HEADS = 64
KV_HEADS = 8
HEAD_DIM = 128
TOK_DEV = 256
PAGE = 128
REQ_DEV = 32
CACHE = 128
EXTRA = 4
STEPS = 4
GROUPS = 4
SPAN = 1024
OWN_PAGES = 2
OWNERS = 16
POOL = 32
REQUESTS = 512


def sign_pattern(key, salt):
    key = jax.random.fold_in(key, salt)
    flips = jax.random.bernoulli(key, 0.5, (KV_HEADS, HEAD_DIM))
    return jnp.where(flips, 1.0, -1.0).astype(jnp.float32)


def mixed_base(key, shape):
    key_normal = jax.random.fold_in(key, 0)
    normal = jnp.clip(jax.random.normal(key_normal, shape, jnp.float32), -4.0, 4.0)
    return normal


def query_rows(key, shape, pattern, aligned):
    key_base, key_strength = jax.random.split(key)
    base = mixed_base(key_base, shape)
    strength = jax.random.uniform(key_strength, shape[:-1] + (1,), jnp.float32, 4.0, 6.0)
    heads_pattern = jnp.repeat(pattern, HEADS // KV_HEADS, axis=0)
    return jnp.where(aligned, strength * heads_pattern[None, None], base)


def key_rows(pattern):
    reduced = 5.0 - 2.0 * math.sqrt(HEAD_DIM) / 5.0
    column = jnp.arange(HEAD_DIM)
    first = 5.0 * pattern
    second = jnp.where(column[None, :] == 0, reduced, 5.0) * pattern
    return (first, second)


def draw_prefill_q(key, part):
    pattern = sign_pattern(key, 101)
    key = jax.random.fold_in(key, 21)
    shape = (GROUPS, SPAN, HEADS, HEAD_DIM)
    position = jnp.arange(SPAN)
    aligned = (position % TOK_DEV == TOK_DEV - 1)[None, :, None, None]
    values = query_rows(key, shape, pattern, aligned)
    return values.astype(jnp.bfloat16)


def draw_prefill_k(key, part):
    pattern = sign_pattern(key, 101)
    key = jax.random.fold_in(key, 22)
    shape = (GROUPS, SPAN, KV_HEADS, HEAD_DIM)
    base = mixed_base(key, shape)
    first, second = key_rows(pattern)
    position = jnp.arange(SPAN)[None, :, None, None]
    values = jnp.where(position == 0, first[None, None], jnp.where(position == 1, second[None, None], base))
    return values.astype(jnp.bfloat16)


def draw_decode_q(key, part):
    pattern = sign_pattern(key, 102)
    key = jax.random.fold_in(key, 23)
    shape = (REQUESTS, STEPS, HEADS, HEAD_DIM)
    aligned = (jnp.arange(REQUESTS) % 4 == 1)[:, None, None, None]
    values = query_rows(key, shape, pattern, aligned)
    return values.astype(jnp.bfloat16)


def draw_decode_k(key, part):
    pattern = sign_pattern(key, 102)
    key = jax.random.fold_in(key, 24)
    shape = (REQUESTS, STEPS, KV_HEADS, HEAD_DIM)
    base = mixed_base(key, shape)
    first, second = key_rows(pattern)
    step = jnp.arange(STEPS)[None, :, None, None]
    return jnp.where(step == 0, second[None, None], base).astype(jnp.bfloat16)


def draw_cache_k(key, part):
    pattern = sign_pattern(key, 102)
    key = jax.random.fold_in(key, 25)
    shape = (REQUESTS, CACHE, KV_HEADS, HEAD_DIM)
    base = mixed_base(key, shape)
    first, second = key_rows(pattern)
    slot = jnp.arange(CACHE)[None, :, None, None]
    return jnp.where(slot == 0, first[None, None], base).astype(jnp.bfloat16)


def draw_cache_len(key, part):
    key = jax.random.fold_in(key, 7)
    lengths = jax.random.randint(key, (REQUESTS,), 1, CACHE + 1)
    lengths = lengths.at[::REQ_DEV].set(CACHE).at[1].set(1)
    return lengths.astype(jnp.int32)


def draw_page_list(key, part):
    key = jax.random.fold_in(key, 11)
    key_pick, key_anchor = jax.random.split(key)
    chosen = jax.random.randint(key_pick, (OWNERS, OWNERS), 0, OWN_PAGES)
    chosen = chosen.at[0, 0].set(0).at[0, OWNERS - 1].set(OWN_PAGES - 1)
    anchor = jax.random.randint(key_anchor, (REQUESTS,), 0, OWNERS)
    anchor = anchor.at[0].set(OWNERS - EXTRA).at[1].set(0)
    owners = (anchor[:, None] + jnp.arange(EXTRA)[None, :]) % OWNERS
    device = jnp.arange(REQUESTS) // REQ_DEV
    return (owners * OWN_PAGES + chosen[device[:, None], owners]).astype(jnp.int32)


def shard_levels(own_key, shape, pieces, low, high):
    level = 1.0
    for dim, blocks in pieces:
        heights = jax.random.uniform(jax.random.fold_in(jax.random.fold_in(own_key, 6), dim), (blocks,), jnp.float32, low / len(pieces), high / len(pieces))
        level = level * jnp.repeat(jnp.exp(heights), shape[dim] // blocks).reshape((-1,) + (1,) * (len(shape) - 1 - dim))
    return level


def centred(stream_key, extent, width, bound, cuts=(), dtype=jnp.bfloat16):
    loudness = shard_levels(stream_key, extent, cuts, -0.22, 0.18) if cuts else 1.0
    drawn = jax.random.normal(stream_key, extent, jnp.float32) * width * loudness
    return jnp.minimum(jnp.maximum(drawn, -bound), bound).astype(dtype)


def setup_inputs(seed: int = 0) -> dict:
    key_of = jax.random.split(jax.random.key(seed), 11)
    return {
        "prefill_q": draw_prefill_q(jax.random.fold_in(key_of[10], 71), 0),
        "prefill_k": draw_prefill_k(jax.random.fold_in(key_of[10], 71), 0),
        "prefill_v": centred(key_of[2], (GROUPS, SPAN, KV_HEADS, HEAD_DIM), 1.0, 6.0, ((0, 4), (1, 4), (2, 2))),
        "decode_q": draw_decode_q(jax.random.fold_in(key_of[10], 71), 0),
        "decode_k": draw_decode_k(jax.random.fold_in(key_of[10], 71), 0),
        "decode_v": centred(key_of[5], (REQUESTS, STEPS, KV_HEADS, HEAD_DIM), 1.0, 6.0, ((0, 16), (2, 2))),
        "cache_k": draw_cache_k(jax.random.fold_in(key_of[10], 71), 0),
        "cache_v": centred(key_of[7], (REQUESTS, CACHE, KV_HEADS, HEAD_DIM), 1.0, 6.0, ((0, 16), (2, 2))),
        "cache_len": draw_cache_len(jax.random.fold_in(key_of[10], 71), 0),
        "page_list": draw_page_list(jax.random.fold_in(key_of[10], 71), 0),
    }


def prefill_group(queries, keys, values):
    group = HEADS // KV_HEADS
    block = min(512, SPAN)
    count = SPAN // block
    inverse_root = 1.0 / math.sqrt(HEAD_DIM)
    grouped = queries.astype(jnp.float32).reshape(count, block, KV_HEADS, group, HEAD_DIM)
    grouped = grouped.transpose(2, 0, 1, 3, 4)
    keys_heads = keys.astype(jnp.float32).transpose(1, 0, 2)
    values_heads = values.astype(jnp.float32).transpose(1, 0, 2)
    columns = jnp.arange(SPAN)
    firsts = jnp.arange(count) * block

    def per_head(inputs):
        query_blocks, key_head, value_head = inputs

        def per_block(block_inputs):
            query_block, first = block_inputs
            rows = first + jnp.arange(block)
            scores = jnp.einsum('qgd,pd->gqp', query_block, key_head) * inverse_root
            allowed = columns[None, :] <= rows[:, None]
            scores = jnp.where(allowed[None], scores, -1e+30)
            peak = lax.optimization_barrier(jnp.max(scores, axis=-1, keepdims=True))
            weights = jnp.where(allowed[None], jnp.exp(scores - peak), 0.0)
            rounded = weights.astype(jnp.bfloat16).astype(jnp.float32)
            summed = jnp.einsum('gqp,pd->gqd', rounded, value_head)
            result = summed / lax.optimization_barrier(jnp.sum(weights, axis=-1))[..., None]
            return result.transpose(1, 0, 2)
        return lax.map(per_block, (query_blocks, firsts))
    outputs = lax.map(per_head, (grouped, keys_heads, values_heads))
    outputs = outputs.transpose(1, 2, 0, 3, 4).reshape(SPAN, HEADS, HEAD_DIM)
    return outputs.astype(jnp.bfloat16)

def reference(prefill_q, prefill_k, prefill_v, decode_q, decode_k, decode_v, cache_k, cache_v, cache_len, page_list):
    prefill_out = jnp.stack([prefill_group(prefill_q[index], prefill_k[index], prefill_v[index]) for index in range(GROUPS)])
    group = HEADS // KV_HEADS
    inverse_root = 1.0 / math.sqrt(HEAD_DIM)
    pool_keys = prefill_k.reshape(POOL, PAGE, KV_HEADS, HEAD_DIM)
    pool_values = prefill_v.reshape(POOL, PAGE, KV_HEADS, HEAD_DIM)
    extra_len = EXTRA * PAGE
    total = extra_len + CACHE + STEPS
    position = jnp.arange(total)
    in_cache = (position >= extra_len) & (position < extra_len + CACHE)
    new_pos = position - extra_len - CACHE
    causal = new_pos[None, :] <= jnp.arange(STEPS)[:, None]

    def per_request(inputs):
        queries, new_keys, new_values, old_keys, old_values, length, pages = inputs
        keys_list = jnp.concatenate([pool_keys[pages].reshape(extra_len, KV_HEADS, HEAD_DIM), old_keys, new_keys], axis=0)
        values_list = jnp.concatenate([pool_values[pages].reshape(extra_len, KV_HEADS, HEAD_DIM), old_values, new_values], axis=0)
        cache_ok = position - extra_len < length
        allowed = jnp.where(in_cache[None, :], cache_ok[None, :], jnp.where(new_pos[None, :] >= 0, causal, True))
        grouped = queries.astype(jnp.float32).reshape(STEPS, KV_HEADS, group, HEAD_DIM)
        scores = jnp.einsum('tkgd,nkd->kgtn', grouped, keys_list.astype(jnp.float32)) * inverse_root
        scores = jnp.where(allowed[None, None], scores, -1e+30)
        peak = lax.optimization_barrier(jnp.max(scores, axis=-1, keepdims=True))
        weights = jnp.where(allowed[None, None], jnp.exp(scores - peak), 0.0)
        rounded = weights.astype(jnp.bfloat16).astype(jnp.float32)
        summed = jnp.einsum('kgtn,nkd->tkgd', rounded, values_list.astype(jnp.float32))
        result = summed / lax.optimization_barrier(jnp.sum(weights, axis=-1)).transpose(2, 0, 1)[..., None]
        return result.reshape(STEPS, HEADS * HEAD_DIM).astype(jnp.bfloat16)
    decode_out = lax.map(per_request, (decode_q, decode_k, decode_v, cache_k, cache_v, cache_len, page_list))
    return (prefill_out, decode_out)
```

```python
import functools
import math

import jax
import jax.numpy as jnp
from jax import lax
from jax.experimental import pallas as pl
from jax.experimental.pallas import tpu as pltpu
from jax.sharding import PartitionSpec as P

PAGE = 128
CHUNKS = 2
LOG2E = 1.4426950408889634
NEG = -1e30
VMEM_LIMIT = 48 * 1024 * 1024


def nt(a, b):
    return lax.dot_general(a, b, (((1,), (1,)), ((), ())), preferred_element_type=jnp.float32)


def nn(a, b):
    return jnp.dot(a, b, preferred_element_type=jnp.float32)


def params():
    return pltpu.CompilerParams(vmem_limit_bytes=VMEM_LIMIT)


def one_hot(out_rows, in_rows, source):
    row = lax.broadcasted_iota(jnp.int32, (out_rows, in_rows), 0)
    col = lax.broadcasted_iota(jnp.int32, (out_rows, in_rows), 1)
    return jnp.where(col == source(row), 1.0, 0.0).astype(jnp.bfloat16)


def split_kernel(heads, per_chunk, tokens, k_ref, v_ref, *outs):
    rows = min(tokens * heads, 256)
    step = rows // heads
    pick = one_hot(rows, rows, lambda i: (i % step) * heads + i // step)
    for which, ref in enumerate((k_ref, v_ref)):
        for j in range(tokens // step):
            moved = nn(pick, ref[pl.ds(j * rows, rows), :]).astype(jnp.bfloat16)
            for h in range(heads):
                outs[h // per_chunk][h % per_chunk, which, pl.ds(j * step, step), :] = moved[
                    h * step : (h + 1) * step
                ]


def split_heads(k, v, chunks):
    _, tokens, heads, width = k.shape
    per_chunk = heads // chunks
    shape = jax.ShapeDtypeStruct((per_chunk, 2, tokens, width), jnp.bfloat16)
    return pl.pallas_call(
        functools.partial(split_kernel, heads, per_chunk, tokens),
        out_shape=[shape] * chunks,
        compiler_params=params(),
        cost_estimate=pl.CostEstimate(flops=10**8, bytes_accessed=2 * 10**6, transcendentals=0),
    )(k.reshape(tokens * heads, width), v.reshape(tokens * heads, width))


def stage_kernel(heads, per_chunk, group, steps, cache, q_ref, dk_ref, dv_ref, ck_ref, cv_ref, *outs):
    chunks = heads // per_chunk
    rows = min(cache * heads, 256)
    step = rows // heads
    pick = one_hot(rows, rows, lambda i: (i % step) * heads + i // step)
    extra = one_hot(
        heads * 16,
        steps * heads,
        lambda i: jnp.where(i % 16 < steps, (i % 16) * heads + i // 16, -1),
    )
    each = group * steps
    q_rows = heads * each
    q_pick = one_hot(
        q_rows,
        q_rows,
        lambda i: (i % steps) * (heads * group) + (i // each) * group + (i % each) // steps,
    )
    for r in range(q_ref.shape[0]):
        moved = nn(q_pick, q_ref[r]).astype(jnp.bfloat16)
        for h in range(heads):
            outs[h // per_chunk][h % per_chunk, r] = moved[h * each : (h + 1) * each]
        for which, (old, new) in enumerate(((ck_ref, dk_ref), (cv_ref, dv_ref))):
            base = (1 + which) * chunks
            for j in range(cache // step):
                moved = nn(pick, old[r, pl.ds(j * rows, rows), :]).astype(jnp.bfloat16)
                for h in range(heads):
                    outs[base + h // per_chunk][h % per_chunk, r, pl.ds(j * step, step), :] = moved[
                        h * step : (h + 1) * step
                    ]
            moved = nn(extra, new[r]).astype(jnp.bfloat16)
            for h in range(heads):
                outs[base + h // per_chunk][h % per_chunk, r, pl.ds(cache, 16), :] = moved[
                    h * 16 : (h + 1) * 16
                ]


def stage_decode(decode_q, decode_k, decode_v, cache_k, cache_v, chunks):
    requests, steps, q_heads, width = decode_q.shape
    heads = cache_k.shape[2]
    cache = cache_k.shape[1]
    group = q_heads // heads
    per_chunk = heads // chunks
    block = min(4, requests)
    q = decode_q.reshape(requests, steps * q_heads, width)
    dk = decode_k.reshape(requests, steps * heads, width)
    dv = decode_v.reshape(requests, steps * heads, width)
    ck = cache_k.reshape(requests, cache * heads, width)
    cv = cache_v.reshape(requests, cache * heads, width)
    in_specs = [
        pl.BlockSpec((block, a.shape[1], width), lambda i: (i, 0, 0)) for a in (q, dk, dv, ck, cv)
    ]
    out_specs, out_shape = [], []
    for length in (group * steps, cache + 16, cache + 16):
        for _ in range(chunks):
            out_specs.append(pl.BlockSpec((per_chunk, block, length, width), lambda i: (0, i, 0, 0)))
            out_shape.append(
                jax.ShapeDtypeStruct((per_chunk, requests, length, width), jnp.bfloat16)
            )
    outs = pl.pallas_call(
        functools.partial(stage_kernel, heads, per_chunk, group, steps, cache),
        grid=(requests // block,),
        in_specs=in_specs,
        out_specs=out_specs,
        out_shape=out_shape,
        compiler_params=params(),
        cost_estimate=pl.CostEstimate(flops=10**9, bytes_accessed=20 * 10**6, transcendentals=0),
    )(q, dk, dv, ck, cv)
    return [(outs[c], outs[chunks + c], outs[2 * chunks + c]) for c in range(chunks)]


def prefill_kernel(
    kinds, group, tokens, scale, earlier_ref, *refs
):
    parts, ring, per_chunk, aliased = kinds
    block = refs[0].shape[1]
    q_ref = refs[0]
    blocks = refs[1 : 1 + parts * ring]
    rest = refs[1 + parts * ring + (1 if aliased else 0) :]
    out_ref, buf, sems = rest
    i = pl.program_id(0)
    heads = parts * per_chunk

    def copies():
        found = []
        place = jnp.int32(0)
        for s in range(1, ring):
            for part in range(parts):
                found.append(
                    (
                        earlier_ref[s],
                        pltpu.make_async_copy(
                            blocks[part * ring + s], buf.at[place, part], sems.at[s, part]
                        ),
                    )
                )
            place = place + earlier_ref[s]
        return found

    @pl.when(i == 0)
    def _():
        for flag, copy in copies():
            @pl.when(flag == 1)
            def _():
                copy.start()
        for flag, copy in copies():
            @pl.when(flag == 1)
            def _():
                copy.wait()

    rows = block * group
    queries = q_ref[0].astype(jnp.float32)
    q = [
        queries[:, h * group : (h + 1) * group, :].reshape(rows, -1).astype(jnp.bfloat16)
        for h in range(heads)
    ]
    row_token = lax.broadcasted_iota(jnp.int32, (rows, tokens), 0) // group + i * block
    column = lax.broadcasted_iota(jnp.int32, (rows, tokens), 1)
    allowed = column <= row_token
    state = []
    for h in range(heads):
        own = blocks[(h // per_chunk) * ring]
        s = nt(q[h], own[h % per_chunk, 0])
        s = jnp.where(allowed, s, NEG)
        m = jnp.max(s, axis=1, keepdims=True)
        p = jnp.exp2((s - m) * scale)
        l = jnp.sum(p, axis=1, keepdims=True)
        acc = nn(p.astype(jnp.bfloat16), own[h % per_chunk, 1])
        state.append((m, l, acc))

    def step(b, state):
        out = []
        for h in range(heads):
            m, l, acc = state[h]
            s = nt(q[h], buf[b, h // per_chunk, h % per_chunk, 0])
            new = jnp.maximum(m, jnp.max(s, axis=1, keepdims=True))
            p = jnp.exp2((s - new) * scale)
            shrink = jnp.exp2((m - new) * scale)
            l = l * shrink + jnp.sum(p, axis=1, keepdims=True)
            acc = acc * shrink + nn(
                p.astype(jnp.bfloat16), buf[b, h // per_chunk, h % per_chunk, 1]
            )
            out.append((new, l, acc))
        return tuple(out)

    state = lax.fori_loop(0, earlier_ref[0], step, tuple(state))
    out = [(acc / l).reshape(block, group, -1) for _, l, acc in state]
    out_ref[0] = jnp.concatenate(out, axis=1).astype(out_ref.dtype)


def prefill(q, parts, earlier, column, previous):
    _, tokens, q_heads, width = q.shape
    ring = len(parts[0])
    per_chunk = parts[0][0].shape[0]
    heads = per_chunk * len(parts)
    group = 8
    block = 64
    q_spec = pl.BlockSpec((1, block, heads * group, width), lambda i, *_: (0, i, column, 0))
    own_spec = pl.BlockSpec(parts[0][0].shape, lambda i, *_: (0, 0, 0, 0))
    any_spec = pl.BlockSpec(memory_space=pl.ANY)
    in_specs = [q_spec]
    operands = [q]
    for part in parts:
        in_specs += [own_spec] + [any_spec] * (ring - 1)
        operands += part
    aliases = {}
    if previous is not None:
        aliases = {1 + len(operands): 0}
        operands.append(previous)
        in_specs.append(any_spec)
    full = q_heads * tokens * tokens * 4 * width * 2
    return pl.pallas_call(
        functools.partial(
            prefill_kernel,
            (len(parts), ring, per_chunk, previous is not None),
            group,
            tokens,
            LOG2E / math.sqrt(width),
        ),
        grid_spec=pltpu.PrefetchScalarGridSpec(
            num_scalar_prefetch=1,
            grid=(tokens // block,),
            in_specs=in_specs,
            out_specs=pl.BlockSpec((1, block, heads * group, width), lambda i, *_: (0, i, column, 0)),
            scratch_shapes=[
                pltpu.VMEM((max(ring - 1, 1), len(parts)) + parts[0][0].shape, jnp.bfloat16),
                pltpu.SemaphoreType.DMA((ring, len(parts))),
            ],
        ),
        out_shape=jax.ShapeDtypeStruct(q.shape, jnp.bfloat16),
        input_output_aliases=aliases,
        compiler_params=params(),
        cost_estimate=pl.CostEstimate(
            flops=full * heads * group // q_heads,
            bytes_accessed=4 * 10**6,
            transcendentals=tokens * heads * group * 1024,
        ),
    )(earlier, *operands)


def decode_kernel(slots, extra, steps, targets, per_block, scale, *refs):
    slot_ref, pick_ref, len_ref, meta_ref = refs[:4]
    q_ref, kc_ref, vc_ref = refs[4:7]
    blocks = refs[7 : 7 + slots]
    outs = refs[7 + slots : 7 + slots + targets]
    buf, sems = refs[7 + slots + targets :]
    i = pl.program_id(0)
    heads, block, q_rows, width = q_ref.shape
    first = ((i + meta_ref[1] * per_block) % (targets * per_block)) * block

    def copies():
        for s in range(slots):
            start = pl.multiple_of(pick_ref[s] * PAGE, PAGE)
            yield pltpu.make_async_copy(
                blocks[s].at[:, :, pl.ds(start, PAGE), :], buf.at[s], sems.at[s]
            )

    @pl.when(i == 0)
    def _():
        for copy in copies():
            copy.start()
        for copy in copies():
            copy.wait()

    length = kc_ref.shape[2]
    cache = length - 16
    column = lax.broadcasted_iota(jnp.int32, (q_rows, length), 1)
    t = lax.broadcasted_iota(jnp.int32, (q_rows, length), 0) % steps
    later = (column >= cache) & (column - cache <= t)

    def attend(r, target):
        request = first + r
        allowed = (column < len_ref[request]) | later
        places = [slot_ref[request * extra + j] for j in range(extra)]
        for h in range(heads):
            q = q_ref[h, r]
            old = jnp.where(allowed, nt(q, kc_ref[h, r]), NEG)
            pages = [nt(q, buf[place, h, 0]) for place in places]
            top = functools.reduce(jnp.maximum, pages)
            m = jnp.maximum(
                jnp.max(top, axis=1, keepdims=True), jnp.max(old, axis=1, keepdims=True)
            )
            p_old = jnp.exp2((old - m) * scale)
            p_pages = [jnp.exp2((s - m) * scale) for s in pages]
            total = jnp.sum(functools.reduce(jnp.add, p_pages), axis=1, keepdims=True)
            total = total + jnp.sum(p_old, axis=1, keepdims=True)
            acc = nn(p_old.astype(jnp.bfloat16), vc_ref[h, r])
            for p, place in zip(p_pages, places):
                acc = acc + nn(p.astype(jnp.bfloat16), buf[place, h, 1])
            target[r, pl.ds(h * q_rows, q_rows), :] = (acc / total).astype(jnp.bfloat16)

    for k in range(targets):
        @pl.when(i // per_block == k)
        def _():
            unroll = min(4, block)

            def body(g, carry):
                for u in range(unroll):
                    attend(g * unroll + u, outs[k])
                return carry

            lax.fori_loop(0, block // unroll, body, 0)


def decode(operands, blocks, scalars, steps, extra, targets):
    q, kc, vc = operands
    heads, requests, q_rows, width = q.shape
    per_target = requests // targets
    block = min(8, per_target)
    per_block = per_target // block
    slots = len(blocks)
    grid = targets * per_block

    def here(i, slot, pick, lens, meta):
        return (0, (i + meta[1] * per_block) % grid, 0, 0)

    in_specs = [pl.BlockSpec((heads, block) + a.shape[2:], here) for a in (q, kc, vc)]
    in_specs += [pl.BlockSpec(memory_space=pl.ANY)] * slots

    def out_index(k):
        return lambda i, *_: (jnp.clip(i - k * per_block, 0, per_block - 1), 0, 0)

    out_specs = [
        pl.BlockSpec((block, heads * q_rows, width), out_index(k)) for k in range(targets)
    ]
    shape = jax.ShapeDtypeStruct((per_target, heads * q_rows, width), jnp.bfloat16)
    keys = extra * PAGE + kc.shape[2]
    return pl.pallas_call(
        functools.partial(
            decode_kernel, slots, extra, steps, targets, per_block, LOG2E / math.sqrt(width)
        ),
        grid_spec=pltpu.PrefetchScalarGridSpec(
            num_scalar_prefetch=4,
            grid=(grid,),
            in_specs=in_specs,
            out_specs=out_specs,
            scratch_shapes=[
                pltpu.VMEM((slots, heads, 2, PAGE, width), jnp.bfloat16),
                pltpu.SemaphoreType.DMA((slots,)),
            ],
        ),
        out_shape=[shape] * targets,
        compiler_params=params(),
        cost_estimate=pl.CostEstimate(
            flops=requests * heads * q_rows * keys * width * 4 * 4,
            bytes_accessed=8 * 10**6,
            transcendentals=requests * heads * q_rows * keys,
        ),
    )(*scalars, q, kc, vc, *blocks)


def join_kernel(targets, chunks, steps, meta_ref, *refs):
    out_ref = refs[-1]
    k = pl.program_id(0)
    rows = refs[0].shape[1]
    each = rows // steps
    for s in range(targets):
        @pl.when(lax.rem(meta_ref[1] + (targets - s), targets) == k)
        def _():
            for c in range(chunks):
                source = refs[s * chunks + c]

                def body(r, carry):
                    value = source[r]
                    for g in range(each):
                        out_ref[r, :, (c * each + g) * 128 : (c * each + g + 1) * 128] = value[
                            g * steps : (g + 1) * steps
                        ]
                    return carry

                lax.fori_loop(0, out_ref.shape[0], body, 0)


def join(pieces, meta, steps, targets, chunks):
    per_target, rows, width = pieces[0].shape
    half = chunks * (rows // steps) * width
    spec = pl.BlockSpec((per_target, rows, width), lambda k, *_: (0, 0, 0))
    return pl.pallas_call(
        functools.partial(join_kernel, targets, chunks, steps),
        grid_spec=pltpu.PrefetchScalarGridSpec(
            num_scalar_prefetch=1,
            grid=(targets,),
            in_specs=[spec] * len(pieces),
            out_specs=pl.BlockSpec((per_target, steps, half), lambda k, *_: (0, 0, k)),
        ),
        out_shape=jax.ShapeDtypeStruct((per_target, steps, half * targets), jnp.bfloat16),
        compiler_params=params(),
        cost_estimate=pl.CostEstimate(flops=0, bytes_accessed=2 * 10**6, transcendentals=0),
    )(meta, *pieces)


def ring_place(index, size):
    return jnp.where(index % 2 == 0, index // 2, size - 1 - index // 2)


def shards(
    roles,
    ring,
    targets,
    prefill_q,
    prefill_k,
    prefill_v,
    decode_q,
    decode_k,
    decode_v,
    cache_k,
    cache_v,
    cache_len,
    page_list,
):
    tokens = prefill_q.shape[1]
    heads = prefill_k.shape[2]
    own_pages = tokens // PAGE
    requests, steps = decode_q.shape[:2]
    extra = page_list.shape[1]
    chunks = math.gcd(CHUNKS, heads)
    role = lax.axis_index("role")
    ctx = lax.axis_index("ctx")
    tp = lax.axis_index("tp")

    order = list(range(0, ring, 2)) + list(range(ring - 1, 0, -2))
    along = [(order[j], order[(j + 1) % ring]) for j in range(ring)]
    flips = [1 << b for b in reversed(range(roles.bit_length() - 1))]

    own = split_heads(prefill_k, prefill_v, chunks)
    gathered = []
    for c in range(chunks):
        line = [own[c]]
        for s in range(1, ring):
            line.append(lax.ppermute(line[-1], "ctx", along))
        by_role = {0: line}
        for flip in flips:
            pairs = [(j, j ^ flip) for j in range(roles)]
            for seen in list(by_role):
                by_role[seen ^ flip] = [lax.ppermute(a, "role", pairs) for a in by_role[seen]]
        gathered.append(by_role)

    owner = page_list // own_pages
    place = (ring_place(ctx, ring) - ring_place(owner % ring, ring)) % ring
    slot = ((owner // ring) ^ role) * ring + place
    hot = slot.reshape(-1, 1) == jnp.arange(roles * ring)[None, :]
    pick = jnp.max(jnp.where(hot, (page_list % own_pages).reshape(-1, 1), 0), axis=0)
    meta = jnp.stack([ctx, tp]).astype(jnp.int32)
    scalars = (
        slot.reshape(-1).astype(jnp.int32),
        pick.astype(jnp.int32),
        cache_len.astype(jnp.int32),
        meta,
    )
    position = jnp.arange(ring)
    before = [order[(order.index(0) - s) % ring] for s in range(ring)]
    del before
    where = ring_place(ctx, ring)
    source = (where - position) % ring
    source_ctx = jnp.where(source < (ring + 1) // 2, 2 * source, 2 * (ring - 1 - source) + 1)
    flags = (source_ctx < ctx).astype(jnp.int32)
    earlier = jnp.where(position == 0, jnp.sum(flags), flags).astype(jnp.int32)

    staged = stage_decode(decode_q, decode_k, decode_v, cache_k, cache_v, chunks)

    pieces = [[] for _ in range(targets)]
    prefill_out = None
    for c in range(chunks):
        prefill_out = prefill(prefill_q, [gathered[c][0]], earlier, c, prefill_out)
        blocks = [a for r in range(roles) for a in gathered[c][r]]
        outs = decode(staged[c], blocks, scalars, steps, extra, targets)
        for s in range(targets):
            if s == 0:
                pieces[0].append(outs[0])
            else:
                shift = [(j, (j + s) % targets) for j in range(targets)]
                pieces[s].append(lax.ppermute(outs[s], "tp", shift))
    decode_out = join(
        [a for piece in pieces for a in piece], meta, steps, targets, chunks
    )
    return (prefill_out, decode_out)


def solution(mesh):
    body = functools.partial(shards, mesh.shape["role"], mesh.shape["ctx"], mesh.shape["tp"])
    return jax.shard_map(
        body,
        mesh=mesh,
        in_specs=(
            P("role", "ctx", "tp", None),
            P("role", "ctx", "tp", None),
            P("role", "ctx", "tp", None),
            P(("role", "ctx"), None, "tp", None),
            P(("role", "ctx"), None, "tp", None),
            P(("role", "ctx"), None, "tp", None),
            P(("role", "ctx"), None, "tp", None),
            P(("role", "ctx"), None, "tp", None),
            P(("role", "ctx")),
            P(("role", "ctx"), None),
        ),
        out_specs=(P("role", "ctx", "tp", None), P(("role", "ctx", "tp"), None, None)),
        check_vma=False,
    )
```

```python
import functools
import math

import jax
import jax.numpy as jnp
from jax import lax
from jax.experimental import pallas as pl
from jax.experimental.pallas import tpu as pltpu
from jax.sharding import PartitionSpec as P

PAGE = 128
CHUNKS = 2
LOG2E = 1.4426950408889634
NEG = -1e30
VMEM_LIMIT = 48 * 1024 * 1024


def nt(a, b):
    return lax.dot_general(a, b, (((1,), (1,)), ((), ())), preferred_element_type=jnp.float32)


def nn(a, b):
    return jnp.dot(a, b, preferred_element_type=jnp.float32)


def tn(a, b):
    return lax.dot_general(a, b, (((0,), (0,)), ((), ())), preferred_element_type=jnp.float32)


def params():
    return pltpu.CompilerParams(vmem_limit_bytes=VMEM_LIMIT)


def one_hot(out_rows, in_rows, source):
    row = lax.broadcasted_iota(jnp.int32, (out_rows, in_rows), 0)
    col = lax.broadcasted_iota(jnp.int32, (out_rows, in_rows), 1)
    return jnp.where(col == source(row), 1.0, 0.0).astype(jnp.bfloat16)


def split_kernel(heads, per_chunk, tokens, k_ref, v_ref, *outs):
    rows = min(tokens * heads, 256)
    step = rows // heads
    pick = one_hot(rows, rows, lambda i: (i % step) * heads + i // step)
    moved = []
    for j in range(tokens // step):
        keys = nn(pick, k_ref[pl.ds(j * rows, rows), :]).astype(jnp.bfloat16)
        moved.append(nn(pick, v_ref[pl.ds(j * rows, rows), :]))
        for h in range(heads):
            outs[h // per_chunk][h % per_chunk, 0, pl.ds(j * step, step), :] = keys[
                h * step : (h + 1) * step
            ]
    for h in range(heads):
        values = jnp.concatenate([a[h * step : (h + 1) * step] for a in moved], axis=0)
        for page in range(tokens // PAGE):
            outs[h // per_chunk][h % per_chunk, 1, pl.ds(page * PAGE, PAGE), :] = values[
                page * PAGE : (page + 1) * PAGE
            ].T.astype(jnp.bfloat16)


def split_heads(k, v, chunks):
    _, tokens, heads, width = k.shape
    per_chunk = heads // chunks
    shape = jax.ShapeDtypeStruct((per_chunk, 2, tokens, width), jnp.bfloat16)
    return pl.pallas_call(
        functools.partial(split_kernel, heads, per_chunk, tokens),
        out_shape=[shape] * chunks,
        compiler_params=params(),
        cost_estimate=pl.CostEstimate(flops=10**8, bytes_accessed=2 * 10**6, transcendentals=0),
    )(k.reshape(tokens * heads, width), v.reshape(tokens * heads, width))


def prefill_kernel(ring, aliased, group, tokens, scale, earlier_ref, *refs):
    q_ref = refs[0]
    blocks = refs[1 : 1 + ring]
    out_ref, buf, m_ref, l_ref, acc_ref, sems = refs[1 + ring + aliased :]
    own = blocks[0]
    heads = own.shape[0]
    block = q_ref.shape[1]
    i = pl.program_id(0)

    def copies():
        found = []
        place = jnp.int32(0)
        for s in range(1, ring):
            copy = pltpu.make_async_copy(blocks[s], buf.at[place], sems.at[s])
            found.append((earlier_ref[s], copy))
            place = place + earlier_ref[s]
        return found

    @pl.when(i == 0)
    def _():
        for flag, copy in copies():
            @pl.when(flag == 1)
            def _():
                copy.start()
        for flag, copy in copies():
            @pl.when(flag == 1)
            def _():
                copy.wait()

    rows = block * group
    queries = q_ref[0].astype(jnp.float32)
    q = [
        queries[:, h * group : (h + 1) * group, :].reshape(rows, -1).astype(jnp.bfloat16)
        for h in range(heads)
    ]

    def first(keys):
        token = lax.broadcasted_iota(jnp.int32, (keys, rows), 1) // group + i * block
        allowed = lax.broadcasted_iota(jnp.int32, (keys, rows), 0) <= token
        for h in range(heads):
            s = jnp.where(allowed, nt(own[h, 0, pl.ds(0, keys), :], q[h]), NEG)
            m = jnp.max(s, axis=0, keepdims=True)
            p = jnp.exp2((s - m) * scale)
            m_ref[h] = m
            l_ref[h] = jnp.sum(p, axis=0, keepdims=True)
            p = p.astype(jnp.bfloat16)
            values = [own[h, 1, pl.ds(j * PAGE, PAGE), :] for j in range(keys // PAGE)]
            acc_ref[h] = nn(jnp.concatenate(values, axis=1), p)

    pages = tokens // PAGE
    for j in range(pages):
        @pl.when((i * block) // PAGE == j)
        def _():
            first((j + 1) * PAGE)

    def step(b, carry):
        for h in range(heads):
            s = nt(buf[b, h, 0], q[h])
            m = m_ref[h]
            new = jnp.maximum(m, jnp.max(s, axis=0, keepdims=True))
            p = jnp.exp2((s - new) * scale)
            shrink = jnp.exp2((m - new) * scale)
            m_ref[h] = new
            l_ref[h] = l_ref[h] * shrink + jnp.sum(p, axis=0, keepdims=True)
            p = p.astype(jnp.bfloat16)
            values = [buf[b, h, 1, pl.ds(j * PAGE, PAGE), :] for j in range(pages)]
            acc_ref[h] = acc_ref[h] * shrink + nn(jnp.concatenate(values, axis=1), p)
        return carry

    lax.fori_loop(0, earlier_ref[0], step, 0)
    out = [(acc_ref[h] / l_ref[h]).T.reshape(block, group, -1) for h in range(heads)]
    out_ref[0] = jnp.concatenate(out, axis=1).astype(out_ref.dtype)


def prefill(q, blocks, earlier, column, previous):
    _, tokens, q_heads, width = q.shape
    ring = len(blocks)
    heads = blocks[0].shape[0]
    group = 8
    block = 64
    rows = block * group
    q_spec = pl.BlockSpec((1, block, heads * group, width), lambda i, *_: (0, i, column, 0))
    own_spec = pl.BlockSpec(blocks[0].shape, lambda i, *_: (0, 0, 0, 0))
    any_spec = pl.BlockSpec(memory_space=pl.ANY)
    in_specs = [q_spec, own_spec] + [any_spec] * (ring - 1)
    operands = [q] + list(blocks)
    aliases = {}
    if previous is not None:
        aliases = {1 + len(operands): 0}
        operands.append(previous)
        in_specs.append(any_spec)
    return pl.pallas_call(
        functools.partial(
            prefill_kernel,
            ring,
            len(aliases),
            group,
            tokens,
            LOG2E / math.sqrt(width),
        ),
        grid_spec=pltpu.PrefetchScalarGridSpec(
            num_scalar_prefetch=1,
            grid=(tokens // block,),
            in_specs=in_specs,
            out_specs=q_spec,
            scratch_shapes=[
                pltpu.VMEM((max(ring - 1, 1),) + blocks[0].shape, jnp.bfloat16),
                pltpu.VMEM((heads, 1, rows), jnp.float32),
                pltpu.VMEM((heads, 1, rows), jnp.float32),
                pltpu.VMEM((heads, width, rows), jnp.float32),
                pltpu.SemaphoreType.DMA((ring,)),
            ],
        ),
        out_shape=jax.ShapeDtypeStruct(q.shape, jnp.bfloat16),
        input_output_aliases=aliases,
        compiler_params=params(),
        cost_estimate=pl.CostEstimate(
            flops=16 * heads * group * tokens * tokens * ring * width,
            bytes_accessed=4 * 10**6,
            transcendentals=tokens * tokens * ring * heads * group,
        ),
    )(earlier, *operands)


def decode_kernel(
    slots, extra, steps, target, targets, chunk, kv_heads, group, scale, pack, unroll, *refs
):
    slot_ref, pick_ref, len_ref, meta_ref = refs[:4]
    q_ref, dk_ref, dv_ref, ck_ref, cv_ref = refs[4:9]
    blocks = refs[9 : 9 + slots]
    out_ref, buf, sems = refs[9 + slots :]
    heads = buf.shape[1]
    block = q_ref.shape[0]
    width = q_ref.shape[2]
    blocks_each = pl.num_programs(0)
    i = pl.program_id(0)
    first = (lax.rem(meta_ref[1] + target, targets) * blocks_each + i) * block

    def copies():
        for s in range(slots):
            start = pl.multiple_of(pick_ref[s] * PAGE, PAGE)
            yield pltpu.make_async_copy(
                blocks[s].at[:, :, pl.ds(start, PAGE), :], buf.at[s], sems.at[s]
            )

    @pl.when(i == 0)
    def _():
        for copy in copies():
            copy.start()
        for copy in copies():
            copy.wait()

    per_step = heads * group
    per_request = steps * per_step
    lanes = pack * per_request
    units = [(p, h) for p in range(pack) for h in range(heads)]

    def unit_of(index):
        return index // per_request * heads + index % per_step // group

    q_row = lax.broadcasted_iota(jnp.int32, (lanes, width), 0)
    unit_rows = [
        jnp.where(unit_of(q_row) == u, 1.0, 0.0).astype(jnp.bfloat16) for u in range(len(units))
    ]
    request_rows = [
        jnp.where(q_row // per_request == p, 1.0, 0.0).astype(jnp.bfloat16) for p in range(pack)
    ]
    lane = lax.broadcasted_iota(jnp.int32, (width, lanes), 1)
    lane_unit = unit_of(lane)
    lane_request = lane // per_request

    def raw_mask(rows):
        row = lax.broadcasted_iota(jnp.int32, (rows, lanes), 0)
        column = lax.broadcasted_iota(jnp.int32, (rows, lanes), 1)
        same = row % kv_heads == column % per_step // group + chunk * heads
        return jnp.where(same, row // kv_heads, 1 << 20), column

    cache_place, _ = raw_mask(ck_ref.shape[1])
    new_place, new_column = raw_mask(dk_ref.shape[1])
    new_allowed = new_place <= new_column % per_request // per_step
    one_lane = lax.broadcasted_iota(jnp.int32, (1, lanes), 1) // per_request
    order = one_hot(
        lanes,
        lanes,
        lambda r: r // per_request * per_request
        + r % steps * per_step
        + r % per_request // steps,
    )

    def queries(r):
        if heads == kv_heads:
            return q_ref[r]
        total = kv_heads * group
        return jnp.concatenate(
            [
                q_ref[r, pl.ds(t * total + chunk * per_step, per_step), :]
                for t in range(steps)
            ],
            axis=0,
        )

    def attend(sets):
        scores = []
        for s in sets:
            base = s * pack
            q = [queries(base + p) for p in range(pack)]
            q = q[0] if pack == 1 else jnp.concatenate(q, axis=0)
            q_units = jnp.concatenate([q * a for a in unit_rows], axis=1)
            q_raw = q if pack == 1 else jnp.concatenate([q * a for a in request_rows], axis=1)
            places = [
                [slot_ref[(first + base + p) * extra + j] for j in range(extra)]
                for p in range(pack)
            ]
            keys = jnp.concatenate(
                [
                    jnp.concatenate([buf[places[p][j], h, 0] for p, h in units], axis=1)
                    for j in range(extra)
                ],
                axis=0,
            )
            raw = jnp.concatenate([ck_ref[base + p] for p in range(pack)], axis=1)
            new = jnp.concatenate([dk_ref[base + p] for p in range(pack)], axis=1)
            length = jnp.zeros((1, lanes), jnp.int32)
            for p in range(pack):
                length = jnp.where(one_lane == p, len_ref[first + base + p], length)
            scores.append(
                (
                    base,
                    places,
                    nt(keys, q_units),
                    jnp.where(cache_place < length, nt(raw, q_raw), NEG),
                    jnp.where(new_allowed, nt(new, q_raw), NEG),
                )
            )
        weights = []
        for base, places, pages, old, new in scores:
            m = jnp.maximum(
                jnp.max(pages, axis=0, keepdims=True), jnp.max(old, axis=0, keepdims=True)
            )
            m = jnp.maximum(m, jnp.max(new, axis=0, keepdims=True))
            pages = jnp.exp2((pages - m) * scale)
            old = jnp.exp2((old - m) * scale)
            new = jnp.exp2((new - m) * scale)
            total = (
                jnp.sum(pages, axis=0, keepdims=True)
                + jnp.sum(old, axis=0, keepdims=True)
                + jnp.sum(new, axis=0, keepdims=True)
            )
            weights.append(
                (
                    base,
                    places,
                    pages.astype(jnp.bfloat16),
                    old.astype(jnp.bfloat16),
                    new.astype(jnp.bfloat16),
                    total,
                )
            )
        for base, places, pages, old, new, total in weights:
            values = jnp.concatenate(
                [
                    jnp.concatenate([buf[places[p][j], h, 1] for j in range(extra)], axis=1)
                    for p, h in units
                ],
                axis=0,
            )
            every = nn(values, pages)
            acc = jnp.zeros((width, lanes), jnp.float32)
            for u in range(len(units)):
                acc = jnp.where(lane_unit == u, every[u * width : (u + 1) * width], acc)
            rest = jnp.zeros((width, lanes), jnp.float32)
            for p in range(pack):
                part = tn(cv_ref[base + p], old) + tn(dv_ref[base + p], new)
                rest = part if pack == 1 else jnp.where(lane_request == p, part, rest)
            result = ((acc + rest) / total).astype(jnp.bfloat16)
            result = nt(order, result).astype(jnp.bfloat16)
            for p in range(pack):
                out_ref[base + p] = result[p * per_request : (p + 1) * per_request]

    def body(g, carry):
        attend([g * unroll + u for u in range(unroll)])
        return carry

    lax.fori_loop(0, block // (pack * unroll), body, 0)


def decode(arrays, blocks, scalars, chunk, target, targets, extra):
    q, dk, dv, ck, cv = arrays
    requests, steps, q_heads, width = q.shape
    kv_heads = ck.shape[2]
    group = q_heads // kv_heads
    heads = blocks[0].shape[0]
    pack = max(1, 4 // heads)
    per_target = requests // targets
    block = min(8, per_target)
    pack = math.gcd(pack, block)
    unroll = math.gcd(2, block // pack)
    per_block = per_target // block
    slots = len(blocks)
    raw = [a.reshape(requests, -1, width) for a in (q, dk, dv, ck, cv)]
    per_request = heads * group * steps

    def here(i, slot, pick, lens, meta):
        return (lax.rem(meta[1] + target, targets) * per_block + i, 0, 0)

    in_specs = [pl.BlockSpec((block,) + a.shape[1:], here) for a in raw]
    in_specs += [pl.BlockSpec(memory_space=pl.ANY)] * slots
    keys = extra * PAGE + ck.shape[1]
    return pl.pallas_call(
        functools.partial(
            decode_kernel,
            slots,
            extra,
            steps,
            target,
            targets,
            chunk,
            kv_heads,
            group,
            LOG2E / math.sqrt(width),
            pack,
            unroll,
        ),
        grid_spec=pltpu.PrefetchScalarGridSpec(
            num_scalar_prefetch=4,
            grid=(per_block,),
            in_specs=in_specs,
            out_specs=pl.BlockSpec((block, per_request, width), lambda i, *_: (i, 0, 0)),
            scratch_shapes=[
                pltpu.VMEM((slots, heads, 2, PAGE, width), jnp.bfloat16),
                pltpu.SemaphoreType.DMA((slots,)),
            ],
        ),
        out_shape=jax.ShapeDtypeStruct((per_target, per_request, width), jnp.bfloat16),
        compiler_params=params(),
        cost_estimate=pl.CostEstimate(
            flops=per_target * per_request * keys * width * 4 * 4,
            bytes_accessed=8 * 10**6,
            transcendentals=per_target * per_request * keys,
        ),
    )(*scalars, *raw, *blocks)


def join_kernel(targets, chunks, steps, meta_ref, *refs):
    out_ref = refs[-1]
    k = pl.program_id(0)
    rows = refs[0].shape[1]
    each = rows // steps
    for s in range(targets):
        @pl.when(lax.rem(meta_ref[1] + (targets - s), targets) == k)
        def _():
            for c in range(chunks):
                source = refs[s * chunks + c]

                def body(r, carry):
                    value = source[r]
                    for g in range(each):
                        out_ref[r, :, (c * each + g) * 128 : (c * each + g + 1) * 128] = value[
                            g * steps : (g + 1) * steps
                        ]
                    return carry

                lax.fori_loop(0, out_ref.shape[0], body, 0)


def join(pieces, meta, steps, targets, chunks):
    per_target, rows, width = pieces[0].shape
    half = chunks * (rows // steps) * width
    spec = pl.BlockSpec((per_target, rows, width), lambda k, *_: (0, 0, 0))
    return pl.pallas_call(
        functools.partial(join_kernel, targets, chunks, steps),
        grid_spec=pltpu.PrefetchScalarGridSpec(
            num_scalar_prefetch=1,
            grid=(targets,),
            in_specs=[spec] * len(pieces),
            out_specs=pl.BlockSpec((per_target, steps, half), lambda k, *_: (0, 0, k)),
        ),
        out_shape=jax.ShapeDtypeStruct((per_target, steps, half * targets), jnp.bfloat16),
        compiler_params=params(),
        cost_estimate=pl.CostEstimate(flops=0, bytes_accessed=2 * 10**6, transcendentals=0),
    )(meta, *pieces)


def ring_place(index, size):
    return jnp.where(index % 2 == 0, index // 2, size - 1 - index // 2)


def shards(
    roles,
    ring,
    targets,
    prefill_q,
    prefill_k,
    prefill_v,
    decode_q,
    decode_k,
    decode_v,
    cache_k,
    cache_v,
    cache_len,
    page_list,
):
    tokens = prefill_q.shape[1]
    heads = prefill_k.shape[2]
    own_pages = tokens // PAGE
    requests, steps = decode_q.shape[:2]
    extra = page_list.shape[1]
    chunks = math.gcd(CHUNKS, heads)
    role = lax.axis_index("role")
    ctx = lax.axis_index("ctx")
    tp = lax.axis_index("tp")

    order = list(range(0, ring, 2)) + list(range(ring - 1, 0, -2))
    along = [(order[j], order[(j + 1) % ring]) for j in range(ring)]
    flips = [1 << b for b in reversed(range(roles.bit_length() - 1))]

    own = split_heads(prefill_k, prefill_v, chunks)
    gathered = []
    for c in range(chunks):
        line = [own[c]]
        for s in range(1, ring):
            line.append(lax.ppermute(line[-1], "ctx", along))
        by_role = {0: line}
        for flip in flips:
            pairs = [(j, j ^ flip) for j in range(roles)]
            for seen in list(by_role):
                by_role[seen ^ flip] = [lax.ppermute(a, "role", pairs) for a in by_role[seen]]
        gathered.append(by_role)

    owner = page_list // own_pages
    place = (ring_place(ctx, ring) - ring_place(owner % ring, ring)) % ring
    slot = ((owner // ring) ^ role) * ring + place
    hot = slot.reshape(-1, 1) == jnp.arange(roles * ring)[None, :]
    pick = jnp.max(jnp.where(hot, (page_list % own_pages).reshape(-1, 1), 0), axis=0)
    meta = jnp.stack([ctx, tp]).astype(jnp.int32)
    scalars = (
        slot.reshape(-1).astype(jnp.int32),
        pick.astype(jnp.int32),
        cache_len.astype(jnp.int32),
        meta,
    )
    position = jnp.arange(ring)
    where = ring_place(ctx, ring)
    source = (where - position) % ring
    source_ctx = jnp.where(source < (ring + 1) // 2, 2 * source, 2 * (ring - 1 - source) + 1)
    flags = (source_ctx < ctx).astype(jnp.int32)
    earlier = jnp.where(position == 0, jnp.sum(flags), flags).astype(jnp.int32)

    arrays = (decode_q, decode_k, decode_v, cache_k, cache_v)
    pieces = [[] for _ in range(targets)]
    prefill_out = None
    for c in range(chunks):
        prefill_out = prefill(prefill_q, gathered[c][0], earlier, c, prefill_out)
        blocks = [a for r in range(roles) for a in gathered[c][r]]
        for s in reversed(range(targets)):
            out = decode(arrays, blocks, scalars, c, s, targets, extra)
            if s:
                shift = [(j, (j + s) % targets) for j in range(targets)]
                out = lax.ppermute(out, "tp", shift)
            pieces[s].append(out)
    decode_out = join(
        [a for piece in pieces for a in piece], meta, steps, targets, chunks
    )
    return (prefill_out, decode_out)


def solution(mesh):
    body = functools.partial(shards, mesh.shape["role"], mesh.shape["ctx"], mesh.shape["tp"])
    return jax.shard_map(
        body,
        mesh=mesh,
        in_specs=(
            P("role", "ctx", "tp", None),
            P("role", "ctx", "tp", None),
            P("role", "ctx", "tp", None),
            P(("role", "ctx"), None, "tp", None),
            P(("role", "ctx"), None, "tp", None),
            P(("role", "ctx"), None, "tp", None),
            P(("role", "ctx"), None, "tp", None),
            P(("role", "ctx"), None, "tp", None),
            P(("role", "ctx")),
            P(("role", "ctx"), None),
        ),
        out_specs=(P("role", "ctx", "tp", None), P(("role", "ctx", "tp"), None, None)),
        check_vma=False,
    )
```

```python
import functools
import math

import jax
import jax.numpy as jnp
from jax import lax
from jax.experimental import pallas as pl
from jax.experimental.pallas import tpu as pltpu
from jax.sharding import PartitionSpec as P

PAGE = 128
LOG2E = 1.4426950408889634
NEG = -1e30
VMEM_LIMIT = 48 * 1024 * 1024


def nt(a, b):
    return lax.dot_general(a, b, (((1,), (1,)), ((), ())), preferred_element_type=jnp.float32)


def nn(a, b):
    return jnp.dot(a, b, preferred_element_type=jnp.float32)


def params():
    return pltpu.CompilerParams(vmem_limit_bytes=VMEM_LIMIT)


def one_hot(out_rows, in_rows, source):
    row = lax.broadcasted_iota(jnp.int32, (out_rows, in_rows), 0)
    col = lax.broadcasted_iota(jnp.int32, (out_rows, in_rows), 1)
    return jnp.where(col == source(row), 1.0, 0.0).astype(jnp.bfloat16)


def split_kernel(heads, tokens, k_ref, v_ref, out_ref):
    rows = min(tokens * heads, 256)
    step = rows // heads
    pick = one_hot(rows, rows, lambda i: (i % step) * heads + i // step)
    moved = []
    for j in range(tokens // step):
        moved.append(nn(pick, k_ref[pl.ds(j * rows, rows), :]))
        values = nn(pick, v_ref[pl.ds(j * rows, rows), :]).astype(jnp.bfloat16)
        for h in range(heads):
            out_ref[h, 1, pl.ds(j * step, step), :] = values[h * step : (h + 1) * step]
    for h in range(heads):
        keys = jnp.concatenate([a[h * step : (h + 1) * step] for a in moved], axis=0)
        for page in range(tokens // PAGE):
            out_ref[h, 0, pl.ds(page * PAGE, PAGE), :] = keys[
                page * PAGE : (page + 1) * PAGE
            ].T.astype(jnp.bfloat16)


def split_heads(k, v):
    _, tokens, heads, width = k.shape
    return pl.pallas_call(
        functools.partial(split_kernel, heads, tokens),
        out_shape=jax.ShapeDtypeStruct((heads, 2, tokens, width), jnp.bfloat16),
        compiler_params=params(),
        cost_estimate=pl.CostEstimate(flops=10**8, bytes_accessed=2 * 10**6, transcendentals=0),
    )(k.reshape(tokens * heads, width), v.reshape(tokens * heads, width))


def prefill_kernel(ring, group, tokens, scale, earlier_ref, *refs):
    q_ref = refs[0]
    blocks = refs[1 : 1 + ring]
    out_ref, buf, s_ref, m_ref, l_ref, acc_ref, sems = refs[1 + ring :]
    own = blocks[0]
    heads = own.shape[0]
    block = q_ref.shape[1]
    pages = tokens // PAGE
    i = pl.program_id(0)

    def copies():
        found = []
        place = jnp.int32(0)
        for s in range(1, ring):
            copy = pltpu.make_async_copy(blocks[s], buf.at[place], sems.at[s])
            found.append((earlier_ref[s], copy))
            place = place + earlier_ref[s]
        return found

    @pl.when(i == 0)
    def _():
        for flag, copy in copies():
            @pl.when(flag == 1)
            def _():
                copy.start()
        for flag, copy in copies():
            @pl.when(flag == 1)
            def _():
                copy.wait()

    rows = block * group
    queries = q_ref[0].astype(jnp.float32)
    q = [
        queries[:, h * group : (h + 1) * group, :].reshape(rows, -1).astype(jnp.bfloat16)
        for h in range(heads)
    ]

    def fold(a, op):
        return functools.reduce(op, [a[:, j * 128 : (j + 1) * 128] for j in range(a.shape[1] // 128)])

    token = lax.broadcasted_iota(jnp.int32, (rows, tokens), 0) // group + i * block
    allowed = lax.broadcasted_iota(jnp.int32, (rows, tokens), 1) <= token

    def keys(ref, h):
        return jnp.concatenate([ref[h, 0, pl.ds(j * PAGE, PAGE), :] for j in range(pages)], axis=1)

    last = ring - 1
    for h in range(heads):
        s = jnp.where(allowed, nn(q[h], keys(own, h)), NEG)
        s_ref[last, h] = s
        m_ref[h] = fold(s, jnp.maximum)

    def look(b, carry):
        for h in range(heads):
            s = nn(q[h], keys(buf.at[b], h))
            s_ref[b, h] = s
            m_ref[h] = jnp.maximum(m_ref[h], fold(s, jnp.maximum))
        return carry

    lax.fori_loop(0, earlier_ref[0], look, 0)
    for h in range(heads):
        m = jnp.max(m_ref[h], axis=1, keepdims=True)
        m_ref[h] = jnp.broadcast_to(m, m_ref.shape[1:])
        p = jnp.exp2((s_ref[last, h] - m) * scale)
        l_ref[h] = fold(p, jnp.add)
        acc_ref[h] = nn(p.astype(jnp.bfloat16), own[h, 1])

    def weigh(b, carry):
        for h in range(heads):
            m = m_ref[h]
            p = [
                jnp.exp2((s_ref[b, h, :, pl.ds(j * 128, 128)] - m) * scale)
                for j in range(tokens // 128)
            ]
            l_ref[h] = l_ref[h] + functools.reduce(jnp.add, p)
            p = jnp.concatenate([a.astype(jnp.bfloat16) for a in p], axis=1)
            acc_ref[h] = acc_ref[h] + nn(p, buf[b, h, 1])
        return carry

    lax.fori_loop(0, earlier_ref[0], weigh, 0)
    out = []
    for h in range(heads):
        total = jnp.sum(l_ref[h], axis=1, keepdims=True)
        out.append((acc_ref[h] / total).reshape(block, group, -1))
    out_ref[0] = jnp.concatenate(out, axis=1).astype(out_ref.dtype)


def prefill(q, blocks, earlier):
    _, tokens, q_heads, width = q.shape
    ring = len(blocks)
    heads = blocks[0].shape[0]
    group = q_heads // heads
    block = 64
    rows = block * group
    q_spec = pl.BlockSpec((1, block, q_heads, width), lambda i, *_: (0, i, 0, 0))
    own_spec = pl.BlockSpec(blocks[0].shape, lambda i, *_: (0, 0, 0, 0))
    return pl.pallas_call(
        functools.partial(prefill_kernel, ring, group, tokens, LOG2E / math.sqrt(width)),
        grid_spec=pltpu.PrefetchScalarGridSpec(
            num_scalar_prefetch=1,
            grid=(tokens // block,),
            in_specs=[q_spec, own_spec] + [pl.BlockSpec(memory_space=pl.ANY)] * (ring - 1),
            out_specs=q_spec,
            scratch_shapes=[
                pltpu.VMEM((max(ring - 1, 1),) + blocks[0].shape, jnp.bfloat16),
                pltpu.VMEM((ring, heads, rows, tokens), jnp.float32),
                pltpu.VMEM((heads, rows, width), jnp.float32),
                pltpu.VMEM((heads, rows, width), jnp.float32),
                pltpu.VMEM((heads, rows, width), jnp.float32),
                pltpu.SemaphoreType.DMA((ring,)),
            ],
        ),
        out_shape=jax.ShapeDtypeStruct(q.shape, jnp.bfloat16),
        compiler_params=params(),
        cost_estimate=pl.CostEstimate(
            flops=16 * q_heads * tokens * tokens * ring * width,
            bytes_accessed=4 * 10**6,
            transcendentals=tokens * tokens * ring * q_heads,
        ),
    )(earlier, q, *blocks)


def by_head(raw, steps, heads, group):
    raw = raw.astype(jnp.float32)
    return jnp.concatenate(
        [
            raw[(t * heads + h) * group : (t * heads + h + 1) * group]
            for h in range(heads)
            for t in range(steps)
        ],
        axis=0,
    ).astype(jnp.bfloat16)


def cache_kernel(steps, heads, group, scale, len_ref, q_ref, dk_ref, dv_ref, ck_ref, cv_ref, acc_ref, ml_ref):
    block, rows, width = q_ref.shape
    cache = ck_ref.shape[1]
    new = dk_ref.shape[1]

    def mask(columns):
        row = lax.broadcasted_iota(jnp.int32, (rows, columns), 0)
        column = lax.broadcasted_iota(jnp.int32, (rows, columns), 1)
        same = column % heads == row // (steps * group)
        return jnp.where(same, column // heads, 1 << 20), row % (steps * group) // group

    place, _ = mask(cache)
    new_place, step = mask(new)
    new_allowed = new_place <= step
    half = lax.broadcasted_iota(jnp.int32, (rows, width), 1) < width // 2
    first = pl.program_id(0) * block
    unroll = math.gcd(4, block)

    def body(g, carry):
        scores = []
        for u in range(unroll):
            r = g * unroll + u
            q = by_head(q_ref[r], steps, heads, group)
            old = jnp.where(place < len_ref[first + r], nt(q, ck_ref[r]), NEG)
            add = jnp.where(new_allowed, nt(q, dk_ref[r]), NEG)
            scores.append((r, old, add))
        weights = []
        for r, old, add in scores:
            m = jnp.maximum(
                jnp.max(old, axis=1, keepdims=True), jnp.max(add, axis=1, keepdims=True)
            )
            old = jnp.exp2((old - m) * scale)
            add = jnp.exp2((add - m) * scale)
            l = jnp.sum(old, axis=1, keepdims=True) + jnp.sum(add, axis=1, keepdims=True)
            ml_ref[r] = jnp.where(half, m, l)
            weights.append((r, old.astype(jnp.bfloat16), add.astype(jnp.bfloat16)))
        for r, old, add in weights:
            acc_ref[r] = nn(old, cv_ref[r]) + nn(add, dv_ref[r])
        return carry

    lax.fori_loop(0, block // unroll, body, 0)


def cache_part(q, dk, dv, ck, cv, lens, steps, heads, group):
    requests, rows, width = q.shape
    block = math.gcd(8, requests)
    spec = [
        pl.BlockSpec((block,) + a.shape[1:], lambda i, *_: (i, 0, 0)) for a in (q, dk, dv, ck, cv)
    ]
    out = pl.BlockSpec((block, rows, width), lambda i, *_: (i, 0, 0))
    shape = jax.ShapeDtypeStruct((requests, rows, width), jnp.float32)
    return pl.pallas_call(
        functools.partial(cache_kernel, steps, heads, group, LOG2E / math.sqrt(width)),
        grid_spec=pltpu.PrefetchScalarGridSpec(
            num_scalar_prefetch=1, grid=(requests // block,), in_specs=spec, out_specs=[out, out]
        ),
        out_shape=[shape, shape],
        compiler_params=params(),
        cost_estimate=pl.CostEstimate(
            flops=requests * rows * ck.shape[1] * width * 16,
            bytes_accessed=14 * 10**6,
            transcendentals=requests * rows * ck.shape[1],
        ),
    )(lens, q, dk, dv, ck, cv)


def decode_kernel(slots, extra, steps, target, targets, heads, group, scale, *refs):
    slot_ref, pick_ref, meta_ref = refs[:3]
    q_ref, acc_ref, ml_ref = refs[3:6]
    blocks = refs[6 : 6 + slots]
    out_ref, buf, sems = refs[6 + slots :]
    block, rows, width = q_ref.shape
    i = pl.program_id(0)
    first = (lax.rem(meta_ref[1] + target, targets) * pl.num_programs(0) + i) * block

    def copies():
        for s in range(slots):
            start = pl.multiple_of(pick_ref[s] * PAGE, PAGE)
            yield pltpu.make_async_copy(
                blocks[s].at[:, :, pl.ds(start, PAGE), :], buf.at[s], sems.at[s]
            )

    @pl.when(i == 0)
    def _():
        for copy in copies():
            copy.start()
        for copy in copies():
            copy.wait()

    each = steps * group
    wide = math.gcd(2, heads)
    order = one_hot(
        rows, rows, lambda r: r // each * each + r % steps * group + r % each // steps
    )
    unroll = math.gcd(2, block)

    def body(g, carry):
        scores = []
        for u in range(unroll):
            r = g * unroll + u
            q = by_head(q_ref[r], steps, heads, group)
            places = [slot_ref[(first + r) * extra + j] for j in range(extra)]
            s = [
                nn(
                    q[h * each : (h + 1) * each],
                    jnp.concatenate([buf[place, h, 0] for place in places], axis=1),
                )
                for h in range(heads)
            ]
            scores.append((r, places, jnp.concatenate(s, axis=0)))
        weights = []
        for r, places, s in scores:
            ml = ml_ref[r]
            old, l = ml[:, :1], ml[:, width // 2 : width // 2 + 1]
            m = jnp.maximum(jnp.max(s, axis=1, keepdims=True), old)
            p = jnp.exp2((s - m) * scale)
            shrink = jnp.exp2((old - m) * scale)
            l = l * shrink + jnp.sum(p, axis=1, keepdims=True)
            weights.append((r, places, p.astype(jnp.bfloat16), shrink, l))
        for r, places, p, shrink, l in weights:
            parts = []
            for h in range(0, heads, wide):
                values = jnp.concatenate(
                    [
                        jnp.concatenate([buf[place, h + w, 1] for w in range(wide)], axis=1)
                        for place in places
                    ],
                    axis=0,
                )
                both = nn(p[h * each : (h + wide) * each], values)
                for w in range(wide):
                    parts.append(both[w * each : (w + 1) * each, w * width : (w + 1) * width])
            acc = acc_ref[r] * shrink + jnp.concatenate(parts, axis=0)
            result = (acc / l).astype(jnp.bfloat16)
            out_ref[r] = nn(order, result).astype(jnp.bfloat16)
        return carry

    lax.fori_loop(0, block // unroll, body, 0)


def decode(q, acc, ml, blocks, scalars, target, targets, extra, steps, heads, group):
    requests, rows, width = q.shape
    per_target = requests // targets
    block = math.gcd(8, per_target)
    per_block = per_target // block
    slots = len(blocks)

    def here(i, slot, pick, meta):
        return (lax.rem(meta[1] + target, targets) * per_block + i, 0, 0)

    in_specs = [pl.BlockSpec((block, rows, width), here)] * 3
    in_specs += [pl.BlockSpec(memory_space=pl.ANY)] * slots
    return pl.pallas_call(
        functools.partial(
            decode_kernel,
            slots,
            extra,
            steps,
            target,
            targets,
            heads,
            group,
            LOG2E / math.sqrt(width),
        ),
        grid_spec=pltpu.PrefetchScalarGridSpec(
            num_scalar_prefetch=3,
            grid=(per_block,),
            in_specs=in_specs,
            out_specs=pl.BlockSpec((block, rows, width), lambda i, *_: (i, 0, 0)),
            scratch_shapes=[
                pltpu.VMEM((slots, heads, 2, PAGE, width), jnp.bfloat16),
                pltpu.SemaphoreType.DMA((slots,)),
            ],
        ),
        out_shape=jax.ShapeDtypeStruct((per_target, rows, width), jnp.bfloat16),
        compiler_params=params(),
        cost_estimate=pl.CostEstimate(
            flops=per_target * rows * extra * PAGE * width * 16,
            bytes_accessed=8 * 10**6,
            transcendentals=per_target * rows * extra * PAGE,
        ),
    )(*scalars, q, acc, ml, *blocks)


def join_kernel(targets, chunks, steps, meta_ref, *refs):
    out_ref = refs[-1]
    k = pl.program_id(0)
    rows = refs[0].shape[1]
    each = rows // steps
    for s in range(targets):
        @pl.when(lax.rem(meta_ref[1] + (targets - s), targets) == k)
        def _():
            for c in range(chunks):
                source = refs[s * chunks + c]

                def body(r, carry):
                    value = source[r]
                    for g in range(each):
                        out_ref[r, :, (c * each + g) * 128 : (c * each + g + 1) * 128] = value[
                            g * steps : (g + 1) * steps
                        ]
                    return carry

                lax.fori_loop(0, out_ref.shape[0], body, 0)


def join(pieces, meta, steps, targets, chunks):
    per_target, rows, width = pieces[0].shape
    half = chunks * (rows // steps) * width
    spec = pl.BlockSpec((per_target, rows, width), lambda k, *_: (0, 0, 0))
    return pl.pallas_call(
        functools.partial(join_kernel, targets, chunks, steps),
        grid_spec=pltpu.PrefetchScalarGridSpec(
            num_scalar_prefetch=1,
            grid=(targets,),
            in_specs=[spec] * len(pieces),
            out_specs=pl.BlockSpec((per_target, steps, half), lambda k, *_: (0, 0, k)),
        ),
        out_shape=jax.ShapeDtypeStruct((per_target, steps, half * targets), jnp.bfloat16),
        compiler_params=params(),
        cost_estimate=pl.CostEstimate(flops=0, bytes_accessed=2 * 10**6, transcendentals=0),
    )(meta, *pieces)


def ring_place(index, size):
    return jnp.where(index % 2 == 0, index // 2, size - 1 - index // 2)


def shards(
    roles,
    ring,
    targets,
    prefill_q,
    prefill_k,
    prefill_v,
    decode_q,
    decode_k,
    decode_v,
    cache_k,
    cache_v,
    cache_len,
    page_list,
):
    tokens, q_heads = prefill_q.shape[1:3]
    heads, width = prefill_k.shape[2:]
    group = q_heads // heads
    own_pages = tokens // PAGE
    requests, steps = decode_q.shape[:2]
    extra = page_list.shape[1]
    role = lax.axis_index("role")
    ctx = lax.axis_index("ctx")
    tp = lax.axis_index("tp")

    order = list(range(0, ring, 2)) + list(range(ring - 1, 0, -2))
    along = [(order[j], order[(j + 1) % ring]) for j in range(ring)]
    flips = [1 << b for b in reversed(range(roles.bit_length() - 1))]

    line = [split_heads(prefill_k, prefill_v)]
    for _ in range(1, ring):
        line.append(lax.ppermute(line[-1], "ctx", along))
    by_role = {0: line}
    for flip in flips:
        pairs = [(j, j ^ flip) for j in range(roles)]
        for seen in list(by_role):
            by_role[seen ^ flip] = [lax.ppermute(a, "role", pairs) for a in by_role[seen]]

    owner = page_list // own_pages
    place = (ring_place(ctx, ring) - ring_place(owner % ring, ring)) % ring
    slot = ((owner // ring) ^ role) * ring + place
    hot = slot.reshape(-1, 1) == jnp.arange(roles * ring)[None, :]
    pick = jnp.max(jnp.where(hot, (page_list % own_pages).reshape(-1, 1), 0), axis=0)
    meta = jnp.stack([ctx, tp]).astype(jnp.int32)
    scalars = (
        slot.reshape(-1).astype(jnp.int32),
        pick.astype(jnp.int32),
        meta,
    )
    position = jnp.arange(ring)
    where = ring_place(ctx, ring)
    source = (where - position) % ring
    source_ctx = jnp.where(source < (ring + 1) // 2, 2 * source, 2 * (ring - 1 - source) + 1)
    flags = (source_ctx < ctx).astype(jnp.int32)
    earlier = jnp.where(position == 0, jnp.sum(flags), flags).astype(jnp.int32)

    raw = [
        a.reshape(requests, -1, width) for a in (decode_q, decode_k, decode_v, cache_k, cache_v)
    ]
    acc, ml = cache_part(*raw, cache_len.astype(jnp.int32), steps, heads, group)
    prefill_out = prefill(prefill_q, line, earlier)
    blocks = [a for r in range(roles) for a in by_role[r]]
    pieces = [None] * targets
    for s in reversed(range(targets)):
        out = decode(raw[0], acc, ml, blocks, scalars, s, targets, extra, steps, heads, group)
        if s:
            shift = [(j, (j + s) % targets) for j in range(targets)]
            out = lax.ppermute(out, "tp", shift)
        pieces[s] = out
    decode_out = join(pieces, meta, steps, targets, 1)
    return (prefill_out, decode_out)


def solution(mesh):
    body = functools.partial(shards, mesh.shape["role"], mesh.shape["ctx"], mesh.shape["tp"])
    return jax.shard_map(
        body,
        mesh=mesh,
        in_specs=(
            P("role", "ctx", "tp", None),
            P("role", "ctx", "tp", None),
            P("role", "ctx", "tp", None),
            P(("role", "ctx"), None, "tp", None),
            P(("role", "ctx"), None, "tp", None),
            P(("role", "ctx"), None, "tp", None),
            P(("role", "ctx"), None, "tp", None),
            P(("role", "ctx"), None, "tp", None),
            P(("role", "ctx")),
            P(("role", "ctx"), None),
        ),
        out_specs=(P("role", "ctx", "tp", None), P(("role", "ctx", "tp"), None, None)),
        check_vma=False,
    )
```

```python
import functools
import math

import jax
import jax.numpy as jnp
from jax import lax
from jax.experimental import pallas as pl
from jax.experimental.pallas import tpu as pltpu
from jax.sharding import PartitionSpec as P

PAGE = 128
LOG2E = 1.4426950408889634
NEG = -1e30
VMEM_LIMIT = 48 * 1024 * 1024


def nt(a, b):
    return lax.dot_general(a, b, (((1,), (1,)), ((), ())), preferred_element_type=jnp.float32)


def nn(a, b):
    return jnp.dot(a, b, preferred_element_type=jnp.float32)


def params():
    return pltpu.CompilerParams(vmem_limit_bytes=VMEM_LIMIT)


def one_hot(out_rows, in_rows, source):
    row = lax.broadcasted_iota(jnp.int32, (out_rows, in_rows), 0)
    col = lax.broadcasted_iota(jnp.int32, (out_rows, in_rows), 1)
    return jnp.where(col == source(row), 1.0, 0.0).astype(jnp.bfloat16)


def split_kernel(heads, tokens, k_ref, v_ref, out_ref):
    rows = min(tokens * heads, 256)
    step = rows // heads
    pick = one_hot(rows, rows, lambda i: (i % step) * heads + i // step)
    moved = []
    for j in range(tokens // step):
        keys = nn(pick, k_ref[pl.ds(j * rows, rows), :]).astype(jnp.bfloat16)
        moved.append(nn(pick, v_ref[pl.ds(j * rows, rows), :]))
        for h in range(heads):
            out_ref[h, 0, pl.ds(j * step, step), :] = keys[h * step : (h + 1) * step]
    for h in range(heads):
        values = jnp.concatenate([a[h * step : (h + 1) * step] for a in moved], axis=0)
        for page in range(tokens // PAGE):
            out_ref[h, 1, pl.ds(page * PAGE, PAGE), :] = values[
                page * PAGE : (page + 1) * PAGE
            ].T.astype(jnp.bfloat16)


def split_heads(k, v):
    _, tokens, heads, width = k.shape
    return pl.pallas_call(
        functools.partial(split_kernel, heads, tokens),
        out_shape=jax.ShapeDtypeStruct((heads, 2, tokens, width), jnp.bfloat16),
        compiler_params=params(),
        cost_estimate=pl.CostEstimate(flops=10**8, bytes_accessed=2 * 10**6, transcendentals=0),
    )(k.reshape(tokens * heads, width), v.reshape(tokens * heads, width))


def prefill_kernel(ring, group, tokens, scale, earlier_ref, *refs):
    q_ref = refs[0]
    blocks = refs[1 : 1 + ring]
    out_ref, buf, s_ref, m_ref, l_ref, acc_ref, sems = refs[1 + ring :]
    own = blocks[0]
    heads = own.shape[0]
    block = q_ref.shape[1]
    pages = tokens // PAGE
    i = pl.program_id(0)

    def copies():
        found = []
        place = jnp.int32(0)
        for s in range(1, ring):
            copy = pltpu.make_async_copy(blocks[s], buf.at[place], sems.at[s])
            found.append((earlier_ref[s], copy))
            place = place + earlier_ref[s]
        return found

    @pl.when(i == 0)
    def _():
        for flag, copy in copies():
            @pl.when(flag == 1)
            def _():
                copy.start()
        for flag, copy in copies():
            @pl.when(flag == 1)
            def _():
                copy.wait()

    rows = block * group
    queries = q_ref[0].astype(jnp.float32)
    q = [
        queries[:, h * group : (h + 1) * group, :].reshape(rows, -1).astype(jnp.bfloat16)
        for h in range(heads)
    ]

    def fold(a, op):
        return functools.reduce(op, [a[:, j * 128 : (j + 1) * 128] for j in range(a.shape[1] // 128)])

    token = lax.broadcasted_iota(jnp.int32, (rows, tokens), 0) // group + i * block
    allowed = lax.broadcasted_iota(jnp.int32, (rows, tokens), 1) <= token

    def values(ref, h):
        return jnp.concatenate([ref[h, 1, pl.ds(j * PAGE, PAGE), :] for j in range(pages)], axis=1)

    last = ring - 1
    for h in range(heads):
        s = jnp.where(allowed, nt(q[h], own[h, 0]), NEG)
        s_ref[last, h] = s
        m_ref[h] = fold(s, jnp.maximum)

    def look(b, carry):
        for h in range(heads):
            s = nt(q[h], buf[b, h, 0])
            s_ref[b, h] = s
            m_ref[h] = jnp.maximum(m_ref[h], fold(s, jnp.maximum))
        return carry

    lax.fori_loop(0, earlier_ref[0], look, 0)
    for h in range(heads):
        m = jnp.max(m_ref[h], axis=1, keepdims=True)
        m_ref[h] = jnp.broadcast_to(m, m_ref.shape[1:])
        p = jnp.exp2((s_ref[last, h] - m) * scale)
        l_ref[h] = fold(p, jnp.add)
        acc_ref[h] = nt(p.astype(jnp.bfloat16), values(own, h))

    def weigh(b, carry):
        for h in range(heads):
            m = m_ref[h]
            p = [
                jnp.exp2((s_ref[b, h, :, pl.ds(j * 128, 128)] - m) * scale)
                for j in range(tokens // 128)
            ]
            l_ref[h] = l_ref[h] + functools.reduce(jnp.add, p)
            p = jnp.concatenate([a.astype(jnp.bfloat16) for a in p], axis=1)
            acc_ref[h] = acc_ref[h] + nt(p, values(buf.at[b], h))
        return carry

    lax.fori_loop(0, earlier_ref[0], weigh, 0)
    out = []
    for h in range(heads):
        total = jnp.sum(l_ref[h], axis=1, keepdims=True)
        out.append((acc_ref[h] / total).reshape(block, group, -1))
    out_ref[0] = jnp.concatenate(out, axis=1).astype(out_ref.dtype)


def prefill(q, blocks, earlier):
    _, tokens, q_heads, width = q.shape
    ring = len(blocks)
    heads = blocks[0].shape[0]
    group = q_heads // heads
    block = 64
    rows = block * group
    q_spec = pl.BlockSpec((1, block, q_heads, width), lambda i, *_: (0, i, 0, 0))
    own_spec = pl.BlockSpec(blocks[0].shape, lambda i, *_: (0, 0, 0, 0))
    return pl.pallas_call(
        functools.partial(prefill_kernel, ring, group, tokens, LOG2E / math.sqrt(width)),
        grid_spec=pltpu.PrefetchScalarGridSpec(
            num_scalar_prefetch=1,
            grid=(tokens // block,),
            in_specs=[q_spec, own_spec] + [pl.BlockSpec(memory_space=pl.ANY)] * (ring - 1),
            out_specs=q_spec,
            scratch_shapes=[
                pltpu.VMEM((max(ring - 1, 1),) + blocks[0].shape, jnp.bfloat16),
                pltpu.VMEM((ring, heads, rows, tokens), jnp.float32),
                pltpu.VMEM((heads, rows, width), jnp.float32),
                pltpu.VMEM((heads, rows, width), jnp.float32),
                pltpu.VMEM((heads, rows, width), jnp.float32),
                pltpu.SemaphoreType.DMA((ring,)),
            ],
        ),
        out_shape=jax.ShapeDtypeStruct(q.shape, jnp.bfloat16),
        compiler_params=params(),
        cost_estimate=pl.CostEstimate(
            flops=16 * q_heads * tokens * tokens * ring * width,
            bytes_accessed=4 * 10**6,
            transcendentals=tokens * tokens * ring * q_heads,
        ),
    )(earlier, q, *blocks)


def cache_kernel(
    steps, heads, group, scale, len_ref, q_ref, dk_ref, dv_ref, ck_ref, cv_ref, acc_ref, ml_ref
):
    block, rows, width = q_ref.shape
    cache = ck_ref.shape[1]
    new = dk_ref.shape[1]
    per_step = heads * group

    def mask(columns):
        row = lax.broadcasted_iota(jnp.int32, (rows, columns), 0)
        column = lax.broadcasted_iota(jnp.int32, (rows, columns), 1)
        same = column % heads == row % per_step // group
        return jnp.where(same, column // heads, 1 << 20), row // per_step

    place, _ = mask(cache)
    new_place, step = mask(new)
    new_allowed = new_place <= step
    low = lax.broadcasted_iota(jnp.int32, (rows, width), 1) < 4
    first = pl.program_id(0) * block
    unroll = math.gcd(4, block)

    def body(g, carry):
        scores = []
        for u in range(unroll):
            r = g * unroll + u
            q = q_ref[r]
            old = jnp.where(place < len_ref[first + r], nt(q, ck_ref[r]), NEG)
            add = jnp.where(new_allowed, nt(q, dk_ref[r]), NEG)
            scores.append((r, old, add))
        weights = []
        for r, old, add in scores:
            m = jnp.maximum(
                jnp.max(old, axis=1, keepdims=True), jnp.max(add, axis=1, keepdims=True)
            )
            old = jnp.exp2((old - m) * scale)
            add = jnp.exp2((add - m) * scale)
            l = jnp.sum(old, axis=1, keepdims=True) + jnp.sum(add, axis=1, keepdims=True)
            ml_ref[r] = jnp.where(low, m, l).T[:8]
            weights.append((r, old.astype(jnp.bfloat16), add.astype(jnp.bfloat16)))
        for r, old, add in weights:
            acc_ref[r] = (nn(old, cv_ref[r]) + nn(add, dv_ref[r])).T
        return carry

    lax.fori_loop(0, block // unroll, body, 0)


def cache_part(q, dk, dv, ck, cv, lens, steps, heads, group):
    requests, rows, width = q.shape
    block = math.gcd(8, requests)
    spec = [
        pl.BlockSpec((block,) + a.shape[1:], lambda i, *_: (i, 0, 0)) for a in (q, dk, dv, ck, cv)
    ]
    shapes = [(requests, width, rows), (requests, 8, rows)]
    return pl.pallas_call(
        functools.partial(cache_kernel, steps, heads, group, LOG2E / math.sqrt(width)),
        grid_spec=pltpu.PrefetchScalarGridSpec(
            num_scalar_prefetch=1,
            grid=(requests // block,),
            in_specs=spec,
            out_specs=[pl.BlockSpec((block,) + a[1:], lambda i, *_: (i, 0, 0)) for a in shapes],
        ),
        out_shape=[jax.ShapeDtypeStruct(a, jnp.float32) for a in shapes],
        compiler_params=params(),
        cost_estimate=pl.CostEstimate(
            flops=requests * rows * ck.shape[1] * width * 16,
            bytes_accessed=14 * 10**6,
            transcendentals=requests * rows * ck.shape[1],
        ),
    )(lens, q, dk, dv, ck, cv)


def decode_kernel(slots, extra, steps, target, targets, heads, group, scale, *refs):
    slot_ref, pick_ref, meta_ref = refs[:3]
    q_ref, acc_ref, ml_ref = refs[3:6]
    blocks = refs[6 : 6 + slots]
    out_ref, buf, sems = refs[6 + slots :]
    block, lanes, width = q_ref.shape
    i = pl.program_id(0)
    first = (lax.rem(meta_ref[1] + target, targets) * pl.num_programs(0) + i) * block

    def copies():
        for s in range(slots):
            start = pl.multiple_of(pick_ref[s] * PAGE, PAGE)
            yield pltpu.make_async_copy(
                blocks[s].at[:, :, pl.ds(start, PAGE), :], buf.at[s], sems.at[s]
            )

    @pl.when(i == 0)
    def _():
        for copy in copies():
            copy.start()
        for copy in copies():
            copy.wait()

    per_step = heads * group
    row_head = lax.broadcasted_iota(jnp.int32, (lanes, width), 0) % per_step // group
    head_rows = [jnp.where(row_head == h, 1.0, 0.0).astype(jnp.bfloat16) for h in range(heads)]
    lane_head = lax.broadcasted_iota(jnp.int32, (width, lanes), 1) % per_step // group
    order = one_hot(lanes, lanes, lambda r: r % steps * per_step + r // steps)
    unroll = math.gcd(2, block)

    def body(g, carry):
        scores = []
        for u in range(unroll):
            r = g * unroll + u
            q = q_ref[r]
            places = [slot_ref[(first + r) * extra + j] for j in range(extra)]
            keys = jnp.concatenate(
                [
                    jnp.concatenate([buf[place, h, 0] for h in range(heads)], axis=1)
                    for place in places
                ],
                axis=0,
            )
            spread = jnp.concatenate([q * a for a in head_rows], axis=1)
            scores.append((r, places, nt(keys, spread)))
        weights = []
        for r, places, s in scores:
            old = ml_ref[r, 0:1]
            m = jnp.maximum(jnp.max(s, axis=0, keepdims=True), old)
            p = jnp.exp2((s - m) * scale)
            shrink = jnp.exp2((old - m) * scale)
            l = ml_ref[r, 4:5] * shrink + jnp.sum(p, axis=0, keepdims=True)
            weights.append((r, places, p.astype(jnp.bfloat16), shrink, l))
        for r, places, p, shrink, l in weights:
            values = jnp.concatenate(
                [
                    jnp.concatenate([buf[place, h, 1] for place in places], axis=1)
                    for h in range(heads)
                ],
                axis=0,
            )
            every = nn(values, p)
            part = every[:width]
            for h in range(1, heads):
                part = jnp.where(lane_head == h, every[h * width : (h + 1) * width], part)
            result = ((acc_ref[r] * shrink + part) / l).astype(jnp.bfloat16)
            out_ref[r] = nt(order, result).astype(jnp.bfloat16)
        return carry

    lax.fori_loop(0, block // unroll, body, 0)


def decode(q, acc, ml, blocks, scalars, target, targets, extra, steps, heads, group):
    requests, lanes, width = q.shape
    per_target = requests // targets
    block = math.gcd(8, per_target)
    per_block = per_target // block
    slots = len(blocks)

    def here(i, slot, pick, meta):
        return (lax.rem(meta[1] + target, targets) * per_block + i, 0, 0)

    in_specs = [pl.BlockSpec((block,) + a.shape[1:], here) for a in (q, acc, ml)]
    in_specs += [pl.BlockSpec(memory_space=pl.ANY)] * slots
    return pl.pallas_call(
        functools.partial(
            decode_kernel,
            slots,
            extra,
            steps,
            target,
            targets,
            heads,
            group,
            LOG2E / math.sqrt(width),
        ),
        grid_spec=pltpu.PrefetchScalarGridSpec(
            num_scalar_prefetch=3,
            grid=(per_block,),
            in_specs=in_specs,
            out_specs=pl.BlockSpec((block, lanes, width), lambda i, *_: (i, 0, 0)),
            scratch_shapes=[
                pltpu.VMEM((slots, heads, 2, PAGE, width), jnp.bfloat16),
                pltpu.SemaphoreType.DMA((slots,)),
            ],
        ),
        out_shape=jax.ShapeDtypeStruct((per_target, lanes, width), jnp.bfloat16),
        compiler_params=params(),
        cost_estimate=pl.CostEstimate(
            flops=per_target * lanes * extra * PAGE * width * 16,
            bytes_accessed=8 * 10**6,
            transcendentals=per_target * lanes * extra * PAGE,
        ),
    )(*scalars, q, acc, ml, *blocks)


def join_kernel(targets, chunks, steps, meta_ref, *refs):
    out_ref = refs[-1]
    k = pl.program_id(0)
    rows = refs[0].shape[1]
    each = rows // steps
    for s in range(targets):
        @pl.when(lax.rem(meta_ref[1] + (targets - s), targets) == k)
        def _():
            for c in range(chunks):
                source = refs[s * chunks + c]

                def body(r, carry):
                    value = source[r]
                    for g in range(each):
                        out_ref[r, :, (c * each + g) * 128 : (c * each + g + 1) * 128] = value[
                            g * steps : (g + 1) * steps
                        ]
                    return carry

                lax.fori_loop(0, out_ref.shape[0], body, 0)


def join(pieces, meta, steps, targets, chunks):
    per_target, rows, width = pieces[0].shape
    half = chunks * (rows // steps) * width
    spec = pl.BlockSpec((per_target, rows, width), lambda k, *_: (0, 0, 0))
    return pl.pallas_call(
        functools.partial(join_kernel, targets, chunks, steps),
        grid_spec=pltpu.PrefetchScalarGridSpec(
            num_scalar_prefetch=1,
            grid=(targets,),
            in_specs=[spec] * len(pieces),
            out_specs=pl.BlockSpec((per_target, steps, half), lambda k, *_: (0, 0, k)),
        ),
        out_shape=jax.ShapeDtypeStruct((per_target, steps, half * targets), jnp.bfloat16),
        compiler_params=params(),
        cost_estimate=pl.CostEstimate(flops=0, bytes_accessed=2 * 10**6, transcendentals=0),
    )(meta, *pieces)


def ring_place(index, size):
    return jnp.where(index % 2 == 0, index // 2, size - 1 - index // 2)


def shards(
    roles,
    ring,
    targets,
    prefill_q,
    prefill_k,
    prefill_v,
    decode_q,
    decode_k,
    decode_v,
    cache_k,
    cache_v,
    cache_len,
    page_list,
):
    tokens, q_heads = prefill_q.shape[1:3]
    heads, width = prefill_k.shape[2:]
    group = q_heads // heads
    own_pages = tokens // PAGE
    requests, steps = decode_q.shape[:2]
    extra = page_list.shape[1]
    role = lax.axis_index("role")
    ctx = lax.axis_index("ctx")
    tp = lax.axis_index("tp")

    order = list(range(0, ring, 2)) + list(range(ring - 1, 0, -2))
    along = [(order[j], order[(j + 1) % ring]) for j in range(ring)]
    flips = [1 << b for b in reversed(range(roles.bit_length() - 1))]

    owner = page_list // own_pages
    place = (ring_place(ctx, ring) - ring_place(owner % ring, ring)) % ring
    slot = ((owner // ring) ^ role) * ring + place
    hot = slot.reshape(-1, 1) == jnp.arange(roles * ring)[None, :]
    pick = jnp.max(jnp.where(hot, (page_list % own_pages).reshape(-1, 1), 0), axis=0)
    meta = jnp.stack([ctx, tp]).astype(jnp.int32)
    scalars = (
        slot.reshape(-1).astype(jnp.int32),
        pick.astype(jnp.int32),
        meta,
    )
    position = jnp.arange(ring)
    where = ring_place(ctx, ring)
    source = (where - position) % ring
    source_ctx = jnp.where(source < (ring + 1) // 2, 2 * source, 2 * (ring - 1 - source) + 1)
    flags = (source_ctx < ctx).astype(jnp.int32)
    earlier = jnp.where(position == 0, jnp.sum(flags), flags).astype(jnp.int32)

    raw = [
        a.reshape(requests, -1, width) for a in (decode_q, decode_k, decode_v, cache_k, cache_v)
    ]

    gathered = {(0, 0): split_heads(prefill_k, prefill_v)}
    fresh = [(0, 0)]
    for k in range(ring + len(flips) - 1):
        arrived = {}
        for code, s in fresh:
            block = gathered[code, s]
            if code == 0 and s + 1 < ring:
                arrived[0, s + 1] = lax.ppermute(block, "ctx", along)
            for flip in flips:
                if code == 0 or flip < code & -code:
                    pairs = [(j, j ^ flip) for j in range(roles)]
                    arrived[code ^ flip, s] = lax.ppermute(block, "role", pairs)
        beside = ()
        if k == 0:
            beside = cache_part(*raw, cache_len.astype(jnp.int32), steps, heads, group)
        if k == ring - 1:
            beside = prefill(prefill_q, [gathered[0, s] for s in range(ring)], earlier)
        arrived, beside = lax.optimization_barrier((arrived, beside))
        if k == 0:
            acc, ml = beside
        if k == ring - 1:
            prefill_out = beside
        gathered.update(arrived)
        fresh = list(arrived)

    blocks = [gathered[r, s] for r in range(roles) for s in range(ring)]
    pieces = [None] * targets
    for s in reversed(range(targets)):
        out = decode(raw[0], acc, ml, blocks, scalars, s, targets, extra, steps, heads, group)
        if s:
            shift = [(j, (j + s) % targets) for j in range(targets)]
            out = lax.ppermute(out, "tp", shift)
        pieces[s] = out
    decode_out = join(pieces, meta, steps, targets, 1)
    return (prefill_out, decode_out)


def solution(mesh):
    body = functools.partial(shards, mesh.shape["role"], mesh.shape["ctx"], mesh.shape["tp"])
    return jax.shard_map(
        body,
        mesh=mesh,
        in_specs=(
            P("role", "ctx", "tp", None),
            P("role", "ctx", "tp", None),
            P("role", "ctx", "tp", None),
            P(("role", "ctx"), None, "tp", None),
            P(("role", "ctx"), None, "tp", None),
            P(("role", "ctx"), None, "tp", None),
            P(("role", "ctx"), None, "tp", None),
            P(("role", "ctx"), None, "tp", None),
            P(("role", "ctx")),
            P(("role", "ctx"), None),
        ),
        out_specs=(P("role", "ctx", "tp", None), P(("role", "ctx", "tp"), None, None)),
        check_vma=False,
    )
```

```python
import functools
import math

import jax
import jax.numpy as jnp
from jax import lax
from jax.experimental import pallas as pl
from jax.experimental.pallas import tpu as pltpu
from jax.sharding import PartitionSpec as P

PAGE = 128
LOG2E = 1.4426950408889634
NEG = -1e30
VMEM_LIMIT = 60 * 1024 * 1024


def nt(a, b):
    return lax.dot_general(a, b, (((1,), (1,)), ((), ())), preferred_element_type=jnp.float32)


def nn(a, b):
    return jnp.dot(a, b, preferred_element_type=jnp.float32)


def params():
    return pltpu.CompilerParams(vmem_limit_bytes=VMEM_LIMIT)


def one_hot(out_rows, in_rows, source):
    row = lax.broadcasted_iota(jnp.int32, (out_rows, in_rows), 0)
    col = lax.broadcasted_iota(jnp.int32, (out_rows, in_rows), 1)
    return jnp.where(col == source(row), 1.0, 0.0).astype(jnp.bfloat16)


def split_kernel(heads, tokens, k_ref, v_ref, out_ref):
    rows = min(tokens * heads, 256)
    step = rows // heads
    pick = one_hot(rows, rows, lambda i: (i % step) * heads + i // step)
    moved = []
    for j in range(tokens // step):
        keys = nn(pick, k_ref[pl.ds(j * rows, rows), :]).astype(jnp.bfloat16)
        moved.append(nn(pick, v_ref[pl.ds(j * rows, rows), :]))
        for h in range(heads):
            out_ref[h, 0, pl.ds(j * step, step), :] = keys[h * step : (h + 1) * step]
    for h in range(heads):
        values = jnp.concatenate([a[h * step : (h + 1) * step] for a in moved], axis=0)
        for page in range(tokens // PAGE):
            out_ref[h, 1, pl.ds(page * PAGE, PAGE), :] = values[
                page * PAGE : (page + 1) * PAGE
            ].T.astype(jnp.bfloat16)


def split_heads(k, v):
    _, tokens, heads, width = k.shape
    return pl.pallas_call(
        functools.partial(split_kernel, heads, tokens),
        out_shape=jax.ShapeDtypeStruct((heads, 2, tokens, width), jnp.bfloat16),
        compiler_params=params(),
        cost_estimate=pl.CostEstimate(flops=10**8, bytes_accessed=2 * 10**6, transcendentals=0),
    )(k.reshape(tokens * heads, width), v.reshape(tokens * heads, width))


def fold(a, op):
    return functools.reduce(op, [a[:, j * 128 : (j + 1) * 128] for j in range(a.shape[1] // 128)])


def head_queries(q_ref, heads):
    block, q_heads, width = q_ref.shape[1:]
    group = q_heads // heads
    queries = q_ref[0].astype(jnp.float32)
    return [
        queries[:, h * group : (h + 1) * group, :].reshape(block * group, width).astype(jnp.bfloat16)
        for h in range(heads)
    ]


def page_values(ref, h):
    pages = ref.shape[2] // PAGE
    return jnp.concatenate([ref[h, 1, pl.ds(j * PAGE, PAGE), :] for j in range(pages)], axis=1)


def prefill_kernel(ring, group, tokens, scale, earlier_ref, *refs):
    q_ref = refs[0]
    blocks = refs[1 : 1 + ring]
    acc_ref, ml_ref, buf, s_ref, m_ref, l_ref, sems = refs[1 + ring :]
    own = blocks[0]
    heads = own.shape[0]
    block = q_ref.shape[1]
    i = pl.program_id(0)

    def copies():
        found = []
        place = jnp.int32(0)
        for s in range(1, ring):
            copy = pltpu.make_async_copy(blocks[s], buf.at[place], sems.at[s])
            found.append((earlier_ref[s], copy))
            place = place + earlier_ref[s]
        return found

    @pl.when(i == 0)
    def _():
        for flag, copy in copies():
            @pl.when(flag == 1)
            def _():
                copy.start()
        for flag, copy in copies():
            @pl.when(flag == 1)
            def _():
                copy.wait()

    rows = block * group
    q = head_queries(q_ref, heads)
    token = lax.broadcasted_iota(jnp.int32, (rows, tokens), 0) // group + i * block
    allowed = lax.broadcasted_iota(jnp.int32, (rows, tokens), 1) <= token

    last = ring - 1
    for h in range(heads):
        s = jnp.where(allowed, nt(q[h], own[h, 0]), NEG)
        s_ref[last, h] = s
        m_ref[h] = fold(s, jnp.maximum)

    def look(b, carry):
        for h in range(heads):
            s = nt(q[h], buf[b, h, 0])
            s_ref[b, h] = s
            m_ref[h] = jnp.maximum(m_ref[h], fold(s, jnp.maximum))
        return carry

    lax.fori_loop(0, earlier_ref[0], look, 0)
    for h in range(heads):
        m = jnp.max(m_ref[h], axis=1, keepdims=True)
        m_ref[h] = jnp.broadcast_to(m, m_ref.shape[1:])
        p = jnp.exp2((s_ref[last, h] - m) * scale)
        l_ref[h] = fold(p, jnp.add)
        acc_ref[0, h] = nt(p.astype(jnp.bfloat16), page_values(own, h))

    def weigh(b, carry):
        for h in range(heads):
            m = m_ref[h]
            p = [
                jnp.exp2((s_ref[b, h, :, pl.ds(j * 128, 128)] - m) * scale)
                for j in range(tokens // 128)
            ]
            l_ref[h] = l_ref[h] + functools.reduce(jnp.add, p)
            p = jnp.concatenate([a.astype(jnp.bfloat16) for a in p], axis=1)
            acc_ref[0, h] = acc_ref[0, h] + nt(p, page_values(buf.at[b], h))
        return carry

    lax.fori_loop(0, earlier_ref[0], weigh, 0)
    low = lax.broadcasted_iota(jnp.int32, m_ref.shape[1:], 1) < 64
    for h in range(heads):
        total = jnp.sum(l_ref[h], axis=1, keepdims=True)
        ml_ref[0, h] = jnp.where(low, m_ref[h], total)


def prefill(q, blocks, earlier):
    _, tokens, q_heads, width = q.shape
    ring = len(blocks)
    heads = blocks[0].shape[0]
    group = q_heads // heads
    block = 64
    rows = block * group
    q_spec = pl.BlockSpec((1, block, q_heads, width), lambda i, *_: (0, i, 0, 0))
    own_spec = pl.BlockSpec(blocks[0].shape, lambda i, *_: (0, 0, 0, 0))
    state = pl.BlockSpec((1, heads, rows, width), lambda i, *_: (i, 0, 0, 0))
    shape = jax.ShapeDtypeStruct((tokens // block, heads, rows, width), jnp.float32)
    return pl.pallas_call(
        functools.partial(prefill_kernel, ring, group, tokens, LOG2E / math.sqrt(width)),
        grid_spec=pltpu.PrefetchScalarGridSpec(
            num_scalar_prefetch=1,
            grid=(tokens // block,),
            in_specs=[q_spec, own_spec] + [pl.BlockSpec(memory_space=pl.ANY)] * (ring - 1),
            out_specs=[state, state],
            scratch_shapes=[
                pltpu.VMEM((max(ring - 1, 1),) + blocks[0].shape, jnp.bfloat16),
                pltpu.VMEM((ring, heads, rows, tokens), jnp.float32),
                pltpu.VMEM((heads, rows, width), jnp.float32),
                pltpu.VMEM((heads, rows, width), jnp.float32),
                pltpu.SemaphoreType.DMA((ring,)),
            ],
        ),
        out_shape=[shape, shape],
        compiler_params=params(),
        cost_estimate=pl.CostEstimate(
            flops=16 * q_heads * tokens * tokens * ring * width,
            bytes_accessed=12 * 10**6,
            transcendentals=tokens * tokens * ring * q_heads,
        ),
    )(earlier, q, *blocks)


def finish_kernel(scale, needed_ref, q_ref, last_ref, acc_ref, ml_ref, out_ref):
    heads = last_ref.shape[0]
    block = q_ref.shape[1]

    def give(parts):
        out = [a.reshape(block, a.shape[0] // block, a.shape[1]) for a in parts]
        out_ref[0] = jnp.concatenate(out, axis=1).astype(out_ref.dtype)

    @pl.when(needed_ref[0] == 0)
    def _():
        give([acc_ref[0, h] / ml_ref[0, h][:, 64:65] for h in range(heads)])

    @pl.when(needed_ref[0] == 1)
    def _():
        q = head_queries(q_ref, heads)
        scores = [nt(q[h], last_ref[h, 0]) for h in range(heads)]
        parts = []
        for h in range(heads):
            s = scores[h]
            ml = ml_ref[0, h]
            old, l = ml[:, :1], ml[:, 64:65]
            m = jnp.maximum(jnp.max(s, axis=1, keepdims=True), old)
            p = jnp.exp2((s - m) * scale)
            shrink = jnp.exp2((old - m) * scale)
            l = l * shrink + jnp.sum(p, axis=1, keepdims=True)
            acc = acc_ref[0, h] * shrink + nt(p.astype(jnp.bfloat16), page_values(last_ref, h))
            parts.append(acc / l)
        give(parts)


def prefill_finish(q, last, needed, acc, ml):
    _, tokens, q_heads, width = q.shape
    block = tokens // acc.shape[0]
    q_spec = pl.BlockSpec((1, block, q_heads, width), lambda i, *_: (0, i, 0, 0))
    last_spec = pl.BlockSpec(last.shape, lambda i, *_: (0, 0, 0, 0))
    state = pl.BlockSpec((1,) + acc.shape[1:], lambda i, *_: (i, 0, 0, 0))
    return pl.pallas_call(
        functools.partial(finish_kernel, LOG2E / math.sqrt(width)),
        grid_spec=pltpu.PrefetchScalarGridSpec(
            num_scalar_prefetch=1,
            grid=(tokens // block,),
            in_specs=[q_spec, last_spec, state, state],
            out_specs=q_spec,
        ),
        out_shape=jax.ShapeDtypeStruct(q.shape, jnp.bfloat16),
        compiler_params=params(),
        cost_estimate=pl.CostEstimate(
            flops=16 * q_heads * tokens * tokens * width,
            bytes_accessed=12 * 10**6,
            transcendentals=tokens * tokens * q_heads,
        ),
    )(needed, q, last, acc, ml)


def cache_kernel(
    steps, heads, group, scale, len_ref, q_ref, dk_ref, dv_ref, ck_ref, cv_ref, acc_ref, ml_ref
):
    block, rows, width = q_ref.shape
    cache = ck_ref.shape[1]
    new = dk_ref.shape[1]
    per_step = heads * group

    def mask(columns):
        row = lax.broadcasted_iota(jnp.int32, (rows, columns), 0)
        column = lax.broadcasted_iota(jnp.int32, (rows, columns), 1)
        same = column % heads == row % per_step // group
        return jnp.where(same, column // heads, 1 << 20), row // per_step

    place, _ = mask(cache)
    new_place, step = mask(new)
    new_allowed = new_place <= step
    low = lax.broadcasted_iota(jnp.int32, (rows, width), 1) < 4
    first = pl.program_id(0) * block
    unroll = math.gcd(4, block)

    def body(g, carry):
        scores = []
        for u in range(unroll):
            r = g * unroll + u
            q = q_ref[r]
            old = jnp.where(place < len_ref[first + r], nt(q, ck_ref[r]), NEG)
            add = jnp.where(new_allowed, nt(q, dk_ref[r]), NEG)
            scores.append((r, old, add))
        weights = []
        for r, old, add in scores:
            m = jnp.maximum(
                jnp.max(old, axis=1, keepdims=True), jnp.max(add, axis=1, keepdims=True)
            )
            old = jnp.exp2((old - m) * scale)
            add = jnp.exp2((add - m) * scale)
            l = jnp.sum(old, axis=1, keepdims=True) + jnp.sum(add, axis=1, keepdims=True)
            ml_ref[r] = jnp.where(low, m, l).T[:8]
            weights.append((r, old.astype(jnp.bfloat16), add.astype(jnp.bfloat16)))
        for r, old, add in weights:
            acc_ref[r] = (nn(old, cv_ref[r]) + nn(add, dv_ref[r])).T
        return carry

    lax.fori_loop(0, block // unroll, body, 0)


def cache_part(q, dk, dv, ck, cv, lens, steps, heads, group):
    requests, rows, width = q.shape
    block = math.gcd(8, requests)
    spec = [
        pl.BlockSpec((block,) + a.shape[1:], lambda i, *_: (i, 0, 0)) for a in (q, dk, dv, ck, cv)
    ]
    shapes = [(requests, width, rows), (requests, 8, rows)]
    return pl.pallas_call(
        functools.partial(cache_kernel, steps, heads, group, LOG2E / math.sqrt(width)),
        grid_spec=pltpu.PrefetchScalarGridSpec(
            num_scalar_prefetch=1,
            grid=(requests // block,),
            in_specs=spec,
            out_specs=[pl.BlockSpec((block,) + a[1:], lambda i, *_: (i, 0, 0)) for a in shapes],
        ),
        out_shape=[jax.ShapeDtypeStruct(a, jnp.float32) for a in shapes],
        compiler_params=params(),
        cost_estimate=pl.CostEstimate(
            flops=requests * rows * ck.shape[1] * width * 16,
            bytes_accessed=14 * 10**6,
            transcendentals=requests * rows * ck.shape[1],
        ),
    )(lens, q, dk, dv, ck, cv)


def decode_kernel(slots, extra, steps, target, targets, heads, group, scale, *refs):
    slot_ref, pick_ref, meta_ref = refs[:3]
    q_ref, acc_ref, ml_ref = refs[3:6]
    blocks = refs[6 : 6 + slots]
    out_ref, buf, sems = refs[6 + slots :]
    block, lanes, width = q_ref.shape
    i = pl.program_id(0)
    first = (lax.rem(meta_ref[1] + target, targets) * pl.num_programs(0) + i) * block

    def copies():
        for s in range(slots):
            start = pl.multiple_of(pick_ref[s] * PAGE, PAGE)
            yield pltpu.make_async_copy(
                blocks[s].at[:, :, pl.ds(start, PAGE), :], buf.at[s], sems.at[s]
            )

    @pl.when(i == 0)
    def _():
        for copy in copies():
            copy.start()
        for copy in copies():
            copy.wait()

    per_step = heads * group
    row_head = lax.broadcasted_iota(jnp.int32, (lanes, width), 0) % per_step // group
    head_rows = [jnp.where(row_head == h, 1.0, 0.0).astype(jnp.bfloat16) for h in range(heads)]
    lane_head = lax.broadcasted_iota(jnp.int32, (width, lanes), 1) % per_step // group
    order = one_hot(lanes, lanes, lambda r: r % steps * per_step + r // steps)
    unroll = math.gcd(2, block)
    count = block // unroll

    def pages_of(r):
        return [slot_ref[(first + r) * extra + j] for j in range(extra)]

    def score(g):
        found = []
        for u in range(unroll):
            r = g * unroll + u
            q = q_ref[r]
            keys = jnp.concatenate(
                [
                    jnp.concatenate([buf[place, h, 0] for h in range(heads)], axis=1)
                    for place in pages_of(r)
                ],
                axis=0,
            )
            spread = jnp.concatenate([q * a for a in head_rows], axis=1)
            found.append(nt(keys, spread))
        return tuple(found)

    def body(g, scores):
        later = score(jnp.minimum(g + 1, count - 1))
        weights = []
        for u in range(unroll):
            r = g * unroll + u
            s = scores[u]
            old = ml_ref[r, 0:1]
            m = jnp.maximum(jnp.max(s, axis=0, keepdims=True), old)
            p = jnp.exp2((s - m) * scale)
            shrink = jnp.exp2((old - m) * scale)
            l = ml_ref[r, 4:5] * shrink + jnp.sum(p, axis=0, keepdims=True)
            weights.append((r, p.astype(jnp.bfloat16), shrink, l))
        for r, p, shrink, l in weights:
            places = pages_of(r)
            values = jnp.concatenate(
                [
                    jnp.concatenate([buf[place, h, 1] for place in places], axis=1)
                    for h in range(heads)
                ],
                axis=0,
            )
            every = nn(values, p)
            part = every[:width]
            for h in range(1, heads):
                part = jnp.where(lane_head == h, every[h * width : (h + 1) * width], part)
            result = ((acc_ref[r] * shrink + part) / l).astype(jnp.bfloat16)
            out_ref[r] = nt(order, result).astype(jnp.bfloat16)
        return later

    lax.fori_loop(0, count, body, score(0))


def decode(q, acc, ml, blocks, scalars, target, targets, extra, steps, heads, group):
    requests, lanes, width = q.shape
    per_target = requests // targets
    block = math.gcd(16, per_target)
    per_block = per_target // block
    slots = len(blocks)

    def here(i, slot, pick, meta):
        return (lax.rem(meta[1] + target, targets) * per_block + i, 0, 0)

    in_specs = [pl.BlockSpec((block,) + a.shape[1:], here) for a in (q, acc, ml)]
    in_specs += [pl.BlockSpec(memory_space=pl.ANY)] * slots
    return pl.pallas_call(
        functools.partial(
            decode_kernel,
            slots,
            extra,
            steps,
            target,
            targets,
            heads,
            group,
            LOG2E / math.sqrt(width),
        ),
        grid_spec=pltpu.PrefetchScalarGridSpec(
            num_scalar_prefetch=3,
            grid=(per_block,),
            in_specs=in_specs,
            out_specs=pl.BlockSpec((block, lanes, width), lambda i, *_: (i, 0, 0)),
            scratch_shapes=[
                pltpu.VMEM((slots, heads, 2, PAGE, width), jnp.bfloat16),
                pltpu.SemaphoreType.DMA((slots,)),
            ],
        ),
        out_shape=jax.ShapeDtypeStruct((per_target, lanes, width), jnp.bfloat16),
        compiler_params=params(),
        cost_estimate=pl.CostEstimate(
            flops=per_target * lanes * extra * PAGE * width * 16,
            bytes_accessed=8 * 10**6,
            transcendentals=per_target * lanes * extra * PAGE,
        ),
    )(*scalars, q, acc, ml, *blocks)


def join_kernel(targets, chunks, steps, meta_ref, *refs):
    out_ref = refs[-1]
    k = pl.program_id(0)
    rows = refs[0].shape[1]
    each = rows // steps
    for s in range(targets):
        @pl.when(lax.rem(meta_ref[1] + (targets - s), targets) == k)
        def _():
            for c in range(chunks):
                source = refs[s * chunks + c]

                def body(r, carry):
                    value = source[r]
                    for g in range(each):
                        out_ref[r, :, (c * each + g) * 128 : (c * each + g + 1) * 128] = value[
                            g * steps : (g + 1) * steps
                        ]
                    return carry

                lax.fori_loop(0, out_ref.shape[0], body, 0)


def join(pieces, meta, steps, targets, chunks):
    per_target, rows, width = pieces[0].shape
    half = chunks * (rows // steps) * width
    spec = pl.BlockSpec((per_target, rows, width), lambda k, *_: (0, 0, 0))
    return pl.pallas_call(
        functools.partial(join_kernel, targets, chunks, steps),
        grid_spec=pltpu.PrefetchScalarGridSpec(
            num_scalar_prefetch=1,
            grid=(targets,),
            in_specs=[spec] * len(pieces),
            out_specs=pl.BlockSpec((per_target, steps, half), lambda k, *_: (0, 0, k)),
        ),
        out_shape=jax.ShapeDtypeStruct((per_target, steps, half * targets), jnp.bfloat16),
        compiler_params=params(),
        cost_estimate=pl.CostEstimate(flops=0, bytes_accessed=2 * 10**6, transcendentals=0),
    )(meta, *pieces)


def ring_place(index, size):
    return jnp.where(index % 2 == 0, index // 2, size - 1 - index // 2)


def shards(
    roles,
    ring,
    targets,
    prefill_q,
    prefill_k,
    prefill_v,
    decode_q,
    decode_k,
    decode_v,
    cache_k,
    cache_v,
    cache_len,
    page_list,
):
    tokens, q_heads = prefill_q.shape[1:3]
    heads, width = prefill_k.shape[2:]
    group = q_heads // heads
    own_pages = tokens // PAGE
    requests, steps = decode_q.shape[:2]
    extra = page_list.shape[1]
    role = lax.axis_index("role")
    ctx = lax.axis_index("ctx")
    tp = lax.axis_index("tp")

    order = list(range(0, ring, 2)) + list(range(ring - 1, 0, -2))
    along = [(order[j], order[(j + 1) % ring]) for j in range(ring)]
    flips = [1 << b for b in reversed(range(roles.bit_length() - 1))]

    owner = page_list // own_pages
    place = (ring_place(ctx, ring) - ring_place(owner % ring, ring)) % ring
    slot = ((owner // ring) ^ role) * ring + place
    hot = slot.reshape(-1, 1) == jnp.arange(roles * ring)[None, :]
    pick = jnp.max(jnp.where(hot, (page_list % own_pages).reshape(-1, 1), 0), axis=0)
    meta = jnp.stack([ctx, tp]).astype(jnp.int32)
    scalars = (
        slot.reshape(-1).astype(jnp.int32),
        pick.astype(jnp.int32),
        meta,
    )
    position = jnp.arange(ring)
    where = ring_place(ctx, ring)
    source = (where - position) % ring
    source_ctx = jnp.where(source < (ring + 1) // 2, 2 * source, 2 * (ring - 1 - source) + 1)
    flags = (source_ctx < ctx).astype(jnp.int32)
    flags = jnp.where(position == 0, 0, flags)
    last_needed = flags[ring - 1 :]
    earlier = jnp.where(position == 0, jnp.sum(flags[: ring - 1]), flags)

    raw = [
        a.reshape(requests, -1, width) for a in (decode_q, decode_k, decode_v, cache_k, cache_v)
    ]

    gathered = {(0, 0): split_heads(prefill_k, prefill_v)}
    fresh = [(0, 0)]
    for k in range(ring + len(flips) - 1):
        arrived = {}
        for code, s in fresh:
            block = gathered[code, s]
            if code == 0 and s + 1 < ring:
                arrived[0, s + 1] = lax.ppermute(block, "ctx", along)
            for flip in flips:
                if code == 0 or flip < code & -code:
                    pairs = [(j, j ^ flip) for j in range(roles)]
                    arrived[code ^ flip, s] = lax.ppermute(block, "role", pairs)
        beside = ()
        if k == 0:
            beside = cache_part(*raw, cache_len.astype(jnp.int32), steps, heads, group)
        if k == ring - 2:
            beside = prefill(prefill_q, [gathered[0, s] for s in range(ring - 1)], earlier)
        if k == ring - 1:
            beside = prefill_finish(prefill_q, gathered[0, ring - 1], last_needed, *state)
        arrived, beside = lax.optimization_barrier((arrived, beside))
        if k == 0:
            acc, ml = beside
        if k == ring - 2:
            state = beside
        if k == ring - 1:
            prefill_out = beside
        gathered.update(arrived)
        fresh = list(arrived)

    blocks = [gathered[r, s] for r in range(roles) for s in range(ring)]
    pieces = [None] * targets
    for s in reversed(range(targets)):
        out = decode(raw[0], acc, ml, blocks, scalars, s, targets, extra, steps, heads, group)
        if s:
            shift = [(j, (j + s) % targets) for j in range(targets)]
            out = lax.ppermute(out, "tp", shift)
        pieces[s] = out
    decode_out = join(pieces, meta, steps, targets, 1)
    return (prefill_out, decode_out)


def solution(mesh):
    body = functools.partial(shards, mesh.shape["role"], mesh.shape["ctx"], mesh.shape["tp"])
    return jax.shard_map(
        body,
        mesh=mesh,
        in_specs=(
            P("role", "ctx", "tp", None),
            P("role", "ctx", "tp", None),
            P("role", "ctx", "tp", None),
            P(("role", "ctx"), None, "tp", None),
            P(("role", "ctx"), None, "tp", None),
            P(("role", "ctx"), None, "tp", None),
            P(("role", "ctx"), None, "tp", None),
            P(("role", "ctx"), None, "tp", None),
            P(("role", "ctx")),
            P(("role", "ctx"), None),
        ),
        out_specs=(P("role", "ctx", "tp", None), P(("role", "ctx", "tp"), None, None)),
        check_vma=False,
    )
```

```python
import functools
import math

import jax
import jax.numpy as jnp
from jax import lax
from jax.experimental import pallas as pl
from jax.experimental.pallas import tpu as pltpu
from jax.sharding import PartitionSpec as P

PAGE = 128
LOG2E = 1.4426950408889634
NEG = -1e30
VMEM_LIMIT = 60 * 1024 * 1024


def nt(a, b):
    return lax.dot_general(a, b, (((1,), (1,)), ((), ())), preferred_element_type=jnp.float32)


def nn(a, b):
    return jnp.dot(a, b, preferred_element_type=jnp.float32)


def params():
    return pltpu.CompilerParams(vmem_limit_bytes=VMEM_LIMIT)


def one_hot(out_rows, in_rows, source):
    row = lax.broadcasted_iota(jnp.int32, (out_rows, in_rows), 0)
    col = lax.broadcasted_iota(jnp.int32, (out_rows, in_rows), 1)
    return jnp.where(col == source(row), 1.0, 0.0).astype(jnp.bfloat16)


def split_kernel(heads, tokens, k_ref, v_ref, out_ref):
    rows = min(tokens * heads, 256)
    step = rows // heads
    pick = one_hot(rows, rows, lambda i: (i % step) * heads + i // step)
    moved, kept = [], []
    for j in range(tokens // step):
        keys = nn(pick, k_ref[pl.ds(j * rows, rows), :]).astype(jnp.bfloat16)
        moved.append(nn(pick, v_ref[pl.ds(j * rows, rows), :]))
        kept.append(keys)
    for h in range(heads):
        keys = jnp.concatenate([a[h * step : (h + 1) * step] for a in kept], axis=0)
        values = jnp.concatenate([a[h * step : (h + 1) * step] for a in moved], axis=0)
        for page in range(tokens // PAGE):
            out_ref[page, h, 0] = keys[page * PAGE : (page + 1) * PAGE]
            out_ref[page, h, 1] = values[page * PAGE : (page + 1) * PAGE].T.astype(jnp.bfloat16)


def split_heads(k, v):
    _, tokens, heads, width = k.shape
    return pl.pallas_call(
        functools.partial(split_kernel, heads, tokens),
        out_shape=jax.ShapeDtypeStruct((tokens // PAGE, heads, 2, PAGE, width), jnp.bfloat16),
        compiler_params=params(),
        cost_estimate=pl.CostEstimate(flops=10**8, bytes_accessed=2 * 10**6, transcendentals=0),
    )(k.reshape(tokens * heads, width), v.reshape(tokens * heads, width))


def prefill_kernel(ring, group, tokens, scale, earlier_ref, *refs):
    q_ref = refs[0]
    blocks = refs[1 : 1 + ring]
    out_ref, buf, s_ref, m_ref, l_ref, acc_ref, sems = refs[1 + ring :]
    own = blocks[0]
    pages, heads = own.shape[:2]
    block = q_ref.shape[1]
    i = pl.program_id(0)

    def copies():
        found = []
        place = jnp.int32(0)
        for s in range(1, ring):
            copy = pltpu.make_async_copy(blocks[s], buf.at[place], sems.at[s])
            found.append((earlier_ref[s], copy))
            place = place + earlier_ref[s]
        return found

    @pl.when(i == 0)
    def _():
        for flag, copy in copies():
            @pl.when(flag == 1)
            def _():
                copy.start()
        for flag, copy in copies():
            @pl.when(flag == 1)
            def _():
                copy.wait()

    rows = block * group
    queries = q_ref[0].astype(jnp.float32)
    q = [
        queries[:, h * group : (h + 1) * group, :].reshape(rows, -1).astype(jnp.bfloat16)
        for h in range(heads)
    ]

    def fold(a, op):
        return functools.reduce(op, [a[:, j * 128 : (j + 1) * 128] for j in range(a.shape[1] // 128)])

    token = lax.broadcasted_iota(jnp.int32, (rows, tokens), 0) // group + i * block
    allowed = lax.broadcasted_iota(jnp.int32, (rows, tokens), 1) <= token

    def keys(ref, h):
        return jnp.concatenate([ref[j, h, 0] for j in range(pages)], axis=0)

    def values(ref, h):
        return jnp.concatenate([ref[j, h, 1] for j in range(pages)], axis=1)

    last = ring - 1
    for h in range(heads):
        s = jnp.where(allowed, nt(q[h], keys(own, h)), NEG)
        s_ref[last, h] = s
        m_ref[h] = fold(s, jnp.maximum)

    def look(b, carry):
        for h in range(heads):
            s = nt(q[h], keys(buf.at[b], h))
            s_ref[b, h] = s
            m_ref[h] = jnp.maximum(m_ref[h], fold(s, jnp.maximum))
        return carry

    lax.fori_loop(0, earlier_ref[0], look, 0)
    for h in range(heads):
        m = jnp.max(m_ref[h], axis=1, keepdims=True)
        m_ref[h] = jnp.broadcast_to(m, m_ref.shape[1:])
        p = jnp.exp2((s_ref[last, h] - m) * scale)
        l_ref[h] = fold(p, jnp.add)
        acc_ref[h] = nt(p.astype(jnp.bfloat16), values(own, h))

    def weigh(b, carry):
        for h in range(heads):
            m = m_ref[h]
            p = [
                jnp.exp2((s_ref[b, h, :, pl.ds(j * 128, 128)] - m) * scale)
                for j in range(tokens // 128)
            ]
            l_ref[h] = l_ref[h] + functools.reduce(jnp.add, p)
            p = jnp.concatenate([a.astype(jnp.bfloat16) for a in p], axis=1)
            acc_ref[h] = acc_ref[h] + nt(p, values(buf.at[b], h))
        return carry

    lax.fori_loop(0, earlier_ref[0], weigh, 0)
    out = []
    for h in range(heads):
        total = jnp.sum(l_ref[h], axis=1, keepdims=True)
        out.append((acc_ref[h] / total).reshape(block, group, -1))
    out_ref[0] = jnp.concatenate(out, axis=1).astype(out_ref.dtype)


def prefill(q, blocks, earlier):
    _, tokens, q_heads, width = q.shape
    ring = len(blocks)
    heads = blocks[0].shape[1]
    group = q_heads // heads
    block = 64
    rows = block * group
    q_spec = pl.BlockSpec((1, block, q_heads, width), lambda i, *_: (0, i, 0, 0))
    own_spec = pl.BlockSpec(blocks[0].shape, lambda i, *_: (0, 0, 0, 0, 0))
    return pl.pallas_call(
        functools.partial(prefill_kernel, ring, group, tokens, LOG2E / math.sqrt(width)),
        grid_spec=pltpu.PrefetchScalarGridSpec(
            num_scalar_prefetch=1,
            grid=(tokens // block,),
            in_specs=[q_spec, own_spec] + [pl.BlockSpec(memory_space=pl.ANY)] * (ring - 1),
            out_specs=q_spec,
            scratch_shapes=[
                pltpu.VMEM((max(ring - 1, 1),) + blocks[0].shape, jnp.bfloat16),
                pltpu.VMEM((ring, heads, rows, tokens), jnp.float32),
                pltpu.VMEM((heads, rows, width), jnp.float32),
                pltpu.VMEM((heads, rows, width), jnp.float32),
                pltpu.VMEM((heads, rows, width), jnp.float32),
                pltpu.SemaphoreType.DMA((ring,)),
            ],
        ),
        out_shape=jax.ShapeDtypeStruct(q.shape, jnp.bfloat16),
        compiler_params=params(),
        cost_estimate=pl.CostEstimate(
            flops=16 * q_heads * tokens * tokens * ring * width,
            bytes_accessed=4 * 10**6,
            transcendentals=tokens * tokens * ring * q_heads,
        ),
    )(earlier, q, *blocks)


def cache_kernel(
    steps, heads, group, scale, len_ref, q_ref, dk_ref, dv_ref, ck_ref, cv_ref, acc_ref, ml_ref
):
    block, rows, width = q_ref.shape
    cache = ck_ref.shape[1]
    new = dk_ref.shape[1]
    per_step = heads * group

    def mask(columns):
        row = lax.broadcasted_iota(jnp.int32, (rows, columns), 0)
        column = lax.broadcasted_iota(jnp.int32, (rows, columns), 1)
        same = column % heads == row % per_step // group
        return jnp.where(same, column // heads, 1 << 20), row // per_step

    place, _ = mask(cache)
    new_place, step = mask(new)
    new_allowed = new_place <= step
    low = lax.broadcasted_iota(jnp.int32, (rows, width), 1) < 4
    first = pl.program_id(0) * block
    unroll = math.gcd(4, block)

    def body(g, carry):
        scores = []
        for u in range(unroll):
            r = g * unroll + u
            q = q_ref[r]
            old = jnp.where(place < len_ref[first + r], nt(q, ck_ref[r]), NEG)
            add = jnp.where(new_allowed, nt(q, dk_ref[r]), NEG)
            scores.append((r, old, add))
        weights = []
        for r, old, add in scores:
            m = jnp.maximum(
                jnp.max(old, axis=1, keepdims=True), jnp.max(add, axis=1, keepdims=True)
            )
            old = jnp.exp2((old - m) * scale)
            add = jnp.exp2((add - m) * scale)
            l = jnp.sum(old, axis=1, keepdims=True) + jnp.sum(add, axis=1, keepdims=True)
            ml_ref[r] = jnp.where(low, m, l).T[:8]
            weights.append((r, old.astype(jnp.bfloat16), add.astype(jnp.bfloat16)))
        for r, old, add in weights:
            acc_ref[r] = (nn(old, cv_ref[r]) + nn(add, dv_ref[r])).T
        return carry

    lax.fori_loop(0, block // unroll, body, 0)


def cache_part(q, dk, dv, ck, cv, lens, steps, heads, group):
    requests, rows, width = q.shape
    block = math.gcd(8, requests)
    spec = [
        pl.BlockSpec((block,) + a.shape[1:], lambda i, *_: (i, 0, 0)) for a in (q, dk, dv, ck, cv)
    ]
    shapes = [(requests, width, rows), (requests, 8, rows)]
    return pl.pallas_call(
        functools.partial(cache_kernel, steps, heads, group, LOG2E / math.sqrt(width)),
        grid_spec=pltpu.PrefetchScalarGridSpec(
            num_scalar_prefetch=1,
            grid=(requests // block,),
            in_specs=spec,
            out_specs=[pl.BlockSpec((block,) + a[1:], lambda i, *_: (i, 0, 0)) for a in shapes],
        ),
        out_shape=[jax.ShapeDtypeStruct(a, jnp.float32) for a in shapes],
        compiler_params=params(),
        cost_estimate=pl.CostEstimate(
            flops=requests * rows * ck.shape[1] * width * 16,
            bytes_accessed=14 * 10**6,
            transcendentals=requests * rows * ck.shape[1],
        ),
    )(lens, q, dk, dv, ck, cv)


def decode_kernel(slots, extra, steps, target, targets, heads, group, scale, *refs):
    slot_ref, pick_ref, meta_ref = refs[:3]
    q_ref, acc_ref, ml_ref = refs[3:6]
    blocks = refs[6 : 6 + slots]
    out_ref, buf, sems = refs[6 + slots :]
    block, lanes, width = q_ref.shape
    i = pl.program_id(0)
    first = (lax.rem(meta_ref[1] + target, targets) * pl.num_programs(0) + i) * block

    def copies():
        for s in range(slots):
            yield pltpu.make_async_copy(blocks[s].at[pick_ref[s]], buf.at[s], sems.at[s])

    @pl.when(i == 0)
    def _():
        for copy in copies():
            copy.start()
        for copy in copies():
            copy.wait()

    per_step = heads * group
    row_head = lax.broadcasted_iota(jnp.int32, (lanes, width), 0) % per_step // group
    head_rows = [jnp.where(row_head == h, 1.0, 0.0).astype(jnp.bfloat16) for h in range(heads)]
    lane_head = lax.broadcasted_iota(jnp.int32, (width, lanes), 1) % per_step // group
    order = one_hot(lanes, lanes, lambda r: r % steps * per_step + r // steps)
    unroll = math.gcd(2, block)
    count = block // unroll

    def pages_of(r):
        return [slot_ref[(first + r) * extra + j] for j in range(extra)]

    def score(g):
        found = []
        for u in range(unroll):
            r = g * unroll + u
            q = q_ref[r]
            keys = jnp.concatenate(
                [
                    jnp.concatenate([buf[place, h, 0] for h in range(heads)], axis=1)
                    for place in pages_of(r)
                ],
                axis=0,
            )
            spread = jnp.concatenate([q * a for a in head_rows], axis=1)
            found.append(nt(keys, spread))
        return tuple(found)

    def body(g, scores):
        later = score(jnp.minimum(g + 1, count - 1))
        weights = []
        for u in range(unroll):
            r = g * unroll + u
            s = scores[u]
            old = ml_ref[r, 0:1]
            m = jnp.maximum(jnp.max(s, axis=0, keepdims=True), old)
            p = jnp.exp2((s - m) * scale)
            shrink = jnp.exp2((old - m) * scale)
            l = ml_ref[r, 4:5] * shrink + jnp.sum(p, axis=0, keepdims=True)
            weights.append((r, p.astype(jnp.bfloat16), shrink, l))
        for r, p, shrink, l in weights:
            places = pages_of(r)
            values = jnp.concatenate(
                [
                    jnp.concatenate([buf[place, h, 1] for place in places], axis=1)
                    for h in range(heads)
                ],
                axis=0,
            )
            every = nn(values, p)
            part = every[:width]
            for h in range(1, heads):
                part = jnp.where(lane_head == h, every[h * width : (h + 1) * width], part)
            result = ((acc_ref[r] * shrink + part) / l).astype(jnp.bfloat16)
            out_ref[r] = nt(order, result).astype(jnp.bfloat16)
        return later

    lax.fori_loop(0, count, body, score(0))


def decode(q, acc, ml, blocks, scalars, target, targets, extra, steps, heads, group):
    requests, lanes, width = q.shape
    per_target = requests // targets
    block = math.gcd(16, per_target)
    per_block = per_target // block
    slots = len(blocks)

    def here(i, slot, pick, meta):
        return (lax.rem(meta[1] + target, targets) * per_block + i, 0, 0)

    in_specs = [pl.BlockSpec((block,) + a.shape[1:], here) for a in (q, acc, ml)]
    in_specs += [pl.BlockSpec(memory_space=pl.ANY)] * slots
    return pl.pallas_call(
        functools.partial(
            decode_kernel,
            slots,
            extra,
            steps,
            target,
            targets,
            heads,
            group,
            LOG2E / math.sqrt(width),
        ),
        grid_spec=pltpu.PrefetchScalarGridSpec(
            num_scalar_prefetch=3,
            grid=(per_block,),
            in_specs=in_specs,
            out_specs=pl.BlockSpec((block, lanes, width), lambda i, *_: (i, 0, 0)),
            scratch_shapes=[
                pltpu.VMEM((slots, heads, 2, PAGE, width), jnp.bfloat16),
                pltpu.SemaphoreType.DMA((slots,)),
            ],
        ),
        out_shape=jax.ShapeDtypeStruct((per_target, lanes, width), jnp.bfloat16),
        compiler_params=params(),
        cost_estimate=pl.CostEstimate(
            flops=per_target * lanes * extra * PAGE * width * 16,
            bytes_accessed=8 * 10**6,
            transcendentals=per_target * lanes * extra * PAGE,
        ),
    )(*scalars, q, acc, ml, *blocks)


def join_kernel(targets, chunks, steps, meta_ref, *refs):
    out_ref = refs[-1]
    k = pl.program_id(0)
    rows = refs[0].shape[1]
    each = rows // steps
    for s in range(targets):
        @pl.when(lax.rem(meta_ref[1] + (targets - s), targets) == k)
        def _():
            for c in range(chunks):
                source = refs[s * chunks + c]

                def body(r, carry):
                    value = source[r]
                    for g in range(each):
                        out_ref[r, :, (c * each + g) * 128 : (c * each + g + 1) * 128] = value[
                            g * steps : (g + 1) * steps
                        ]
                    return carry

                lax.fori_loop(0, out_ref.shape[0], body, 0)


def join(pieces, meta, steps, targets, chunks):
    per_target, rows, width = pieces[0].shape
    half = chunks * (rows // steps) * width
    spec = pl.BlockSpec((per_target, rows, width), lambda k, *_: (0, 0, 0))
    return pl.pallas_call(
        functools.partial(join_kernel, targets, chunks, steps),
        grid_spec=pltpu.PrefetchScalarGridSpec(
            num_scalar_prefetch=1,
            grid=(targets,),
            in_specs=[spec] * len(pieces),
            out_specs=pl.BlockSpec((per_target, steps, half), lambda k, *_: (0, 0, k)),
        ),
        out_shape=jax.ShapeDtypeStruct((per_target, steps, half * targets), jnp.bfloat16),
        compiler_params=pltpu.CompilerParams(vmem_limit_bytes=16 * 1024 * 1024),
        cost_estimate=pl.CostEstimate(flops=0, bytes_accessed=2 * 10**6, transcendentals=0),
    )(meta, *pieces)


def ring_place(index, size):
    return jnp.where(index % 2 == 0, index // 2, size - 1 - index // 2)


def shards(
    roles,
    ring,
    targets,
    prefill_q,
    prefill_k,
    prefill_v,
    decode_q,
    decode_k,
    decode_v,
    cache_k,
    cache_v,
    cache_len,
    page_list,
):
    tokens, q_heads = prefill_q.shape[1:3]
    heads, width = prefill_k.shape[2:]
    group = q_heads // heads
    own_pages = tokens // PAGE
    requests, steps = decode_q.shape[:2]
    extra = page_list.shape[1]
    role = lax.axis_index("role")
    ctx = lax.axis_index("ctx")
    tp = lax.axis_index("tp")

    order = list(range(0, ring, 2)) + list(range(ring - 1, 0, -2))
    along = [(order[j], order[(j + 1) % ring]) for j in range(ring)]
    flips = [1 << b for b in reversed(range(roles.bit_length() - 1))]

    owner = page_list // own_pages
    place = (ring_place(ctx, ring) - ring_place(owner % ring, ring)) % ring
    slot = ((owner // ring) ^ role) * ring + place
    hot = slot.reshape(-1, 1) == jnp.arange(roles * ring)[None, :]
    pick = jnp.max(jnp.where(hot, (page_list % own_pages).reshape(-1, 1), 0), axis=0)
    meta = jnp.stack([ctx, tp]).astype(jnp.int32)
    scalars = (
        slot.reshape(-1).astype(jnp.int32),
        pick.astype(jnp.int32),
        meta,
    )
    position = jnp.arange(ring)
    where = ring_place(ctx, ring)
    source = (where - position) % ring
    source_ctx = jnp.where(source < (ring + 1) // 2, 2 * source, 2 * (ring - 1 - source) + 1)
    flags = (source_ctx < ctx).astype(jnp.int32)
    earlier = jnp.where(position == 0, jnp.sum(flags), flags)

    raw = [
        a.reshape(requests, -1, width) for a in (decode_q, decode_k, decode_v, cache_k, cache_v)
    ]

    gathered = {(0, 0): split_heads(prefill_k, prefill_v)}
    fresh = [(0, 0)]
    for k in range(ring + len(flips) - 1):
        arrived = {}
        for code, s in fresh:
            block = gathered[code, s]
            if code == 0 and s + 1 < ring:
                arrived[0, s + 1] = lax.ppermute(block, "ctx", along)
            for flip in flips:
                if code == 0 or flip < code & -code:
                    pairs = [(j, j ^ flip) for j in range(roles)]
                    arrived[code ^ flip, s] = lax.ppermute(block, "role", pairs)
        beside = ()
        if k == 0:
            beside = cache_part(*raw, cache_len.astype(jnp.int32), steps, heads, group)
        if k == ring - 1:
            beside = prefill(prefill_q, [gathered[0, s] for s in range(ring)], earlier)
        arrived, beside = lax.optimization_barrier((arrived, beside))
        if k == 0:
            acc, ml = beside
        if k == ring - 1:
            prefill_out = beside
        gathered.update(arrived)
        fresh = list(arrived)

    blocks = [gathered[r, s] for r in range(roles) for s in range(ring)]
    pieces = [None] * targets
    for s in reversed(range(targets)):
        out = decode(raw[0], acc, ml, blocks, scalars, s, targets, extra, steps, heads, group)
        if s:
            shift = [(j, (j + s) % targets) for j in range(targets)]
            out = lax.ppermute(out, "tp", shift)
        pieces[s] = out
    decode_out = join(pieces, meta, steps, targets, 1)
    return (prefill_out, decode_out)


def solution(mesh):
    body = functools.partial(shards, mesh.shape["role"], mesh.shape["ctx"], mesh.shape["tp"])
    return jax.shard_map(
        body,
        mesh=mesh,
        in_specs=(
            P("role", "ctx", "tp", None),
            P("role", "ctx", "tp", None),
            P("role", "ctx", "tp", None),
            P(("role", "ctx"), None, "tp", None),
            P(("role", "ctx"), None, "tp", None),
            P(("role", "ctx"), None, "tp", None),
            P(("role", "ctx"), None, "tp", None),
            P(("role", "ctx"), None, "tp", None),
            P(("role", "ctx")),
            P(("role", "ctx"), None),
        ),
        out_specs=(P("role", "ctx", "tp", None), P(("role", "ctx", "tp"), None, None)),
        check_vma=False,
    )
```

```python
import functools
import math

import jax
import jax.numpy as jnp
from jax import lax
from jax.experimental import pallas as pl
from jax.experimental.pallas import tpu as pltpu
from jax.sharding import PartitionSpec as P

PAGE = 128
LOG2E = 1.4426950408889634
NEG = -1e30
VMEM_LIMIT = 60 * 1024 * 1024


def nt(a, b):
    return lax.dot_general(a, b, (((1,), (1,)), ((), ())), preferred_element_type=jnp.float32)


def nn(a, b):
    return jnp.dot(a, b, preferred_element_type=jnp.float32)


def params():
    return pltpu.CompilerParams(vmem_limit_bytes=VMEM_LIMIT)


def one_hot(out_rows, in_rows, source):
    row = lax.broadcasted_iota(jnp.int32, (out_rows, in_rows), 0)
    col = lax.broadcasted_iota(jnp.int32, (out_rows, in_rows), 1)
    return jnp.where(col == source(row), 1.0, 0.0).astype(jnp.bfloat16)


def split_kernel(heads, tokens, k_ref, v_ref, out_ref):
    rows = min(tokens * heads, 256)
    step = rows // heads
    pick = one_hot(rows, rows, lambda i: (i % step) * heads + i // step)
    moved, kept = [], []
    for j in range(tokens // step):
        keys = nn(pick, k_ref[pl.ds(j * rows, rows), :]).astype(jnp.bfloat16)
        moved.append(nn(pick, v_ref[pl.ds(j * rows, rows), :]))
        kept.append(keys)
    for h in range(heads):
        keys = jnp.concatenate([a[h * step : (h + 1) * step] for a in kept], axis=0)
        values = jnp.concatenate([a[h * step : (h + 1) * step] for a in moved], axis=0)
        for page in range(tokens // PAGE):
            out_ref[page, h, 0] = keys[page * PAGE : (page + 1) * PAGE]
            out_ref[page, h, 1] = values[page * PAGE : (page + 1) * PAGE].T.astype(jnp.bfloat16)


def split_heads(k, v):
    _, tokens, heads, width = k.shape
    return pl.pallas_call(
        functools.partial(split_kernel, heads, tokens),
        out_shape=jax.ShapeDtypeStruct((tokens // PAGE, heads, 2, PAGE, width), jnp.bfloat16),
        compiler_params=params(),
        cost_estimate=pl.CostEstimate(flops=10**8, bytes_accessed=2 * 10**6, transcendentals=0),
    )(k.reshape(tokens * heads, width), v.reshape(tokens * heads, width))


def prefill_kernel(own, count, slots, group, tokens, scale, needed_ref, *refs):
    q_ref = refs[0]
    blocks = refs[1 : 1 + count]
    refs = refs[1 + count :]
    if own:
        out_ref, lse_ref, buf, s_ref, m_ref, l_ref, acc_ref, sems = refs
    else:
        old_ref, old_lse_ref, out_ref, buf, s_ref, m_ref, l_ref, acc_ref, sems = refs
    pages, heads = blocks[0].shape[:2]
    block = q_ref.shape[1]
    i = pl.program_id(0)
    rest = range(1 if own else 0, count)
    total = sum(needed_ref[slots[c]] for c in rest)

    def copies():
        found = []
        place = jnp.int32(0)
        for c in rest:
            flag = needed_ref[slots[c]]
            found.append((flag, pltpu.make_async_copy(blocks[c], buf.at[place], sems.at[c])))
            place = place + flag
        return found

    @pl.when(i == 0)
    def _():
        for flag, copy in copies():
            @pl.when(flag == 1)
            def _():
                copy.start()
        for flag, copy in copies():
            @pl.when(flag == 1)
            def _():
                copy.wait()

    rows = block * group
    queries = q_ref[0].astype(jnp.float32)
    q = [
        queries[:, h * group : (h + 1) * group, :].reshape(rows, -1).astype(jnp.bfloat16)
        for h in range(heads)
    ]

    def fold(a, op):
        return functools.reduce(op, [a[:, j * 128 : (j + 1) * 128] for j in range(a.shape[1] // 128)])

    def keys(ref, h):
        return jnp.concatenate([ref[j, h, 0] for j in range(pages)], axis=0)

    def values(ref, h):
        return jnp.concatenate([ref[j, h, 1] for j in range(pages)], axis=1)

    last = count - 1
    if own:
        token = lax.broadcasted_iota(jnp.int32, (rows, tokens), 0) // group + i * block
        allowed = lax.broadcasted_iota(jnp.int32, (rows, tokens), 1) <= token
        for h in range(heads):
            s = jnp.where(allowed, nt(q[h], keys(blocks[0], h)), NEG)
            s_ref[last, h] = s
            m_ref[h] = fold(s, jnp.maximum)
    else:
        for h in range(heads):
            m_ref[h] = old_lse_ref[0, h]

    def look(b, carry):
        for h in range(heads):
            s = nt(q[h], keys(buf.at[b], h))
            s_ref[b, h] = s
            m_ref[h] = jnp.maximum(m_ref[h], fold(s, jnp.maximum))
        return carry

    lax.fori_loop(0, total, look, 0)
    for h in range(heads):
        m = jnp.broadcast_to(jnp.max(m_ref[h], axis=1, keepdims=True), m_ref.shape[1:])
        m_ref[h] = m
        if own:
            p = [
                jnp.exp2((s_ref[last, h, :, pl.ds(j * 128, 128)] - m) * scale)
                for j in range(tokens // 128)
            ]
            l_ref[h] = functools.reduce(jnp.add, p)
            p = jnp.concatenate([a.astype(jnp.bfloat16) for a in p], axis=1)
            acc_ref[h] = nt(p, values(blocks[0], h))
        else:
            share = jnp.exp2((old_lse_ref[0, h] - m) * scale)
            first = lax.broadcasted_iota(jnp.int32, share.shape, 1) == 0
            l_ref[h] = jnp.where(first, share, 0.0)
            acc_ref[h] = old_ref[0, h] * share

    def weigh(b, carry):
        for h in range(heads):
            m = m_ref[h]
            p = [
                jnp.exp2((s_ref[b, h, :, pl.ds(j * 128, 128)] - m) * scale)
                for j in range(tokens // 128)
            ]
            l_ref[h] = l_ref[h] + functools.reduce(jnp.add, p)
            p = jnp.concatenate([a.astype(jnp.bfloat16) for a in p], axis=1)
            acc_ref[h] = acc_ref[h] + nt(p, values(buf.at[b], h))
        return carry

    lax.fori_loop(0, total, weigh, 0)
    out = []
    for h in range(heads):
        l = jnp.sum(l_ref[h], axis=1, keepdims=True)
        l = jnp.broadcast_to(l, m_ref.shape[1:])
        if own:
            out_ref[0, h] = acc_ref[h] / l
            lse_ref[0, h] = m_ref[h] + jnp.log2(l) * (1.0 / scale)
        else:
            out.append((acc_ref[h] / l).reshape(block, group, -1))
    if not own:
        out_ref[0] = jnp.concatenate(out, axis=1).astype(out_ref.dtype)


def prefill(q, blocks, slots, needed, state):
    _, tokens, q_heads, width = q.shape
    own = state is None
    count = len(blocks)
    heads = blocks[0].shape[1]
    group = q_heads // heads
    block = 64
    rows = block * group
    q_spec = pl.BlockSpec((1, block, q_heads, width), lambda i, *_: (0, i, 0, 0))
    own_spec = pl.BlockSpec(blocks[0].shape, lambda i, *_: (0, 0, 0, 0, 0))
    any_spec = pl.BlockSpec(memory_space=pl.ANY)
    state_spec = pl.BlockSpec((1, heads, rows, width), lambda i, *_: (i, 0, 0, 0))
    shape = jax.ShapeDtypeStruct((tokens // block, heads, rows, width), jnp.float32)
    if own:
        in_specs = [q_spec, own_spec] + [any_spec] * (count - 1)
        out_specs, out_shape, state = [state_spec] * 2, [shape] * 2, ()
    else:
        in_specs = [q_spec] + [any_spec] * count + [state_spec] * 2
        out_specs, out_shape = q_spec, jax.ShapeDtypeStruct(q.shape, jnp.bfloat16)
    return pl.pallas_call(
        functools.partial(
            prefill_kernel, own, count, slots, group, tokens, LOG2E / math.sqrt(width)
        ),
        grid_spec=pltpu.PrefetchScalarGridSpec(
            num_scalar_prefetch=1,
            grid=(tokens // block,),
            in_specs=in_specs,
            out_specs=out_specs,
            scratch_shapes=[
                pltpu.VMEM((count,) + blocks[0].shape, jnp.bfloat16),
                pltpu.VMEM((count, heads, rows, tokens), jnp.float32),
                pltpu.VMEM((heads, rows, width), jnp.float32),
                pltpu.VMEM((heads, rows, width), jnp.float32),
                pltpu.VMEM((heads, rows, width), jnp.float32),
                pltpu.SemaphoreType.DMA((count,)),
            ],
        ),
        out_shape=out_shape,
        compiler_params=params(),
        cost_estimate=pl.CostEstimate(
            flops=16 * q_heads * tokens * tokens * count * width,
            bytes_accessed=12 * 10**6,
            transcendentals=tokens * tokens * count * q_heads,
        ),
    )(needed, q, *blocks, *state)


def cache_kernel(
    steps, heads, group, scale, len_ref, q_ref, dk_ref, dv_ref, ck_ref, cv_ref, acc_ref, ml_ref
):
    block, rows, width = q_ref.shape
    cache = ck_ref.shape[1]
    new = dk_ref.shape[1]
    per_step = heads * group

    def mask(columns):
        row = lax.broadcasted_iota(jnp.int32, (rows, columns), 0)
        column = lax.broadcasted_iota(jnp.int32, (rows, columns), 1)
        same = column % heads == row % per_step // group
        return jnp.where(same, column // heads, 1 << 20), row // per_step

    place, _ = mask(cache)
    new_place, step = mask(new)
    new_allowed = new_place <= step
    low = lax.broadcasted_iota(jnp.int32, (rows, width), 1) < 4
    first = pl.program_id(0) * block
    unroll = math.gcd(4, block)

    def body(g, carry):
        scores = []
        for u in range(unroll):
            r = g * unroll + u
            q = q_ref[r]
            old = jnp.where(place < len_ref[first + r], nt(q, ck_ref[r]), NEG)
            add = jnp.where(new_allowed, nt(q, dk_ref[r]), NEG)
            scores.append((r, old, add))
        weights = []
        for r, old, add in scores:
            m = jnp.maximum(
                jnp.max(old, axis=1, keepdims=True), jnp.max(add, axis=1, keepdims=True)
            )
            old = jnp.exp2((old - m) * scale)
            add = jnp.exp2((add - m) * scale)
            l = jnp.sum(old, axis=1, keepdims=True) + jnp.sum(add, axis=1, keepdims=True)
            ml_ref[r] = jnp.where(low, m, l).T[:8]
            weights.append((r, old.astype(jnp.bfloat16), add.astype(jnp.bfloat16)))
        for r, old, add in weights:
            acc_ref[r] = (nn(old, cv_ref[r]) + nn(add, dv_ref[r])).T
        return carry

    lax.fori_loop(0, block // unroll, body, 0)


def cache_part(q, dk, dv, ck, cv, lens, steps, heads, group):
    requests, rows, width = q.shape
    block = math.gcd(8, requests)
    spec = [
        pl.BlockSpec((block,) + a.shape[1:], lambda i, *_: (i, 0, 0)) for a in (q, dk, dv, ck, cv)
    ]
    shapes = [(requests, width, rows), (requests, 8, rows)]
    return pl.pallas_call(
        functools.partial(cache_kernel, steps, heads, group, LOG2E / math.sqrt(width)),
        grid_spec=pltpu.PrefetchScalarGridSpec(
            num_scalar_prefetch=1,
            grid=(requests // block,),
            in_specs=spec,
            out_specs=[pl.BlockSpec((block,) + a[1:], lambda i, *_: (i, 0, 0)) for a in shapes],
        ),
        out_shape=[jax.ShapeDtypeStruct(a, jnp.float32) for a in shapes],
        compiler_params=params(),
        cost_estimate=pl.CostEstimate(
            flops=requests * rows * ck.shape[1] * width * 16,
            bytes_accessed=14 * 10**6,
            transcendentals=requests * rows * ck.shape[1],
        ),
    )(lens, q, dk, dv, ck, cv)


def decode_kernel(slots, extra, steps, target, targets, heads, group, scale, *refs):
    slot_ref, pick_ref, meta_ref = refs[:3]
    q_ref, acc_ref, ml_ref = refs[3:6]
    blocks = refs[6 : 6 + slots]
    out_ref, buf, sems = refs[6 + slots :]
    block, lanes, width = q_ref.shape
    i = pl.program_id(0)
    first = (lax.rem(meta_ref[1] + target, targets) * pl.num_programs(0) + i) * block

    def copies():
        for s in range(slots):
            yield pltpu.make_async_copy(blocks[s].at[pick_ref[s]], buf.at[s], sems.at[s])

    @pl.when(i == 0)
    def _():
        for copy in copies():
            copy.start()
        for copy in copies():
            copy.wait()

    per_step = heads * group
    row_head = lax.broadcasted_iota(jnp.int32, (lanes, width), 0) % per_step // group
    head_rows = [jnp.where(row_head == h, 1.0, 0.0).astype(jnp.bfloat16) for h in range(heads)]
    lane_head = lax.broadcasted_iota(jnp.int32, (width, lanes), 1) % per_step // group
    order = one_hot(lanes, lanes, lambda r: r % steps * per_step + r // steps)
    unroll = math.gcd(2, block)
    count = block // unroll

    def pages_of(r):
        return [slot_ref[(first + r) * extra + j] for j in range(extra)]

    def score(g):
        found = []
        for u in range(unroll):
            r = g * unroll + u
            q = q_ref[r]
            keys = jnp.concatenate(
                [
                    jnp.concatenate([buf[place, h, 0] for h in range(heads)], axis=1)
                    for place in pages_of(r)
                ],
                axis=0,
            )
            spread = jnp.concatenate([q * a for a in head_rows], axis=1)
            found.append(nt(keys, spread))
        return tuple(found)

    def body(g, scores):
        later = score(jnp.minimum(g + 1, count - 1))
        weights = []
        for u in range(unroll):
            r = g * unroll + u
            s = scores[u]
            old = ml_ref[r, 0:1]
            m = jnp.maximum(jnp.max(s, axis=0, keepdims=True), old)
            p = jnp.exp2((s - m) * scale)
            shrink = jnp.exp2((old - m) * scale)
            l = ml_ref[r, 4:5] * shrink + jnp.sum(p, axis=0, keepdims=True)
            weights.append((r, p.astype(jnp.bfloat16), shrink, l))
        for r, p, shrink, l in weights:
            places = pages_of(r)
            values = jnp.concatenate(
                [
                    jnp.concatenate([buf[place, h, 1] for place in places], axis=1)
                    for h in range(heads)
                ],
                axis=0,
            )
            every = nn(values, p)
            part = every[:width]
            for h in range(1, heads):
                part = jnp.where(lane_head == h, every[h * width : (h + 1) * width], part)
            result = ((acc_ref[r] * shrink + part) / l).astype(jnp.bfloat16)
            out_ref[r] = nt(order, result).astype(jnp.bfloat16)
        return later

    lax.fori_loop(0, count, body, score(0))


def decode(q, acc, ml, blocks, scalars, target, targets, extra, steps, heads, group):
    requests, lanes, width = q.shape
    per_target = requests // targets
    block = math.gcd(16, per_target)
    per_block = per_target // block
    slots = len(blocks)

    def here(i, slot, pick, meta):
        return (lax.rem(meta[1] + target, targets) * per_block + i, 0, 0)

    in_specs = [pl.BlockSpec((block,) + a.shape[1:], here) for a in (q, acc, ml)]
    in_specs += [pl.BlockSpec(memory_space=pl.ANY)] * slots
    return pl.pallas_call(
        functools.partial(
            decode_kernel,
            slots,
            extra,
            steps,
            target,
            targets,
            heads,
            group,
            LOG2E / math.sqrt(width),
        ),
        grid_spec=pltpu.PrefetchScalarGridSpec(
            num_scalar_prefetch=3,
            grid=(per_block,),
            in_specs=in_specs,
            out_specs=pl.BlockSpec((block, lanes, width), lambda i, *_: (i, 0, 0)),
            scratch_shapes=[
                pltpu.VMEM((slots, heads, 2, PAGE, width), jnp.bfloat16),
                pltpu.SemaphoreType.DMA((slots,)),
            ],
        ),
        out_shape=jax.ShapeDtypeStruct((per_target, lanes, width), jnp.bfloat16),
        compiler_params=params(),
        cost_estimate=pl.CostEstimate(
            flops=per_target * lanes * extra * PAGE * width * 16,
            bytes_accessed=8 * 10**6,
            transcendentals=per_target * lanes * extra * PAGE,
        ),
    )(*scalars, q, acc, ml, *blocks)


def join_kernel(targets, chunks, steps, meta_ref, *refs):
    out_ref = refs[-1]
    k = pl.program_id(0)
    rows = refs[0].shape[1]
    each = rows // steps
    for s in range(targets):
        @pl.when(lax.rem(meta_ref[1] + (targets - s), targets) == k)
        def _():
            for c in range(chunks):
                source = refs[s * chunks + c]

                def body(r, carry):
                    value = source[r]
                    for g in range(each):
                        out_ref[r, :, (c * each + g) * 128 : (c * each + g + 1) * 128] = value[
                            g * steps : (g + 1) * steps
                        ]
                    return carry

                lax.fori_loop(0, out_ref.shape[0], body, 0)


def join(pieces, meta, steps, targets, chunks):
    per_target, rows, width = pieces[0].shape
    half = chunks * (rows // steps) * width
    spec = pl.BlockSpec((per_target, rows, width), lambda k, *_: (0, 0, 0))
    return pl.pallas_call(
        functools.partial(join_kernel, targets, chunks, steps),
        grid_spec=pltpu.PrefetchScalarGridSpec(
            num_scalar_prefetch=1,
            grid=(targets,),
            in_specs=[spec] * len(pieces),
            out_specs=pl.BlockSpec((per_target, steps, half), lambda k, *_: (0, 0, k)),
        ),
        out_shape=jax.ShapeDtypeStruct((per_target, steps, half * targets), jnp.bfloat16),
        compiler_params=pltpu.CompilerParams(vmem_limit_bytes=16 * 1024 * 1024),
        cost_estimate=pl.CostEstimate(flops=0, bytes_accessed=2 * 10**6, transcendentals=0),
    )(meta, *pieces)


def ring_place(index, size):
    return jnp.where(index % 2 == 0, index // 2, size - 1 - index // 2)


def shards(
    roles,
    ring,
    targets,
    prefill_q,
    prefill_k,
    prefill_v,
    decode_q,
    decode_k,
    decode_v,
    cache_k,
    cache_v,
    cache_len,
    page_list,
):
    tokens, q_heads = prefill_q.shape[1:3]
    heads, width = prefill_k.shape[2:]
    group = q_heads // heads
    own_pages = tokens // PAGE
    requests, steps = decode_q.shape[:2]
    extra = page_list.shape[1]
    role = lax.axis_index("role")
    ctx = lax.axis_index("ctx")
    tp = lax.axis_index("tp")

    order = list(range(0, ring, 2)) + list(range(ring - 1, 0, -2))
    along = [(order[j], order[(j + 1) % ring]) for j in range(ring)]
    flips = [1 << b for b in reversed(range(roles.bit_length() - 1))]

    owner = page_list // own_pages
    place = (ring_place(ctx, ring) - ring_place(owner % ring, ring)) % ring
    slot = ((owner // ring) ^ role) * ring + place
    hot = slot.reshape(-1, 1) == jnp.arange(roles * ring)[None, :]
    pick = jnp.max(jnp.where(hot, (page_list % own_pages).reshape(-1, 1), 0), axis=0)
    meta = jnp.stack([ctx, tp]).astype(jnp.int32)
    scalars = (
        slot.reshape(-1).astype(jnp.int32),
        pick.astype(jnp.int32),
        meta,
    )
    position = jnp.arange(ring)
    where = ring_place(ctx, ring)
    source = (where - position) % ring
    source_ctx = jnp.where(source < (ring + 1) // 2, 2 * source, 2 * (ring - 1 - source) + 1)
    needed = (source_ctx < ctx).astype(jnp.int32)

    raw = [
        a.reshape(requests, -1, width) for a in (decode_q, decode_k, decode_v, cache_k, cache_v)
    ]

    gathered = {(0, 0): split_heads(prefill_k, prefill_v)}
    fresh = [(0, 0)]
    for k in range(ring + len(flips) - 1):
        sends = []
        for code, s in fresh:
            for flip in reversed(flips):
                if code == 0 or flip < code & -code:
                    pairs = [(j, j ^ flip) for j in range(roles)]
                    sends.append((flip, (code, s), (code ^ flip, s), "role", pairs))
            if code == 0 and s + 1 < ring:
                sends.append((roles, (code, s), (0, s + 1), "ctx", along))
        arrived = {
            to: lax.ppermute(gathered[of], axis, pairs)
            for _, of, to, axis, pairs in sorted(sends, key=lambda a: a[0])
        }
        beside = ()
        if k == 0:
            beside = cache_part(*raw, cache_len.astype(jnp.int32), steps, heads, group)
        if k == 1:
            beside = prefill(prefill_q, [gathered[0, s] for s in (0, 1)], (0, 1), needed, None)
        if k == ring - 1:
            later = tuple(range(2, ring))
            beside = prefill(prefill_q, [gathered[0, s] for s in later], later, needed, state)
        arrived, beside = lax.optimization_barrier((arrived, beside))
        if k == 0:
            acc, ml = beside
        if k == 1:
            state = beside
        if k == ring - 1:
            prefill_out = beside
        gathered.update(arrived)
        fresh = list(arrived)

    blocks = [gathered[r, s] for r in range(roles) for s in range(ring)]
    pieces = [None] * targets
    for s in reversed(range(targets)):
        out = decode(raw[0], acc, ml, blocks, scalars, s, targets, extra, steps, heads, group)
        if s:
            shift = [(j, (j + s) % targets) for j in range(targets)]
            out = lax.ppermute(out, "tp", shift)
        pieces[s] = out
    decode_out = join(pieces, meta, steps, targets, 1)
    return (prefill_out, decode_out)


def solution(mesh):
    body = functools.partial(shards, mesh.shape["role"], mesh.shape["ctx"], mesh.shape["tp"])
    return jax.shard_map(
        body,
        mesh=mesh,
        in_specs=(
            P("role", "ctx", "tp", None),
            P("role", "ctx", "tp", None),
            P("role", "ctx", "tp", None),
            P(("role", "ctx"), None, "tp", None),
            P(("role", "ctx"), None, "tp", None),
            P(("role", "ctx"), None, "tp", None),
            P(("role", "ctx"), None, "tp", None),
            P(("role", "ctx"), None, "tp", None),
            P(("role", "ctx")),
            P(("role", "ctx"), None),
        ),
        out_specs=(P("role", "ctx", "tp", None), P(("role", "ctx", "tp"), None, None)),
        check_vma=False,
    )
```

```python
import functools
import math

import jax
import jax.numpy as jnp
from jax import lax
from jax.experimental import pallas as pl
from jax.experimental.pallas import tpu as pltpu
from jax.sharding import PartitionSpec as P

PAGE = 128
LOG2E = 1.4426950408889634
NEG = -1e30
VMEM_LIMIT = 60 * 1024 * 1024


def nt(a, b):
    return lax.dot_general(a, b, (((1,), (1,)), ((), ())), preferred_element_type=jnp.float32)


def nn(a, b):
    return jnp.dot(a, b, preferred_element_type=jnp.float32)


def params():
    return pltpu.CompilerParams(vmem_limit_bytes=VMEM_LIMIT)


def one_hot(out_rows, in_rows, source):
    row = lax.broadcasted_iota(jnp.int32, (out_rows, in_rows), 0)
    col = lax.broadcasted_iota(jnp.int32, (out_rows, in_rows), 1)
    return jnp.where(col == source(row), 1.0, 0.0).astype(jnp.bfloat16)


def split_kernel(heads, tokens, k_ref, v_ref, out_ref):
    rows = min(tokens * heads, 256)
    step = rows // heads
    pick = one_hot(rows, rows, lambda i: (i % step) * heads + i // step)
    moved, kept = [], []
    for j in range(tokens // step):
        keys = nn(pick, k_ref[pl.ds(j * rows, rows), :]).astype(jnp.bfloat16)
        moved.append(nn(pick, v_ref[pl.ds(j * rows, rows), :]))
        kept.append(keys)
    for h in range(heads):
        keys = jnp.concatenate([a[h * step : (h + 1) * step] for a in kept], axis=0)
        values = jnp.concatenate([a[h * step : (h + 1) * step] for a in moved], axis=0)
        for page in range(tokens // PAGE):
            out_ref[page, h, 0] = keys[page * PAGE : (page + 1) * PAGE]
            out_ref[page, h, 1] = values[page * PAGE : (page + 1) * PAGE].T.astype(jnp.bfloat16)


def split_heads(k, v):
    _, tokens, heads, width = k.shape
    return pl.pallas_call(
        functools.partial(split_kernel, heads, tokens),
        out_shape=jax.ShapeDtypeStruct((tokens // PAGE, heads, 2, PAGE, width), jnp.bfloat16),
        compiler_params=params(),
        cost_estimate=pl.CostEstimate(flops=10**8, bytes_accessed=2 * 10**6, transcendentals=0),
    )(k.reshape(tokens * heads, width), v.reshape(tokens * heads, width))


def prefill_kernel(own, count, slots, group, tokens, scale, needed_ref, *refs):
    q_ref = refs[0]
    blocks = refs[1 : 1 + count]
    refs = refs[1 + count :]
    if own:
        out_ref, lse_ref, buf, s_ref, m_ref, l_ref, acc_ref, sems = refs
    else:
        old_ref, old_lse_ref, out_ref, buf, s_ref, m_ref, l_ref, acc_ref, sems = refs
    pages, heads = blocks[0].shape[:2]
    block = q_ref.shape[1]
    i = pl.program_id(0)
    rest = range(1 if own else 0, count)
    total = sum(needed_ref[slots[c]] for c in rest)

    def copies():
        found = []
        place = jnp.int32(0)
        for c in rest:
            flag = needed_ref[slots[c]]
            found.append((flag, pltpu.make_async_copy(blocks[c], buf.at[place], sems.at[c])))
            place = place + flag
        return found

    @pl.when(i == 0)
    def _():
        for flag, copy in copies():
            @pl.when(flag == 1)
            def _():
                copy.start()
        for flag, copy in copies():
            @pl.when(flag == 1)
            def _():
                copy.wait()

    rows = block * group
    queries = q_ref[0].astype(jnp.float32)
    q = [
        queries[:, h * group : (h + 1) * group, :].reshape(rows, -1).astype(jnp.bfloat16)
        for h in range(heads)
    ]

    def fold(a, op):
        return functools.reduce(op, [a[:, j * 128 : (j + 1) * 128] for j in range(a.shape[1] // 128)])

    def keys(ref, h):
        return jnp.concatenate([ref[j, h, 0] for j in range(pages)], axis=0)

    def values(ref, h):
        return jnp.concatenate([ref[j, h, 1] for j in range(pages)], axis=1)

    last = count - 1
    if own:
        token = lax.broadcasted_iota(jnp.int32, (rows, tokens), 0) // group + i * block
        allowed = lax.broadcasted_iota(jnp.int32, (rows, tokens), 1) <= token
        for h in range(heads):
            s = jnp.where(allowed, nt(q[h], keys(blocks[0], h)), NEG)
            s_ref[last, h] = s
            m_ref[h] = fold(s, jnp.maximum)
    else:
        for h in range(heads):
            m_ref[h] = old_lse_ref[0, h]

    def look(b, carry):
        for h in range(heads):
            s = nt(q[h], keys(buf.at[b], h))
            s_ref[b, h] = s
            m_ref[h] = jnp.maximum(m_ref[h], fold(s, jnp.maximum))
        return carry

    lax.fori_loop(0, total, look, 0)
    for h in range(heads):
        m = jnp.broadcast_to(jnp.max(m_ref[h], axis=1, keepdims=True), m_ref.shape[1:])
        m_ref[h] = m
        if own:
            p = [
                jnp.exp2((s_ref[last, h, :, pl.ds(j * 128, 128)] - m) * scale)
                for j in range(tokens // 128)
            ]
            l_ref[h] = functools.reduce(jnp.add, p)
            p = jnp.concatenate([a.astype(jnp.bfloat16) for a in p], axis=1)
            acc_ref[h] = nt(p, values(blocks[0], h))
        else:
            share = jnp.exp2((old_lse_ref[0, h] - m) * scale)
            first = lax.broadcasted_iota(jnp.int32, share.shape, 1) == 0
            l_ref[h] = jnp.where(first, share, 0.0)
            acc_ref[h] = old_ref[0, h] * share

    def weigh(b, carry):
        for h in range(heads):
            m = m_ref[h]
            p = [
                jnp.exp2((s_ref[b, h, :, pl.ds(j * 128, 128)] - m) * scale)
                for j in range(tokens // 128)
            ]
            l_ref[h] = l_ref[h] + functools.reduce(jnp.add, p)
            p = jnp.concatenate([a.astype(jnp.bfloat16) for a in p], axis=1)
            acc_ref[h] = acc_ref[h] + nt(p, values(buf.at[b], h))
        return carry

    lax.fori_loop(0, total, weigh, 0)
    out = []
    for h in range(heads):
        l = jnp.sum(l_ref[h], axis=1, keepdims=True)
        l = jnp.broadcast_to(l, m_ref.shape[1:])
        if own:
            out_ref[0, h] = acc_ref[h] / l
            lse_ref[0, h] = m_ref[h] + jnp.log2(l) * (1.0 / scale)
        else:
            out.append((acc_ref[h] / l).reshape(block, group, -1))
    if not own:
        out_ref[0] = jnp.concatenate(out, axis=1).astype(out_ref.dtype)


def prefill(q, blocks, slots, needed, state):
    _, tokens, q_heads, width = q.shape
    own = state is None
    count = len(blocks)
    heads = blocks[0].shape[1]
    group = q_heads // heads
    block = 64
    rows = block * group
    q_spec = pl.BlockSpec((1, block, q_heads, width), lambda i, *_: (0, i, 0, 0))
    own_spec = pl.BlockSpec(blocks[0].shape, lambda i, *_: (0, 0, 0, 0, 0))
    any_spec = pl.BlockSpec(memory_space=pl.ANY)
    state_spec = pl.BlockSpec((1, heads, rows, width), lambda i, *_: (i, 0, 0, 0))
    shape = jax.ShapeDtypeStruct((tokens // block, heads, rows, width), jnp.float32)
    if own:
        in_specs = [q_spec, own_spec] + [any_spec] * (count - 1)
        out_specs, out_shape, state = [state_spec] * 2, [shape] * 2, ()
    else:
        in_specs = [q_spec] + [any_spec] * count + [state_spec] * 2
        out_specs, out_shape = q_spec, jax.ShapeDtypeStruct(q.shape, jnp.bfloat16)
    return pl.pallas_call(
        functools.partial(
            prefill_kernel, own, count, slots, group, tokens, LOG2E / math.sqrt(width)
        ),
        grid_spec=pltpu.PrefetchScalarGridSpec(
            num_scalar_prefetch=1,
            grid=(tokens // block,),
            in_specs=in_specs,
            out_specs=out_specs,
            scratch_shapes=[
                pltpu.VMEM((count,) + blocks[0].shape, jnp.bfloat16),
                pltpu.VMEM((count, heads, rows, tokens), jnp.float32),
                pltpu.VMEM((heads, rows, width), jnp.float32),
                pltpu.VMEM((heads, rows, width), jnp.float32),
                pltpu.VMEM((heads, rows, width), jnp.float32),
                pltpu.SemaphoreType.DMA((count,)),
            ],
        ),
        out_shape=out_shape,
        compiler_params=params(),
        cost_estimate=pl.CostEstimate(
            flops=16 * q_heads * tokens * tokens * count * width,
            bytes_accessed=12 * 10**6,
            transcendentals=tokens * tokens * count * q_heads,
        ),
    )(needed, q, *blocks, *state)


def cache_kernel(
    steps, heads, group, scale, len_ref, q_ref, dk_ref, dv_ref, ck_ref, cv_ref, acc_ref, ml_ref
):
    block, rows, width = q_ref.shape
    cache = ck_ref.shape[1]
    new = dk_ref.shape[1]
    per_step = heads * group

    def mask(columns):
        row = lax.broadcasted_iota(jnp.int32, (rows, columns), 0)
        column = lax.broadcasted_iota(jnp.int32, (rows, columns), 1)
        same = column % heads == row % per_step // group
        return jnp.where(same, column // heads, 1 << 20), row // per_step

    place, _ = mask(cache)
    new_place, step = mask(new)
    new_allowed = new_place <= step
    low = lax.broadcasted_iota(jnp.int32, (rows, width), 1) < 4
    first = pl.program_id(0) * block
    unroll = math.gcd(4, block)

    def body(g, carry):
        scores = []
        for u in range(unroll):
            r = g * unroll + u
            q = q_ref[r]
            old = jnp.where(place < len_ref[first + r], nt(q, ck_ref[r]), NEG)
            add = jnp.where(new_allowed, nt(q, dk_ref[r]), NEG)
            scores.append((r, old, add))
        weights = []
        for r, old, add in scores:
            m = jnp.maximum(
                jnp.max(old, axis=1, keepdims=True), jnp.max(add, axis=1, keepdims=True)
            )
            old = jnp.exp2((old - m) * scale)
            add = jnp.exp2((add - m) * scale)
            l = jnp.sum(old, axis=1, keepdims=True) + jnp.sum(add, axis=1, keepdims=True)
            ml_ref[r] = jnp.where(low, m, l).T[:8]
            weights.append((r, old.astype(jnp.bfloat16), add.astype(jnp.bfloat16)))
        for r, old, add in weights:
            acc_ref[r] = (nn(old, cv_ref[r]) + nn(add, dv_ref[r])).T
        return carry

    lax.fori_loop(0, block // unroll, body, 0)


def cache_part(q, dk, dv, ck, cv, lens, steps, heads, group):
    requests, rows, width = q.shape
    block = math.gcd(8, requests)
    spec = [
        pl.BlockSpec((block,) + a.shape[1:], lambda i, *_: (i, 0, 0)) for a in (q, dk, dv, ck, cv)
    ]
    shapes = [(requests, width, rows), (requests, 8, rows)]
    return pl.pallas_call(
        functools.partial(cache_kernel, steps, heads, group, LOG2E / math.sqrt(width)),
        grid_spec=pltpu.PrefetchScalarGridSpec(
            num_scalar_prefetch=1,
            grid=(requests // block,),
            in_specs=spec,
            out_specs=[pl.BlockSpec((block,) + a[1:], lambda i, *_: (i, 0, 0)) for a in shapes],
        ),
        out_shape=[jax.ShapeDtypeStruct(a, jnp.float32) for a in shapes],
        compiler_params=params(),
        cost_estimate=pl.CostEstimate(
            flops=requests * rows * ck.shape[1] * width * 16,
            bytes_accessed=14 * 10**6,
            transcendentals=requests * rows * ck.shape[1],
        ),
    )(lens, q, dk, dv, ck, cv)


def decode_kernel(slots, extra, steps, target, targets, heads, group, scale, *refs):
    slot_ref, pick_ref, meta_ref = refs[:3]
    q_ref, acc_ref, ml_ref = refs[3:6]
    blocks = refs[6 : 6 + slots]
    out_ref, buf, sems = refs[6 + slots :]
    block, lanes, width = q_ref.shape
    i = pl.program_id(0)
    first = (lax.rem(meta_ref[1] + target, targets) * pl.num_programs(0) + i) * block

    def copies():
        for s in range(slots):
            yield pltpu.make_async_copy(blocks[s].at[pick_ref[s]], buf.at[s], sems.at[s])

    @pl.when(i == 0)
    def _():
        for copy in copies():
            copy.start()
        for copy in copies():
            copy.wait()

    per_step = heads * group
    row_head = lax.broadcasted_iota(jnp.int32, (lanes, width), 0) % per_step // group
    head_rows = [jnp.where(row_head == h, 1.0, 0.0).astype(jnp.bfloat16) for h in range(heads)]
    lane_head = lax.broadcasted_iota(jnp.int32, (width, lanes), 1) % per_step // group
    order = one_hot(lanes, lanes, lambda r: r % steps * per_step + r // steps)
    unroll = math.gcd(8 if target else 4, block)

    def body(g, carry):
        scores = []
        for u in range(unroll):
            r = g * unroll + u
            q = q_ref[r]
            places = [slot_ref[(first + r) * extra + j] for j in range(extra)]
            spread = jnp.concatenate([q * a for a in head_rows], axis=1)
            s = [
                nt(jnp.concatenate([buf[place, h, 0] for h in range(heads)], axis=1), spread)
                for place in places
            ]
            scores.append((r, places, s))
        weights = []
        for r, places, s in scores:
            old = ml_ref[r, 0:1]
            m = jnp.max(functools.reduce(jnp.maximum, s), axis=0, keepdims=True)
            m = jnp.maximum(m, old)
            p = [jnp.exp2((a - m) * scale) for a in s]
            shrink = jnp.exp2((old - m) * scale)
            l = jnp.sum(functools.reduce(jnp.add, p), axis=0, keepdims=True)
            l = ml_ref[r, 4:5] * shrink + l
            p = jnp.concatenate([a.astype(jnp.bfloat16) for a in p], axis=0)
            weights.append((r, places, p, shrink, l))
        results = []
        for r, places, p, shrink, l in weights:
            part = None
            for h in range(heads):
                values = jnp.concatenate([buf[place, h, 1] for place in places], axis=1)
                mine = nn(values, p)
                part = mine if h == 0 else jnp.where(lane_head == h, mine, part)
            results.append((r, ((acc_ref[r] * shrink + part) / l).astype(jnp.bfloat16)))
        for r, result in results:
            out_ref[r] = nt(order, result).astype(jnp.bfloat16)
        return carry

    lax.fori_loop(0, block // unroll, body, 0)


def decode(q, acc, ml, blocks, scalars, target, targets, extra, steps, heads, group):
    requests, lanes, width = q.shape
    per_target = requests // targets
    block = math.gcd(16, per_target)
    per_block = per_target // block
    slots = len(blocks)

    def here(i, slot, pick, meta):
        return (lax.rem(meta[1] + target, targets) * per_block + i, 0, 0)

    in_specs = [pl.BlockSpec((block,) + a.shape[1:], here) for a in (q, acc, ml)]
    in_specs += [pl.BlockSpec(memory_space=pl.ANY)] * slots
    return pl.pallas_call(
        functools.partial(
            decode_kernel,
            slots,
            extra,
            steps,
            target,
            targets,
            heads,
            group,
            LOG2E / math.sqrt(width),
        ),
        grid_spec=pltpu.PrefetchScalarGridSpec(
            num_scalar_prefetch=3,
            grid=(per_block,),
            in_specs=in_specs,
            out_specs=pl.BlockSpec((block, lanes, width), lambda i, *_: (i, 0, 0)),
            scratch_shapes=[
                pltpu.VMEM((slots, heads, 2, PAGE, width), jnp.bfloat16),
                pltpu.SemaphoreType.DMA((slots,)),
            ],
        ),
        out_shape=jax.ShapeDtypeStruct((per_target, lanes, width), jnp.bfloat16),
        compiler_params=params(),
        cost_estimate=pl.CostEstimate(
            flops=per_target * lanes * extra * PAGE * width * 16,
            bytes_accessed=8 * 10**6,
            transcendentals=per_target * lanes * extra * PAGE,
        ),
    )(*scalars, q, acc, ml, *blocks)


def join_kernel(targets, chunks, steps, meta_ref, *refs):
    out_ref = refs[-1]
    k = pl.program_id(0)
    rows = refs[0].shape[1]
    each = rows // steps
    for s in range(targets):
        @pl.when(lax.rem(meta_ref[1] + (targets - s), targets) == k)
        def _():
            for c in range(chunks):
                source = refs[s * chunks + c]

                def body(r, carry):
                    value = source[r]
                    for g in range(each):
                        out_ref[r, :, (c * each + g) * 128 : (c * each + g + 1) * 128] = value[
                            g * steps : (g + 1) * steps
                        ]
                    return carry

                lax.fori_loop(0, out_ref.shape[0], body, 0)


def join(pieces, meta, steps, targets, chunks):
    per_target, rows, width = pieces[0].shape
    half = chunks * (rows // steps) * width
    spec = pl.BlockSpec((per_target, rows, width), lambda k, *_: (0, 0, 0))
    return pl.pallas_call(
        functools.partial(join_kernel, targets, chunks, steps),
        grid_spec=pltpu.PrefetchScalarGridSpec(
            num_scalar_prefetch=1,
            grid=(targets,),
            in_specs=[spec] * len(pieces),
            out_specs=pl.BlockSpec((per_target, steps, half), lambda k, *_: (0, 0, k)),
        ),
        out_shape=jax.ShapeDtypeStruct((per_target, steps, half * targets), jnp.bfloat16),
        compiler_params=pltpu.CompilerParams(vmem_limit_bytes=16 * 1024 * 1024),
        cost_estimate=pl.CostEstimate(flops=0, bytes_accessed=2 * 10**6, transcendentals=0),
    )(meta, *pieces)


def ring_place(index, size):
    return jnp.where(index % 2 == 0, index // 2, size - 1 - index // 2)


def shards(
    roles,
    ring,
    targets,
    prefill_q,
    prefill_k,
    prefill_v,
    decode_q,
    decode_k,
    decode_v,
    cache_k,
    cache_v,
    cache_len,
    page_list,
):
    tokens, q_heads = prefill_q.shape[1:3]
    heads, width = prefill_k.shape[2:]
    group = q_heads // heads
    own_pages = tokens // PAGE
    requests, steps = decode_q.shape[:2]
    extra = page_list.shape[1]
    role = lax.axis_index("role")
    ctx = lax.axis_index("ctx")
    tp = lax.axis_index("tp")

    order = list(range(0, ring, 2)) + list(range(ring - 1, 0, -2))
    along = [(order[j], order[(j + 1) % ring]) for j in range(ring)]
    flips = [1 << b for b in reversed(range(roles.bit_length() - 1))]

    owner = page_list // own_pages
    place = (ring_place(ctx, ring) - ring_place(owner % ring, ring)) % ring
    slot = ((owner // ring) ^ role) * ring + place
    hot = slot.reshape(-1, 1) == jnp.arange(roles * ring)[None, :]
    pick = jnp.max(jnp.where(hot, (page_list % own_pages).reshape(-1, 1), 0), axis=0)
    meta = jnp.stack([ctx, tp]).astype(jnp.int32)
    scalars = (
        slot.reshape(-1).astype(jnp.int32),
        pick.astype(jnp.int32),
        meta,
    )
    position = jnp.arange(ring)
    where = ring_place(ctx, ring)
    source = (where - position) % ring
    source_ctx = jnp.where(source < (ring + 1) // 2, 2 * source, 2 * (ring - 1 - source) + 1)
    needed = (source_ctx < ctx).astype(jnp.int32)

    raw = [
        a.reshape(requests, -1, width) for a in (decode_q, decode_k, decode_v, cache_k, cache_v)
    ]

    gathered = {(0, 0): split_heads(prefill_k, prefill_v)}
    fresh = [(0, 0)]
    for k in range(ring + len(flips) - 1):
        sends = []
        for code, s in fresh:
            for flip in reversed(flips):
                if code == 0 or flip < code & -code:
                    pairs = [(j, j ^ flip) for j in range(roles)]
                    sends.append((flip, (code, s), (code ^ flip, s), "role", pairs))
            if code == 0 and s + 1 < ring:
                sends.append((roles, (code, s), (0, s + 1), "ctx", along))
        arrived = {
            to: lax.ppermute(gathered[of], axis, pairs)
            for _, of, to, axis, pairs in sorted(sends, key=lambda a: a[0])
        }
        beside = ()
        if k == 0:
            beside = cache_part(*raw, cache_len.astype(jnp.int32), steps, heads, group)
        if k == 1:
            beside = prefill(prefill_q, [gathered[0, s] for s in (0, 1)], (0, 1), needed, None)
        if k == ring - 1:
            later = tuple(range(2, ring))
            beside = prefill(prefill_q, [gathered[0, s] for s in later], later, needed, state)
        arrived, beside = lax.optimization_barrier((arrived, beside))
        if k == 0:
            acc, ml = beside
        if k == 1:
            state = beside
        if k == ring - 1:
            prefill_out = beside
        gathered.update(arrived)
        fresh = list(arrived)

    blocks = [gathered[r, s] for r in range(roles) for s in range(ring)]
    pieces = [None] * targets
    for s in reversed(range(targets)):
        out = decode(raw[0], acc, ml, blocks, scalars, s, targets, extra, steps, heads, group)
        if s:
            shift = [(j, (j + s) % targets) for j in range(targets)]
            out = lax.ppermute(out, "tp", shift)
        pieces[s] = out
    decode_out = join(pieces, meta, steps, targets, 1)
    return (prefill_out, decode_out)


def solution(mesh):
    body = functools.partial(shards, mesh.shape["role"], mesh.shape["ctx"], mesh.shape["tp"])
    return jax.shard_map(
        body,
        mesh=mesh,
        in_specs=(
            P("role", "ctx", "tp", None),
            P("role", "ctx", "tp", None),
            P("role", "ctx", "tp", None),
            P(("role", "ctx"), None, "tp", None),
            P(("role", "ctx"), None, "tp", None),
            P(("role", "ctx"), None, "tp", None),
            P(("role", "ctx"), None, "tp", None),
            P(("role", "ctx"), None, "tp", None),
            P(("role", "ctx")),
            P(("role", "ctx"), None),
        ),
        out_specs=(P("role", "ctx", "tp", None), P(("role", "ctx", "tp"), None, None)),
        check_vma=False,
    )
```

```python
import functools
import math

import jax
import jax.numpy as jnp
from jax import lax
from jax.experimental import pallas as pl
from jax.experimental.pallas import tpu as pltpu
from jax.sharding import PartitionSpec as P

PAGE = 128
LOG2E = 1.4426950408889634
NEG = -1e30
VMEM_LIMIT = 60 * 1024 * 1024


def nt(a, b):
    return lax.dot_general(a, b, (((1,), (1,)), ((), ())), preferred_element_type=jnp.float32)


def nn(a, b):
    return jnp.dot(a, b, preferred_element_type=jnp.float32)


def params():
    return pltpu.CompilerParams(vmem_limit_bytes=VMEM_LIMIT)


def one_hot(out_rows, in_rows, source):
    row = lax.broadcasted_iota(jnp.int32, (out_rows, in_rows), 0)
    col = lax.broadcasted_iota(jnp.int32, (out_rows, in_rows), 1)
    return jnp.where(col == source(row), 1.0, 0.0).astype(jnp.bfloat16)


def split_kernel(heads, tokens, k_ref, v_ref, out_ref):
    rows = min(tokens * heads, 256)
    step = rows // heads
    pick = one_hot(rows, rows, lambda i: (i % step) * heads + i // step)
    moved, kept = [], []
    for j in range(tokens // step):
        keys = nn(pick, k_ref[pl.ds(j * rows, rows), :]).astype(jnp.bfloat16)
        moved.append(nn(pick, v_ref[pl.ds(j * rows, rows), :]))
        kept.append(keys)
    for h in range(heads):
        keys = jnp.concatenate([a[h * step : (h + 1) * step] for a in kept], axis=0)
        values = jnp.concatenate([a[h * step : (h + 1) * step] for a in moved], axis=0)
        for page in range(tokens // PAGE):
            out_ref[page, h, 0] = keys[page * PAGE : (page + 1) * PAGE]
            out_ref[page, h, 1] = values[page * PAGE : (page + 1) * PAGE].T.astype(jnp.bfloat16)


def split_heads(k, v):
    _, tokens, heads, width = k.shape
    return pl.pallas_call(
        functools.partial(split_kernel, heads, tokens),
        out_shape=jax.ShapeDtypeStruct((tokens // PAGE, heads, 2, PAGE, width), jnp.bfloat16),
        compiler_params=params(),
        cost_estimate=pl.CostEstimate(flops=10**8, bytes_accessed=2 * 10**6, transcendentals=0),
    )(k.reshape(tokens * heads, width), v.reshape(tokens * heads, width))


def prefill_kernel(own, count, slots, group, tokens, scale, needed_ref, *refs):
    q_ref = refs[0]
    blocks = refs[1 : 1 + count]
    refs = refs[1 + count :]
    if own:
        out_ref, lse_ref, buf, s_ref, m_ref, l_ref, acc_ref, sems = refs
    else:
        old_ref, old_lse_ref, out_ref, buf, s_ref, m_ref, l_ref, acc_ref, sems = refs
    pages, heads = blocks[0].shape[:2]
    block = q_ref.shape[1]
    i = pl.program_id(0)
    rest = range(1 if own else 0, count)
    total = sum(needed_ref[slots[c]] for c in rest)

    def copies():
        found = []
        place = jnp.int32(0)
        for c in rest:
            flag = needed_ref[slots[c]]
            found.append((flag, pltpu.make_async_copy(blocks[c], buf.at[place], sems.at[c])))
            place = place + flag
        return found

    @pl.when(i == 0)
    def _():
        for flag, copy in copies():
            @pl.when(flag == 1)
            def _():
                copy.start()
        for flag, copy in copies():
            @pl.when(flag == 1)
            def _():
                copy.wait()

    rows = block * group
    queries = q_ref[0].astype(jnp.float32)
    q = [
        queries[:, h * group : (h + 1) * group, :].reshape(rows, -1).astype(jnp.bfloat16)
        for h in range(heads)
    ]

    def fold(a, op):
        return functools.reduce(op, [a[:, j * 128 : (j + 1) * 128] for j in range(a.shape[1] // 128)])

    def keys(ref, h):
        return jnp.concatenate([ref[j, h, 0] for j in range(pages)], axis=0)

    def values(ref, h):
        return jnp.concatenate([ref[j, h, 1] for j in range(pages)], axis=1)

    last = count - 1
    if own:
        token = lax.broadcasted_iota(jnp.int32, (rows, tokens), 0) // group + i * block
        allowed = lax.broadcasted_iota(jnp.int32, (rows, tokens), 1) <= token
        for h in range(heads):
            s = jnp.where(allowed, nt(q[h], keys(blocks[0], h)), NEG)
            s_ref[last, h] = s
            m_ref[h] = fold(s, jnp.maximum)
    else:
        for h in range(heads):
            m_ref[h] = old_lse_ref[0, h]

    def look(b, carry):
        for h in range(heads):
            s = nt(q[h], keys(buf.at[b], h))
            s_ref[b, h] = s
            m_ref[h] = jnp.maximum(m_ref[h], fold(s, jnp.maximum))
        return carry

    lax.fori_loop(0, total, look, 0)
    for h in range(heads):
        m = jnp.broadcast_to(jnp.max(m_ref[h], axis=1, keepdims=True), m_ref.shape[1:])
        m_ref[h] = m
        if own:
            p = [
                jnp.exp2((s_ref[last, h, :, pl.ds(j * 128, 128)] - m) * scale)
                for j in range(tokens // 128)
            ]
            l_ref[h] = functools.reduce(jnp.add, p)
            p = jnp.concatenate([a.astype(jnp.bfloat16) for a in p], axis=1)
            acc_ref[h] = nt(p, values(blocks[0], h))
        else:
            share = jnp.exp2((old_lse_ref[0, h] - m) * scale)
            first = lax.broadcasted_iota(jnp.int32, share.shape, 1) == 0
            l_ref[h] = jnp.where(first, share, 0.0)
            acc_ref[h] = old_ref[0, h] * share

    def weigh(b, carry):
        for h in range(heads):
            m = m_ref[h]
            p = [
                jnp.exp2((s_ref[b, h, :, pl.ds(j * 128, 128)] - m) * scale)
                for j in range(tokens // 128)
            ]
            l_ref[h] = l_ref[h] + functools.reduce(jnp.add, p)
            p = jnp.concatenate([a.astype(jnp.bfloat16) for a in p], axis=1)
            acc_ref[h] = acc_ref[h] + nt(p, values(buf.at[b], h))
        return carry

    lax.fori_loop(0, total, weigh, 0)
    out = []
    for h in range(heads):
        l = jnp.sum(l_ref[h], axis=1, keepdims=True)
        l = jnp.broadcast_to(l, m_ref.shape[1:])
        if own:
            out_ref[0, h] = acc_ref[h] / l
            lse_ref[0, h] = m_ref[h] + jnp.log2(l) * (1.0 / scale)
        else:
            out.append((acc_ref[h] / l).reshape(block, group, -1))
    if not own:
        out_ref[0] = jnp.concatenate(out, axis=1).astype(out_ref.dtype)


def prefill(q, blocks, slots, needed, state):
    _, tokens, q_heads, width = q.shape
    own = state is None
    count = len(blocks)
    heads = blocks[0].shape[1]
    group = q_heads // heads
    block = 64
    rows = block * group
    q_spec = pl.BlockSpec((1, block, q_heads, width), lambda i, *_: (0, i, 0, 0))
    own_spec = pl.BlockSpec(blocks[0].shape, lambda i, *_: (0, 0, 0, 0, 0))
    any_spec = pl.BlockSpec(memory_space=pl.ANY)
    state_spec = pl.BlockSpec((1, heads, rows, width), lambda i, *_: (i, 0, 0, 0))
    shape = jax.ShapeDtypeStruct((tokens // block, heads, rows, width), jnp.float32)
    if own:
        in_specs = [q_spec, own_spec] + [any_spec] * (count - 1)
        out_specs, out_shape, state = [state_spec] * 2, [shape] * 2, ()
    else:
        in_specs = [q_spec] + [any_spec] * count + [state_spec] * 2
        out_specs, out_shape = q_spec, jax.ShapeDtypeStruct(q.shape, jnp.bfloat16)
    return pl.pallas_call(
        functools.partial(
            prefill_kernel, own, count, slots, group, tokens, LOG2E / math.sqrt(width)
        ),
        grid_spec=pltpu.PrefetchScalarGridSpec(
            num_scalar_prefetch=1,
            grid=(tokens // block,),
            in_specs=in_specs,
            out_specs=out_specs,
            scratch_shapes=[
                pltpu.VMEM((count,) + blocks[0].shape, jnp.bfloat16),
                pltpu.VMEM((count, heads, rows, tokens), jnp.float32),
                pltpu.VMEM((heads, rows, width), jnp.float32),
                pltpu.VMEM((heads, rows, width), jnp.float32),
                pltpu.VMEM((heads, rows, width), jnp.float32),
                pltpu.SemaphoreType.DMA((count,)),
            ],
        ),
        out_shape=out_shape,
        compiler_params=params(),
        cost_estimate=pl.CostEstimate(
            flops=16 * q_heads * tokens * tokens * count * width,
            bytes_accessed=12 * 10**6,
            transcendentals=tokens * tokens * count * q_heads,
        ),
    )(needed, q, *blocks, *state)


def cache_kernel(
    steps, heads, group, scale, len_ref, q_ref, dk_ref, dv_ref, ck_ref, cv_ref, acc_ref, ml_ref
):
    block, rows, width = q_ref.shape
    cache = ck_ref.shape[1]
    new = dk_ref.shape[1]
    per_step = heads * group

    def mask(columns):
        row = lax.broadcasted_iota(jnp.int32, (rows, columns), 0)
        column = lax.broadcasted_iota(jnp.int32, (rows, columns), 1)
        same = column % heads == row % per_step // group
        return jnp.where(same, column // heads, 1 << 20), row // per_step

    piece = min(cache, 128)
    pieces = range(0, cache, piece)
    place, _ = mask(piece)
    new_place, step = mask(new)
    new_allowed = new_place <= step
    low = lax.broadcasted_iota(jnp.int32, (rows, width), 1) < 4
    first = pl.program_id(0) * block
    unroll = math.gcd(4, block)

    def body(g, carry):
        scores = []
        for u in range(unroll):
            r = g * unroll + u
            q = q_ref[r]
            length = len_ref[first + r]
            old = [
                jnp.where(
                    place < length - c // heads, nt(q, ck_ref[r, pl.ds(c, piece), :]), NEG
                )
                for c in pieces
            ]
            add = jnp.where(new_allowed, nt(q, dk_ref[r]), NEG)
            scores.append((r, old, add))
        weights = []
        for r, old, add in scores:
            top = functools.reduce(jnp.maximum, old)
            m = jnp.maximum(
                jnp.max(top, axis=1, keepdims=True), jnp.max(add, axis=1, keepdims=True)
            )
            old = [jnp.exp2((a - m) * scale) for a in old]
            add = jnp.exp2((add - m) * scale)
            l = jnp.sum(functools.reduce(jnp.add, old), axis=1, keepdims=True)
            l = l + jnp.sum(add, axis=1, keepdims=True)
            ml_ref[r] = jnp.where(low, m, l).T[:8]
            weights.append((r, [a.astype(jnp.bfloat16) for a in old], add.astype(jnp.bfloat16)))
        for r, old, add in weights:
            acc = nn(add, dv_ref[r])
            for c, p in zip(pieces, old):
                acc = acc + nn(p, cv_ref[r, pl.ds(c, piece), :])
            acc_ref[r] = acc.T
        return carry

    lax.fori_loop(0, block // unroll, body, 0)


def cache_part(q, dk, dv, ck, cv, lens, steps, heads, group):
    requests, rows, width = q.shape
    block = math.gcd(8, requests)
    spec = [
        pl.BlockSpec((block,) + a.shape[1:], lambda i, *_: (i, 0, 0)) for a in (q, dk, dv, ck, cv)
    ]
    shapes = [(requests, width, rows), (requests, 8, rows)]
    return pl.pallas_call(
        functools.partial(cache_kernel, steps, heads, group, LOG2E / math.sqrt(width)),
        grid_spec=pltpu.PrefetchScalarGridSpec(
            num_scalar_prefetch=1,
            grid=(requests // block,),
            in_specs=spec,
            out_specs=[pl.BlockSpec((block,) + a[1:], lambda i, *_: (i, 0, 0)) for a in shapes],
        ),
        out_shape=[jax.ShapeDtypeStruct(a, jnp.float32) for a in shapes],
        compiler_params=params(),
        cost_estimate=pl.CostEstimate(
            flops=requests * rows * ck.shape[1] * width * 16,
            bytes_accessed=14 * 10**6,
            transcendentals=requests * rows * ck.shape[1],
        ),
    )(lens, q, dk, dv, ck, cv)


def decode_kernel(slots, extra, steps, target, targets, heads, group, scale, *refs):
    slot_ref, pick_ref, meta_ref = refs[:3]
    q_ref, acc_ref, ml_ref = refs[3:6]
    blocks = refs[6 : 6 + slots]
    out_ref, buf, sems = refs[6 + slots :]
    block, lanes, width = q_ref.shape
    i = pl.program_id(0)
    first = (lax.rem(meta_ref[1] + target, targets) * pl.num_programs(0) + i) * block

    def copies():
        for s in range(slots):
            yield pltpu.make_async_copy(blocks[s].at[pick_ref[s]], buf.at[s], sems.at[s])

    @pl.when(i == 0)
    def _():
        for copy in copies():
            copy.start()
        for copy in copies():
            copy.wait()

    per_step = heads * group
    row_head = lax.broadcasted_iota(jnp.int32, (lanes, width), 0) % per_step // group
    head_rows = [jnp.where(row_head == h, 1.0, 0.0).astype(jnp.bfloat16) for h in range(heads)]
    lane_head = lax.broadcasted_iota(jnp.int32, (width, lanes), 1) % per_step // group
    order = one_hot(lanes, lanes, lambda r: r % steps * per_step + r // steps)
    unroll = math.gcd(8, block)
    both = math.gcd(2 if target else 1, heads)

    def body(g, carry):
        scores = []
        for u in range(unroll):
            r = g * unroll + u
            q = q_ref[r]
            places = [slot_ref[(first + r) * extra + j] for j in range(extra)]
            spread = jnp.concatenate([q * a for a in head_rows], axis=1)
            keys = [
                jnp.concatenate([buf[place, h, 0] for h in range(heads)], axis=1)
                for place in places
            ]
            s = []
            for j in range(0, extra, both):
                pair = jnp.concatenate(keys[j : j + both], axis=0)
                s.append(nt(pair, spread))
            scores.append((r, places, s))
        weights = []
        for r, places, s in scores:
            old = ml_ref[r, 0:1]
            m = jnp.max(functools.reduce(jnp.maximum, s), axis=0, keepdims=True)
            m = jnp.maximum(m, old)
            p = [jnp.exp2((a - m) * scale) for a in s]
            shrink = jnp.exp2((old - m) * scale)
            l = jnp.sum(functools.reduce(jnp.add, p), axis=0, keepdims=True)
            l = ml_ref[r, 4:5] * shrink + l
            p = jnp.concatenate([a.astype(jnp.bfloat16) for a in p], axis=0)
            weights.append((r, places, p, shrink, l))
        results = []
        for r, places, p, shrink, l in weights:
            part = None
            values = [
                jnp.concatenate([buf[place, h, 1] for place in places], axis=1)
                for h in range(heads)
            ]
            for h in range(0, heads, both):
                pair = nn(jnp.concatenate(values[h : h + both], axis=0), p)
                for w in range(both):
                    mine = pair[w * width : (w + 1) * width]
                    part = mine if h + w == 0 else jnp.where(lane_head == h + w, mine, part)
            results.append((r, ((acc_ref[r] * shrink + part) / l).astype(jnp.bfloat16)))
        for r, result in results:
            out_ref[r] = nt(order, result).astype(jnp.bfloat16)
        return carry

    lax.fori_loop(0, block // unroll, body, 0)


def decode(q, acc, ml, blocks, scalars, target, targets, extra, steps, heads, group):
    requests, lanes, width = q.shape
    per_target = requests // targets
    block = math.gcd(16, per_target)
    per_block = per_target // block
    slots = len(blocks)

    def here(i, slot, pick, meta):
        return (lax.rem(meta[1] + target, targets) * per_block + i, 0, 0)

    in_specs = [pl.BlockSpec((block,) + a.shape[1:], here) for a in (q, acc, ml)]
    in_specs += [pl.BlockSpec(memory_space=pl.ANY)] * slots
    return pl.pallas_call(
        functools.partial(
            decode_kernel,
            slots,
            extra,
            steps,
            target,
            targets,
            heads,
            group,
            LOG2E / math.sqrt(width),
        ),
        grid_spec=pltpu.PrefetchScalarGridSpec(
            num_scalar_prefetch=3,
            grid=(per_block,),
            in_specs=in_specs,
            out_specs=pl.BlockSpec((block, lanes, width), lambda i, *_: (i, 0, 0)),
            scratch_shapes=[
                pltpu.VMEM((slots, heads, 2, PAGE, width), jnp.bfloat16),
                pltpu.SemaphoreType.DMA((slots,)),
            ],
        ),
        out_shape=jax.ShapeDtypeStruct((per_target, lanes, width), jnp.bfloat16),
        compiler_params=params(),
        cost_estimate=pl.CostEstimate(
            flops=per_target * lanes * extra * PAGE * width * 16,
            bytes_accessed=8 * 10**6,
            transcendentals=per_target * lanes * extra * PAGE,
        ),
    )(*scalars, q, acc, ml, *blocks)


def join_kernel(targets, steps, meta_ref, *refs):
    out_ref = refs[-1]
    rows = refs[0].shape[1]
    each = rows // steps
    for s in range(targets):
        start = lax.rem(meta_ref[1] + (targets - s), targets) * (each * 128)
        for r in range(out_ref.shape[0]):
            value = refs[s][r]
            for g in range(each):
                column = pl.multiple_of(start + g * 128, 128)
                out_ref[r, :, pl.ds(column, 128)] = value[g * steps : (g + 1) * steps]


def join(pieces, meta, steps, targets):
    per_target, rows, width = pieces[0].shape
    whole = rows // steps * width * targets
    block = math.gcd(4, per_target)
    spec = pl.BlockSpec((block, rows, width), lambda k, *_: (k, 0, 0))
    return pl.pallas_call(
        functools.partial(join_kernel, targets, steps),
        grid_spec=pltpu.PrefetchScalarGridSpec(
            num_scalar_prefetch=1,
            grid=(per_target // block,),
            in_specs=[spec] * len(pieces),
            out_specs=pl.BlockSpec((block, steps, whole), lambda k, *_: (k, 0, 0)),
        ),
        out_shape=jax.ShapeDtypeStruct((per_target, steps, whole), jnp.bfloat16),
        compiler_params=params(),
        cost_estimate=pl.CostEstimate(flops=0, bytes_accessed=2 * 10**6, transcendentals=0),
    )(meta, *pieces)


def ring_place(index, size):
    return jnp.where(index % 2 == 0, index // 2, size - 1 - index // 2)


def shards(
    roles,
    ring,
    targets,
    prefill_q,
    prefill_k,
    prefill_v,
    decode_q,
    decode_k,
    decode_v,
    cache_k,
    cache_v,
    cache_len,
    page_list,
):
    tokens, q_heads = prefill_q.shape[1:3]
    heads, width = prefill_k.shape[2:]
    group = q_heads // heads
    own_pages = tokens // PAGE
    requests, steps = decode_q.shape[:2]
    extra = page_list.shape[1]
    role = lax.axis_index("role")
    ctx = lax.axis_index("ctx")
    tp = lax.axis_index("tp")

    order = list(range(0, ring, 2)) + list(range(ring - 1, 0, -2))
    along = [(order[j], order[(j + 1) % ring]) for j in range(ring)]
    flips = [1 << b for b in reversed(range(roles.bit_length() - 1))]

    owner = page_list // own_pages
    place = (ring_place(ctx, ring) - ring_place(owner % ring, ring)) % ring
    slot = ((owner // ring) ^ role) * ring + place
    hot = slot.reshape(-1, 1) == jnp.arange(roles * ring)[None, :]
    pick = jnp.max(jnp.where(hot, (page_list % own_pages).reshape(-1, 1), 0), axis=0)
    meta = jnp.stack([ctx, tp]).astype(jnp.int32)
    scalars = (
        slot.reshape(-1).astype(jnp.int32),
        pick.astype(jnp.int32),
        meta,
    )
    position = jnp.arange(ring)
    where = ring_place(ctx, ring)
    source = (where - position) % ring
    source_ctx = jnp.where(source < (ring + 1) // 2, 2 * source, 2 * (ring - 1 - source) + 1)
    needed = (source_ctx < ctx).astype(jnp.int32)

    raw = [
        a.reshape(requests, -1, width) for a in (decode_q, decode_k, decode_v, cache_k, cache_v)
    ]

    gathered = {(0, 0): split_heads(prefill_k, prefill_v)}
    fresh = [(0, 0)]
    for k in range(ring + len(flips) - 1):
        sends = []
        for code, s in fresh:
            for flip in reversed(flips):
                if code == 0 or flip < code & -code:
                    pairs = [(j, j ^ flip) for j in range(roles)]
                    sends.append((flip, (code, s), (code ^ flip, s), "role", pairs))
            if code == 0 and s + 1 < ring:
                sends.append((roles, (code, s), (0, s + 1), "ctx", along))
        sends.sort(key=lambda a: a[0])
        names = [to for _, _, to, _, _ in sends]
        arrived = [lax.ppermute(gathered[of], axis, pairs) for _, of, _, axis, pairs in sends]
        beside = ()
        if k == 0:
            beside = cache_part(*raw, cache_len.astype(jnp.int32), steps, heads, group)
        if k == 1:
            beside = prefill(prefill_q, [gathered[0, s] for s in (0, 1)], (0, 1), needed, None)
        if k == ring - 1:
            later = tuple(range(2, ring))
            beside = prefill(prefill_q, [gathered[0, s] for s in later], later, needed, state)
        if k == ring - 2 and k > 1:
            beside = scalars
        arrived, beside = lax.optimization_barrier((arrived, beside))
        if k == 0:
            acc, ml = beside
        if k == 1:
            state = beside
        if k == ring - 2 and k > 1:
            scalars = beside
        if k == ring - 1:
            prefill_out = beside
        gathered.update(zip(names, arrived))
        fresh = names

    blocks = [gathered[r, s] for r in range(roles) for s in range(ring)]
    pieces = [None] * targets
    for s in reversed(range(targets)):
        out = decode(raw[0], acc, ml, blocks, scalars, s, targets, extra, steps, heads, group)
        if s:
            shift = [(j, (j + s) % targets) for j in range(targets)]
            out = lax.ppermute(out, "tp", shift)
        pieces[s] = out
    decode_out = join(pieces, scalars[2], steps, targets)
    return (prefill_out, decode_out)


def solution(mesh):
    body = functools.partial(shards, mesh.shape["role"], mesh.shape["ctx"], mesh.shape["tp"])
    return jax.shard_map(
        body,
        mesh=mesh,
        in_specs=(
            P("role", "ctx", "tp", None),
            P("role", "ctx", "tp", None),
            P("role", "ctx", "tp", None),
            P(("role", "ctx"), None, "tp", None),
            P(("role", "ctx"), None, "tp", None),
            P(("role", "ctx"), None, "tp", None),
            P(("role", "ctx"), None, "tp", None),
            P(("role", "ctx"), None, "tp", None),
            P(("role", "ctx")),
            P(("role", "ctx"), None),
        ),
        out_specs=(P("role", "ctx", "tp", None), P(("role", "ctx", "tp"), None, None)),
        check_vma=False,
    )
```

```python
import functools
import math

import jax
import jax.numpy as jnp
from jax import lax
from jax.experimental import pallas as pl
from jax.experimental.pallas import tpu as pltpu
from jax.sharding import PartitionSpec as P

PAGE = 128
LOG2E = 1.4426950408889634
NEG = -1e30
VMEM_LIMIT = 32 * 1024 * 1024


def nt(a, b):
    return lax.dot_general(a, b, (((1,), (1,)), ((), ())), preferred_element_type=jnp.float32)


def nn(a, b):
    return jnp.dot(a, b, preferred_element_type=jnp.float32)


def in_hbm(*arrays):
    return [pltpu.with_memory_space_constraint(a, pltpu.HBM) for a in arrays]


def params():
    return pltpu.CompilerParams(vmem_limit_bytes=VMEM_LIMIT)


def one_hot(out_rows, in_rows, source):
    row = lax.broadcasted_iota(jnp.int32, (out_rows, in_rows), 0)
    col = lax.broadcasted_iota(jnp.int32, (out_rows, in_rows), 1)
    return jnp.where(col == source(row), 1.0, 0.0).astype(jnp.bfloat16)


def split_kernel(heads, tokens, k_ref, v_ref, out_ref):
    rows = min(tokens * heads, 256)
    step = rows // heads
    pick = one_hot(rows, rows, lambda i: (i % step) * heads + i // step)
    moved, kept = [], []
    for j in range(tokens // step):
        keys = nn(pick, k_ref[pl.ds(j * rows, rows), :]).astype(jnp.bfloat16)
        moved.append(nn(pick, v_ref[pl.ds(j * rows, rows), :]))
        kept.append(keys)
    for h in range(heads):
        keys = jnp.concatenate([a[h * step : (h + 1) * step] for a in kept], axis=0)
        values = jnp.concatenate([a[h * step : (h + 1) * step] for a in moved], axis=0)
        for page in range(tokens // PAGE):
            out_ref[page, h, 0] = keys[page * PAGE : (page + 1) * PAGE]
            out_ref[page, h, 1] = values[page * PAGE : (page + 1) * PAGE].T.astype(jnp.bfloat16)


def split_heads(k, v):
    _, tokens, heads, width = k.shape
    return pl.pallas_call(
        functools.partial(split_kernel, heads, tokens),
        out_shape=jax.ShapeDtypeStruct((tokens // PAGE, heads, 2, PAGE, width), jnp.bfloat16),
        compiler_params=params(),
        cost_estimate=pl.CostEstimate(flops=10**8, bytes_accessed=2 * 10**6, transcendentals=0),
    )(k.reshape(tokens * heads, width), v.reshape(tokens * heads, width))


def prefill_kernel(own, count, slots, group, tokens, scale, needed_ref, *refs):
    q_ref = refs[0]
    blocks = refs[1 : 1 + count]
    refs = refs[1 + count :]
    i = pl.program_id(0)
    if own:
        acc_ref, m_ref, l_ref, buf, s_ref, sems = refs
        acc_ref, m_ref, l_ref = acc_ref.at[i], m_ref.at[i], l_ref.at[i]
    else:
        old_acc_ref, old_m_ref, old_l_ref, out_ref, buf, s_ref, acc_ref, m_ref, l_ref, sems = refs
    pages, heads = blocks[0].shape[:2]
    block = q_ref.shape[1]
    rest = range(1 if own else 0, count)
    total = sum(needed_ref[slots[c]] for c in rest)

    def copies():
        found = []
        place = jnp.int32(0)
        for c in rest:
            flag = needed_ref[slots[c]]
            found.append((flag, pltpu.make_async_copy(blocks[c], buf.at[place], sems.at[c])))
            place = place + flag
        return found

    @pl.when(i == 0)
    def _():
        for flag, copy in copies():
            @pl.when(flag == 1)
            def _():
                copy.start()
        for flag, copy in copies():
            @pl.when(flag == 1)
            def _():
                copy.wait()

    rows = block * group
    piece = min(rows, 256)
    parts = [(h, pl.ds(c, piece)) for h in range(heads) for c in range(0, rows, piece)]
    queries = q_ref[0].astype(jnp.float32)
    q = [
        queries[:, h * group : (h + 1) * group, :].reshape(rows, -1).astype(jnp.bfloat16)
        for h in range(heads)
    ]
    q = [q[h][c : c + piece] for h in range(heads) for c in range(0, rows, piece)]

    def fold(a, op):
        return functools.reduce(op, [a[:, j * 128 : (j + 1) * 128] for j in range(a.shape[1] // 128)])

    def keys(ref, h):
        return jnp.concatenate([ref[j, h, 0] for j in range(pages)], axis=0)

    def values(ref, h):
        return jnp.concatenate([ref[j, h, 1] for j in range(pages)], axis=1)

    def weights(place, h, at, m):
        return [
            jnp.exp2((s_ref[place, h, at, pl.ds(j * 128, 128)] - m) * scale)
            for j in range(tokens // 128)
        ]

    last = count - 1
    if own:
        for n, (h, at) in enumerate(parts):
            row = lax.broadcasted_iota(jnp.int32, (piece, tokens), 0) + n * piece % rows
            allowed = lax.broadcasted_iota(jnp.int32, (piece, tokens), 1) <= row // group + i * block
            s = jnp.where(allowed, nt(q[n], keys(blocks[0], h)), NEG)
            s_ref[last, h, at] = s
            m_ref[h, at] = fold(s, jnp.maximum)
    else:
        m_ref[...] = old_m_ref[i]

    def look(b, carry):
        for n, (h, at) in enumerate(parts):
            s = nt(q[n], keys(buf.at[b], h))
            s_ref[b, h, at] = s
            m_ref[h, at] = jnp.maximum(m_ref[h, at], fold(s, jnp.maximum))
        return carry

    lax.fori_loop(0, total, look, 0)
    for h, at in parts:
        m = m_ref[h, at]
        m = jnp.broadcast_to(jnp.max(m, axis=1, keepdims=True), m.shape)
        m_ref[h, at] = m
        if own:
            p = weights(last, h, at, m)
            l_ref[h, at] = functools.reduce(jnp.add, p)
            p = jnp.concatenate([a.astype(jnp.bfloat16) for a in p], axis=1)
            acc_ref[h, at] = nt(p, values(blocks[0], h))
        else:
            share = jnp.exp2((old_m_ref[i, h, at] - m) * scale)
            l_ref[h, at] = old_l_ref[i, h, at] * share
            acc_ref[h, at] = old_acc_ref[i, h, at] * share

    def weigh(b, carry):
        for h, at in parts:
            p = weights(b, h, at, m_ref[h, at])
            l_ref[h, at] = l_ref[h, at] + functools.reduce(jnp.add, p)
            p = jnp.concatenate([a.astype(jnp.bfloat16) for a in p], axis=1)
            acc_ref[h, at] = acc_ref[h, at] + nt(p, values(buf.at[b], h))
        return carry

    lax.fori_loop(0, total, weigh, 0)
    if not own:
        out = []
        for h in range(heads):
            l = jnp.sum(l_ref[h], axis=1, keepdims=True)
            out.append((acc_ref[h] / l).reshape(block, group, -1))
        out_ref[0] = jnp.concatenate(out, axis=1).astype(out_ref.dtype)


def prefill(q, blocks, slots, needed, state):
    _, tokens, q_heads, width = q.shape
    own = state is None
    count = len(blocks)
    heads = blocks[0].shape[1]
    group = q_heads // heads
    block = 64
    rows = block * group
    q_spec = pl.BlockSpec((1, block, q_heads, width), lambda i, *_: (0, i, 0, 0))
    own_spec = pl.BlockSpec(blocks[0].shape, lambda i, *_: (0, 0, 0, 0, 0))
    any_spec = pl.BlockSpec(memory_space=pl.ANY)
    on_chip = pl.BlockSpec(memory_space=pltpu.VMEM)
    scratch = [
        pltpu.VMEM((count,) + blocks[0].shape, jnp.bfloat16),
        pltpu.VMEM((count, heads, rows, tokens), jnp.float32),
    ]
    if own:
        in_specs = [q_spec, own_spec] + [any_spec] * (count - 1)
        out_specs, state = [on_chip] * 3, ()
        out_shape = [pltpu.VMEM((tokens // block, heads, rows, width), jnp.float32)] * 3
    else:
        in_specs = [q_spec] + [any_spec] * count + [on_chip] * 3
        out_specs, out_shape = q_spec, jax.ShapeDtypeStruct(q.shape, jnp.bfloat16)
        scratch += [pltpu.VMEM((heads, rows, width), jnp.float32)] * 3
    return pl.pallas_call(
        functools.partial(
            prefill_kernel, own, count, slots, group, tokens, LOG2E / math.sqrt(width)
        ),
        grid_spec=pltpu.PrefetchScalarGridSpec(
            num_scalar_prefetch=1,
            grid=(tokens // block,),
            in_specs=in_specs,
            out_specs=out_specs,
            scratch_shapes=scratch + [pltpu.SemaphoreType.DMA((count,))],
        ),
        out_shape=out_shape,
        compiler_params=params(),
        cost_estimate=pl.CostEstimate(
            flops=16 * q_heads * tokens * tokens * count * width,
            bytes_accessed=12 * 10**6,
            transcendentals=tokens * tokens * count * q_heads,
        ),
    )(needed, *in_hbm(q), *blocks, *state)


def cache_kernel(
    steps, heads, group, target, targets, scale, len_ref, meta_ref, *refs
):
    q_ref, dk_ref, dv_ref, ck_ref, cv_ref, acc_ref, ml_ref = refs
    block, rows, width = q_ref.shape
    cache = ck_ref.shape[1]
    new = dk_ref.shape[1]
    per_step = heads * group

    def mask(columns):
        row = lax.broadcasted_iota(jnp.int32, (rows, columns), 0)
        column = lax.broadcasted_iota(jnp.int32, (rows, columns), 1)
        same = column % heads == row % per_step // group
        return jnp.where(same, column // heads, 1 << 20), row // per_step

    piece = min(cache, 128)
    pieces = range(0, cache, piece)
    place, _ = mask(piece)
    new_place, step = mask(new)
    new_allowed = new_place <= step
    low = lax.broadcasted_iota(jnp.int32, (rows, width), 1) < 4
    i = pl.program_id(0)
    first = (lax.rem(meta_ref[1] + target, targets) * pl.num_programs(0) + i) * block
    unroll = math.gcd(4, block)

    def body(g, carry):
        scores = []
        for u in range(unroll):
            r = g * unroll + u
            q = q_ref[r]
            length = len_ref[first + r]
            old = [
                jnp.where(
                    place < length - c // heads, nt(q, ck_ref[r, pl.ds(c, piece), :]), NEG
                )
                for c in pieces
            ]
            add = jnp.where(new_allowed, nt(q, dk_ref[r]), NEG)
            scores.append((r, old, add))
        weights = []
        for r, old, add in scores:
            top = functools.reduce(jnp.maximum, old)
            m = jnp.maximum(
                jnp.max(top, axis=1, keepdims=True), jnp.max(add, axis=1, keepdims=True)
            )
            old = [jnp.exp2((a - m) * scale) for a in old]
            add = jnp.exp2((add - m) * scale)
            l = jnp.sum(functools.reduce(jnp.add, old), axis=1, keepdims=True)
            l = l + jnp.sum(add, axis=1, keepdims=True)
            ml_ref[i * block + r] = jnp.where(low, m, l).T[:8]
            weights.append((r, [a.astype(jnp.bfloat16) for a in old], add.astype(jnp.bfloat16)))
        for r, old, add in weights:
            acc = nn(add, dv_ref[r])
            for c, p in zip(pieces, old):
                acc = acc + nn(p, cv_ref[r, pl.ds(c, piece), :])
            acc_ref[i * block + r] = acc.T
        return carry

    lax.fori_loop(0, block // unroll, body, 0)


def cache_part(q, dk, dv, ck, cv, lens, meta, target, targets, steps, heads, group):
    requests, rows, width = q.shape
    per_target = requests // targets
    block = math.gcd(8, per_target)
    per_block = per_target // block

    def here(i, lens, meta):
        return (lax.rem(meta[1] + target, targets) * per_block + i, 0, 0)

    spec = [pl.BlockSpec((block,) + a.shape[1:], here) for a in (q, dk, dv, ck, cv)]
    shapes = [(per_target, width, rows), (per_target, 8, rows)]
    return pl.pallas_call(
        functools.partial(
            cache_kernel, steps, heads, group, target, targets, LOG2E / math.sqrt(width)
        ),
        grid_spec=pltpu.PrefetchScalarGridSpec(
            num_scalar_prefetch=2,
            grid=(per_block,),
            in_specs=spec,
            out_specs=[pl.BlockSpec(memory_space=pltpu.VMEM)] * 2,
        ),
        out_shape=[pltpu.VMEM(a, jnp.float32) for a in shapes],
        compiler_params=params(),
        cost_estimate=pl.CostEstimate(
            flops=per_target * rows * ck.shape[1] * width * 16,
            bytes_accessed=7 * 10**6,
            transcendentals=per_target * rows * ck.shape[1],
        ),
    )(lens, meta, *in_hbm(q, dk, dv, ck, cv))


def decode_kernel(slots, extra, steps, target, targets, heads, group, scale, *refs):
    slot_ref, pick_ref, meta_ref = refs[:3]
    q_ref, acc_ref, ml_ref = refs[3:6]
    blocks = refs[6 : 6 + slots]
    out_ref, buf, sems = refs[6 + slots :]
    block, lanes, width = q_ref.shape
    i = pl.program_id(0)
    first = (lax.rem(meta_ref[1] + target, targets) * pl.num_programs(0) + i) * block

    def copies():
        for s in range(slots):
            yield pltpu.make_async_copy(blocks[s].at[pick_ref[s]], buf.at[s], sems.at[s])

    @pl.when(i == 0)
    def _():
        for copy in copies():
            copy.start()
        for copy in copies():
            copy.wait()

    per_step = heads * group
    row_head = lax.broadcasted_iota(jnp.int32, (lanes, width), 0) % per_step // group
    head_rows = [jnp.where(row_head == h, 1.0, 0.0).astype(jnp.bfloat16) for h in range(heads)]
    lane_head = lax.broadcasted_iota(jnp.int32, (width, lanes), 1) % per_step // group
    order = one_hot(lanes, lanes, lambda r: r % steps * per_step + r // steps)
    unroll = math.gcd(8, block)
    both = math.gcd(2 if target else 1, heads)

    def body(g, carry):
        scores = []
        for u in range(unroll):
            r = g * unroll + u
            q = q_ref[r]
            places = [slot_ref[(first + r) * extra + j] for j in range(extra)]
            spread = jnp.concatenate([q * a for a in head_rows], axis=1)
            keys = [
                jnp.concatenate([buf[place, h, 0] for h in range(heads)], axis=1)
                for place in places
            ]
            s = []
            for j in range(0, extra, both):
                pair = jnp.concatenate(keys[j : j + both], axis=0)
                s.append(nt(pair, spread))
            scores.append((r, places, s))
        weights = []
        for r, places, s in scores:
            old = ml_ref[i * block + r, 0:1]
            m = jnp.max(functools.reduce(jnp.maximum, s), axis=0, keepdims=True)
            m = jnp.maximum(m, old)
            p = [jnp.exp2((a - m) * scale) for a in s]
            shrink = jnp.exp2((old - m) * scale)
            l = jnp.sum(functools.reduce(jnp.add, p), axis=0, keepdims=True)
            l = ml_ref[i * block + r, 4:5] * shrink + l
            p = jnp.concatenate([a.astype(jnp.bfloat16) for a in p], axis=0)
            weights.append((r, places, p, shrink, l))
        results = []
        for r, places, p, shrink, l in weights:
            part = None
            values = [
                jnp.concatenate([buf[place, h, 1] for place in places], axis=1)
                for h in range(heads)
            ]
            for h in range(0, heads, both):
                pair = nn(jnp.concatenate(values[h : h + both], axis=0), p)
                for w in range(both):
                    mine = pair[w * width : (w + 1) * width]
                    part = mine if h + w == 0 else jnp.where(lane_head == h + w, mine, part)
            results.append((r, ((acc_ref[i * block + r] * shrink + part) / l).astype(jnp.bfloat16)))
        for r, result in results:
            out_ref[r] = nt(order, result).astype(jnp.bfloat16)
        return carry

    lax.fori_loop(0, block // unroll, body, 0)


def decode(q, acc, ml, blocks, scalars, target, targets, extra, steps, heads, group):
    requests, lanes, width = q.shape
    per_target = requests // targets
    block = math.gcd(16, per_target)
    per_block = per_target // block
    slots = len(blocks)

    def here(i, slot, pick, meta):
        return (lax.rem(meta[1] + target, targets) * per_block + i, 0, 0)

    in_specs = [pl.BlockSpec((block,) + q.shape[1:], here)]
    in_specs += [pl.BlockSpec(memory_space=pltpu.VMEM)] * 2
    in_specs += [pl.BlockSpec(memory_space=pl.ANY)] * slots
    return pl.pallas_call(
        functools.partial(
            decode_kernel,
            slots,
            extra,
            steps,
            target,
            targets,
            heads,
            group,
            LOG2E / math.sqrt(width),
        ),
        grid_spec=pltpu.PrefetchScalarGridSpec(
            num_scalar_prefetch=3,
            grid=(per_block,),
            in_specs=in_specs,
            out_specs=pl.BlockSpec((block, lanes, width), lambda i, *_: (i, 0, 0)),
            scratch_shapes=[
                pltpu.VMEM((slots, heads, 2, PAGE, width), jnp.bfloat16),
                pltpu.SemaphoreType.DMA((slots,)),
            ],
        ),
        out_shape=jax.ShapeDtypeStruct((per_target, lanes, width), jnp.bfloat16),
        compiler_params=params(),
        cost_estimate=pl.CostEstimate(
            flops=per_target * lanes * extra * PAGE * width * 16,
            bytes_accessed=8 * 10**6,
            transcendentals=per_target * lanes * extra * PAGE,
        ),
    )(*scalars, *in_hbm(q), acc, ml, *blocks)


def join_kernel(targets, chunks, steps, meta_ref, *refs):
    out_ref = refs[-1]
    k = pl.program_id(0)
    rows = refs[0].shape[1]
    each = rows // steps
    for s in range(targets):
        @pl.when(lax.rem(meta_ref[1] + (targets - s), targets) == k)
        def _():
            for c in range(chunks):
                source = refs[s * chunks + c]

                def body(r, carry):
                    value = source[r]
                    for g in range(each):
                        out_ref[r, :, (c * each + g) * 128 : (c * each + g + 1) * 128] = value[
                            g * steps : (g + 1) * steps
                        ]
                    return carry

                lax.fori_loop(0, out_ref.shape[0], body, 0)


def join(pieces, meta, steps, targets, chunks):
    per_target, rows, width = pieces[0].shape
    half = chunks * (rows // steps) * width
    spec = pl.BlockSpec((per_target, rows, width), lambda k, *_: (0, 0, 0))
    return pl.pallas_call(
        functools.partial(join_kernel, targets, chunks, steps),
        grid_spec=pltpu.PrefetchScalarGridSpec(
            num_scalar_prefetch=1,
            grid=(targets,),
            in_specs=[spec] * len(pieces),
            out_specs=pl.BlockSpec((per_target, steps, half), lambda k, *_: (0, 0, k)),
        ),
        out_shape=jax.ShapeDtypeStruct((per_target, steps, half * targets), jnp.bfloat16),
        compiler_params=pltpu.CompilerParams(vmem_limit_bytes=16 * 1024 * 1024),
        cost_estimate=pl.CostEstimate(flops=0, bytes_accessed=2 * 10**6, transcendentals=0),
    )(meta, *pieces)


def ring_place(index, size):
    return jnp.where(index % 2 == 0, index // 2, size - 1 - index // 2)


def shards(
    roles,
    ring,
    targets,
    prefill_q,
    prefill_k,
    prefill_v,
    decode_q,
    decode_k,
    decode_v,
    cache_k,
    cache_v,
    cache_len,
    page_list,
):
    tokens, q_heads = prefill_q.shape[1:3]
    heads, width = prefill_k.shape[2:]
    group = q_heads // heads
    own_pages = tokens // PAGE
    requests, steps = decode_q.shape[:2]
    extra = page_list.shape[1]
    role = lax.axis_index("role")
    ctx = lax.axis_index("ctx")
    tp = lax.axis_index("tp")

    order = list(range(0, ring, 2)) + list(range(ring - 1, 0, -2))
    along = [(order[j], order[(j + 1) % ring]) for j in range(ring)]
    flips = [1 << b for b in reversed(range(roles.bit_length() - 1))]

    owner = page_list // own_pages
    place = (ring_place(ctx, ring) - ring_place(owner % ring, ring)) % ring
    slot = ((owner // ring) ^ role) * ring + place
    hot = slot.reshape(-1, 1) == jnp.arange(roles * ring)[None, :]
    pick = jnp.max(jnp.where(hot, (page_list % own_pages).reshape(-1, 1), 0), axis=0)
    meta = jnp.stack([ctx, tp]).astype(jnp.int32)
    scalars = (
        slot.reshape(-1).astype(jnp.int32),
        pick.astype(jnp.int32),
        meta,
    )
    position = jnp.arange(ring)
    where = ring_place(ctx, ring)
    source = (where - position) % ring
    source_ctx = jnp.where(source < (ring + 1) // 2, 2 * source, 2 * (ring - 1 - source) + 1)
    needed = (source_ctx < ctx).astype(jnp.int32)

    raw = [
        a.reshape(requests, -1, width) for a in (decode_q, decode_k, decode_v, cache_k, cache_v)
    ]

    def cache(target):
        lens = cache_len.astype(jnp.int32)
        return cache_part(*raw, lens, meta, target, targets, steps, heads, group)

    gathered = {(0, 0): split_heads(prefill_k, prefill_v)}
    fresh = [(0, 0)]
    for k in range(ring + len(flips) - 1):
        sends = []
        for code, s in fresh:
            for flip in reversed(flips):
                if code == 0 or flip < code & -code:
                    pairs = [(j, j ^ flip) for j in range(roles)]
                    sends.append((flip, (code, s), (code ^ flip, s), "role", pairs))
            if code == 0 and s + 1 < ring:
                sends.append((roles, (code, s), (0, s + 1), "ctx", along))
        sends.sort(key=lambda a: a[0])
        names = [to for _, _, to, _, _ in sends]
        arrived = [lax.ppermute(gathered[of], axis, pairs) for _, of, _, axis, pairs in sends]
        beside = ()
        if k == 0:
            beside = cache(targets - 1)
        if k == 1:
            beside = prefill(prefill_q, [gathered[0, s] for s in (0, 1)], (0, 1), needed, None)
        if k == ring - 1:
            later = tuple(range(2, ring))
            beside = prefill(prefill_q, [gathered[0, s] for s in later], later, needed, state)
        if k == ring - 2 and k > 1:
            beside = scalars, {s: cache(s) for s in range(targets - 1)}
        arrived, beside = lax.optimization_barrier((arrived, beside))
        if k == 0:
            cached = {targets - 1: beside}
        if k == 1:
            state = beside
        if k == ring - 2 and k > 1:
            scalars, others = beside
            cached.update(others)
        if k == ring - 1:
            prefill_out = beside
        gathered.update(zip(names, arrived))
        fresh = names

    blocks = [gathered[r, s] for r in range(roles) for s in range(ring)]
    pieces = [None] * targets
    for s in reversed(range(targets)):
        out = decode(raw[0], *cached[s], blocks, scalars, s, targets, extra, steps, heads, group)
        if s:
            shift = [(j, (j + s) % targets) for j in range(targets)]
            out = lax.ppermute(out, "tp", shift)
        pieces[s] = out
    decode_out = join(pieces, scalars[2], steps, targets, 1)
    return (prefill_out, decode_out)


def solution(mesh):
    body = functools.partial(shards, mesh.shape["role"], mesh.shape["ctx"], mesh.shape["tp"])
    return jax.shard_map(
        body,
        mesh=mesh,
        in_specs=(
            P("role", "ctx", "tp", None),
            P("role", "ctx", "tp", None),
            P("role", "ctx", "tp", None),
            P(("role", "ctx"), None, "tp", None),
            P(("role", "ctx"), None, "tp", None),
            P(("role", "ctx"), None, "tp", None),
            P(("role", "ctx"), None, "tp", None),
            P(("role", "ctx"), None, "tp", None),
            P(("role", "ctx")),
            P(("role", "ctx"), None),
        ),
        out_specs=(P("role", "ctx", "tp", None), P(("role", "ctx", "tp"), None, None)),
        check_vma=False,
    )
```

```python
import functools
import math

import jax
import jax.numpy as jnp
from jax import lax
from jax.experimental import pallas as pl
from jax.experimental.pallas import tpu as pltpu
from jax.sharding import PartitionSpec as P

PAGE = 128
LOG2E = 1.4426950408889634
NEG = -1e30
VMEM_LIMIT = 16 * 1024 * 1024


def nt(a, b):
    return lax.dot_general(a, b, (((1,), (1,)), ((), ())), preferred_element_type=jnp.float32)


def nn(a, b):
    return jnp.dot(a, b, preferred_element_type=jnp.float32)


def in_hbm(*arrays):
    return [pltpu.with_memory_space_constraint(a, pltpu.HBM) for a in arrays]


def params():
    return pltpu.CompilerParams(vmem_limit_bytes=VMEM_LIMIT)


def one_hot(out_rows, in_rows, source):
    row = lax.broadcasted_iota(jnp.int32, (out_rows, in_rows), 0)
    col = lax.broadcasted_iota(jnp.int32, (out_rows, in_rows), 1)
    return jnp.where(col == source(row), 1.0, 0.0).astype(jnp.bfloat16)


def split_kernel(heads, tokens, k_ref, v_ref, out_ref):
    rows = min(tokens * heads, 256)
    step = rows // heads
    pick = one_hot(rows, rows, lambda i: (i % step) * heads + i // step)
    moved, kept = [], []
    for j in range(tokens // step):
        keys = nn(pick, k_ref[pl.ds(j * rows, rows), :]).astype(jnp.bfloat16)
        moved.append(nn(pick, v_ref[pl.ds(j * rows, rows), :]))
        kept.append(keys)
    for h in range(heads):
        keys = jnp.concatenate([a[h * step : (h + 1) * step] for a in kept], axis=0)
        values = jnp.concatenate([a[h * step : (h + 1) * step] for a in moved], axis=0)
        for page in range(tokens // PAGE):
            out_ref[page, h, 0] = keys[page * PAGE : (page + 1) * PAGE]
            out_ref[page, h, 1] = values[page * PAGE : (page + 1) * PAGE].T.astype(jnp.bfloat16)


def split_heads(k, v):
    _, tokens, heads, width = k.shape
    return pl.pallas_call(
        functools.partial(split_kernel, heads, tokens),
        out_specs=pl.BlockSpec(memory_space=pltpu.VMEM),
        out_shape=pltpu.VMEM((tokens // PAGE, heads, 2, PAGE, width), jnp.bfloat16),
        compiler_params=params(),
        cost_estimate=pl.CostEstimate(flops=10**8, bytes_accessed=2 * 10**6, transcendentals=0),
    )(*in_hbm(k.reshape(tokens * heads, width), v.reshape(tokens * heads, width)))


def prefill_kernel(own, count, slots, group, tokens, scale, needed_ref, *refs):
    q_ref = refs[0]
    blocks = refs[1 : 1 + count]
    refs = refs[1 + count :]
    i = pl.program_id(0)
    if own:
        acc_ref, m_ref, l_ref, buf, s_ref, sems = refs
        acc_ref, m_ref, l_ref = acc_ref.at[i], m_ref.at[i], l_ref.at[i]
    else:
        old_acc_ref, old_m_ref, old_l_ref, out_ref, buf, s_ref, acc_ref, m_ref, l_ref, sems = refs
    pages, heads = blocks[0].shape[:2]
    block = q_ref.shape[1]
    rest = range(1 if own else 0, count)
    total = sum(needed_ref[slots[c]] for c in rest)

    def copies():
        found = []
        place = jnp.int32(0)
        for c in rest:
            flag = needed_ref[slots[c]]
            found.append((flag, pltpu.make_async_copy(blocks[c], buf.at[place], sems.at[c])))
            place = place + flag
        return found

    @pl.when(i == 0)
    def _():
        for flag, copy in copies():
            @pl.when(flag == 1)
            def _():
                copy.start()
        for flag, copy in copies():
            @pl.when(flag == 1)
            def _():
                copy.wait()

    rows = block * group
    piece = min(rows, 256)
    parts = [(h, pl.ds(c, piece)) for h in range(heads) for c in range(0, rows, piece)]
    queries = q_ref[0].astype(jnp.float32)
    q = [
        queries[:, h * group : (h + 1) * group, :].reshape(rows, -1).astype(jnp.bfloat16)
        for h in range(heads)
    ]
    q = [q[h][c : c + piece] for h in range(heads) for c in range(0, rows, piece)]

    def fold(a, op):
        return functools.reduce(op, [a[:, j * 128 : (j + 1) * 128] for j in range(a.shape[1] // 128)])

    def keys(ref, h):
        return jnp.concatenate([ref[j, h, 0] for j in range(pages)], axis=0)

    def values(ref, h):
        return jnp.concatenate([ref[j, h, 1] for j in range(pages)], axis=1)

    def weights(place, h, at, m):
        return [
            jnp.exp2((s_ref[place, h, at, pl.ds(j * 128, 128)] - m) * scale)
            for j in range(tokens // 128)
        ]

    last = count - 1
    if own:
        for n, (h, at) in enumerate(parts):
            row = lax.broadcasted_iota(jnp.int32, (piece, tokens), 0) + n * piece % rows
            allowed = lax.broadcasted_iota(jnp.int32, (piece, tokens), 1) <= row // group + i * block
            s = jnp.where(allowed, nt(q[n], keys(blocks[0], h)), NEG)
            s_ref[last, h, at] = s
            m_ref[h, at] = fold(s, jnp.maximum)
    else:
        m_ref[...] = old_m_ref[i]

    def look(b, carry):
        for n, (h, at) in enumerate(parts):
            s = nt(q[n], keys(buf.at[b], h))
            s_ref[b, h, at] = s
            m_ref[h, at] = jnp.maximum(m_ref[h, at], fold(s, jnp.maximum))
        return carry

    lax.fori_loop(0, total, look, 0)
    for h, at in parts:
        m = m_ref[h, at]
        m = jnp.broadcast_to(jnp.max(m, axis=1, keepdims=True), m.shape)
        m_ref[h, at] = m
        if own:
            p = weights(last, h, at, m)
            l_ref[h, at] = functools.reduce(jnp.add, p)
            p = jnp.concatenate([a.astype(jnp.bfloat16) for a in p], axis=1)
            acc_ref[h, at] = nt(p, values(blocks[0], h))
        else:
            share = jnp.exp2((old_m_ref[i, h, at] - m) * scale)
            l_ref[h, at] = old_l_ref[i, h, at] * share
            acc_ref[h, at] = old_acc_ref[i, h, at] * share

    def weigh(b, carry):
        for h, at in parts:
            p = weights(b, h, at, m_ref[h, at])
            l_ref[h, at] = l_ref[h, at] + functools.reduce(jnp.add, p)
            p = jnp.concatenate([a.astype(jnp.bfloat16) for a in p], axis=1)
            acc_ref[h, at] = acc_ref[h, at] + nt(p, values(buf.at[b], h))
        return carry

    lax.fori_loop(0, total, weigh, 0)
    if not own:
        out = []
        for h in range(heads):
            l = jnp.sum(l_ref[h], axis=1, keepdims=True)
            out.append((acc_ref[h] / l).reshape(block, group, -1))
        out_ref[0] = jnp.concatenate(out, axis=1).astype(out_ref.dtype)


def prefill(q, blocks, slots, needed, state):
    _, tokens, q_heads, width = q.shape
    own = state is None
    count = len(blocks)
    heads = blocks[0].shape[1]
    group = q_heads // heads
    block = 64
    rows = block * group
    q_spec = pl.BlockSpec((1, block, q_heads, width), lambda i, *_: (0, i, 0, 0))
    own_spec = pl.BlockSpec(blocks[0].shape, lambda i, *_: (0, 0, 0, 0, 0))
    any_spec = pl.BlockSpec(memory_space=pl.ANY)
    on_chip = pl.BlockSpec(memory_space=pltpu.VMEM)
    scratch = [
        pltpu.VMEM((count,) + blocks[0].shape, jnp.bfloat16),
        pltpu.VMEM((count, heads, rows, tokens), jnp.float32),
    ]
    if own:
        in_specs = [q_spec, own_spec] + [any_spec] * (count - 1)
        out_specs, state = [on_chip] * 3, ()
        out_shape = [pltpu.VMEM((tokens // block, heads, rows, width), jnp.float32)] * 3
    else:
        in_specs = [q_spec] + [any_spec] * count + [on_chip] * 3
        out_specs, out_shape = q_spec, jax.ShapeDtypeStruct(q.shape, jnp.bfloat16)
        scratch += [pltpu.VMEM((heads, rows, width), jnp.float32)] * 3
    return pl.pallas_call(
        functools.partial(
            prefill_kernel, own, count, slots, group, tokens, LOG2E / math.sqrt(width)
        ),
        grid_spec=pltpu.PrefetchScalarGridSpec(
            num_scalar_prefetch=1,
            grid=(tokens // block,),
            in_specs=in_specs,
            out_specs=out_specs,
            scratch_shapes=scratch + [pltpu.SemaphoreType.DMA((count,))],
        ),
        out_shape=out_shape,
        compiler_params=params(),
        cost_estimate=pl.CostEstimate(
            flops=16 * q_heads * tokens * tokens * count * width,
            bytes_accessed=12 * 10**6,
            transcendentals=tokens * tokens * count * q_heads,
        ),
    )(needed, *in_hbm(q), *blocks, *state)


def cache_kernel(
    steps, heads, group, target, targets, scale, len_ref, meta_ref, *refs
):
    q_ref, dk_ref, dv_ref, ck_ref, cv_ref, acc_ref, ml_ref = refs
    block, rows, width = q_ref.shape
    cache = ck_ref.shape[1]
    new = dk_ref.shape[1]
    per_step = heads * group

    def mask(columns):
        row = lax.broadcasted_iota(jnp.int32, (rows, columns), 0)
        column = lax.broadcasted_iota(jnp.int32, (rows, columns), 1)
        same = column % heads == row % per_step // group
        return jnp.where(same, column // heads, 1 << 20), row // per_step

    piece = min(cache, 128)
    pieces = range(0, cache, piece)
    place, _ = mask(piece)
    new_place, step = mask(new)
    new_allowed = new_place <= step
    low = lax.broadcasted_iota(jnp.int32, (rows, width), 1) < 4
    i = pl.program_id(0)
    first = (lax.rem(meta_ref[1] + target, targets) * pl.num_programs(0) + i) * block
    unroll = math.gcd(4, block)

    def body(g, carry):
        scores = []
        for u in range(unroll):
            r = g * unroll + u
            q = q_ref[r]
            length = len_ref[first + r]
            old = [
                jnp.where(
                    place < length - c // heads, nt(q, ck_ref[r, pl.ds(c, piece), :]), NEG
                )
                for c in pieces
            ]
            add = jnp.where(new_allowed, nt(q, dk_ref[r]), NEG)
            scores.append((r, old, add))
        weights = []
        for r, old, add in scores:
            top = functools.reduce(jnp.maximum, old)
            m = jnp.maximum(
                jnp.max(top, axis=1, keepdims=True), jnp.max(add, axis=1, keepdims=True)
            )
            old = [jnp.exp2((a - m) * scale) for a in old]
            add = jnp.exp2((add - m) * scale)
            l = jnp.sum(functools.reduce(jnp.add, old), axis=1, keepdims=True)
            l = l + jnp.sum(add, axis=1, keepdims=True)
            ml_ref[i * block + r] = jnp.where(low, m, l).T[:8]
            weights.append((r, [a.astype(jnp.bfloat16) for a in old], add.astype(jnp.bfloat16)))
        for r, old, add in weights:
            acc = nn(add, dv_ref[r])
            for c, p in zip(pieces, old):
                acc = acc + nn(p, cv_ref[r, pl.ds(c, piece), :])
            acc_ref[i * block + r] = acc.T
        return carry

    lax.fori_loop(0, block // unroll, body, 0)


def cache_part(q, dk, dv, ck, cv, lens, meta, target, targets, steps, heads, group):
    requests, rows, width = q.shape
    per_target = requests // targets
    block = math.gcd(8, per_target)
    per_block = per_target // block

    def here(i, lens, meta):
        return (lax.rem(meta[1] + target, targets) * per_block + i, 0, 0)

    spec = [pl.BlockSpec((block,) + a.shape[1:], here) for a in (q, dk, dv, ck, cv)]
    shapes = [(per_target, width, rows), (per_target, 8, rows)]
    return pl.pallas_call(
        functools.partial(
            cache_kernel, steps, heads, group, target, targets, LOG2E / math.sqrt(width)
        ),
        grid_spec=pltpu.PrefetchScalarGridSpec(
            num_scalar_prefetch=2,
            grid=(per_block,),
            in_specs=spec,
            out_specs=[pl.BlockSpec(memory_space=pltpu.VMEM)] * 2,
        ),
        out_shape=[pltpu.VMEM(a, jnp.float32) for a in shapes],
        compiler_params=params(),
        cost_estimate=pl.CostEstimate(
            flops=per_target * rows * ck.shape[1] * width * 16,
            bytes_accessed=7 * 10**6,
            transcendentals=per_target * rows * ck.shape[1],
        ),
    )(lens, meta, *in_hbm(q, dk, dv, ck, cv))


def decode_kernel(
    slots, extra, steps, target, targets, part, parts, heads, group, scale, *refs
):
    slot_ref, pick_ref, meta_ref = refs[:3]
    q_ref, acc_ref, ml_ref = refs[3:6]
    blocks = refs[6 : 6 + slots]
    out_ref, buf, sems = refs[6 + slots :]
    block, lanes, width = q_ref.shape
    i = pl.program_id(0)
    kept = (part * pl.num_programs(0) + i) * block
    first = lax.rem(meta_ref[1] + target, targets) * (parts * pl.num_programs(0) * block) + kept

    def copies():
        for s in range(slots):
            yield pltpu.make_async_copy(blocks[s].at[pick_ref[s]], buf.at[s], sems.at[s])

    @pl.when(i == 0)
    def _():
        for copy in copies():
            copy.start()
        for copy in copies():
            copy.wait()

    per_step = heads * group
    row_head = lax.broadcasted_iota(jnp.int32, (lanes, width), 0) % per_step // group
    head_rows = [jnp.where(row_head == h, 1.0, 0.0).astype(jnp.bfloat16) for h in range(heads)]
    lane_head = lax.broadcasted_iota(jnp.int32, (width, lanes), 1) % per_step // group
    order = one_hot(lanes, lanes, lambda r: r % steps * per_step + r // steps)
    unroll = math.gcd(8, block)
    both = math.gcd(2 if target else 1, heads)

    def body(g, carry):
        scores = []
        for u in range(unroll):
            r = g * unroll + u
            q = q_ref[r]
            places = [slot_ref[(first + r) * extra + j] for j in range(extra)]
            spread = jnp.concatenate([q * a for a in head_rows], axis=1)
            keys = [
                jnp.concatenate([buf[place, h, 0] for h in range(heads)], axis=1)
                for place in places
            ]
            s = []
            for j in range(0, extra, both):
                pair = jnp.concatenate(keys[j : j + both], axis=0)
                s.append(nt(pair, spread))
            scores.append((r, places, s))
        weights = []
        for r, places, s in scores:
            old = ml_ref[kept + r, 0:1]
            m = jnp.max(functools.reduce(jnp.maximum, s), axis=0, keepdims=True)
            m = jnp.maximum(m, old)
            p = [jnp.exp2((a - m) * scale) for a in s]
            shrink = jnp.exp2((old - m) * scale)
            l = jnp.sum(functools.reduce(jnp.add, p), axis=0, keepdims=True)
            l = ml_ref[kept + r, 4:5] * shrink + l
            p = jnp.concatenate([a.astype(jnp.bfloat16) for a in p], axis=0)
            weights.append((r, places, p, shrink, l))
        results = []
        for r, places, p, shrink, l in weights:
            values = [
                jnp.concatenate([buf[place, h, 1] for place in places], axis=1)
                for h in range(heads)
            ]
            for h in range(0, heads, both):
                pair = nn(jnp.concatenate(values[h : h + both], axis=0), p)
                for w in range(both):
                    mine = pair[w * width : (w + 1) * width]
                    found = mine if h + w == 0 else jnp.where(lane_head == h + w, mine, found)
            results.append((r, ((acc_ref[kept + r] * shrink + found) / l).astype(jnp.bfloat16)))
        for r, result in results:
            out_ref[r] = nt(order, result).astype(jnp.bfloat16)
        return carry

    lax.fori_loop(0, block // unroll, body, 0)


def decode(q, acc, ml, blocks, scalars, target, targets, part, parts, extra, steps, heads, group):
    requests, lanes, width = q.shape
    count = requests // targets // parts
    block = math.gcd(16, count)
    per_block = count // block
    slots = len(blocks)

    def here(i, slot, pick, meta):
        return ((lax.rem(meta[1] + target, targets) * parts + part) * per_block + i, 0, 0)

    in_specs = [pl.BlockSpec((block,) + q.shape[1:], here)]
    in_specs += [pl.BlockSpec(memory_space=pltpu.VMEM)] * 2
    in_specs += [pl.BlockSpec(memory_space=pl.ANY)] * slots
    return pl.pallas_call(
        functools.partial(
            decode_kernel,
            slots,
            extra,
            steps,
            target,
            targets,
            part,
            parts,
            heads,
            group,
            LOG2E / math.sqrt(width),
        ),
        grid_spec=pltpu.PrefetchScalarGridSpec(
            num_scalar_prefetch=3,
            grid=(per_block,),
            in_specs=in_specs,
            out_specs=pl.BlockSpec((block, lanes, width), lambda i, *_: (i, 0, 0)),
            scratch_shapes=[
                pltpu.VMEM((slots, heads, 2, PAGE, width), jnp.bfloat16),
                pltpu.SemaphoreType.DMA((slots,)),
            ],
        ),
        out_shape=jax.ShapeDtypeStruct((count, lanes, width), jnp.bfloat16),
        compiler_params=params(),
        cost_estimate=pl.CostEstimate(
            flops=10**6, bytes_accessed=10**6, transcendentals=0
        ),
    )(*scalars, *in_hbm(q), acc, ml, *blocks)


def join_kernel(counts, steps, meta_ref, *refs):
    out_ref = refs[-1]
    k = pl.program_id(0)
    rows = refs[0].shape[1]
    targets = len(counts)
    sources = iter(refs)
    for s, count in enumerate(counts):
        parts = [next(sources) for _ in range(count)]

        @pl.when(lax.rem(meta_ref[1] + (targets - s), targets) == k)
        def _():
            for n, source in enumerate(parts):

                def body(r, carry):
                    value = source[r]
                    for g in range(rows // steps):
                        out_ref[n * source.shape[0] + r, :, g * 128 : (g + 1) * 128] = value[
                            g * steps : (g + 1) * steps
                        ]
                    return carry

                lax.fori_loop(0, source.shape[0], body, 0)


def join(pieces, meta, steps):
    flat = [a for parts in pieces for a in parts]
    rows, width = flat[0].shape[1:]
    targets = len(pieces)
    per_target = sum(a.shape[0] for a in pieces[0])
    half = rows // steps * width
    return pl.pallas_call(
        functools.partial(join_kernel, [len(parts) for parts in pieces], steps),
        grid_spec=pltpu.PrefetchScalarGridSpec(
            num_scalar_prefetch=1,
            grid=(targets,),
            in_specs=[pl.BlockSpec(a.shape, lambda k, *_: (0, 0, 0)) for a in flat],
            out_specs=pl.BlockSpec((per_target, steps, half), lambda k, *_: (0, 0, k)),
        ),
        out_shape=jax.ShapeDtypeStruct((per_target, steps, half * targets), jnp.bfloat16),
        compiler_params=params(),
        cost_estimate=pl.CostEstimate(flops=0, bytes_accessed=2 * 10**6, transcendentals=0),
    )(meta, *flat)


def ring_place(index, size):
    return jnp.where(index % 2 == 0, index // 2, size - 1 - index // 2)


def shards(
    roles,
    ring,
    targets,
    prefill_q,
    prefill_k,
    prefill_v,
    decode_q,
    decode_k,
    decode_v,
    cache_k,
    cache_v,
    cache_len,
    page_list,
):
    tokens, q_heads = prefill_q.shape[1:3]
    heads, width = prefill_k.shape[2:]
    group = q_heads // heads
    own_pages = tokens // PAGE
    requests, steps = decode_q.shape[:2]
    extra = page_list.shape[1]
    role = lax.axis_index("role")
    ctx = lax.axis_index("ctx")
    tp = lax.axis_index("tp")

    order = list(range(0, ring, 2)) + list(range(ring - 1, 0, -2))
    along = [(order[j], order[(j + 1) % ring]) for j in range(ring)]
    flips = [1 << b for b in reversed(range(roles.bit_length() - 1))]

    owner = page_list // own_pages
    place = (ring_place(ctx, ring) - ring_place(owner % ring, ring)) % ring
    slot = ((owner // ring) ^ role) * ring + place
    hot = slot.reshape(-1, 1) == jnp.arange(roles * ring)[None, :]
    pick = jnp.max(jnp.where(hot, (page_list % own_pages).reshape(-1, 1), 0), axis=0)
    meta = jnp.stack([ctx, tp]).astype(jnp.int32)
    scalars = (
        slot.reshape(-1).astype(jnp.int32),
        pick.astype(jnp.int32),
        meta,
    )
    position = jnp.arange(ring)
    where = ring_place(ctx, ring)
    source = (where - position) % ring
    source_ctx = jnp.where(source < (ring + 1) // 2, 2 * source, 2 * (ring - 1 - source) + 1)
    needed = (source_ctx < ctx).astype(jnp.int32)

    raw = [
        a.reshape(requests, -1, width) for a in (decode_q, decode_k, decode_v, cache_k, cache_v)
    ]

    def cache(target):
        lens = cache_len.astype(jnp.int32)
        return cache_part(*raw, lens, meta, target, targets, steps, heads, group)

    gathered = {(0, 0): split_heads(prefill_k, prefill_v)}
    fresh = [(0, 0)]
    for k in range(ring + len(flips) - 1):
        sends = []
        for code, s in fresh:
            for flip in reversed(flips):
                if code == 0 or flip < code & -code:
                    pairs = [(j, j ^ flip) for j in range(roles)]
                    sends.append((flip, (code, s), (code ^ flip, s), "role", pairs))
            if code == 0 and s + 1 < ring:
                sends.append((roles, (code, s), (0, s + 1), "ctx", along))
        sends.sort(key=lambda a: a[0])
        names = [to for _, _, to, _, _ in sends]
        arrived = [lax.ppermute(gathered[of], axis, pairs) for _, of, _, axis, pairs in sends]
        beside = ()
        if k == 0:
            beside = cache(targets - 1)
        if k == 1:
            beside = prefill(prefill_q, [gathered[0, s] for s in (0, 1)], (0, 1), needed, None)
        if k == ring - 1:
            later = tuple(range(2, ring))
            beside = prefill(prefill_q, [gathered[0, s] for s in later], later, needed, state)
        if k == ring - 2 and k > 1:
            beside = scalars, {s: cache(s) for s in range(targets - 1)}
        arrived, beside = lax.optimization_barrier((arrived, beside))
        if k == 0:
            cached = {targets - 1: beside}
        if k == 1:
            state = beside
        if k == ring - 2 and k > 1:
            scalars, others = beside
            cached.update(others)
        if k == ring - 1:
            prefill_out = beside
        gathered.update(zip(names, arrived))
        fresh = names

    blocks = [gathered[r, s] for r in range(roles) for s in range(ring)]
    pieces = [None] * targets
    for s in reversed(range(targets)):
        parts = math.gcd(2, requests // targets) if s else 1
        pieces[s] = []
        if s == 0 and targets > 1:
            sent = [p[0] for p in pieces[1:]]
            cached[0], sent = lax.optimization_barrier((cached[0], sent))
            for p, a in zip(pieces[1:], sent):
                p[0] = a
        for part in range(parts):
            out = decode(
                raw[0], *cached[s], blocks, scalars, s, targets, part, parts, extra, steps, heads, group
            )
            if s:
                shift = [(j, (j + s) % targets) for j in range(targets)]
                out = lax.ppermute(out, "tp", shift)
            pieces[s].append(out)
    decode_out = join(pieces, scalars[2], steps)
    return (prefill_out, decode_out)


def solution(mesh):
    body = functools.partial(shards, mesh.shape["role"], mesh.shape["ctx"], mesh.shape["tp"])
    return jax.shard_map(
        body,
        mesh=mesh,
        in_specs=(
            P("role", "ctx", "tp", None),
            P("role", "ctx", "tp", None),
            P("role", "ctx", "tp", None),
            P(("role", "ctx"), None, "tp", None),
            P(("role", "ctx"), None, "tp", None),
            P(("role", "ctx"), None, "tp", None),
            P(("role", "ctx"), None, "tp", None),
            P(("role", "ctx"), None, "tp", None),
            P(("role", "ctx")),
            P(("role", "ctx"), None),
        ),
        out_specs=(P("role", "ctx", "tp", None), P(("role", "ctx", "tp"), None, None)),
        check_vma=False,
    )
```

```python
import functools
import math

import jax
import jax.numpy as jnp
from jax import lax
from jax.experimental import pallas as pl
from jax.experimental.pallas import tpu as pltpu
from jax.sharding import PartitionSpec as P

PAGE = 128
LOG2E = 1.4426950408889634
NEG = -1e30
VMEM_LIMIT = 16 * 1024 * 1024


def nt(a, b):
    return lax.dot_general(a, b, (((1,), (1,)), ((), ())), preferred_element_type=jnp.float32)


def nn(a, b):
    return jnp.dot(a, b, preferred_element_type=jnp.float32)


def in_hbm(*arrays):
    return [pltpu.with_memory_space_constraint(a, pltpu.HBM) for a in arrays]


def params():
    return pltpu.CompilerParams(vmem_limit_bytes=VMEM_LIMIT)


def one_hot(out_rows, in_rows, source):
    row = lax.broadcasted_iota(jnp.int32, (out_rows, in_rows), 0)
    col = lax.broadcasted_iota(jnp.int32, (out_rows, in_rows), 1)
    return jnp.where(col == source(row), 1.0, 0.0).astype(jnp.bfloat16)


def split_kernel(heads, tokens, k_ref, v_ref, out_ref):
    rows = min(tokens * heads, 256)
    step = rows // heads
    pick = one_hot(rows, rows, lambda i: (i % step) * heads + i // step)
    moved, kept = [], []
    for j in range(tokens // step):
        keys = nn(pick, k_ref[pl.ds(j * rows, rows), :]).astype(jnp.bfloat16)
        moved.append(nn(pick, v_ref[pl.ds(j * rows, rows), :]))
        kept.append(keys)
    for h in range(heads):
        keys = jnp.concatenate([a[h * step : (h + 1) * step] for a in kept], axis=0)
        values = jnp.concatenate([a[h * step : (h + 1) * step] for a in moved], axis=0)
        for page in range(tokens // PAGE):
            out_ref[page, h, 0] = keys[page * PAGE : (page + 1) * PAGE]
            out_ref[page, h, 1] = values[page * PAGE : (page + 1) * PAGE].T.astype(jnp.bfloat16)


def split_heads(k, v):
    _, tokens, heads, width = k.shape
    return pl.pallas_call(
        functools.partial(split_kernel, heads, tokens),
        out_specs=pl.BlockSpec(memory_space=pltpu.VMEM),
        out_shape=pltpu.VMEM((tokens // PAGE, heads, 2, PAGE, width), jnp.bfloat16),
        compiler_params=params(),
        cost_estimate=pl.CostEstimate(flops=10**8, bytes_accessed=2 * 10**6, transcendentals=0),
    )(*in_hbm(k.reshape(tokens * heads, width), v.reshape(tokens * heads, width)))


def prefill_kernel(own, count, slots, group, tokens, scale, needed_ref, *refs):
    q_ref = refs[0]
    blocks = refs[1 : 1 + count]
    refs = refs[1 + count :]
    i = pl.program_id(0)
    if own:
        acc_ref, m_ref, l_ref, buf, s_ref, sems = refs
        acc_ref, m_ref, l_ref = acc_ref.at[i], m_ref.at[i], l_ref.at[i]
    else:
        old_acc_ref, old_m_ref, old_l_ref, out_ref, buf, s_ref, acc_ref, m_ref, l_ref, sems = refs
    pages, heads = blocks[0].shape[:2]
    block = q_ref.shape[1]
    rest = range(1 if own else 0, count)
    total = sum(needed_ref[slots[c]] for c in rest)

    def copies():
        found = []
        place = jnp.int32(0)
        for c in rest:
            flag = needed_ref[slots[c]]
            found.append((flag, pltpu.make_async_copy(blocks[c], buf.at[place], sems.at[c])))
            place = place + flag
        return found

    @pl.when(i == 0)
    def _():
        for flag, copy in copies():
            @pl.when(flag == 1)
            def _():
                copy.start()
        for flag, copy in copies():
            @pl.when(flag == 1)
            def _():
                copy.wait()

    rows = block * group
    piece = min(rows, 256)
    parts = [(h, pl.ds(c, piece)) for h in range(heads) for c in range(0, rows, piece)]
    queries = q_ref[0].astype(jnp.float32)
    q = [
        queries[:, h * group : (h + 1) * group, :].reshape(rows, -1).astype(jnp.bfloat16)
        for h in range(heads)
    ]
    q = [q[h][c : c + piece] for h in range(heads) for c in range(0, rows, piece)]

    def fold(a, op):
        return functools.reduce(op, [a[:, j * 128 : (j + 1) * 128] for j in range(a.shape[1] // 128)])

    def keys(ref, h):
        return jnp.concatenate([ref[j, h, 0] for j in range(pages)], axis=0)

    def values(ref, h):
        return jnp.concatenate([ref[j, h, 1] for j in range(pages)], axis=1)

    def weights(place, h, at, m):
        return [
            jnp.exp2((s_ref[place, h, at, pl.ds(j * 128, 128)] - m) * scale)
            for j in range(tokens // 128)
        ]

    last = count - 1
    if own:
        for n, (h, at) in enumerate(parts):
            row = lax.broadcasted_iota(jnp.int32, (piece, tokens), 0) + n * piece % rows
            allowed = lax.broadcasted_iota(jnp.int32, (piece, tokens), 1) <= row // group + i * block
            s = jnp.where(allowed, nt(q[n], keys(blocks[0], h)), NEG)
            s_ref[last, h, at] = s
            m_ref[h, at] = fold(s, jnp.maximum)
    else:
        m_ref[...] = old_m_ref[i]

    def look(b, carry):
        for n, (h, at) in enumerate(parts):
            s = nt(q[n], keys(buf.at[b], h))
            s_ref[b, h, at] = s
            m_ref[h, at] = jnp.maximum(m_ref[h, at], fold(s, jnp.maximum))
        return carry

    lax.fori_loop(0, total, look, 0)
    for h, at in parts:
        m = m_ref[h, at]
        m = jnp.broadcast_to(jnp.max(m, axis=1, keepdims=True), m.shape)
        m_ref[h, at] = m
        if own:
            p = weights(last, h, at, m)
            l_ref[h, at] = functools.reduce(jnp.add, p)
            p = jnp.concatenate([a.astype(jnp.bfloat16) for a in p], axis=1)
            acc_ref[h, at] = nt(p, values(blocks[0], h))
        else:
            share = jnp.exp2((old_m_ref[i, h, at] - m) * scale)
            l_ref[h, at] = old_l_ref[i, h, at] * share
            acc_ref[h, at] = old_acc_ref[i, h, at] * share

    def weigh(b, carry):
        for h, at in parts:
            p = weights(b, h, at, m_ref[h, at])
            l_ref[h, at] = l_ref[h, at] + functools.reduce(jnp.add, p)
            p = jnp.concatenate([a.astype(jnp.bfloat16) for a in p], axis=1)
            acc_ref[h, at] = acc_ref[h, at] + nt(p, values(buf.at[b], h))
        return carry

    lax.fori_loop(0, total, weigh, 0)
    if not own:
        out = []
        for h in range(heads):
            l = jnp.sum(l_ref[h], axis=1, keepdims=True)
            out.append((acc_ref[h] / l).reshape(block, group, -1))
        out_ref[0] = jnp.concatenate(out, axis=1).astype(out_ref.dtype)


def prefill(q, blocks, slots, needed, state):
    _, tokens, q_heads, width = q.shape
    own = state is None
    count = len(blocks)
    heads = blocks[0].shape[1]
    group = q_heads // heads
    block = 64
    rows = block * group
    q_spec = pl.BlockSpec((1, block, q_heads, width), lambda i, *_: (0, i, 0, 0))
    own_spec = pl.BlockSpec(blocks[0].shape, lambda i, *_: (0, 0, 0, 0, 0))
    any_spec = pl.BlockSpec(memory_space=pl.ANY)
    on_chip = pl.BlockSpec(memory_space=pltpu.VMEM)
    scratch = [
        pltpu.VMEM((count,) + blocks[0].shape, jnp.bfloat16),
        pltpu.VMEM((count, heads, rows, tokens), jnp.float32),
    ]
    if own:
        in_specs = [q_spec, own_spec] + [any_spec] * (count - 1)
        out_specs, state = [on_chip] * 3, ()
        out_shape = [pltpu.VMEM((tokens // block, heads, rows, width), jnp.float32)] * 3
    else:
        in_specs = [q_spec] + [any_spec] * count + [on_chip] * 3
        out_specs, out_shape = q_spec, jax.ShapeDtypeStruct(q.shape, jnp.bfloat16)
        scratch += [pltpu.VMEM((heads, rows, width), jnp.float32)] * 3
    return pl.pallas_call(
        functools.partial(
            prefill_kernel, own, count, slots, group, tokens, LOG2E / math.sqrt(width)
        ),
        grid_spec=pltpu.PrefetchScalarGridSpec(
            num_scalar_prefetch=1,
            grid=(tokens // block,),
            in_specs=in_specs,
            out_specs=out_specs,
            scratch_shapes=scratch + [pltpu.SemaphoreType.DMA((count,))],
        ),
        out_shape=out_shape,
        compiler_params=params(),
        cost_estimate=pl.CostEstimate(
            flops=16 * q_heads * tokens * tokens * count * width,
            bytes_accessed=12 * 10**6,
            transcendentals=tokens * tokens * count * q_heads,
        ),
    )(needed, *in_hbm(q), *blocks, *state)


def cache_kernel(
    steps, heads, group, target, targets, scale, len_ref, meta_ref, *refs
):
    q_ref, dk_ref, dv_ref, ck_ref, cv_ref, acc_ref, ml_ref = refs
    block, rows, width = q_ref.shape
    cache = ck_ref.shape[1]
    new = dk_ref.shape[1]
    per_step = heads * group

    def mask(columns):
        row = lax.broadcasted_iota(jnp.int32, (rows, columns), 0)
        column = lax.broadcasted_iota(jnp.int32, (rows, columns), 1)
        same = column % heads == row % per_step // group
        return jnp.where(same, column // heads, 1 << 20), row // per_step

    piece = min(cache, 128)
    pieces = range(0, cache, piece)
    place, _ = mask(piece)
    new_place, step = mask(new)
    new_allowed = new_place <= step
    low = lax.broadcasted_iota(jnp.int32, (rows, width), 1) < 4
    i = pl.program_id(0)
    first = (lax.rem(meta_ref[1] + target, targets) * pl.num_programs(0) + i) * block
    unroll = math.gcd(4, block)

    def body(g, carry):
        scores = []
        for u in range(unroll):
            r = g * unroll + u
            q = q_ref[r]
            length = len_ref[first + r]
            old = [
                jnp.where(
                    place < length - c // heads, nt(q, ck_ref[r, pl.ds(c, piece), :]), NEG
                )
                for c in pieces
            ]
            add = jnp.where(new_allowed, nt(q, dk_ref[r]), NEG)
            scores.append((r, old, add))
        weights = []
        for r, old, add in scores:
            top = functools.reduce(jnp.maximum, old)
            m = jnp.maximum(
                jnp.max(top, axis=1, keepdims=True), jnp.max(add, axis=1, keepdims=True)
            )
            old = [jnp.exp2((a - m) * scale) for a in old]
            add = jnp.exp2((add - m) * scale)
            l = jnp.sum(functools.reduce(jnp.add, old), axis=1, keepdims=True)
            l = l + jnp.sum(add, axis=1, keepdims=True)
            ml_ref[i * block + r] = jnp.where(low, m, l).T[:8]
            weights.append((r, [a.astype(jnp.bfloat16) for a in old], add.astype(jnp.bfloat16)))
        for r, old, add in weights:
            acc = nn(add, dv_ref[r])
            for c, p in zip(pieces, old):
                acc = acc + nn(p, cv_ref[r, pl.ds(c, piece), :])
            acc_ref[i * block + r] = acc.T
        return carry

    lax.fori_loop(0, block // unroll, body, 0)


def cache_part(q, dk, dv, ck, cv, lens, meta, target, targets, steps, heads, group):
    requests, rows, width = q.shape
    per_target = requests // targets
    block = math.gcd(8, per_target)
    per_block = per_target // block

    def here(i, lens, meta):
        return (lax.rem(meta[1] + target, targets) * per_block + i, 0, 0)

    spec = [pl.BlockSpec((block,) + a.shape[1:], here) for a in (q, dk, dv, ck, cv)]
    shapes = [(per_target, width, rows), (per_target, 8, rows)]
    return pl.pallas_call(
        functools.partial(
            cache_kernel, steps, heads, group, target, targets, LOG2E / math.sqrt(width)
        ),
        grid_spec=pltpu.PrefetchScalarGridSpec(
            num_scalar_prefetch=2,
            grid=(per_block,),
            in_specs=spec,
            out_specs=[pl.BlockSpec(memory_space=pltpu.VMEM)] * 2,
        ),
        out_shape=[pltpu.VMEM(a, jnp.float32) for a in shapes],
        compiler_params=params(),
        cost_estimate=pl.CostEstimate(
            flops=per_target * rows * ck.shape[1] * width * 16,
            bytes_accessed=7 * 10**6,
            transcendentals=per_target * rows * ck.shape[1],
        ),
    )(lens, meta, *in_hbm(q, dk, dv, ck, cv))


def collect_kernel(pick_ref, *refs):
    blocks, out_ref, sems = refs[:-2], refs[-2], refs[-1]
    copies = [
        pltpu.make_async_copy(block.at[pick_ref[s]], out_ref.at[s], sems.at[s])
        for s, block in enumerate(blocks)
    ]
    for copy in copies:
        copy.start()
    for copy in copies:
        copy.wait()


def collect(pick, blocks):
    slots = len(blocks)
    return pl.pallas_call(
        collect_kernel,
        grid_spec=pltpu.PrefetchScalarGridSpec(
            num_scalar_prefetch=1,
            grid=(1,),
            in_specs=[pl.BlockSpec(memory_space=pl.ANY)] * slots,
            out_specs=pl.BlockSpec(memory_space=pltpu.VMEM),
            scratch_shapes=[pltpu.SemaphoreType.DMA((slots,))],
        ),
        out_shape=pltpu.VMEM((slots,) + blocks[0].shape[1:], jnp.bfloat16),
        compiler_params=params(),
        cost_estimate=pl.CostEstimate(flops=0, bytes_accessed=8 * 10**6, transcendentals=0),
    )(pick, *blocks)


def decode_kernel(
    extra, steps, target, targets, part, parts, heads, group, scale, slot_ref, meta_ref, *refs
):
    q_ref, acc_ref, ml_ref, buf, out_ref = refs
    block, lanes, width = q_ref.shape
    i = pl.program_id(0)
    kept = (part * pl.num_programs(0) + i) * block
    first = lax.rem(meta_ref[1] + target, targets) * (parts * pl.num_programs(0) * block) + kept

    per_step = heads * group
    row_head = lax.broadcasted_iota(jnp.int32, (lanes, width), 0) % per_step // group
    head_rows = [jnp.where(row_head == h, 1.0, 0.0).astype(jnp.bfloat16) for h in range(heads)]
    lane_head = lax.broadcasted_iota(jnp.int32, (width, lanes), 1) % per_step // group
    order = one_hot(lanes, lanes, lambda r: r % steps * per_step + r // steps)
    unroll = math.gcd(8, block)
    both = math.gcd(2 if target else 1, heads)

    def body(g, carry):
        scores = []
        for u in range(unroll):
            r = g * unroll + u
            q = q_ref[r]
            places = [slot_ref[(first + r) * extra + j] for j in range(extra)]
            spread = jnp.concatenate([q * a for a in head_rows], axis=1)
            keys = [
                jnp.concatenate([buf[place, h, 0] for h in range(heads)], axis=1)
                for place in places
            ]
            s = []
            for j in range(0, extra, both):
                pair = jnp.concatenate(keys[j : j + both], axis=0)
                s.append(nt(pair, spread))
            scores.append((r, places, s))
        weights = []
        for r, places, s in scores:
            old = ml_ref[kept + r, 0:1]
            m = jnp.max(functools.reduce(jnp.maximum, s), axis=0, keepdims=True)
            m = jnp.maximum(m, old)
            p = [jnp.exp2((a - m) * scale) for a in s]
            shrink = jnp.exp2((old - m) * scale)
            l = jnp.sum(functools.reduce(jnp.add, p), axis=0, keepdims=True)
            l = ml_ref[kept + r, 4:5] * shrink + l
            p = jnp.concatenate([a.astype(jnp.bfloat16) for a in p], axis=0)
            weights.append((r, places, p, shrink, l))
        results = []
        for r, places, p, shrink, l in weights:
            values = [
                jnp.concatenate([buf[place, h, 1] for place in places], axis=1)
                for h in range(heads)
            ]
            for h in range(0, heads, both):
                pair = nn(jnp.concatenate(values[h : h + both], axis=0), p)
                for w in range(both):
                    mine = pair[w * width : (w + 1) * width]
                    found = mine if h + w == 0 else jnp.where(lane_head == h + w, mine, found)
            results.append((r, ((acc_ref[kept + r] * shrink + found) / l).astype(jnp.bfloat16)))
        for r, result in results:
            out_ref[r] = nt(order, result).astype(jnp.bfloat16)
        return carry

    lax.fori_loop(0, block // unroll, body, 0)


def decode(q, acc, ml, pages, slot, meta, target, targets, part, parts, extra, steps, heads, group):
    requests, lanes, width = q.shape
    count = requests // targets // parts
    block = math.gcd(16, count)
    per_block = count // block

    def here(i, slot, meta):
        return ((lax.rem(meta[1] + target, targets) * parts + part) * per_block + i, 0, 0)

    on_chip = pl.BlockSpec(memory_space=pltpu.VMEM)
    return pl.pallas_call(
        functools.partial(
            decode_kernel,
            extra,
            steps,
            target,
            targets,
            part,
            parts,
            heads,
            group,
            LOG2E / math.sqrt(width),
        ),
        grid_spec=pltpu.PrefetchScalarGridSpec(
            num_scalar_prefetch=2,
            grid=(per_block,),
            in_specs=[pl.BlockSpec((block,) + q.shape[1:], here)] + [on_chip] * 3,
            out_specs=pl.BlockSpec((block, lanes, width), lambda i, *_: (i, 0, 0)),
        ),
        out_shape=jax.ShapeDtypeStruct((count, lanes, width), jnp.bfloat16),
        compiler_params=params(),
        cost_estimate=pl.CostEstimate(
            flops=10**6, bytes_accessed=10**6, transcendentals=0
        ),
    )(slot, meta, *in_hbm(q), acc, ml, pages)


def join_kernel(counts, steps, meta_ref, *refs):
    out_ref = refs[-1]
    k = pl.program_id(0)
    rows = refs[0].shape[1]
    targets = len(counts)
    sources = iter(refs)
    for s, count in enumerate(counts):
        parts = [next(sources) for _ in range(count)]

        @pl.when(lax.rem(meta_ref[1] + (targets - s), targets) == k)
        def _():
            for n, source in enumerate(parts):

                def body(r, carry):
                    value = source[r]
                    for g in range(rows // steps):
                        out_ref[n * source.shape[0] + r, :, g * 128 : (g + 1) * 128] = value[
                            g * steps : (g + 1) * steps
                        ]
                    return carry

                lax.fori_loop(0, source.shape[0], body, 0)


def join(pieces, meta, steps):
    flat = [a for parts in pieces for a in parts]
    rows, width = flat[0].shape[1:]
    targets = len(pieces)
    per_target = sum(a.shape[0] for a in pieces[0])
    half = rows // steps * width
    return pl.pallas_call(
        functools.partial(join_kernel, [len(parts) for parts in pieces], steps),
        grid_spec=pltpu.PrefetchScalarGridSpec(
            num_scalar_prefetch=1,
            grid=(targets,),
            in_specs=[pl.BlockSpec(a.shape, lambda k, *_: (0, 0, 0)) for a in flat],
            out_specs=pl.BlockSpec((per_target, steps, half), lambda k, *_: (0, 0, k)),
        ),
        out_shape=jax.ShapeDtypeStruct((per_target, steps, half * targets), jnp.bfloat16),
        compiler_params=params(),
        cost_estimate=pl.CostEstimate(flops=0, bytes_accessed=2 * 10**6, transcendentals=0),
    )(meta, *flat)


def ring_place(index, size):
    return jnp.where(index % 2 == 0, index // 2, size - 1 - index // 2)


def shards(
    roles,
    ring,
    targets,
    prefill_q,
    prefill_k,
    prefill_v,
    decode_q,
    decode_k,
    decode_v,
    cache_k,
    cache_v,
    cache_len,
    page_list,
):
    tokens, q_heads = prefill_q.shape[1:3]
    heads, width = prefill_k.shape[2:]
    group = q_heads // heads
    own_pages = tokens // PAGE
    requests, steps = decode_q.shape[:2]
    extra = page_list.shape[1]
    role = lax.axis_index("role")
    ctx = lax.axis_index("ctx")
    tp = lax.axis_index("tp")

    order = list(range(0, ring, 2)) + list(range(ring - 1, 0, -2))
    along = [(order[j], order[(j + 1) % ring]) for j in range(ring)]
    flips = [1 << b for b in reversed(range(roles.bit_length() - 1))]

    owner = page_list // own_pages
    place = (ring_place(ctx, ring) - ring_place(owner % ring, ring)) % ring
    slot = ((owner // ring) ^ role) * ring + place
    hot = slot.reshape(-1, 1) == jnp.arange(roles * ring)[None, :]
    pick = jnp.max(jnp.where(hot, (page_list % own_pages).reshape(-1, 1), 0), axis=0)
    meta = jnp.stack([ctx, tp]).astype(jnp.int32)
    scalars = (
        slot.reshape(-1).astype(jnp.int32),
        pick.astype(jnp.int32),
        meta,
    )
    position = jnp.arange(ring)
    where = ring_place(ctx, ring)
    source = (where - position) % ring
    source_ctx = jnp.where(source < (ring + 1) // 2, 2 * source, 2 * (ring - 1 - source) + 1)
    needed = (source_ctx < ctx).astype(jnp.int32)

    raw = [
        a.reshape(requests, -1, width) for a in (decode_q, decode_k, decode_v, cache_k, cache_v)
    ]

    def cache(target):
        lens = cache_len.astype(jnp.int32)
        return cache_part(*raw, lens, meta, target, targets, steps, heads, group)

    gathered = {(0, 0): split_heads(prefill_k, prefill_v)}
    fresh = [(0, 0)]
    for k in range(ring + len(flips) - 1):
        sends = []
        for code, s in fresh:
            for flip in reversed(flips):
                if code == 0 or flip < code & -code:
                    pairs = [(j, j ^ flip) for j in range(roles)]
                    sends.append((flip, (code, s), (code ^ flip, s), "role", pairs))
            if code == 0 and s + 1 < ring:
                sends.append((roles, (code, s), (0, s + 1), "ctx", along))
        sends.sort(key=lambda a: a[0])
        names = [to for _, _, to, _, _ in sends]
        arrived = [lax.ppermute(gathered[of], axis, pairs) for _, of, _, axis, pairs in sends]
        beside = ()
        if k == 0:
            beside = cache(targets - 1)
        if k == 1:
            beside = scalars, {s: cache(s) for s in range(targets - 1)}
        if k == ring - 2:
            first = tuple(range(ring - 1))
            beside = prefill(prefill_q, [gathered[0, s] for s in first], first, needed, None)
        if k == ring - 1:
            final = (ring - 1,)
            beside = prefill(prefill_q, [gathered[0, s] for s in final], final, needed, state)
        arrived, beside = lax.optimization_barrier((arrived, beside))
        if k == 0:
            cached = {targets - 1: beside}
        if k == 1:
            scalars, others = beside
            cached.update(others)
        if k == ring - 2:
            state = beside
        if k == ring - 1:
            prefill_out = beside
        gathered.update(zip(names, arrived))
        fresh = names

    blocks = [gathered[r, s] for r in range(roles) for s in range(ring)]
    slot, pick, meta = scalars
    pages = collect(pick, blocks)
    pieces = [None] * targets
    for s in reversed(range(targets)):
        parts = math.gcd(2, requests // targets) if s else 1
        pieces[s] = []
        if s == 0 and targets > 1:
            sent = [p[0] for p in pieces[1:]]
            cached[0], sent = lax.optimization_barrier((cached[0], sent))
            for p, a in zip(pieces[1:], sent):
                p[0] = a
        for part in range(parts):
            out = decode(
                raw[0], *cached[s], pages, slot, meta, s, targets, part, parts, extra, steps, heads, group
            )
            if s:
                shift = [(j, (j + s) % targets) for j in range(targets)]
                out = lax.ppermute(out, "tp", shift)
            pieces[s].append(out)
    decode_out = join(pieces, meta, steps)
    return (prefill_out, decode_out)


def solution(mesh):
    body = functools.partial(shards, mesh.shape["role"], mesh.shape["ctx"], mesh.shape["tp"])
    return jax.shard_map(
        body,
        mesh=mesh,
        in_specs=(
            P("role", "ctx", "tp", None),
            P("role", "ctx", "tp", None),
            P("role", "ctx", "tp", None),
            P(("role", "ctx"), None, "tp", None),
            P(("role", "ctx"), None, "tp", None),
            P(("role", "ctx"), None, "tp", None),
            P(("role", "ctx"), None, "tp", None),
            P(("role", "ctx"), None, "tp", None),
            P(("role", "ctx")),
            P(("role", "ctx"), None),
        ),
        out_specs=(P("role", "ctx", "tp", None), P(("role", "ctx", "tp"), None, None)),
        check_vma=False,
    )
```

```python
import functools
import math

import jax
import jax.numpy as jnp
from jax import lax
from jax.experimental import pallas as pl
from jax.experimental.pallas import tpu as pltpu
from jax.sharding import PartitionSpec as P

PAGE = 128
LOG2E = 1.4426950408889634
NEG = -1e30
VMEM_LIMIT = 16 * 1024 * 1024


def nt(a, b):
    return lax.dot_general(a, b, (((1,), (1,)), ((), ())), preferred_element_type=jnp.float32)


def nn(a, b):
    return jnp.dot(a, b, preferred_element_type=jnp.float32)


def in_hbm(*arrays):
    return [pltpu.with_memory_space_constraint(a, pltpu.HBM) for a in arrays]


def params():
    return pltpu.CompilerParams(vmem_limit_bytes=VMEM_LIMIT)


def one_hot(out_rows, in_rows, source):
    row = lax.broadcasted_iota(jnp.int32, (out_rows, in_rows), 0)
    col = lax.broadcasted_iota(jnp.int32, (out_rows, in_rows), 1)
    return jnp.where(col == source(row), 1.0, 0.0).astype(jnp.bfloat16)


def split_kernel(heads, tokens, k_ref, v_ref, out_ref):
    rows = min(tokens * heads, 256)
    step = rows // heads
    pick = one_hot(rows, rows, lambda i: (i % step) * heads + i // step)
    moved, kept = [], []
    for j in range(tokens // step):
        keys = nn(pick, k_ref[pl.ds(j * rows, rows), :]).astype(jnp.bfloat16)
        moved.append(nn(pick, v_ref[pl.ds(j * rows, rows), :]))
        kept.append(keys)
    for h in range(heads):
        keys = jnp.concatenate([a[h * step : (h + 1) * step] for a in kept], axis=0)
        values = jnp.concatenate([a[h * step : (h + 1) * step] for a in moved], axis=0)
        for page in range(tokens // PAGE):
            out_ref[page, h, 0] = keys[page * PAGE : (page + 1) * PAGE]
            out_ref[page, h, 1] = values[page * PAGE : (page + 1) * PAGE].T.astype(jnp.bfloat16)


def split_heads(k, v):
    _, tokens, heads, width = k.shape
    return pl.pallas_call(
        functools.partial(split_kernel, heads, tokens),
        out_specs=pl.BlockSpec(memory_space=pltpu.VMEM),
        out_shape=pltpu.VMEM((tokens // PAGE, heads, 2, PAGE, width), jnp.bfloat16),
        compiler_params=params(),
        cost_estimate=pl.CostEstimate(flops=10**8, bytes_accessed=2 * 10**6, transcendentals=0),
    )(*in_hbm(k.reshape(tokens * heads, width), v.reshape(tokens * heads, width)))


def prefill_kernel(own, done, count, slots, group, tokens, scale, needed_ref, *refs):
    q_ref = refs[0]
    blocks = refs[1 : 1 + count]
    refs = refs[1 + count :]
    i = pl.program_id(0)
    if own:
        acc_ref, m_ref, l_ref, buf, s_ref, sems = refs
        acc_ref, m_ref, l_ref = acc_ref.at[i], m_ref.at[i], l_ref.at[i]
    elif done:
        old_acc_ref, old_m_ref, old_l_ref, out_ref, buf, s_ref, acc_ref, m_ref, l_ref, sems = refs
    else:
        old_acc_ref, old_m_ref, old_l_ref, acc_ref, top_ref, l_ref, buf, s_ref, m_ref, sems = refs
        acc_ref, l_ref = acc_ref.at[i], l_ref.at[i]
    pages, heads = blocks[0].shape[:2]
    block = q_ref.shape[1]
    rest = range(1 if own else 0, count)
    total = sum(needed_ref[slots[c]] for c in rest)

    def copies():
        found = []
        place = jnp.int32(0)
        for c in rest:
            flag = needed_ref[slots[c]]
            found.append((flag, pltpu.make_async_copy(blocks[c], buf.at[place], sems.at[c])))
            place = place + flag
        return found

    @pl.when(i == 0)
    def _():
        for flag, copy in copies():
            @pl.when(flag == 1)
            def _():
                copy.start()
        for flag, copy in copies():
            @pl.when(flag == 1)
            def _():
                copy.wait()

    rows = block * group
    piece = min(rows, 256)
    parts = [(h, pl.ds(c, piece)) for h in range(heads) for c in range(0, rows, piece)]
    queries = q_ref[0].astype(jnp.float32)
    q = [
        queries[:, h * group : (h + 1) * group, :].reshape(rows, -1).astype(jnp.bfloat16)
        for h in range(heads)
    ]
    q = [q[h][c : c + piece] for h in range(heads) for c in range(0, rows, piece)]

    def fold(a, op):
        return functools.reduce(op, [a[:, j * 128 : (j + 1) * 128] for j in range(a.shape[1] // 128)])

    def keys(ref, h):
        return jnp.concatenate([ref[j, h, 0] for j in range(pages)], axis=0)

    def values(ref, h):
        return jnp.concatenate([ref[j, h, 1] for j in range(pages)], axis=1)

    def weights(place, h, at, m):
        return [
            jnp.exp2((s_ref[place, h, at, pl.ds(j * 128, 128)] - m) * scale)
            for j in range(tokens // 128)
        ]

    last = count - 1
    if own:
        for n, (h, at) in enumerate(parts):
            row = lax.broadcasted_iota(jnp.int32, (piece, tokens), 0) + n * piece % rows
            allowed = lax.broadcasted_iota(jnp.int32, (piece, tokens), 1) <= row // group + i * block
            s = jnp.where(allowed, nt(q[n], keys(blocks[0], h)), NEG)
            s_ref[last, h, at] = s
            m_ref[h, at] = fold(s, jnp.maximum)
    else:
        m_ref[...] = old_m_ref[i]

    def look(b, carry):
        for n, (h, at) in enumerate(parts):
            s = nt(q[n], keys(buf.at[b], h))
            s_ref[b, h, at] = s
            m_ref[h, at] = jnp.maximum(m_ref[h, at], fold(s, jnp.maximum))
        return carry

    lax.fori_loop(0, total, look, 0)
    for h, at in parts:
        m = m_ref[h, at]
        m = jnp.broadcast_to(jnp.max(m, axis=1, keepdims=True), m.shape)
        m_ref[h, at] = m
        if own:
            p = weights(last, h, at, m)
            l_ref[h, at] = functools.reduce(jnp.add, p)
            p = jnp.concatenate([a.astype(jnp.bfloat16) for a in p], axis=1)
            acc_ref[h, at] = nt(p, values(blocks[0], h))
        else:
            share = jnp.exp2((old_m_ref[i, h, at] - m) * scale)
            l_ref[h, at] = old_l_ref[i, h, at] * share
            acc_ref[h, at] = old_acc_ref[i, h, at] * share
            if not done:
                top_ref[i, h, at] = m

    def weigh(b, carry):
        for h, at in parts:
            p = weights(b, h, at, m_ref[h, at])
            l_ref[h, at] = l_ref[h, at] + functools.reduce(jnp.add, p)
            p = jnp.concatenate([a.astype(jnp.bfloat16) for a in p], axis=1)
            acc_ref[h, at] = acc_ref[h, at] + nt(p, values(buf.at[b], h))
        return carry

    lax.fori_loop(0, total, weigh, 0)
    if done:
        out = []
        for h in range(heads):
            l = jnp.sum(l_ref[h], axis=1, keepdims=True)
            out.append((acc_ref[h] / l).reshape(block, group, -1))
        out_ref[0] = jnp.concatenate(out, axis=1).astype(out_ref.dtype)


def prefill(q, blocks, slots, needed, state, done):
    _, tokens, q_heads, width = q.shape
    own = state is None
    count = len(blocks)
    heads = blocks[0].shape[1]
    group = q_heads // heads
    block = 64
    rows = block * group
    q_spec = pl.BlockSpec((1, block, q_heads, width), lambda i, *_: (0, i, 0, 0))
    own_spec = pl.BlockSpec(blocks[0].shape, lambda i, *_: (0, 0, 0, 0, 0))
    any_spec = pl.BlockSpec(memory_space=pl.ANY)
    on_chip = pl.BlockSpec(memory_space=pltpu.VMEM)
    scratch = [
        pltpu.VMEM((count,) + blocks[0].shape, jnp.bfloat16),
        pltpu.VMEM((count, heads, rows, tokens), jnp.float32),
    ]
    aliases = {}
    if own:
        in_specs = [q_spec, own_spec] + [any_spec] * (count - 1)
        state = ()
    else:
        in_specs = [q_spec] + [any_spec] * count + [on_chip] * 3
    if done:
        out_specs, out_shape = q_spec, jax.ShapeDtypeStruct(q.shape, jnp.bfloat16)
        scratch += [pltpu.VMEM((heads, rows, width), jnp.float32)] * 3
    else:
        out_specs = [on_chip] * 3
        out_shape = [pltpu.VMEM((tokens // block, heads, rows, width), jnp.float32)] * 3
        if not own:
            aliases = {2 + count + j: j for j in range(3)}
            scratch += [pltpu.VMEM((heads, rows, width), jnp.float32)]
    return pl.pallas_call(
        functools.partial(
            prefill_kernel, own, done, count, slots, group, tokens, LOG2E / math.sqrt(width)
        ),
        grid_spec=pltpu.PrefetchScalarGridSpec(
            num_scalar_prefetch=1,
            grid=(tokens // block,),
            in_specs=in_specs,
            out_specs=out_specs,
            scratch_shapes=scratch + [pltpu.SemaphoreType.DMA((count,))],
        ),
        out_shape=out_shape,
        input_output_aliases=aliases,
        compiler_params=params(),
        cost_estimate=pl.CostEstimate(
            flops=16 * q_heads * tokens * tokens * count * width,
            bytes_accessed=12 * 10**6,
            transcendentals=tokens * tokens * count * q_heads,
        ),
    )(needed, *in_hbm(q), *blocks, *state)


def cache_kernel(
    steps, heads, group, target, targets, scale, len_ref, meta_ref, *refs
):
    q_ref, dk_ref, dv_ref, ck_ref, cv_ref, acc_ref, ml_ref = refs
    block, rows, width = q_ref.shape
    cache = ck_ref.shape[1]
    new = dk_ref.shape[1]
    per_step = heads * group

    def mask(columns):
        row = lax.broadcasted_iota(jnp.int32, (rows, columns), 0)
        column = lax.broadcasted_iota(jnp.int32, (rows, columns), 1)
        same = column % heads == row % per_step // group
        return jnp.where(same, column // heads, 1 << 20), row // per_step

    piece = min(cache, 128)
    pieces = range(0, cache, piece)
    place, _ = mask(piece)
    new_place, step = mask(new)
    new_allowed = new_place <= step
    low = lax.broadcasted_iota(jnp.int32, (rows, width), 1) < 4
    i = pl.program_id(0)
    first = (lax.rem(meta_ref[1] + target, targets) * pl.num_programs(0) + i) * block
    unroll = math.gcd(4, block)

    def body(g, carry):
        scores = []
        for u in range(unroll):
            r = g * unroll + u
            q = q_ref[r]
            length = len_ref[first + r]
            old = [
                jnp.where(
                    place < length - c // heads, nt(q, ck_ref[r, pl.ds(c, piece), :]), NEG
                )
                for c in pieces
            ]
            add = jnp.where(new_allowed, nt(q, dk_ref[r]), NEG)
            scores.append((r, old, add))
        weights = []
        for r, old, add in scores:
            top = functools.reduce(jnp.maximum, old)
            m = jnp.maximum(
                jnp.max(top, axis=1, keepdims=True), jnp.max(add, axis=1, keepdims=True)
            )
            old = [jnp.exp2((a - m) * scale) for a in old]
            add = jnp.exp2((add - m) * scale)
            l = jnp.sum(functools.reduce(jnp.add, old), axis=1, keepdims=True)
            l = l + jnp.sum(add, axis=1, keepdims=True)
            ml_ref[i * block + r] = jnp.where(low, m, l).T[:8]
            weights.append((r, [a.astype(jnp.bfloat16) for a in old], add.astype(jnp.bfloat16)))
        for r, old, add in weights:
            acc = nn(add, dv_ref[r])
            for c, p in zip(pieces, old):
                acc = acc + nn(p, cv_ref[r, pl.ds(c, piece), :])
            acc_ref[i * block + r] = acc.T
        return carry

    lax.fori_loop(0, block // unroll, body, 0)


def cache_part(q, dk, dv, ck, cv, lens, meta, target, targets, steps, heads, group):
    requests, rows, width = q.shape
    per_target = requests // targets
    block = math.gcd(8, per_target)
    per_block = per_target // block

    def here(i, lens, meta):
        return (lax.rem(meta[1] + target, targets) * per_block + i, 0, 0)

    spec = [pl.BlockSpec((block,) + a.shape[1:], here) for a in (q, dk, dv, ck, cv)]
    shapes = [(per_target, width, rows), (per_target, 8, rows)]
    return pl.pallas_call(
        functools.partial(
            cache_kernel, steps, heads, group, target, targets, LOG2E / math.sqrt(width)
        ),
        grid_spec=pltpu.PrefetchScalarGridSpec(
            num_scalar_prefetch=2,
            grid=(per_block,),
            in_specs=spec,
            out_specs=[pl.BlockSpec(memory_space=pltpu.VMEM)] * 2,
        ),
        out_shape=[pltpu.VMEM(a, jnp.float32) for a in shapes],
        compiler_params=params(),
        cost_estimate=pl.CostEstimate(
            flops=per_target * rows * ck.shape[1] * width * 16,
            bytes_accessed=7 * 10**6,
            transcendentals=per_target * rows * ck.shape[1],
        ),
    )(lens, meta, *in_hbm(q, dk, dv, ck, cv))


def collect_kernel(pick_ref, *refs):
    blocks, out_ref, sems = refs[:-2], refs[-2], refs[-1]
    copies = [
        pltpu.make_async_copy(block.at[pick_ref[s]], out_ref.at[s], sems.at[s])
        for s, block in enumerate(blocks)
    ]
    for copy in copies:
        copy.start()
    for copy in copies:
        copy.wait()


def collect(pick, blocks):
    slots = len(blocks)
    return pl.pallas_call(
        collect_kernel,
        grid_spec=pltpu.PrefetchScalarGridSpec(
            num_scalar_prefetch=1,
            grid=(1,),
            in_specs=[pl.BlockSpec(memory_space=pl.ANY)] * slots,
            out_specs=pl.BlockSpec(memory_space=pltpu.VMEM),
            scratch_shapes=[pltpu.SemaphoreType.DMA((slots,))],
        ),
        out_shape=pltpu.VMEM((slots,) + blocks[0].shape[1:], jnp.bfloat16),
        compiler_params=params(),
        cost_estimate=pl.CostEstimate(flops=0, bytes_accessed=8 * 10**6, transcendentals=0),
    )(pick, *blocks)


def decode_kernel(
    extra, steps, target, targets, part, parts, heads, group, scale, slot_ref, meta_ref, *refs
):
    q_ref, acc_ref, ml_ref, buf, out_ref = refs
    block, lanes, width = q_ref.shape
    i = pl.program_id(0)
    kept = (part * pl.num_programs(0) + i) * block
    first = lax.rem(meta_ref[1] + target, targets) * (parts * pl.num_programs(0) * block) + kept

    per_step = heads * group
    row_head = lax.broadcasted_iota(jnp.int32, (lanes, width), 0) % per_step // group
    head_rows = [jnp.where(row_head == h, 1.0, 0.0).astype(jnp.bfloat16) for h in range(heads)]
    lane_head = lax.broadcasted_iota(jnp.int32, (width, lanes), 1) % per_step // group
    order = one_hot(lanes, lanes, lambda r: r % steps * per_step + r // steps)
    unroll = math.gcd(8, block)
    both = math.gcd(2 if target else 1, heads)

    def body(g, carry):
        scores = []
        for u in range(unroll):
            r = g * unroll + u
            q = q_ref[r]
            places = [slot_ref[(first + r) * extra + j] for j in range(extra)]
            spread = jnp.concatenate([q * a for a in head_rows], axis=1)
            keys = [
                jnp.concatenate([buf[place, h, 0] for h in range(heads)], axis=1)
                for place in places
            ]
            s = []
            for j in range(0, extra, both):
                pair = jnp.concatenate(keys[j : j + both], axis=0)
                s.append(nt(pair, spread))
            scores.append((r, places, s))
        weights = []
        for r, places, s in scores:
            old = ml_ref[kept + r, 0:1]
            m = jnp.max(functools.reduce(jnp.maximum, s), axis=0, keepdims=True)
            m = jnp.maximum(m, old)
            p = [jnp.exp2((a - m) * scale) for a in s]
            shrink = jnp.exp2((old - m) * scale)
            l = jnp.sum(functools.reduce(jnp.add, p), axis=0, keepdims=True)
            l = ml_ref[kept + r, 4:5] * shrink + l
            p = jnp.concatenate([a.astype(jnp.bfloat16) for a in p], axis=0)
            weights.append((r, places, p, shrink, l))
        results = []
        for r, places, p, shrink, l in weights:
            values = [
                jnp.concatenate([buf[place, h, 1] for place in places], axis=1)
                for h in range(heads)
            ]
            for h in range(0, heads, both):
                pair = nn(jnp.concatenate(values[h : h + both], axis=0), p)
                for w in range(both):
                    mine = pair[w * width : (w + 1) * width]
                    found = mine if h + w == 0 else jnp.where(lane_head == h + w, mine, found)
            results.append((r, ((acc_ref[kept + r] * shrink + found) / l).astype(jnp.bfloat16)))
        for r, result in results:
            out_ref[r] = nt(order, result).astype(jnp.bfloat16)
        return carry

    lax.fori_loop(0, block // unroll, body, 0)


def decode(q, acc, ml, pages, slot, meta, target, targets, part, parts, extra, steps, heads, group):
    requests, lanes, width = q.shape
    count = requests // targets // parts
    block = math.gcd(16, count)
    per_block = count // block

    def here(i, slot, meta):
        return ((lax.rem(meta[1] + target, targets) * parts + part) * per_block + i, 0, 0)

    on_chip = pl.BlockSpec(memory_space=pltpu.VMEM)
    return pl.pallas_call(
        functools.partial(
            decode_kernel,
            extra,
            steps,
            target,
            targets,
            part,
            parts,
            heads,
            group,
            LOG2E / math.sqrt(width),
        ),
        grid_spec=pltpu.PrefetchScalarGridSpec(
            num_scalar_prefetch=2,
            grid=(per_block,),
            in_specs=[pl.BlockSpec((block,) + q.shape[1:], here)] + [on_chip] * 3,
            out_specs=pl.BlockSpec((block, lanes, width), lambda i, *_: (i, 0, 0)),
        ),
        out_shape=jax.ShapeDtypeStruct((count, lanes, width), jnp.bfloat16),
        compiler_params=params(),
        cost_estimate=pl.CostEstimate(
            flops=10**6, bytes_accessed=10**6, transcendentals=0
        ),
    )(slot, meta, *in_hbm(q), acc, ml, pages)


def join_kernel(counts, steps, meta_ref, *refs):
    out_ref = refs[-1]
    k = pl.program_id(0)
    rows = refs[0].shape[1]
    targets = len(counts)
    sources = iter(refs)
    for s, count in enumerate(counts):
        parts = [next(sources) for _ in range(count)]

        @pl.when(lax.rem(meta_ref[1] + (targets - s), targets) == k)
        def _():
            for n, source in enumerate(parts):

                def body(r, carry):
                    value = source[r]
                    for g in range(rows // steps):
                        out_ref[n * source.shape[0] + r, :, g * 128 : (g + 1) * 128] = value[
                            g * steps : (g + 1) * steps
                        ]
                    return carry

                lax.fori_loop(0, source.shape[0], body, 0)


def join(pieces, meta, steps):
    flat = [a for parts in pieces for a in parts]
    rows, width = flat[0].shape[1:]
    targets = len(pieces)
    per_target = sum(a.shape[0] for a in pieces[0])
    half = rows // steps * width
    return pl.pallas_call(
        functools.partial(join_kernel, [len(parts) for parts in pieces], steps),
        grid_spec=pltpu.PrefetchScalarGridSpec(
            num_scalar_prefetch=1,
            grid=(targets,),
            in_specs=[pl.BlockSpec(a.shape, lambda k, *_: (0, 0, 0)) for a in flat],
            out_specs=pl.BlockSpec((per_target, steps, half), lambda k, *_: (0, 0, k)),
        ),
        out_shape=jax.ShapeDtypeStruct((per_target, steps, half * targets), jnp.bfloat16),
        compiler_params=params(),
        cost_estimate=pl.CostEstimate(flops=0, bytes_accessed=2 * 10**6, transcendentals=0),
    )(meta, *flat)


def ring_place(index, size):
    return jnp.where(index % 2 == 0, index // 2, size - 1 - index // 2)


def shards(
    roles,
    ring,
    targets,
    prefill_q,
    prefill_k,
    prefill_v,
    decode_q,
    decode_k,
    decode_v,
    cache_k,
    cache_v,
    cache_len,
    page_list,
):
    tokens, q_heads = prefill_q.shape[1:3]
    heads, width = prefill_k.shape[2:]
    group = q_heads // heads
    own_pages = tokens // PAGE
    requests, steps = decode_q.shape[:2]
    extra = page_list.shape[1]
    role = lax.axis_index("role")
    ctx = lax.axis_index("ctx")
    tp = lax.axis_index("tp")

    order = list(range(0, ring, 2)) + list(range(ring - 1, 0, -2))
    along = [(order[j], order[(j + 1) % ring]) for j in range(ring)]
    flips = [1 << b for b in reversed(range(roles.bit_length() - 1))]

    owner = page_list // own_pages
    place = (ring_place(ctx, ring) - ring_place(owner % ring, ring)) % ring
    slot = ((owner // ring) ^ role) * ring + place
    hot = slot.reshape(-1, 1) == jnp.arange(roles * ring)[None, :]
    pick = jnp.max(jnp.where(hot, (page_list % own_pages).reshape(-1, 1), 0), axis=0)
    meta = jnp.stack([ctx, tp]).astype(jnp.int32)
    scalars = (
        slot.reshape(-1).astype(jnp.int32),
        pick.astype(jnp.int32),
        meta,
    )
    position = jnp.arange(ring)
    where = ring_place(ctx, ring)
    source = (where - position) % ring
    source_ctx = jnp.where(source < (ring + 1) // 2, 2 * source, 2 * (ring - 1 - source) + 1)
    needed = (source_ctx < ctx).astype(jnp.int32)

    raw = [
        a.reshape(requests, -1, width) for a in (decode_q, decode_k, decode_v, cache_k, cache_v)
    ]

    def cache(target):
        lens = cache_len.astype(jnp.int32)
        return cache_part(*raw, lens, meta, target, targets, steps, heads, group)

    gathered = {(0, 0): split_heads(prefill_k, prefill_v)}
    state = None
    fresh = [(0, 0)]
    for k in range(ring + len(flips) - 1):
        sends = []
        for code, s in fresh:
            for flip in reversed(flips):
                if code == 0 or flip < code & -code:
                    pairs = [(j, j ^ flip) for j in range(roles)]
                    sends.append((flip, (code, s), (code ^ flip, s), "role", pairs))
            if code == 0 and s + 1 < ring:
                sends.append((roles, (code, s), (0, s + 1), "ctx", along))
        sends.sort(key=lambda a: a[0])
        names = [to for _, _, to, _, _ in sends]
        arrived = [lax.ppermute(gathered[of], axis, pairs) for _, of, _, axis, pairs in sends]
        beside = ()
        if k == 0:
            beside = scalars, {s: cache(s) for s in range(targets)}
        else:
            slots = (0, 1) if k == 1 else (k,)
            if k < ring:
                mine = [gathered[0, s] for s in slots]
                beside = prefill(prefill_q, mine, slots, needed, state, k == ring - 1)
        arrived, beside = lax.optimization_barrier((arrived, beside))
        if k == 0:
            scalars, cached = beside
        elif k < ring - 1:
            state = beside
        elif k == ring - 1:
            prefill_out = beside
        gathered.update(zip(names, arrived))
        fresh = names

    blocks = [gathered[r, s] for r in range(roles) for s in range(ring)]
    slot, pick, meta = scalars
    pages = collect(pick, blocks)
    pieces = [None] * targets
    for s in reversed(range(targets)):
        parts = math.gcd(2, requests // targets)
        pieces[s] = []
        for part in range(parts):
            if s == 0 and part == parts - 1 and targets > 1:
                sent = [p[0] for p in pieces[1:]]
                cached[0], sent = lax.optimization_barrier((cached[0], sent))
                for p, a in zip(pieces[1:], sent):
                    p[0] = a
            out = decode(
                raw[0], *cached[s], pages, slot, meta, s, targets, part, parts, extra, steps, heads, group
            )
            if s:
                shift = [(j, (j + s) % targets) for j in range(targets)]
                out = lax.ppermute(out, "tp", shift)
            pieces[s].append(out)
    decode_out = join(pieces, meta, steps)
    return (prefill_out, decode_out)


def solution(mesh):
    body = functools.partial(shards, mesh.shape["role"], mesh.shape["ctx"], mesh.shape["tp"])
    return jax.shard_map(
        body,
        mesh=mesh,
        in_specs=(
            P("role", "ctx", "tp", None),
            P("role", "ctx", "tp", None),
            P("role", "ctx", "tp", None),
            P(("role", "ctx"), None, "tp", None),
            P(("role", "ctx"), None, "tp", None),
            P(("role", "ctx"), None, "tp", None),
            P(("role", "ctx"), None, "tp", None),
            P(("role", "ctx"), None, "tp", None),
            P(("role", "ctx")),
            P(("role", "ctx"), None),
        ),
        out_specs=(P("role", "ctx", "tp", None), P(("role", "ctx", "tp"), None, None)),
        check_vma=False,
    )
```

```python
import functools
import math

import jax
import jax.numpy as jnp
from jax import lax
from jax.experimental import pallas as pl
from jax.experimental.pallas import tpu as pltpu
from jax.sharding import PartitionSpec as P

PAGE = 128
LOG2E = 1.4426950408889634
NEG = -1e30
VMEM_LIMIT = 16 * 1024 * 1024


def nt(a, b):
    return lax.dot_general(a, b, (((1,), (1,)), ((), ())), preferred_element_type=jnp.float32)


def nn(a, b):
    return jnp.dot(a, b, preferred_element_type=jnp.float32)


def in_hbm(*arrays):
    return [pltpu.with_memory_space_constraint(a, pltpu.HBM) for a in arrays]


def params():
    return pltpu.CompilerParams(vmem_limit_bytes=VMEM_LIMIT)


def one_hot(out_rows, in_rows, source):
    row = lax.broadcasted_iota(jnp.int32, (out_rows, in_rows), 0)
    col = lax.broadcasted_iota(jnp.int32, (out_rows, in_rows), 1)
    return jnp.where(col == source(row), 1.0, 0.0).astype(jnp.bfloat16)


def split_kernel(heads, tokens, k_ref, v_ref, out_ref):
    rows = min(tokens * heads, 256)
    step = rows // heads
    pick = one_hot(rows, rows, lambda i: (i % step) * heads + i // step)
    moved, kept = [], []
    for j in range(tokens // step):
        keys = nn(pick, k_ref[pl.ds(j * rows, rows), :]).astype(jnp.bfloat16)
        moved.append(nn(pick, v_ref[pl.ds(j * rows, rows), :]))
        kept.append(keys)
    for h in range(heads):
        keys = jnp.concatenate([a[h * step : (h + 1) * step] for a in kept], axis=0)
        values = jnp.concatenate([a[h * step : (h + 1) * step] for a in moved], axis=0)
        for page in range(tokens // PAGE):
            out_ref[page, h, 0] = keys[page * PAGE : (page + 1) * PAGE]
            out_ref[page, h, 1] = values[page * PAGE : (page + 1) * PAGE].T.astype(jnp.bfloat16)


def split_heads(k, v):
    _, tokens, heads, width = k.shape
    return pl.pallas_call(
        functools.partial(split_kernel, heads, tokens),
        out_specs=pl.BlockSpec(memory_space=pltpu.VMEM),
        out_shape=pltpu.VMEM((tokens // PAGE, heads, 2, PAGE, width), jnp.bfloat16),
        compiler_params=params(),
        cost_estimate=pl.CostEstimate(flops=10**8, bytes_accessed=2 * 10**6, transcendentals=0),
    )(*in_hbm(k.reshape(tokens * heads, width), v.reshape(tokens * heads, width)))


def prefill_kernel(own, done, count, slots, group, tokens, scale, needed_ref, *refs):
    q_ref = refs[0]
    blocks = refs[1 : 1 + count]
    refs = refs[1 + count :]
    i = pl.program_id(0)
    if own:
        acc_ref, m_ref, l_ref, buf, s_ref, sems = refs
        acc_ref, m_ref, l_ref = acc_ref.at[i], m_ref.at[i], l_ref.at[i]
    elif done:
        old_acc_ref, old_m_ref, old_l_ref, out_ref, buf, s_ref, acc_ref, m_ref, l_ref, sems = refs
    else:
        old_acc_ref, old_m_ref, old_l_ref, acc_ref, top_ref, l_ref, buf, s_ref, m_ref, sems = refs
        acc_ref, l_ref = acc_ref.at[i], l_ref.at[i]
    pages, heads = blocks[0].shape[:2]
    block = q_ref.shape[1]
    rest = range(1 if own else 0, count)
    total = sum(needed_ref[slots[c]] for c in rest)

    def copies():
        found = []
        place = jnp.int32(0)
        for c in rest:
            flag = needed_ref[slots[c]]
            found.append((flag, pltpu.make_async_copy(blocks[c], buf.at[place], sems.at[c])))
            place = place + flag
        return found

    @pl.when(i == 0)
    def _():
        for flag, copy in copies():
            @pl.when(flag == 1)
            def _():
                copy.start()
        for flag, copy in copies():
            @pl.when(flag == 1)
            def _():
                copy.wait()

    rows = block * group
    piece = min(rows, 256)
    parts = [(h, pl.ds(c, piece)) for h in range(heads) for c in range(0, rows, piece)]
    queries = q_ref[0].astype(jnp.float32)
    q = [
        queries[:, h * group : (h + 1) * group, :].reshape(rows, -1).astype(jnp.bfloat16)
        for h in range(heads)
    ]
    q = [q[h][c : c + piece] for h in range(heads) for c in range(0, rows, piece)]

    def fold(a, op):
        return functools.reduce(op, [a[:, j * 128 : (j + 1) * 128] for j in range(a.shape[1] // 128)])

    def keys(ref, h):
        return jnp.concatenate([ref[j, h, 0] for j in range(pages)], axis=0)

    def values(ref, h):
        return jnp.concatenate([ref[j, h, 1] for j in range(pages)], axis=1)

    def weights(place, h, at, m):
        return [
            jnp.exp2((s_ref[place, h, at, pl.ds(j * 128, 128)] - m) * scale)
            for j in range(tokens // 128)
        ]

    last = count - 1
    if own:
        for n, (h, at) in enumerate(parts):
            row = lax.broadcasted_iota(jnp.int32, (piece, tokens), 0) + n * piece % rows
            allowed = lax.broadcasted_iota(jnp.int32, (piece, tokens), 1) <= row // group + i * block
            s = jnp.where(allowed, nt(q[n], keys(blocks[0], h)), NEG)
            s_ref[last, h, at] = s
            m_ref[h, at] = fold(s, jnp.maximum)
    else:
        m_ref[...] = old_m_ref[i]

    def look(b, carry):
        for n, (h, at) in enumerate(parts):
            s = nt(q[n], keys(buf.at[b], h))
            s_ref[b, h, at] = s
            m_ref[h, at] = jnp.maximum(m_ref[h, at], fold(s, jnp.maximum))
        return carry

    lax.fori_loop(0, total, look, 0)
    for h, at in parts:
        m = m_ref[h, at]
        m = jnp.broadcast_to(jnp.max(m, axis=1, keepdims=True), m.shape)
        m_ref[h, at] = m
        if own:
            p = weights(last, h, at, m)
            l_ref[h, at] = functools.reduce(jnp.add, p)
            p = jnp.concatenate([a.astype(jnp.bfloat16) for a in p], axis=1)
            acc_ref[h, at] = nt(p, values(blocks[0], h))
        else:
            share = jnp.exp2((old_m_ref[i, h, at] - m) * scale)
            l_ref[h, at] = old_l_ref[i, h, at] * share
            acc_ref[h, at] = old_acc_ref[i, h, at] * share
            if not done:
                top_ref[i, h, at] = m

    def weigh(b, carry):
        for h, at in parts:
            p = weights(b, h, at, m_ref[h, at])
            l_ref[h, at] = l_ref[h, at] + functools.reduce(jnp.add, p)
            p = jnp.concatenate([a.astype(jnp.bfloat16) for a in p], axis=1)
            acc_ref[h, at] = acc_ref[h, at] + nt(p, values(buf.at[b], h))
        return carry

    lax.fori_loop(0, total, weigh, 0)
    if done:
        out = []
        for h in range(heads):
            l = jnp.sum(l_ref[h], axis=1, keepdims=True)
            out.append((acc_ref[h] / l).reshape(block, group, -1))
        out_ref[0] = jnp.concatenate(out, axis=1).astype(out_ref.dtype)


def prefill(q, blocks, slots, needed, state, done):
    _, tokens, q_heads, width = q.shape
    own = state is None
    count = len(blocks)
    heads = blocks[0].shape[1]
    group = q_heads // heads
    block = 64
    rows = block * group
    q_spec = pl.BlockSpec((1, block, q_heads, width), lambda i, *_: (0, i, 0, 0))
    own_spec = pl.BlockSpec(blocks[0].shape, lambda i, *_: (0, 0, 0, 0, 0))
    any_spec = pl.BlockSpec(memory_space=pl.ANY)
    on_chip = pl.BlockSpec(memory_space=pltpu.VMEM)
    scratch = [
        pltpu.VMEM((count,) + blocks[0].shape, jnp.bfloat16),
        pltpu.VMEM((count, heads, rows, tokens), jnp.float32),
    ]
    aliases = {}
    if own:
        in_specs = [q_spec, own_spec] + [any_spec] * (count - 1)
        state = ()
    else:
        in_specs = [q_spec] + [any_spec] * count + [on_chip] * 3
    if done:
        out_specs, out_shape = q_spec, jax.ShapeDtypeStruct(q.shape, jnp.bfloat16)
        scratch += [pltpu.VMEM((heads, rows, width), jnp.float32)] * 3
    else:
        out_specs = [on_chip] * 3
        out_shape = [pltpu.VMEM((tokens // block, heads, rows, width), jnp.float32)] * 3
        if not own:
            aliases = {2 + count + j: j for j in range(3)}
            scratch += [pltpu.VMEM((heads, rows, width), jnp.float32)]
    return pl.pallas_call(
        functools.partial(
            prefill_kernel, own, done, count, slots, group, tokens, LOG2E / math.sqrt(width)
        ),
        grid_spec=pltpu.PrefetchScalarGridSpec(
            num_scalar_prefetch=1,
            grid=(tokens // block,),
            in_specs=in_specs,
            out_specs=out_specs,
            scratch_shapes=scratch + [pltpu.SemaphoreType.DMA((count,))],
        ),
        out_shape=out_shape,
        input_output_aliases=aliases,
        compiler_params=params(),
        cost_estimate=pl.CostEstimate(
            flops=16 * q_heads * tokens * tokens * count * width,
            bytes_accessed=12 * 10**6,
            transcendentals=tokens * tokens * count * q_heads,
        ),
    )(needed, *in_hbm(q), *blocks, *state)


def cache_kernel(
    steps, heads, group, target, targets, part, parts, scale, len_ref, meta_ref, *refs
):
    q_ref, dk_ref, dv_ref, ck_ref, cv_ref, acc_ref, ml_ref = refs
    block, rows, width = q_ref.shape
    cache = ck_ref.shape[1]
    new = dk_ref.shape[1]
    per_step = heads * group

    def mask(columns):
        row = lax.broadcasted_iota(jnp.int32, (rows, columns), 0)
        column = lax.broadcasted_iota(jnp.int32, (rows, columns), 1)
        same = column % heads == row % per_step // group
        return jnp.where(same, column // heads, 1 << 20), row // per_step

    piece = min(cache, 128)
    pieces = range(0, cache, piece)
    place, _ = mask(piece)
    new_place, step = mask(new)
    new_allowed = new_place <= step
    low = lax.broadcasted_iota(jnp.int32, (rows, width), 1) < 4
    i = pl.program_id(0)
    place_here = lax.rem(meta_ref[1] + target, targets) * parts + part
    first = (place_here * pl.num_programs(0) + i) * block
    unroll = math.gcd(4, block)

    def body(g, carry):
        scores = []
        for u in range(unroll):
            r = g * unroll + u
            q = q_ref[r]
            length = len_ref[first + r]
            old = [
                jnp.where(
                    place < length - c // heads, nt(q, ck_ref[r, pl.ds(c, piece), :]), NEG
                )
                for c in pieces
            ]
            add = jnp.where(new_allowed, nt(q, dk_ref[r]), NEG)
            scores.append((r, old, add))
        weights = []
        for r, old, add in scores:
            top = functools.reduce(jnp.maximum, old)
            m = jnp.maximum(
                jnp.max(top, axis=1, keepdims=True), jnp.max(add, axis=1, keepdims=True)
            )
            old = [jnp.exp2((a - m) * scale) for a in old]
            add = jnp.exp2((add - m) * scale)
            l = jnp.sum(functools.reduce(jnp.add, old), axis=1, keepdims=True)
            l = l + jnp.sum(add, axis=1, keepdims=True)
            ml_ref[i * block + r] = jnp.where(low, m, l).T[:8]
            weights.append((r, [a.astype(jnp.bfloat16) for a in old], add.astype(jnp.bfloat16)))
        for r, old, add in weights:
            acc = nn(add, dv_ref[r])
            for c, p in zip(pieces, old):
                acc = acc + nn(p, cv_ref[r, pl.ds(c, piece), :])
            acc_ref[i * block + r] = acc.T
        return carry

    lax.fori_loop(0, block // unroll, body, 0)


def cache_part(q, dk, dv, ck, cv, lens, meta, target, targets, part, parts, steps, heads, group):
    requests, rows, width = q.shape
    count = requests // targets // parts
    block = math.gcd(4, count)
    per_block = count // block

    def here(i, lens, meta):
        return ((lax.rem(meta[1] + target, targets) * parts + part) * per_block + i, 0, 0)

    spec = [pl.BlockSpec((block,) + a.shape[1:], here) for a in (q, dk, dv, ck, cv)]
    shapes = [(count, width, rows), (count, 8, rows)]
    return pl.pallas_call(
        functools.partial(
            cache_kernel,
            steps,
            heads,
            group,
            target,
            targets,
            part,
            parts,
            LOG2E / math.sqrt(width),
        ),
        grid_spec=pltpu.PrefetchScalarGridSpec(
            num_scalar_prefetch=2,
            grid=(per_block,),
            in_specs=spec,
            out_specs=[pl.BlockSpec(memory_space=pltpu.VMEM)] * 2,
        ),
        out_shape=[pltpu.VMEM(a, jnp.float32) for a in shapes],
        compiler_params=params(),
        cost_estimate=pl.CostEstimate(
            flops=count * rows * ck.shape[1] * width * 16,
            bytes_accessed=7 * 10**6,
            transcendentals=count * rows * ck.shape[1],
        ),
    )(lens, meta, *in_hbm(q, dk, dv, ck, cv))


def collect_kernel(pick_ref, *refs):
    blocks, out_ref, sems = refs[:-2], refs[-2], refs[-1]
    copies = [
        pltpu.make_async_copy(block.at[pick_ref[s]], out_ref.at[s], sems.at[s])
        for s, block in enumerate(blocks)
    ]
    for copy in copies:
        copy.start()
    for copy in copies:
        copy.wait()


def collect(pick, blocks):
    slots = len(blocks)
    return pl.pallas_call(
        collect_kernel,
        grid_spec=pltpu.PrefetchScalarGridSpec(
            num_scalar_prefetch=1,
            grid=(1,),
            in_specs=[pl.BlockSpec(memory_space=pl.ANY)] * slots,
            out_specs=pl.BlockSpec(memory_space=pltpu.VMEM),
            scratch_shapes=[pltpu.SemaphoreType.DMA((slots,))],
        ),
        out_shape=pltpu.VMEM((slots,) + blocks[0].shape[1:], jnp.bfloat16),
        compiler_params=params(),
        cost_estimate=pl.CostEstimate(flops=0, bytes_accessed=8 * 10**6, transcendentals=0),
    )(pick, *blocks)


def decode_kernel(
    extra, steps, target, targets, part, parts, heads, group, scale, slot_ref, meta_ref, *refs
):
    q_ref, acc_ref, ml_ref, buf, out_ref = refs
    block, lanes, width = q_ref.shape
    i = pl.program_id(0)
    kept = i * block
    place_here = lax.rem(meta_ref[1] + target, targets) * parts + part
    first = place_here * pl.num_programs(0) * block + kept

    per_step = heads * group
    row_head = lax.broadcasted_iota(jnp.int32, (lanes, width), 0) % per_step // group
    head_rows = [jnp.where(row_head == h, 1.0, 0.0).astype(jnp.bfloat16) for h in range(heads)]
    lane_head = lax.broadcasted_iota(jnp.int32, (width, lanes), 1) % per_step // group
    order = one_hot(lanes, lanes, lambda r: r % steps * per_step + r // steps)
    unroll = math.gcd(8, block)
    both = math.gcd(2 if target else 1, heads)

    def body(g, carry):
        scores = []
        for u in range(unroll):
            r = g * unroll + u
            q = q_ref[r]
            places = [slot_ref[(first + r) * extra + j] for j in range(extra)]
            spread = jnp.concatenate([q * a for a in head_rows], axis=1)
            keys = [
                jnp.concatenate([buf[place, h, 0] for h in range(heads)], axis=1)
                for place in places
            ]
            s = []
            for j in range(0, extra, both):
                pair = jnp.concatenate(keys[j : j + both], axis=0)
                s.append(nt(pair, spread))
            scores.append((r, places, s))
        weights = []
        for r, places, s in scores:
            old = ml_ref[kept + r, 0:1]
            m = jnp.max(functools.reduce(jnp.maximum, s), axis=0, keepdims=True)
            m = jnp.maximum(m, old)
            p = [jnp.exp2((a - m) * scale) for a in s]
            shrink = jnp.exp2((old - m) * scale)
            l = jnp.sum(functools.reduce(jnp.add, p), axis=0, keepdims=True)
            l = ml_ref[kept + r, 4:5] * shrink + l
            p = jnp.concatenate([a.astype(jnp.bfloat16) for a in p], axis=0)
            weights.append((r, places, p, shrink, l))
        results = []
        for r, places, p, shrink, l in weights:
            values = [
                jnp.concatenate([buf[place, h, 1] for place in places], axis=1)
                for h in range(heads)
            ]
            for h in range(0, heads, both):
                pair = nn(jnp.concatenate(values[h : h + both], axis=0), p)
                for w in range(both):
                    mine = pair[w * width : (w + 1) * width]
                    found = mine if h + w == 0 else jnp.where(lane_head == h + w, mine, found)
            results.append((r, ((acc_ref[kept + r] * shrink + found) / l).astype(jnp.bfloat16)))
        for r, result in results:
            out_ref[r] = nt(order, result).astype(jnp.bfloat16)
        return carry

    lax.fori_loop(0, block // unroll, body, 0)


def decode(q, acc, ml, pages, slot, meta, target, targets, part, parts, extra, steps, heads, group):
    requests, lanes, width = q.shape
    count = requests // targets // parts
    block = math.gcd(16, count)
    per_block = count // block

    def here(i, slot, meta):
        return ((lax.rem(meta[1] + target, targets) * parts + part) * per_block + i, 0, 0)

    on_chip = pl.BlockSpec(memory_space=pltpu.VMEM)
    return pl.pallas_call(
        functools.partial(
            decode_kernel,
            extra,
            steps,
            target,
            targets,
            part,
            parts,
            heads,
            group,
            LOG2E / math.sqrt(width),
        ),
        grid_spec=pltpu.PrefetchScalarGridSpec(
            num_scalar_prefetch=2,
            grid=(per_block,),
            in_specs=[pl.BlockSpec((block,) + q.shape[1:], here)] + [on_chip] * 3,
            out_specs=pl.BlockSpec((block, lanes, width), lambda i, *_: (i, 0, 0)),
        ),
        out_shape=jax.ShapeDtypeStruct((count, lanes, width), jnp.bfloat16),
        compiler_params=params(),
        cost_estimate=pl.CostEstimate(
            flops=10**6, bytes_accessed=10**6, transcendentals=0
        ),
    )(slot, meta, *in_hbm(q), acc, ml, pages)


def join_kernel(counts, steps, meta_ref, *refs):
    out_ref = refs[-1]
    k = pl.program_id(0)
    rows = refs[0].shape[1]
    targets = len(counts)
    sources = iter(refs)
    for s, count in enumerate(counts):
        parts = [next(sources) for _ in range(count)]

        @pl.when(lax.rem(meta_ref[1] + (targets - s), targets) == k)
        def _():
            for n, source in enumerate(parts):

                def body(r, carry):
                    value = source[r]
                    for g in range(rows // steps):
                        out_ref[n * source.shape[0] + r, :, g * 128 : (g + 1) * 128] = value[
                            g * steps : (g + 1) * steps
                        ]
                    return carry

                lax.fori_loop(0, source.shape[0], body, 0)


def join(pieces, meta, steps):
    flat = [a for parts in pieces for a in parts]
    rows, width = flat[0].shape[1:]
    targets = len(pieces)
    per_target = sum(a.shape[0] for a in pieces[0])
    half = rows // steps * width
    return pl.pallas_call(
        functools.partial(join_kernel, [len(parts) for parts in pieces], steps),
        grid_spec=pltpu.PrefetchScalarGridSpec(
            num_scalar_prefetch=1,
            grid=(targets,),
            in_specs=[pl.BlockSpec(a.shape, lambda k, *_: (0, 0, 0)) for a in flat],
            out_specs=pl.BlockSpec((per_target, steps, half), lambda k, *_: (0, 0, k)),
        ),
        out_shape=jax.ShapeDtypeStruct((per_target, steps, half * targets), jnp.bfloat16),
        compiler_params=params(),
        cost_estimate=pl.CostEstimate(flops=0, bytes_accessed=2 * 10**6, transcendentals=0),
    )(meta, *flat)


def ring_place(index, size):
    return jnp.where(index % 2 == 0, index // 2, size - 1 - index // 2)


def shards(
    roles,
    ring,
    targets,
    prefill_q,
    prefill_k,
    prefill_v,
    decode_q,
    decode_k,
    decode_v,
    cache_k,
    cache_v,
    cache_len,
    page_list,
):
    tokens, q_heads = prefill_q.shape[1:3]
    heads, width = prefill_k.shape[2:]
    group = q_heads // heads
    own_pages = tokens // PAGE
    requests, steps = decode_q.shape[:2]
    extra = page_list.shape[1]
    role = lax.axis_index("role")
    ctx = lax.axis_index("ctx")
    tp = lax.axis_index("tp")

    order = list(range(0, ring, 2)) + list(range(ring - 1, 0, -2))
    along = [(order[j], order[(j + 1) % ring]) for j in range(ring)]
    flips = [1 << b for b in reversed(range(roles.bit_length() - 1))]

    owner = page_list // own_pages
    place = (ring_place(ctx, ring) - ring_place(owner % ring, ring)) % ring
    slot = ((owner // ring) ^ role) * ring + place
    hot = slot.reshape(-1, 1) == jnp.arange(roles * ring)[None, :]
    pick = jnp.max(jnp.where(hot, (page_list % own_pages).reshape(-1, 1), 0), axis=0)
    meta = jnp.stack([ctx, tp]).astype(jnp.int32)
    scalars = (
        slot.reshape(-1).astype(jnp.int32),
        pick.astype(jnp.int32),
        meta,
    )
    position = jnp.arange(ring)
    where = ring_place(ctx, ring)
    source = (where - position) % ring
    source_ctx = jnp.where(source < (ring + 1) // 2, 2 * source, 2 * (ring - 1 - source) + 1)
    needed = (source_ctx < ctx).astype(jnp.int32)

    raw = [
        a.reshape(requests, -1, width) for a in (decode_q, decode_k, decode_v, cache_k, cache_v)
    ]

    parts = math.gcd(2, requests // targets)
    lens = cache_len.astype(jnp.int32)
    latest = (0, parts - 1)

    def cache(where, arrays):
        return cache_part(*arrays, lens, meta, where[0], targets, where[1], parts, steps, heads, group)

    gathered = {(0, 0): split_heads(prefill_k, prefill_v)}
    state = None
    fresh = [(0, 0)]
    for k in range(ring + len(flips) - 1):
        sends = []
        for code, s in fresh:
            for flip in reversed(flips):
                if code == 0 or flip < code & -code:
                    pairs = [(j, j ^ flip) for j in range(roles)]
                    sends.append((flip, (code, s), (code ^ flip, s), "role", pairs))
            if code == 0 and s + 1 < ring:
                sends.append((roles, (code, s), (0, s + 1), "ctx", along))
        sends.sort(key=lambda a: a[0])
        names = [to for _, _, to, _, _ in sends]
        arrived = [lax.ppermute(gathered[of], axis, pairs) for _, of, _, axis, pairs in sends]
        beside = ()
        if k == 0:
            pairs = [(s, part) for s in range(targets) for part in range(parts)]
            beside = scalars, {w: cache(w, raw) for w in pairs if w != latest}
        else:
            slots = (0, 1) if k == 1 else (k,)
            if k < ring:
                mine = [gathered[0, s] for s in slots]
                beside = prefill(prefill_q, mine, slots, needed, state, k == ring - 1)
            if k == ring - 1:
                arrays, prefill_out = lax.optimization_barrier((raw, beside))
                beside = prefill_out, cache(latest, arrays)
        arrived, beside = lax.optimization_barrier((arrived, beside))
        if k == 0:
            scalars, cached = beside
        elif k < ring - 1:
            state = beside
        elif k == ring - 1:
            prefill_out, cached[latest] = beside
        gathered.update(zip(names, arrived))
        fresh = names

    blocks = [gathered[r, s] for r in range(roles) for s in range(ring)]
    slot, pick, meta = scalars
    pages = collect(pick, blocks)
    pieces = [None] * targets
    for s in reversed(range(targets)):
        pieces[s] = []
        for part in range(parts):
            if (s, part) == latest and targets > 1:
                sent = [p[0] for p in pieces[1:]]
                cached[latest], sent = lax.optimization_barrier((cached[latest], sent))
                for p, a in zip(pieces[1:], sent):
                    p[0] = a
            state = cached[s, part]
            out = decode(
                raw[0], *state, pages, slot, meta, s, targets, part, parts, extra, steps, heads, group
            )
            if s:
                shift = [(j, (j + s) % targets) for j in range(targets)]
                out = lax.ppermute(out, "tp", shift)
            pieces[s].append(out)
    decode_out = join(pieces, meta, steps)
    return (prefill_out, decode_out)


def solution(mesh):
    body = functools.partial(shards, mesh.shape["role"], mesh.shape["ctx"], mesh.shape["tp"])
    return jax.shard_map(
        body,
        mesh=mesh,
        in_specs=(
            P("role", "ctx", "tp", None),
            P("role", "ctx", "tp", None),
            P("role", "ctx", "tp", None),
            P(("role", "ctx"), None, "tp", None),
            P(("role", "ctx"), None, "tp", None),
            P(("role", "ctx"), None, "tp", None),
            P(("role", "ctx"), None, "tp", None),
            P(("role", "ctx"), None, "tp", None),
            P(("role", "ctx")),
            P(("role", "ctx"), None),
        ),
        out_specs=(P("role", "ctx", "tp", None), P(("role", "ctx", "tp"), None, None)),
        check_vma=False,
    )
```

```python
import functools
import math

import jax
import jax.numpy as jnp
from jax import lax
from jax.experimental import pallas as pl
from jax.experimental.pallas import tpu as pltpu
from jax.sharding import PartitionSpec as P

PAGE = 128
LOG2E = 1.4426950408889634
NEG = -1e30
VMEM_LIMIT = 16 * 1024 * 1024


def nt(a, b):
    return lax.dot_general(a, b, (((1,), (1,)), ((), ())), preferred_element_type=jnp.float32)


def nn(a, b):
    return jnp.dot(a, b, preferred_element_type=jnp.float32)


def in_hbm(*arrays):
    return [pltpu.with_memory_space_constraint(a, pltpu.HBM) for a in arrays]


def params():
    return pltpu.CompilerParams(vmem_limit_bytes=VMEM_LIMIT)


def one_hot(out_rows, in_rows, source):
    row = lax.broadcasted_iota(jnp.int32, (out_rows, in_rows), 0)
    col = lax.broadcasted_iota(jnp.int32, (out_rows, in_rows), 1)
    return jnp.where(col == source(row), 1.0, 0.0).astype(jnp.bfloat16)


def split_kernel(heads, tokens, k_ref, v_ref, out_ref):
    rows = min(tokens * heads, 256)
    step = rows // heads
    pick = one_hot(rows, rows, lambda i: (i % step) * heads + i // step)
    moved, kept = [], []
    for j in range(tokens // step):
        keys = nn(pick, k_ref[pl.ds(j * rows, rows), :]).astype(jnp.bfloat16)
        moved.append(nn(pick, v_ref[pl.ds(j * rows, rows), :]))
        kept.append(keys)
    for h in range(heads):
        keys = jnp.concatenate([a[h * step : (h + 1) * step] for a in kept], axis=0)
        values = jnp.concatenate([a[h * step : (h + 1) * step] for a in moved], axis=0)
        for page in range(tokens // PAGE):
            out_ref[page, h, 0] = keys[page * PAGE : (page + 1) * PAGE]
            out_ref[page, h, 1] = values[page * PAGE : (page + 1) * PAGE].T.astype(jnp.bfloat16)


def split_heads(k, v):
    _, tokens, heads, width = k.shape
    return pl.pallas_call(
        functools.partial(split_kernel, heads, tokens),
        out_specs=pl.BlockSpec(memory_space=pltpu.VMEM),
        out_shape=pltpu.VMEM((tokens // PAGE, heads, 2, PAGE, width), jnp.bfloat16),
        compiler_params=params(),
        cost_estimate=pl.CostEstimate(flops=10**8, bytes_accessed=2 * 10**6, transcendentals=0),
    )(*in_hbm(k.reshape(tokens * heads, width), v.reshape(tokens * heads, width)))


def prefill_kernel(own, count, slots, group, tokens, scale, needed_ref, *refs):
    q_ref = refs[0]
    blocks = refs[1 : 1 + count]
    refs = refs[1 + count :]
    i = pl.program_id(0)
    if own:
        old_acc_ref, old_m_ref, old_l_ref, out_ref, buf, s_ref, acc_ref, m_ref, l_ref, sems = refs
    else:
        acc_ref, m_ref, l_ref, buf, s_ref, sems = refs
        acc_ref, m_ref, l_ref = acc_ref.at[i], m_ref.at[i], l_ref.at[i]
    pages, heads = blocks[0].shape[:2]
    block = q_ref.shape[1]
    rest = range(1 if own else 0, count)
    total = sum(needed_ref[slots[c]] for c in rest)

    def copies():
        found = []
        place = jnp.int32(0)
        for c in rest:
            flag = needed_ref[slots[c]]
            found.append((flag, pltpu.make_async_copy(blocks[c], buf.at[place], sems.at[c])))
            place = place + flag
        return found

    @pl.when(i == 0)
    def _():
        for flag, copy in copies():
            @pl.when(flag == 1)
            def _():
                copy.start()
        for flag, copy in copies():
            @pl.when(flag == 1)
            def _():
                copy.wait()

    rows = block * group
    piece = min(rows, 256)
    parts = [(h, pl.ds(c, piece)) for h in range(heads) for c in range(0, rows, piece)]
    queries = q_ref[0].astype(jnp.float32)
    q = [
        queries[:, h * group : (h + 1) * group, :].reshape(rows, -1).astype(jnp.bfloat16)
        for h in range(heads)
    ]
    q = [q[h][c : c + piece] for h in range(heads) for c in range(0, rows, piece)]

    def fold(a, op):
        return functools.reduce(op, [a[:, j * 128 : (j + 1) * 128] for j in range(a.shape[1] // 128)])

    def keys(ref, h):
        return jnp.concatenate([ref[j, h, 0] for j in range(pages)], axis=0)

    def values(ref, h):
        return jnp.concatenate([ref[j, h, 1] for j in range(pages)], axis=1)

    def weights(place, h, at, m):
        return [
            jnp.exp2((s_ref[place, h, at, pl.ds(j * 128, 128)] - m) * scale)
            for j in range(tokens // 128)
        ]

    last = count - 1
    if own:
        m_ref[...] = old_m_ref[i]
        for j in range(pages):
            @pl.when((i + 1) * block > j * PAGE)
            def _():
                for n, (h, at) in enumerate(parts):
                    row = lax.broadcasted_iota(jnp.int32, (piece, PAGE), 0) + n * piece % rows
                    column = lax.broadcasted_iota(jnp.int32, (piece, PAGE), 1) + j * PAGE
                    s = nt(q[n], blocks[0][j, h, 0])
                    s = jnp.where(column <= row // group + i * block, s, NEG)
                    s_ref[last, h, at, pl.ds(j * PAGE, PAGE)] = s
                    m_ref[h, at] = jnp.maximum(m_ref[h, at], s)
    else:
        m_ref[...] = jnp.full(m_ref.shape, NEG, jnp.float32)

    def look(b, carry):
        for n, (h, at) in enumerate(parts):
            s = nt(q[n], keys(buf.at[b], h))
            s_ref[b, h, at] = s
            m_ref[h, at] = jnp.maximum(m_ref[h, at], fold(s, jnp.maximum))
        return carry

    lax.fori_loop(0, total, look, 0)
    for h, at in parts:
        m = m_ref[h, at]
        m = jnp.broadcast_to(jnp.max(m, axis=1, keepdims=True), m.shape)
        m_ref[h, at] = m
        if own:
            share = jnp.exp2((old_m_ref[i, h, at] - m) * scale)
            l_ref[h, at] = old_l_ref[i, h, at] * share
            acc_ref[h, at] = old_acc_ref[i, h, at] * share
        else:
            l_ref[h, at] = jnp.zeros(m.shape, jnp.float32)
            acc_ref[h, at] = jnp.zeros(m.shape, jnp.float32)
    if own:
        for j in range(pages):
            @pl.when((i + 1) * block > j * PAGE)
            def _():
                for h, at in parts:
                    p = s_ref[last, h, at, pl.ds(j * PAGE, PAGE)]
                    p = jnp.exp2((p - m_ref[h, at]) * scale)
                    l_ref[h, at] = l_ref[h, at] + p
                    acc_ref[h, at] = acc_ref[h, at] + nt(p.astype(jnp.bfloat16), blocks[0][j, h, 1])

    def weigh(b, carry):
        for h, at in parts:
            p = weights(b, h, at, m_ref[h, at])
            l_ref[h, at] = l_ref[h, at] + functools.reduce(jnp.add, p)
            p = jnp.concatenate([a.astype(jnp.bfloat16) for a in p], axis=1)
            acc_ref[h, at] = acc_ref[h, at] + nt(p, values(buf.at[b], h))
        return carry

    lax.fori_loop(0, total, weigh, 0)
    if own:
        out = []
        for h in range(heads):
            l = jnp.sum(l_ref[h], axis=1, keepdims=True)
            out.append((acc_ref[h] / l).reshape(block, group, -1))
        out_ref[0] = jnp.concatenate(out, axis=1).astype(out_ref.dtype)


def prefill(q, blocks, slots, needed, state):
    _, tokens, q_heads, width = q.shape
    own = state is not None
    count = len(blocks)
    heads = blocks[0].shape[1]
    group = q_heads // heads
    block = 64
    rows = block * group
    q_spec = pl.BlockSpec((1, block, q_heads, width), lambda i, *_: (0, i, 0, 0))
    own_spec = pl.BlockSpec(blocks[0].shape, lambda i, *_: (0, 0, 0, 0, 0))
    any_spec = pl.BlockSpec(memory_space=pl.ANY)
    on_chip = pl.BlockSpec(memory_space=pltpu.VMEM)
    scratch = [
        pltpu.VMEM((count,) + blocks[0].shape, jnp.bfloat16),
        pltpu.VMEM((count, heads, rows, tokens), jnp.float32),
    ]
    if own:
        in_specs = [q_spec, own_spec] + [any_spec] * (count - 1) + [on_chip] * 3
        out_specs, out_shape = q_spec, jax.ShapeDtypeStruct(q.shape, jnp.bfloat16)
        scratch += [pltpu.VMEM((heads, rows, width), jnp.float32)] * 3
    else:
        in_specs = [q_spec] + [any_spec] * count
        out_specs, state = [on_chip] * 3, ()
        out_shape = [pltpu.VMEM((tokens // block, heads, rows, width), jnp.float32)] * 3
    return pl.pallas_call(
        functools.partial(
            prefill_kernel, own, count, slots, group, tokens, LOG2E / math.sqrt(width)
        ),
        grid_spec=pltpu.PrefetchScalarGridSpec(
            num_scalar_prefetch=1,
            grid=(tokens // block,),
            in_specs=in_specs,
            out_specs=out_specs,
            scratch_shapes=scratch + [pltpu.SemaphoreType.DMA((count,))],
        ),
        out_shape=out_shape,
        compiler_params=params(),
        cost_estimate=pl.CostEstimate(
            flops=16 * q_heads * tokens * tokens * count * width,
            bytes_accessed=12 * 10**6,
            transcendentals=tokens * tokens * count * q_heads,
        ),
    )(needed, *in_hbm(q), *blocks, *state)


def cache_kernel(
    steps, heads, group, target, targets, scale, len_ref, meta_ref, *refs
):
    q_ref, dk_ref, dv_ref, ck_ref, cv_ref, acc_ref, ml_ref = refs
    block, rows, width = q_ref.shape
    cache = ck_ref.shape[1]
    new = dk_ref.shape[1]
    per_step = heads * group

    def mask(columns):
        row = lax.broadcasted_iota(jnp.int32, (rows, columns), 0)
        column = lax.broadcasted_iota(jnp.int32, (rows, columns), 1)
        same = column % heads == row % per_step // group
        return jnp.where(same, column // heads, 1 << 20), row // per_step

    piece = min(cache, 128)
    pieces = range(0, cache, piece)
    place, _ = mask(piece)
    new_place, step = mask(new)
    new_allowed = new_place <= step
    low = lax.broadcasted_iota(jnp.int32, (rows, width), 1) < 4
    i = pl.program_id(0)
    first = (lax.rem(meta_ref[1] + target, targets) * pl.num_programs(0) + i) * block
    unroll = math.gcd(4, block)

    def body(g, carry):
        scores = []
        for u in range(unroll):
            r = g * unroll + u
            q = q_ref[r]
            length = len_ref[first + r]
            old = [
                jnp.where(
                    place < length - c // heads, nt(q, ck_ref[r, pl.ds(c, piece), :]), NEG
                )
                for c in pieces
            ]
            add = jnp.where(new_allowed, nt(q, dk_ref[r]), NEG)
            scores.append((r, old, add))
        weights = []
        for r, old, add in scores:
            top = functools.reduce(jnp.maximum, old)
            m = jnp.maximum(
                jnp.max(top, axis=1, keepdims=True), jnp.max(add, axis=1, keepdims=True)
            )
            old = [jnp.exp2((a - m) * scale) for a in old]
            add = jnp.exp2((add - m) * scale)
            l = jnp.sum(functools.reduce(jnp.add, old), axis=1, keepdims=True)
            l = l + jnp.sum(add, axis=1, keepdims=True)
            ml_ref[i * block + r] = jnp.where(low, m, l).T[:8]
            weights.append((r, [a.astype(jnp.bfloat16) for a in old], add.astype(jnp.bfloat16)))
        for r, old, add in weights:
            acc = nn(add, dv_ref[r])
            for c, p in zip(pieces, old):
                acc = acc + nn(p, cv_ref[r, pl.ds(c, piece), :])
            acc_ref[i * block + r] = acc.T
        return carry

    lax.fori_loop(0, block // unroll, body, 0)


def cache_part(q, dk, dv, ck, cv, lens, meta, target, targets, steps, heads, group):
    requests, rows, width = q.shape
    per_target = requests // targets
    block = math.gcd(8, per_target)
    per_block = per_target // block

    def here(i, lens, meta):
        return (lax.rem(meta[1] + target, targets) * per_block + i, 0, 0)

    spec = [pl.BlockSpec((block,) + a.shape[1:], here) for a in (q, dk, dv, ck, cv)]
    shapes = [(per_target, width, rows), (per_target, 8, rows)]
    return pl.pallas_call(
        functools.partial(
            cache_kernel, steps, heads, group, target, targets, LOG2E / math.sqrt(width)
        ),
        grid_spec=pltpu.PrefetchScalarGridSpec(
            num_scalar_prefetch=2,
            grid=(per_block,),
            in_specs=spec,
            out_specs=[pl.BlockSpec(memory_space=pltpu.VMEM)] * 2,
        ),
        out_shape=[pltpu.VMEM(a, jnp.float32) for a in shapes],
        compiler_params=params(),
        cost_estimate=pl.CostEstimate(
            flops=per_target * rows * ck.shape[1] * width * 16,
            bytes_accessed=7 * 10**6,
            transcendentals=per_target * rows * ck.shape[1],
        ),
    )(lens, meta, *in_hbm(q, dk, dv, ck, cv))


def collect_kernel(pick_ref, *refs):
    blocks, out_ref, sems = refs[:-2], refs[-2], refs[-1]
    copies = [
        pltpu.make_async_copy(block.at[pick_ref[s]], out_ref.at[s], sems.at[s])
        for s, block in enumerate(blocks)
    ]
    for copy in copies:
        copy.start()
    for copy in copies:
        copy.wait()


def collect(pick, blocks):
    slots = len(blocks)
    return pl.pallas_call(
        collect_kernel,
        grid_spec=pltpu.PrefetchScalarGridSpec(
            num_scalar_prefetch=1,
            grid=(1,),
            in_specs=[pl.BlockSpec(memory_space=pl.ANY)] * slots,
            out_specs=pl.BlockSpec(memory_space=pltpu.VMEM),
            scratch_shapes=[pltpu.SemaphoreType.DMA((slots,))],
        ),
        out_shape=pltpu.VMEM((slots,) + blocks[0].shape[1:], jnp.bfloat16),
        compiler_params=params(),
        cost_estimate=pl.CostEstimate(flops=0, bytes_accessed=8 * 10**6, transcendentals=0),
    )(pick, *blocks)


def decode_kernel(
    extra, steps, target, targets, part, parts, heads, group, scale, slot_ref, meta_ref, *refs
):
    q_ref, acc_ref, ml_ref, buf, out_ref = refs
    block, lanes, width = q_ref.shape
    i = pl.program_id(0)
    kept = (part * pl.num_programs(0) + i) * block
    first = lax.rem(meta_ref[1] + target, targets) * (parts * pl.num_programs(0) * block) + kept

    per_step = heads * group
    row_head = lax.broadcasted_iota(jnp.int32, (lanes, width), 0) % per_step // group
    head_rows = [jnp.where(row_head == h, 1.0, 0.0).astype(jnp.bfloat16) for h in range(heads)]
    lane_head = lax.broadcasted_iota(jnp.int32, (width, lanes), 1) % per_step // group
    order = one_hot(lanes, lanes, lambda r: r % steps * per_step + r // steps)
    unroll = math.gcd(8, block)
    both = math.gcd(2 if target else 1, heads)

    def body(g, carry):
        scores = []
        for u in range(unroll):
            r = g * unroll + u
            q = q_ref[r]
            places = [slot_ref[(first + r) * extra + j] for j in range(extra)]
            spread = jnp.concatenate([q * a for a in head_rows], axis=1)
            keys = [
                jnp.concatenate([buf[place, h, 0] for h in range(heads)], axis=1)
                for place in places
            ]
            s = []
            for j in range(0, extra, both):
                pair = jnp.concatenate(keys[j : j + both], axis=0)
                s.append(nt(pair, spread))
            scores.append((r, places, s))
        weights = []
        for r, places, s in scores:
            old = ml_ref[kept + r, 0:1]
            m = jnp.max(functools.reduce(jnp.maximum, s), axis=0, keepdims=True)
            m = jnp.maximum(m, old)
            p = [jnp.exp2((a - m) * scale) for a in s]
            shrink = jnp.exp2((old - m) * scale)
            l = jnp.sum(functools.reduce(jnp.add, p), axis=0, keepdims=True)
            l = ml_ref[kept + r, 4:5] * shrink + l
            p = jnp.concatenate([a.astype(jnp.bfloat16) for a in p], axis=0)
            weights.append((r, places, p, shrink, l))
        results = []
        for r, places, p, shrink, l in weights:
            values = [
                jnp.concatenate([buf[place, h, 1] for place in places], axis=1)
                for h in range(heads)
            ]
            for h in range(0, heads, both):
                pair = nn(jnp.concatenate(values[h : h + both], axis=0), p)
                for w in range(both):
                    mine = pair[w * width : (w + 1) * width]
                    found = mine if h + w == 0 else jnp.where(lane_head == h + w, mine, found)
            results.append((r, ((acc_ref[kept + r] * shrink + found) / l).astype(jnp.bfloat16)))
        for r, result in results:
            out_ref[r] = nt(order, result).astype(jnp.bfloat16)
        return carry

    lax.fori_loop(0, block // unroll, body, 0)


def decode(q, acc, ml, pages, slot, meta, target, targets, part, parts, extra, steps, heads, group):
    requests, lanes, width = q.shape
    count = requests // targets // parts
    block = math.gcd(16, count)
    per_block = count // block

    def here(i, slot, meta):
        return ((lax.rem(meta[1] + target, targets) * parts + part) * per_block + i, 0, 0)

    on_chip = pl.BlockSpec(memory_space=pltpu.VMEM)
    return pl.pallas_call(
        functools.partial(
            decode_kernel,
            extra,
            steps,
            target,
            targets,
            part,
            parts,
            heads,
            group,
            LOG2E / math.sqrt(width),
        ),
        grid_spec=pltpu.PrefetchScalarGridSpec(
            num_scalar_prefetch=2,
            grid=(per_block,),
            in_specs=[pl.BlockSpec((block,) + q.shape[1:], here)] + [on_chip] * 3,
            out_specs=pl.BlockSpec((block, lanes, width), lambda i, *_: (i, 0, 0)),
        ),
        out_shape=jax.ShapeDtypeStruct((count, lanes, width), jnp.bfloat16),
        compiler_params=params(),
        cost_estimate=pl.CostEstimate(
            flops=10**6, bytes_accessed=10**6, transcendentals=0
        ),
    )(slot, meta, *in_hbm(q), acc, ml, pages)


def join_kernel(counts, steps, meta_ref, *refs):
    out_ref = refs[-1]
    k = pl.program_id(0)
    rows = refs[0].shape[1]
    targets = len(counts)
    sources = iter(refs)
    for s, count in enumerate(counts):
        parts = [next(sources) for _ in range(count)]

        @pl.when(lax.rem(meta_ref[1] + (targets - s), targets) == k)
        def _():
            for n, source in enumerate(parts):

                def body(r, carry):
                    value = source[r]
                    for g in range(rows // steps):
                        out_ref[n * source.shape[0] + r, :, g * 128 : (g + 1) * 128] = value[
                            g * steps : (g + 1) * steps
                        ]
                    return carry

                lax.fori_loop(0, source.shape[0], body, 0)


def join(pieces, meta, steps):
    flat = [a for parts in pieces for a in parts]
    rows, width = flat[0].shape[1:]
    targets = len(pieces)
    per_target = sum(a.shape[0] for a in pieces[0])
    half = rows // steps * width
    return pl.pallas_call(
        functools.partial(join_kernel, [len(parts) for parts in pieces], steps),
        grid_spec=pltpu.PrefetchScalarGridSpec(
            num_scalar_prefetch=1,
            grid=(targets,),
            in_specs=[pl.BlockSpec(a.shape, lambda k, *_: (0, 0, 0)) for a in flat],
            out_specs=pl.BlockSpec((per_target, steps, half), lambda k, *_: (0, 0, k)),
        ),
        out_shape=jax.ShapeDtypeStruct((per_target, steps, half * targets), jnp.bfloat16),
        compiler_params=params(),
        cost_estimate=pl.CostEstimate(flops=0, bytes_accessed=2 * 10**6, transcendentals=0),
    )(meta, *flat)


def ring_place(index, size):
    return jnp.where(index % 2 == 0, index // 2, size - 1 - index // 2)


def shards(
    roles,
    ring,
    targets,
    prefill_q,
    prefill_k,
    prefill_v,
    decode_q,
    decode_k,
    decode_v,
    cache_k,
    cache_v,
    cache_len,
    page_list,
):
    tokens, q_heads = prefill_q.shape[1:3]
    heads, width = prefill_k.shape[2:]
    group = q_heads // heads
    own_pages = tokens // PAGE
    requests, steps = decode_q.shape[:2]
    extra = page_list.shape[1]
    role = lax.axis_index("role")
    ctx = lax.axis_index("ctx")
    tp = lax.axis_index("tp")

    order = list(range(0, ring, 2)) + list(range(ring - 1, 0, -2))
    along = [(order[j], order[(j + 1) % ring]) for j in range(ring)]
    flips = [1 << b for b in reversed(range(roles.bit_length() - 1))]

    owner = page_list // own_pages
    place = (ring_place(ctx, ring) - ring_place(owner % ring, ring)) % ring
    slot = ((owner // ring) ^ role) * ring + place
    hot = slot.reshape(-1, 1) == jnp.arange(roles * ring)[None, :]
    pick = jnp.max(jnp.where(hot, (page_list % own_pages).reshape(-1, 1), 0), axis=0)
    meta = jnp.stack([ctx, tp]).astype(jnp.int32)
    scalars = (
        slot.reshape(-1).astype(jnp.int32),
        pick.astype(jnp.int32),
        meta,
    )
    position = jnp.arange(ring)
    where = ring_place(ctx, ring)
    source = (where - position) % ring
    source_ctx = jnp.where(source < (ring + 1) // 2, 2 * source, 2 * (ring - 1 - source) + 1)
    needed = (source_ctx < ctx).astype(jnp.int32)

    raw = [
        a.reshape(requests, -1, width) for a in (decode_q, decode_k, decode_v, cache_k, cache_v)
    ]

    def cache(target):
        lens = cache_len.astype(jnp.int32)
        return cache_part(*raw, lens, meta, target, targets, steps, heads, group)

    gathered = {(0, 0): split_heads(prefill_k, prefill_v)}
    fresh = [(0, 0)]
    for k in range(ring + len(flips) - 1):
        sends = []
        for code, s in fresh:
            for flip in reversed(flips):
                if code == 0 or flip < code & -code:
                    pairs = [(j, j ^ flip) for j in range(roles)]
                    sends.append((flip, (code, s), (code ^ flip, s), "role", pairs))
            if code == 0 and s + 1 < ring:
                sends.append((roles, (code, s), (0, s + 1), "ctx", along))
        sends.sort(key=lambda a: a[0])
        names = [to for _, _, to, _, _ in sends]
        arrived = [lax.ppermute(gathered[of], axis, pairs) for _, of, _, axis, pairs in sends]
        beside = ()
        if k == 0:
            beside = cache(targets - 1)
        if k == 1:
            beside = scalars, {s: cache(s) for s in range(targets - 1)}
        if k == ring - 2:
            slots = tuple(range(1, ring - 1))
            mine = [gathered[0, s] for s in slots]
            beside = prefill(prefill_q, mine, slots, needed, None)
        if k == ring - 1:
            slots = (0, ring - 1)
            mine = [gathered[0, s] for s in slots]
            beside = prefill(prefill_q, mine, slots, needed, state)
        arrived, beside = lax.optimization_barrier((arrived, beside))
        if k == 0:
            cached = {targets - 1: beside}
        if k == 1:
            scalars, others = beside
            cached.update(others)
        if k == ring - 2:
            state = beside
        if k == ring - 1:
            prefill_out = beside
        gathered.update(zip(names, arrived))
        fresh = names

    blocks = [gathered[r, s] for r in range(roles) for s in range(ring)]
    slot, pick, meta = scalars
    pages = collect(pick, blocks)
    pieces = [None] * targets
    for s in reversed(range(targets)):
        parts = math.gcd(2, requests // targets)
        pieces[s] = []
        for part in range(parts):
            if s == 0 and part == parts - 1 and targets > 1:
                sent = [p[0] for p in pieces[1:]]
                cached[0], sent = lax.optimization_barrier((cached[0], sent))
                for p, a in zip(pieces[1:], sent):
                    p[0] = a
            out = decode(
                raw[0], *cached[s], pages, slot, meta, s, targets, part, parts, extra, steps, heads, group
            )
            if s:
                shift = [(j, (j + s) % targets) for j in range(targets)]
                out = lax.ppermute(out, "tp", shift)
            pieces[s].append(out)
    decode_out = join(pieces, meta, steps)
    return (prefill_out, decode_out)


def solution(mesh):
    body = functools.partial(shards, mesh.shape["role"], mesh.shape["ctx"], mesh.shape["tp"])
    return jax.shard_map(
        body,
        mesh=mesh,
        in_specs=(
            P("role", "ctx", "tp", None),
            P("role", "ctx", "tp", None),
            P("role", "ctx", "tp", None),
            P(("role", "ctx"), None, "tp", None),
            P(("role", "ctx"), None, "tp", None),
            P(("role", "ctx"), None, "tp", None),
            P(("role", "ctx"), None, "tp", None),
            P(("role", "ctx"), None, "tp", None),
            P(("role", "ctx")),
            P(("role", "ctx"), None),
        ),
        out_specs=(P("role", "ctx", "tp", None), P(("role", "ctx", "tp"), None, None)),
        check_vma=False,
    )
```

```python
import functools
import math

import jax
import jax.numpy as jnp
from jax import lax
from jax.experimental import pallas as pl
from jax.experimental.pallas import tpu as pltpu
from jax.sharding import PartitionSpec as P

PAGE = 128
LOG2E = 1.4426950408889634
NEG = -1e30
VMEM_LIMIT = 16 * 1024 * 1024


def nt(a, b):
    return lax.dot_general(a, b, (((1,), (1,)), ((), ())), preferred_element_type=jnp.float32)


def nn(a, b):
    return jnp.dot(a, b, preferred_element_type=jnp.float32)


def in_hbm(*arrays):
    return [pltpu.with_memory_space_constraint(a, pltpu.HBM) for a in arrays]


def params():
    return pltpu.CompilerParams(vmem_limit_bytes=VMEM_LIMIT)


def one_hot(out_rows, in_rows, source):
    row = lax.broadcasted_iota(jnp.int32, (out_rows, in_rows), 0)
    col = lax.broadcasted_iota(jnp.int32, (out_rows, in_rows), 1)
    return jnp.where(col == source(row), 1.0, 0.0).astype(jnp.bfloat16)


def split_kernel(heads, tokens, k_ref, v_ref, out_ref):
    rows = min(tokens * heads, 256)
    step = rows // heads
    pick = one_hot(rows, rows, lambda i: (i % step) * heads + i // step)
    moved, kept = [], []
    for j in range(tokens // step):
        keys = nn(pick, k_ref[pl.ds(j * rows, rows), :]).astype(jnp.bfloat16)
        moved.append(nn(pick, v_ref[pl.ds(j * rows, rows), :]))
        kept.append(keys)
    for h in range(heads):
        keys = jnp.concatenate([a[h * step : (h + 1) * step] for a in kept], axis=0)
        values = jnp.concatenate([a[h * step : (h + 1) * step] for a in moved], axis=0)
        for page in range(tokens // PAGE):
            out_ref[page, h, 0] = keys[page * PAGE : (page + 1) * PAGE]
            out_ref[page, h, 1] = values[page * PAGE : (page + 1) * PAGE].T.astype(jnp.bfloat16)


def split_heads(k, v):
    _, tokens, heads, width = k.shape
    return pl.pallas_call(
        functools.partial(split_kernel, heads, tokens),
        out_specs=pl.BlockSpec(memory_space=pltpu.VMEM),
        out_shape=pltpu.VMEM((tokens // PAGE, heads, 2, PAGE, width), jnp.bfloat16),
        compiler_params=params(),
        cost_estimate=pl.CostEstimate(flops=10**8, bytes_accessed=2 * 10**6, transcendentals=0),
    )(*in_hbm(k.reshape(tokens * heads, width), v.reshape(tokens * heads, width)))


def prefill_kernel(own, count, slots, group, tokens, scale, needed_ref, *refs):
    q_ref = refs[0]
    blocks = refs[1 : 1 + count]
    refs = refs[1 + count :]
    i = pl.program_id(0)
    if own:
        old_acc_ref, old_m_ref, old_l_ref, out_ref, buf, s_ref, acc_ref, m_ref, l_ref, sems = refs
    else:
        acc_ref, m_ref, l_ref, buf, s_ref, sems = refs
        acc_ref, m_ref, l_ref = acc_ref.at[i], m_ref.at[i], l_ref.at[i]
    pages, heads = blocks[0].shape[:2]
    block = q_ref.shape[1]
    rest = range(1 if own else 0, count)
    total = sum(needed_ref[slots[c]] for c in rest)

    def copies():
        found = []
        place = jnp.int32(0)
        for c in rest:
            flag = needed_ref[slots[c]]
            found.append((flag, pltpu.make_async_copy(blocks[c], buf.at[place], sems.at[c])))
            place = place + flag
        return found

    @pl.when(i == 0)
    def _():
        for flag, copy in copies():
            @pl.when(flag == 1)
            def _():
                copy.start()

    rows = block * group
    piece = min(rows, 256)
    parts = [(h, pl.ds(c, piece)) for h in range(heads) for c in range(0, rows, piece)]
    queries = q_ref[0].astype(jnp.float32)
    q = [
        queries[:, h * group : (h + 1) * group, :].reshape(rows, -1).astype(jnp.bfloat16)
        for h in range(heads)
    ]
    q = [q[h][c : c + piece] for h in range(heads) for c in range(0, rows, piece)]

    def fold(a, op):
        return functools.reduce(op, [a[:, j * 128 : (j + 1) * 128] for j in range(a.shape[1] // 128)])

    def keys(ref, h):
        return jnp.concatenate([ref[j, h, 0] for j in range(pages)], axis=0)

    def values(ref, h):
        return jnp.concatenate([ref[j, h, 1] for j in range(pages)], axis=1)

    def weights(place, h, at, m):
        return [
            jnp.exp2((s_ref[place, h, at, pl.ds(j * 128, 128)] - m) * scale)
            for j in range(tokens // 128)
        ]

    last = count - 1
    if own:
        m_ref[...] = old_m_ref[i]
        for j in range(pages):
            @pl.when((i + 1) * block > j * PAGE)
            def _():
                for n, (h, at) in enumerate(parts):
                    row = lax.broadcasted_iota(jnp.int32, (piece, PAGE), 0) + n * piece % rows
                    column = lax.broadcasted_iota(jnp.int32, (piece, PAGE), 1) + j * PAGE
                    s = nt(q[n], blocks[0][j, h, 0])
                    s = jnp.where(column <= row // group + i * block, s, NEG)
                    s_ref[last, h, at, pl.ds(j * PAGE, PAGE)] = s
                    m_ref[h, at] = jnp.maximum(m_ref[h, at], s)
    else:
        m_ref[...] = jnp.full(m_ref.shape, NEG, jnp.float32)

    @pl.when(i == 0)
    def _():
        for flag, copy in copies():
            @pl.when(flag == 1)
            def _():
                copy.wait()

    def look(b, carry):
        for n, (h, at) in enumerate(parts):
            s = nt(q[n], keys(buf.at[b], h))
            s_ref[b, h, at] = s
            m_ref[h, at] = jnp.maximum(m_ref[h, at], fold(s, jnp.maximum))
        return carry

    lax.fori_loop(0, total, look, 0)
    for h, at in parts:
        m = m_ref[h, at]
        m = jnp.broadcast_to(jnp.max(m, axis=1, keepdims=True), m.shape)
        m_ref[h, at] = m
        if own:
            share = jnp.exp2((old_m_ref[i, h, at] - m) * scale)
            l_ref[h, at] = old_l_ref[i, h, at] * share
            acc_ref[h, at] = old_acc_ref[i, h, at] * share
        else:
            l_ref[h, at] = jnp.zeros(m.shape, jnp.float32)
            acc_ref[h, at] = jnp.zeros(m.shape, jnp.float32)
    if own:
        for j in range(pages):
            @pl.when((i + 1) * block > j * PAGE)
            def _():
                for h, at in parts:
                    p = s_ref[last, h, at, pl.ds(j * PAGE, PAGE)]
                    p = jnp.exp2((p - m_ref[h, at]) * scale)
                    l_ref[h, at] = l_ref[h, at] + p
                    acc_ref[h, at] = acc_ref[h, at] + nt(p.astype(jnp.bfloat16), blocks[0][j, h, 1])

    def weigh(b, carry):
        for h, at in parts:
            p = weights(b, h, at, m_ref[h, at])
            l_ref[h, at] = l_ref[h, at] + functools.reduce(jnp.add, p)
            p = jnp.concatenate([a.astype(jnp.bfloat16) for a in p], axis=1)
            acc_ref[h, at] = acc_ref[h, at] + nt(p, values(buf.at[b], h))
        return carry

    lax.fori_loop(0, total, weigh, 0)
    if own:
        out = []
        for h in range(heads):
            l = jnp.sum(l_ref[h], axis=1, keepdims=True)
            out.append((acc_ref[h] / l).reshape(block, group, -1))
        out_ref[0] = jnp.concatenate(out, axis=1).astype(out_ref.dtype)


def prefill(q, blocks, slots, needed, state):
    _, tokens, q_heads, width = q.shape
    own = state is not None
    count = len(blocks)
    heads = blocks[0].shape[1]
    group = q_heads // heads
    block = 64
    rows = block * group
    q_spec = pl.BlockSpec((1, block, q_heads, width), lambda i, *_: (0, i, 0, 0))
    own_spec = pl.BlockSpec(blocks[0].shape, lambda i, *_: (0, 0, 0, 0, 0))
    any_spec = pl.BlockSpec(memory_space=pl.ANY)
    on_chip = pl.BlockSpec(memory_space=pltpu.VMEM)
    scratch = [
        pltpu.VMEM((count,) + blocks[0].shape, jnp.bfloat16),
        pltpu.VMEM((count, heads, rows, tokens), jnp.float32),
    ]
    if own:
        in_specs = [q_spec, own_spec] + [any_spec] * (count - 1) + [on_chip] * 3
        out_specs, out_shape = q_spec, jax.ShapeDtypeStruct(q.shape, jnp.bfloat16)
        scratch += [pltpu.VMEM((heads, rows, width), jnp.float32)] * 3
    else:
        in_specs = [q_spec] + [any_spec] * count
        out_specs, state = [on_chip] * 3, ()
        out_shape = [pltpu.VMEM((tokens // block, heads, rows, width), jnp.float32)] * 3
    return pl.pallas_call(
        functools.partial(
            prefill_kernel, own, count, slots, group, tokens, LOG2E / math.sqrt(width)
        ),
        grid_spec=pltpu.PrefetchScalarGridSpec(
            num_scalar_prefetch=1,
            grid=(tokens // block,),
            in_specs=in_specs,
            out_specs=out_specs,
            scratch_shapes=scratch + [pltpu.SemaphoreType.DMA((count,))],
        ),
        out_shape=out_shape,
        compiler_params=params(),
        cost_estimate=pl.CostEstimate(
            flops=16 * q_heads * tokens * tokens * count * width,
            bytes_accessed=12 * 10**6,
            transcendentals=tokens * tokens * count * q_heads,
        ),
    )(needed, *in_hbm(q), *blocks, *state)


def cache_kernel(
    steps, heads, group, target, targets, scale, len_ref, meta_ref, *refs
):
    q_ref, dk_ref, dv_ref, ck_ref, cv_ref, acc_ref, ml_ref = refs
    block, rows, width = q_ref.shape
    cache = ck_ref.shape[1]
    new = dk_ref.shape[1]
    per_step = heads * group

    def mask(columns):
        row = lax.broadcasted_iota(jnp.int32, (rows, columns), 0)
        column = lax.broadcasted_iota(jnp.int32, (rows, columns), 1)
        same = column % heads == row % per_step // group
        return jnp.where(same, column // heads, 1 << 20), row // per_step

    piece = min(cache, 128)
    pieces = range(0, cache, piece)
    place, _ = mask(piece)
    new_place, step = mask(new)
    new_allowed = new_place <= step
    low = lax.broadcasted_iota(jnp.int32, (rows, width), 1) < 4
    i = pl.program_id(0)
    first = (lax.rem(meta_ref[1] + target, targets) * pl.num_programs(0) + i) * block
    unroll = math.gcd(4, block)

    def body(g, carry):
        scores = []
        for u in range(unroll):
            r = g * unroll + u
            q = q_ref[r]
            length = len_ref[first + r]
            old = [
                jnp.where(
                    place < length - c // heads, nt(q, ck_ref[r, pl.ds(c, piece), :]), NEG
                )
                for c in pieces
            ]
            add = jnp.where(new_allowed, nt(q, dk_ref[r]), NEG)
            scores.append((r, old, add))
        weights = []
        for r, old, add in scores:
            top = functools.reduce(jnp.maximum, old)
            m = jnp.maximum(
                jnp.max(top, axis=1, keepdims=True), jnp.max(add, axis=1, keepdims=True)
            )
            old = [jnp.exp2((a - m) * scale) for a in old]
            add = jnp.exp2((add - m) * scale)
            l = jnp.sum(functools.reduce(jnp.add, old), axis=1, keepdims=True)
            l = l + jnp.sum(add, axis=1, keepdims=True)
            ml_ref[i * block + r] = jnp.where(low, m, l).T[:8]
            weights.append((r, [a.astype(jnp.bfloat16) for a in old], add.astype(jnp.bfloat16)))
        for r, old, add in weights:
            acc = nn(add, dv_ref[r])
            for c, p in zip(pieces, old):
                acc = acc + nn(p, cv_ref[r, pl.ds(c, piece), :])
            acc_ref[i * block + r] = acc.T
        return carry

    lax.fori_loop(0, block // unroll, body, 0)


def cache_part(q, dk, dv, ck, cv, lens, meta, target, targets, steps, heads, group):
    requests, rows, width = q.shape
    per_target = requests // targets
    block = math.gcd(8, per_target)
    per_block = per_target // block

    def here(i, lens, meta):
        return (lax.rem(meta[1] + target, targets) * per_block + i, 0, 0)

    spec = [pl.BlockSpec((block,) + a.shape[1:], here) for a in (q, dk, dv, ck, cv)]
    shapes = [(per_target, width, rows), (per_target, 8, rows)]
    return pl.pallas_call(
        functools.partial(
            cache_kernel, steps, heads, group, target, targets, LOG2E / math.sqrt(width)
        ),
        grid_spec=pltpu.PrefetchScalarGridSpec(
            num_scalar_prefetch=2,
            grid=(per_block,),
            in_specs=spec,
            out_specs=[pl.BlockSpec(memory_space=pltpu.VMEM)] * 2,
        ),
        out_shape=[pltpu.VMEM(a, jnp.float32) for a in shapes],
        compiler_params=params(),
        cost_estimate=pl.CostEstimate(
            flops=per_target * rows * ck.shape[1] * width * 16,
            bytes_accessed=7 * 10**6,
            transcendentals=per_target * rows * ck.shape[1],
        ),
    )(lens, meta, *in_hbm(q, dk, dv, ck, cv))


def collect_kernel(pick_ref, q_ref, *refs):
    blocks, (out_ref, q_out_ref, sems) = refs[:-3], refs[-3:]
    copies = [
        pltpu.make_async_copy(block.at[pick_ref[s]], out_ref.at[s], sems.at[s])
        for s, block in enumerate(blocks)
    ]
    copies.append(pltpu.make_async_copy(q_ref, q_out_ref, sems.at[len(blocks)]))
    for copy in copies:
        copy.start()
    for copy in copies:
        copy.wait()


def collect(pick, q, blocks):
    slots = len(blocks)
    return pl.pallas_call(
        collect_kernel,
        grid_spec=pltpu.PrefetchScalarGridSpec(
            num_scalar_prefetch=1,
            grid=(1,),
            in_specs=[pl.BlockSpec(memory_space=pl.ANY)] * (1 + slots),
            out_specs=[pl.BlockSpec(memory_space=pltpu.VMEM)] * 2,
            scratch_shapes=[pltpu.SemaphoreType.DMA((slots + 1,))],
        ),
        out_shape=[
            pltpu.VMEM((slots,) + blocks[0].shape[1:], jnp.bfloat16),
            pltpu.VMEM(q.shape, jnp.bfloat16),
        ],
        compiler_params=params(),
        cost_estimate=pl.CostEstimate(flops=0, bytes_accessed=8 * 10**6, transcendentals=0),
    )(pick, *in_hbm(q), *blocks)


def decode_kernel(
    extra, steps, target, targets, part, parts, heads, group, block, scale, slot_ref, meta_ref, *refs
):
    q_ref, acc_ref, ml_ref, buf, out_ref = refs
    lanes, width = q_ref.shape[1:]
    i = pl.program_id(0)
    kept = (part * pl.num_programs(0) + i) * block
    first = lax.rem(meta_ref[1] + target, targets) * (parts * pl.num_programs(0) * block) + kept

    per_step = heads * group
    row_head = lax.broadcasted_iota(jnp.int32, (lanes, width), 0) % per_step // group
    head_rows = [jnp.where(row_head == h, 1.0, 0.0).astype(jnp.bfloat16) for h in range(heads)]
    lane_head = lax.broadcasted_iota(jnp.int32, (width, lanes), 1) % per_step // group
    order = one_hot(lanes, lanes, lambda r: r % steps * per_step + r // steps)
    unroll = math.gcd(8, block)
    both = math.gcd(2 if target else 1, heads)

    def body(g, carry):
        scores = []
        for u in range(unroll):
            r = g * unroll + u
            q = q_ref[first + r]
            places = [slot_ref[(first + r) * extra + j] for j in range(extra)]
            spread = jnp.concatenate([q * a for a in head_rows], axis=1)
            keys = [
                jnp.concatenate([buf[place, h, 0] for h in range(heads)], axis=1)
                for place in places
            ]
            s = []
            for j in range(0, extra, both):
                pair = jnp.concatenate(keys[j : j + both], axis=0)
                s.append(nt(pair, spread))
            scores.append((r, places, s))
        weights = []
        for r, places, s in scores:
            old = ml_ref[kept + r, 0:1]
            m = jnp.max(functools.reduce(jnp.maximum, s), axis=0, keepdims=True)
            m = jnp.maximum(m, old)
            p = [jnp.exp2((a - m) * scale) for a in s]
            shrink = jnp.exp2((old - m) * scale)
            l = jnp.sum(functools.reduce(jnp.add, p), axis=0, keepdims=True)
            l = ml_ref[kept + r, 4:5] * shrink + l
            p = jnp.concatenate([a.astype(jnp.bfloat16) for a in p], axis=0)
            weights.append((r, places, p, shrink, l))
        results = []
        for r, places, p, shrink, l in weights:
            values = [
                jnp.concatenate([buf[place, h, 1] for place in places], axis=1)
                for h in range(heads)
            ]
            for h in range(0, heads, both):
                pair = nn(jnp.concatenate(values[h : h + both], axis=0), p)
                for w in range(both):
                    mine = pair[w * width : (w + 1) * width]
                    found = mine if h + w == 0 else jnp.where(lane_head == h + w, mine, found)
            results.append((r, ((acc_ref[kept + r] * shrink + found) / l).astype(jnp.bfloat16)))
        for r, result in results:
            out_ref[i * block + r] = nt(order, result).astype(jnp.bfloat16)
        return carry

    lax.fori_loop(0, block // unroll, body, 0)


def decode(q, acc, ml, pages, slot, meta, target, targets, part, parts, extra, steps, heads, group):
    requests, lanes, width = q.shape
    count = requests // targets // parts
    block = math.gcd(16, count)
    per_block = count // block

    on_chip = pl.BlockSpec(memory_space=pltpu.VMEM)
    return pl.pallas_call(
        functools.partial(
            decode_kernel,
            extra,
            steps,
            target,
            targets,
            part,
            parts,
            heads,
            group,
            block,
            LOG2E / math.sqrt(width),
        ),
        grid_spec=pltpu.PrefetchScalarGridSpec(
            num_scalar_prefetch=2,
            grid=(per_block,),
            in_specs=[on_chip] * 4,
            out_specs=on_chip,
        ),
        out_shape=pltpu.VMEM((count, lanes, width), jnp.bfloat16),
        compiler_params=params(),
        cost_estimate=pl.CostEstimate(
            flops=10**6, bytes_accessed=10**6, transcendentals=0
        ),
    )(slot, meta, q, acc, ml, pages)


def join_kernel(counts, steps, meta_ref, *refs):
    out_ref = refs[-1]
    k = pl.program_id(0)
    rows = refs[0].shape[1]
    targets = len(counts)
    sources = iter(refs)
    for s, count in enumerate(counts):
        parts = [next(sources) for _ in range(count)]

        @pl.when(lax.rem(meta_ref[1] + (targets - s), targets) == k)
        def _():
            for n, source in enumerate(parts):

                def body(r, carry):
                    value = source[r]
                    for g in range(rows // steps):
                        out_ref[n * source.shape[0] + r, :, g * 128 : (g + 1) * 128] = value[
                            g * steps : (g + 1) * steps
                        ]
                    return carry

                lax.fori_loop(0, source.shape[0], body, 0)


def join(pieces, meta, steps):
    flat = [a for parts in pieces for a in parts]
    rows, width = flat[0].shape[1:]
    targets = len(pieces)
    per_target = sum(a.shape[0] for a in pieces[0])
    half = rows // steps * width
    return pl.pallas_call(
        functools.partial(join_kernel, [len(parts) for parts in pieces], steps),
        grid_spec=pltpu.PrefetchScalarGridSpec(
            num_scalar_prefetch=1,
            grid=(targets,),
            in_specs=[pl.BlockSpec(memory_space=pltpu.VMEM)] * len(flat),
            out_specs=pl.BlockSpec((per_target, steps, half), lambda k, *_: (0, 0, k)),
        ),
        out_shape=jax.ShapeDtypeStruct((per_target, steps, half * targets), jnp.bfloat16),
        compiler_params=params(),
        cost_estimate=pl.CostEstimate(flops=0, bytes_accessed=2 * 10**6, transcendentals=0),
    )(meta, *flat)


def ring_place(index, size):
    return jnp.where(index % 2 == 0, index // 2, size - 1 - index // 2)


def shards(
    roles,
    ring,
    targets,
    prefill_q,
    prefill_k,
    prefill_v,
    decode_q,
    decode_k,
    decode_v,
    cache_k,
    cache_v,
    cache_len,
    page_list,
):
    tokens, q_heads = prefill_q.shape[1:3]
    heads, width = prefill_k.shape[2:]
    group = q_heads // heads
    own_pages = tokens // PAGE
    requests, steps = decode_q.shape[:2]
    extra = page_list.shape[1]
    role = lax.axis_index("role")
    ctx = lax.axis_index("ctx")
    tp = lax.axis_index("tp")

    order = list(range(0, ring, 2)) + list(range(ring - 1, 0, -2))
    along = [(order[j], order[(j + 1) % ring]) for j in range(ring)]
    flips = [1 << b for b in reversed(range(roles.bit_length() - 1))]

    owner = page_list // own_pages
    place = (ring_place(ctx, ring) - ring_place(owner % ring, ring)) % ring
    slot = ((owner // ring) ^ role) * ring + place
    hot = slot.reshape(-1, 1) == jnp.arange(roles * ring)[None, :]
    pick = jnp.max(jnp.where(hot, (page_list % own_pages).reshape(-1, 1), 0), axis=0)
    meta = jnp.stack([ctx, tp]).astype(jnp.int32)
    scalars = (
        slot.reshape(-1).astype(jnp.int32),
        pick.astype(jnp.int32),
        meta,
    )
    position = jnp.arange(ring)
    where = ring_place(ctx, ring)
    source = (where - position) % ring
    source_ctx = jnp.where(source < (ring + 1) // 2, 2 * source, 2 * (ring - 1 - source) + 1)
    needed = (source_ctx < ctx).astype(jnp.int32)

    raw = [
        a.reshape(requests, -1, width) for a in (decode_q, decode_k, decode_v, cache_k, cache_v)
    ]

    def cache(target):
        lens = cache_len.astype(jnp.int32)
        return cache_part(*raw, lens, meta, target, targets, steps, heads, group)

    gathered = {(0, 0): split_heads(prefill_k, prefill_v)}
    fresh = [(0, 0)]
    for k in range(ring + len(flips) - 1):
        sends = []
        for code, s in fresh:
            for flip in reversed(flips):
                if code == 0 or flip < code & -code:
                    pairs = [(j, j ^ flip) for j in range(roles)]
                    sends.append((flip, (code, s), (code ^ flip, s), "role", pairs))
            if code == 0 and s + 1 < ring:
                sends.append((roles, (code, s), (0, s + 1), "ctx", along))
        sends.sort(key=lambda a: a[0])
        names = [to for _, _, to, _, _ in sends]
        arrived = [lax.ppermute(gathered[of], axis, pairs) for _, of, _, axis, pairs in sends]
        beside = ()
        if k == 0:
            beside = cache(targets - 1)
        if k == 1:
            beside = scalars, {s: cache(s) for s in range(targets - 1)}
        if k == ring - 2:
            slots = tuple(range(1, ring - 1))
            mine = [gathered[0, s] for s in slots]
            beside = prefill(prefill_q, mine, slots, needed, None)
        if k == ring - 1:
            slots = (0, ring - 1)
            mine = [gathered[0, s] for s in slots]
            beside = prefill(prefill_q, mine, slots, needed, state)
        arrived, beside = lax.optimization_barrier((arrived, beside))
        if k == 0:
            cached = {targets - 1: beside}
        if k == 1:
            scalars, others = beside
            cached.update(others)
        if k == ring - 2:
            state = beside
        if k == ring - 1:
            prefill_out = beside
        gathered.update(zip(names, arrived))
        fresh = names

    blocks = [gathered[r, s] for r in range(roles) for s in range(ring)]
    slot, pick, meta = scalars
    pages, queries = collect(pick, raw[0], blocks)
    pieces = [None] * targets
    for s in reversed(range(targets)):
        parts = math.gcd(2, requests // targets)
        pieces[s] = []
        for part in range(parts):
            if s == 0 and part == parts - 1 and targets > 1:
                sent = [p[0] for p in pieces[1:]]
                cached[0], sent = lax.optimization_barrier((cached[0], sent))
                for p, a in zip(pieces[1:], sent):
                    p[0] = a
            out = decode(
                queries, *cached[s], pages, slot, meta, s, targets, part, parts, extra, steps, heads, group
            )
            if s:
                shift = [(j, (j + s) % targets) for j in range(targets)]
                out = lax.ppermute(out, "tp", shift)
            pieces[s].append(out)
    decode_out = join(pieces, meta, steps)
    return (prefill_out, decode_out)


def solution(mesh):
    body = functools.partial(shards, mesh.shape["role"], mesh.shape["ctx"], mesh.shape["tp"])
    return jax.shard_map(
        body,
        mesh=mesh,
        in_specs=(
            P("role", "ctx", "tp", None),
            P("role", "ctx", "tp", None),
            P("role", "ctx", "tp", None),
            P(("role", "ctx"), None, "tp", None),
            P(("role", "ctx"), None, "tp", None),
            P(("role", "ctx"), None, "tp", None),
            P(("role", "ctx"), None, "tp", None),
            P(("role", "ctx"), None, "tp", None),
            P(("role", "ctx")),
            P(("role", "ctx"), None),
        ),
        out_specs=(P("role", "ctx", "tp", None), P(("role", "ctx", "tp"), None, None)),
        check_vma=False,
    )
```

```python
import functools
import math

import jax
import jax.numpy as jnp
from jax import lax
from jax.experimental import pallas as pl
from jax.experimental.pallas import tpu as pltpu
from jax.sharding import PartitionSpec as P

PAGE = 128
LOG2E = 1.4426950408889634
NEG = -1e30
VMEM_LIMIT = 16 * 1024 * 1024


def nt(a, b):
    return lax.dot_general(a, b, (((1,), (1,)), ((), ())), preferred_element_type=jnp.float32)


def nn(a, b):
    return jnp.dot(a, b, preferred_element_type=jnp.float32)


def in_hbm(*arrays):
    return [pltpu.with_memory_space_constraint(a, pltpu.HBM) for a in arrays]


def params():
    return pltpu.CompilerParams(vmem_limit_bytes=VMEM_LIMIT)


def one_hot(out_rows, in_rows, source):
    row = lax.broadcasted_iota(jnp.int32, (out_rows, in_rows), 0)
    col = lax.broadcasted_iota(jnp.int32, (out_rows, in_rows), 1)
    return jnp.where(col == source(row), 1.0, 0.0).astype(jnp.bfloat16)


def split_kernel(heads, tokens, k_ref, v_ref, out_ref):
    rows = min(tokens * heads, 256)
    step = rows // heads
    pick = one_hot(rows, rows, lambda i: (i % step) * heads + i // step)
    moved, kept = [], []
    for j in range(tokens // step):
        keys = nn(pick, k_ref[pl.ds(j * rows, rows), :]).astype(jnp.bfloat16)
        moved.append(nn(pick, v_ref[pl.ds(j * rows, rows), :]))
        kept.append(keys)
    for h in range(heads):
        keys = jnp.concatenate([a[h * step : (h + 1) * step] for a in kept], axis=0)
        values = jnp.concatenate([a[h * step : (h + 1) * step] for a in moved], axis=0)
        for page in range(tokens // PAGE):
            out_ref[page, h, 0] = keys[page * PAGE : (page + 1) * PAGE]
            out_ref[page, h, 1] = values[page * PAGE : (page + 1) * PAGE].T.astype(jnp.bfloat16)


def split_heads(k, v):
    _, tokens, heads, width = k.shape
    return pl.pallas_call(
        functools.partial(split_kernel, heads, tokens),
        out_specs=pl.BlockSpec(memory_space=pltpu.VMEM),
        out_shape=pltpu.VMEM((tokens // PAGE, heads, 2, PAGE, width), jnp.bfloat16),
        compiler_params=params(),
        cost_estimate=pl.CostEstimate(flops=10**8, bytes_accessed=2 * 10**6, transcendentals=0),
    )(*in_hbm(k.reshape(tokens * heads, width), v.reshape(tokens * heads, width)))


def prefill_kernel(own, count, slots, group, tokens, scale, needed_ref, *refs):
    q_ref = refs[0]
    blocks = refs[1 : 1 + count]
    refs = refs[1 + count :]
    i = pl.program_id(0)
    if own:
        old_acc_ref, old_m_ref, old_l_ref, out_ref, buf, s_ref, acc_ref, m_ref, l_ref, sems = refs
    else:
        acc_ref, m_ref, l_ref, buf, s_ref, sems = refs
        acc_ref, m_ref, l_ref = acc_ref.at[i], m_ref.at[i], l_ref.at[i]
    pages, heads = blocks[0].shape[:2]
    block = q_ref.shape[1]
    rest = range(1 if own else 0, count)
    total = sum(needed_ref[slots[c]] for c in rest)

    def copies():
        found = []
        place = jnp.int32(0)
        for c in rest:
            flag = needed_ref[slots[c]]
            found.append((flag, pltpu.make_async_copy(blocks[c], buf.at[place], sems.at[c])))
            place = place + flag
        return found

    @pl.when(i == 0)
    def _():
        for flag, copy in copies():
            @pl.when(flag == 1)
            def _():
                copy.start()

    rows = block * group
    piece = min(rows, 256)
    parts = [(h, pl.ds(c, piece)) for h in range(heads) for c in range(0, rows, piece)]
    queries = q_ref[0].astype(jnp.float32)
    q = [
        queries[:, h * group : (h + 1) * group, :].reshape(rows, -1).astype(jnp.bfloat16)
        for h in range(heads)
    ]
    q = [q[h][c : c + piece] for h in range(heads) for c in range(0, rows, piece)]

    def fold(a, op):
        return functools.reduce(op, [a[:, j * 128 : (j + 1) * 128] for j in range(a.shape[1] // 128)])

    def keys(ref, h):
        return jnp.concatenate([ref[j, h, 0] for j in range(pages)], axis=0)

    def values(ref, h):
        return jnp.concatenate([ref[j, h, 1] for j in range(pages)], axis=1)

    def weights(place, h, at, m):
        return [
            jnp.exp2((s_ref[place, h, at, pl.ds(j * 128, 128)] - m) * scale)
            for j in range(tokens // 128)
        ]

    last = count - 1
    if own:
        m_ref[...] = old_m_ref[i]
        for j in range(pages):
            @pl.when((i + 1) * block > j * PAGE)
            def _():
                for n, (h, at) in enumerate(parts):
                    row = lax.broadcasted_iota(jnp.int32, (piece, PAGE), 0) + n * piece % rows
                    column = lax.broadcasted_iota(jnp.int32, (piece, PAGE), 1) + j * PAGE
                    s = nt(q[n], blocks[0][j, h, 0])
                    s = jnp.where(column <= row // group + i * block, s, NEG)
                    s_ref[last, h, at, pl.ds(j * PAGE, PAGE)] = s
                    m_ref[h, at] = jnp.maximum(m_ref[h, at], s)
    else:
        m_ref[...] = jnp.full(m_ref.shape, NEG, jnp.float32)

    @pl.when(i == 0)
    def _():
        for flag, copy in copies():
            @pl.when(flag == 1)
            def _():
                copy.wait()

    def look(b, carry):
        for n, (h, at) in enumerate(parts):
            s = nt(q[n], keys(buf.at[b], h))
            s_ref[b, h, at] = s
            m_ref[h, at] = jnp.maximum(m_ref[h, at], fold(s, jnp.maximum))
        return carry

    lax.fori_loop(0, total, look, 0)
    for h, at in parts:
        m = m_ref[h, at]
        m = jnp.broadcast_to(jnp.max(m, axis=1, keepdims=True), m.shape)
        m_ref[h, at] = m
        if own:
            share = jnp.exp2((old_m_ref[i, h, at] - m) * scale)
            l_ref[h, at] = old_l_ref[i, h, at] * share
            acc_ref[h, at] = old_acc_ref[i, h, at] * share
        else:
            l_ref[h, at] = jnp.zeros(m.shape, jnp.float32)
            acc_ref[h, at] = jnp.zeros(m.shape, jnp.float32)
    if own:
        for j in range(pages):
            @pl.when((i + 1) * block > j * PAGE)
            def _():
                for h, at in parts:
                    p = s_ref[last, h, at, pl.ds(j * PAGE, PAGE)]
                    p = jnp.exp2((p - m_ref[h, at]) * scale)
                    l_ref[h, at] = l_ref[h, at] + p
                    acc_ref[h, at] = acc_ref[h, at] + nt(p.astype(jnp.bfloat16), blocks[0][j, h, 1])

    def weigh(b, carry):
        for h, at in parts:
            p = weights(b, h, at, m_ref[h, at])
            l_ref[h, at] = l_ref[h, at] + functools.reduce(jnp.add, p)
            p = jnp.concatenate([a.astype(jnp.bfloat16) for a in p], axis=1)
            acc_ref[h, at] = acc_ref[h, at] + nt(p, values(buf.at[b], h))
        return carry

    lax.fori_loop(0, total, weigh, 0)
    if own:
        out = []
        for h in range(heads):
            l = jnp.sum(l_ref[h], axis=1, keepdims=True)
            out.append((acc_ref[h] / l).reshape(block, group, -1))
        out_ref[0] = jnp.concatenate(out, axis=1).astype(out_ref.dtype)


def prefill(q, blocks, slots, needed, state):
    _, tokens, q_heads, width = q.shape
    own = state is not None
    count = len(blocks)
    heads = blocks[0].shape[1]
    group = q_heads // heads
    block = 64
    rows = block * group
    q_spec = pl.BlockSpec((1, block, q_heads, width), lambda i, *_: (0, i, 0, 0))
    own_spec = pl.BlockSpec(blocks[0].shape, lambda i, *_: (0, 0, 0, 0, 0))
    any_spec = pl.BlockSpec(memory_space=pl.ANY)
    on_chip = pl.BlockSpec(memory_space=pltpu.VMEM)
    scratch = [
        pltpu.VMEM((count,) + blocks[0].shape, jnp.bfloat16),
        pltpu.VMEM((count, heads, rows, tokens), jnp.float32),
    ]
    if own:
        in_specs = [q_spec, own_spec] + [any_spec] * (count - 1) + [on_chip] * 3
        out_specs, out_shape = q_spec, jax.ShapeDtypeStruct(q.shape, jnp.bfloat16)
        scratch += [pltpu.VMEM((heads, rows, width), jnp.float32)] * 3
    else:
        in_specs = [q_spec] + [any_spec] * count
        out_specs, state = [on_chip] * 3, ()
        out_shape = [pltpu.VMEM((tokens // block, heads, rows, width), jnp.float32)] * 3
    return pl.pallas_call(
        functools.partial(
            prefill_kernel, own, count, slots, group, tokens, LOG2E / math.sqrt(width)
        ),
        grid_spec=pltpu.PrefetchScalarGridSpec(
            num_scalar_prefetch=1,
            grid=(tokens // block,),
            in_specs=in_specs,
            out_specs=out_specs,
            scratch_shapes=scratch + [pltpu.SemaphoreType.DMA((count,))],
        ),
        out_shape=out_shape,
        compiler_params=params(),
        cost_estimate=pl.CostEstimate(
            flops=16 * q_heads * tokens * tokens * count * width,
            bytes_accessed=12 * 10**6,
            transcendentals=tokens * tokens * count * q_heads,
        ),
    )(needed, *in_hbm(q), *blocks, *state)


def cache_kernel(
    steps, heads, group, target, targets, scale, len_ref, meta_ref, *refs
):
    q_ref, dk_ref, dv_ref, ck_ref, cv_ref, acc_ref, ml_ref = refs
    block, rows, width = q_ref.shape
    cache = ck_ref.shape[1]
    new = dk_ref.shape[1]
    per_step = heads * group

    def mask(columns):
        row = lax.broadcasted_iota(jnp.int32, (rows, columns), 0)
        column = lax.broadcasted_iota(jnp.int32, (rows, columns), 1)
        same = column % heads == row % per_step // group
        return jnp.where(same, column // heads, 1 << 20), row // per_step

    piece = min(cache, 128)
    pieces = range(0, cache, piece)
    place, _ = mask(piece)
    new_place, step = mask(new)
    new_allowed = new_place <= step
    low = lax.broadcasted_iota(jnp.int32, (rows, width), 1) < 4
    i = pl.program_id(0)
    first = (lax.rem(meta_ref[1] + target, targets) * pl.num_programs(0) + i) * block
    unroll = math.gcd(4, block)

    def body(g, carry):
        scores = []
        for u in range(unroll):
            r = g * unroll + u
            q = q_ref[r]
            length = len_ref[first + r]
            old = [
                jnp.where(
                    place < length - c // heads, nt(q, ck_ref[r, pl.ds(c, piece), :]), NEG
                )
                for c in pieces
            ]
            add = jnp.where(new_allowed, nt(q, dk_ref[r]), NEG)
            scores.append((r, old, add))
        weights = []
        for r, old, add in scores:
            top = functools.reduce(jnp.maximum, old)
            m = jnp.maximum(
                jnp.max(top, axis=1, keepdims=True), jnp.max(add, axis=1, keepdims=True)
            )
            old = [jnp.exp2((a - m) * scale) for a in old]
            add = jnp.exp2((add - m) * scale)
            l = jnp.sum(functools.reduce(jnp.add, old), axis=1, keepdims=True)
            l = l + jnp.sum(add, axis=1, keepdims=True)
            ml_ref[i * block + r] = jnp.where(low, m, l).T[:8]
            weights.append((r, [a.astype(jnp.bfloat16) for a in old], add.astype(jnp.bfloat16)))
        for r, old, add in weights:
            acc = nn(add, dv_ref[r])
            for c, p in zip(pieces, old):
                acc = acc + nn(p, cv_ref[r, pl.ds(c, piece), :])
            acc_ref[i * block + r] = acc.T
        return carry

    lax.fori_loop(0, block // unroll, body, 0)


def cache_part(q, dk, dv, ck, cv, lens, meta, target, targets, steps, heads, group):
    requests, rows, width = q.shape
    per_target = requests // targets
    block = math.gcd(8, per_target)
    per_block = per_target // block

    def here(i, lens, meta):
        return (lax.rem(meta[1] + target, targets) * per_block + i, 0, 0)

    spec = [pl.BlockSpec((block,) + a.shape[1:], here) for a in (q, dk, dv, ck, cv)]
    shapes = [(per_target, width, rows), (per_target, 8, rows)]
    return pl.pallas_call(
        functools.partial(
            cache_kernel, steps, heads, group, target, targets, LOG2E / math.sqrt(width)
        ),
        grid_spec=pltpu.PrefetchScalarGridSpec(
            num_scalar_prefetch=2,
            grid=(per_block,),
            in_specs=spec,
            out_specs=[pl.BlockSpec(memory_space=pltpu.VMEM)] * 2,
        ),
        out_shape=[pltpu.VMEM(a, jnp.float32) for a in shapes],
        compiler_params=params(),
        cost_estimate=pl.CostEstimate(
            flops=per_target * rows * ck.shape[1] * width * 16,
            bytes_accessed=7 * 10**6,
            transcendentals=per_target * rows * ck.shape[1],
        ),
    )(lens, meta, *in_hbm(q, dk, dv, ck, cv))


def collect_kernel(pick_ref, q_ref, *refs):
    blocks, (out_ref, q_out_ref, sems) = refs[:-3], refs[-3:]
    copies = [
        pltpu.make_async_copy(block.at[pick_ref[s]], out_ref.at[s], sems.at[s])
        for s, block in enumerate(blocks)
    ]
    copies.append(pltpu.make_async_copy(q_ref, q_out_ref, sems.at[len(blocks)]))
    for copy in copies:
        copy.start()
    for copy in copies:
        copy.wait()


def collect(pick, q, blocks):
    slots = len(blocks)
    return pl.pallas_call(
        collect_kernel,
        grid_spec=pltpu.PrefetchScalarGridSpec(
            num_scalar_prefetch=1,
            grid=(1,),
            in_specs=[pl.BlockSpec(memory_space=pl.ANY)] * (1 + slots),
            out_specs=[pl.BlockSpec(memory_space=pltpu.VMEM)] * 2,
            scratch_shapes=[pltpu.SemaphoreType.DMA((slots + 1,))],
        ),
        out_shape=[
            pltpu.VMEM((slots,) + blocks[0].shape[1:], jnp.bfloat16),
            pltpu.VMEM(q.shape, jnp.bfloat16),
        ],
        compiler_params=params(),
        cost_estimate=pl.CostEstimate(flops=0, bytes_accessed=8 * 10**6, transcendentals=0),
    )(pick, *in_hbm(q), *blocks)


def decode_kernel(
    extra, steps, target, targets, part, parts, heads, group, block, scale, slot_ref, meta_ref, *refs
):
    q_ref, acc_ref, ml_ref, buf, out_ref = refs
    lanes, width = q_ref.shape[1:]
    i = pl.program_id(0)
    kept = (part * pl.num_programs(0) + i) * block
    first = lax.rem(meta_ref[1] + target, targets) * (parts * pl.num_programs(0) * block) + kept

    per_step = heads * group
    row_head = lax.broadcasted_iota(jnp.int32, (lanes, width), 0) % per_step // group
    head_rows = [jnp.where(row_head == h, 1.0, 0.0).astype(jnp.bfloat16) for h in range(heads)]
    lane_head = lax.broadcasted_iota(jnp.int32, (width, lanes), 1) % per_step // group
    order = one_hot(lanes, lanes, lambda r: r % steps * per_step + r // steps)
    unroll = math.gcd(8, block)
    both = math.gcd(2 if target else 1, heads)

    def body(g, carry):
        scores = []
        for u in range(unroll):
            r = g * unroll + u
            q = q_ref[first + r]
            places = [slot_ref[(first + r) * extra + j] for j in range(extra)]
            spread = jnp.concatenate([q * a for a in head_rows], axis=1)
            keys = [
                jnp.concatenate([buf[place, h, 0] for h in range(heads)], axis=1)
                for place in places
            ]
            s = []
            for j in range(0, extra, both):
                pair = jnp.concatenate(keys[j : j + both], axis=0)
                s.append(nt(pair, spread))
            scores.append((r, places, s))
        weights = []
        for r, places, s in scores:
            old = ml_ref[kept + r, 0:1]
            m = jnp.max(functools.reduce(jnp.maximum, s), axis=0, keepdims=True)
            m = jnp.maximum(m, old)
            p = [jnp.exp2((a - m) * scale) for a in s]
            shrink = jnp.exp2((old - m) * scale)
            l = jnp.sum(functools.reduce(jnp.add, p), axis=0, keepdims=True)
            l = ml_ref[kept + r, 4:5] * shrink + l
            p = jnp.concatenate([a.astype(jnp.bfloat16) for a in p], axis=0)
            weights.append((r, places, p, shrink, l))
        results = []
        for r, places, p, shrink, l in weights:
            values = [
                jnp.concatenate([buf[place, h, 1] for place in places], axis=1)
                for h in range(heads)
            ]
            for h in range(0, heads, both):
                pair = nn(jnp.concatenate(values[h : h + both], axis=0), p)
                for w in range(both):
                    mine = pair[w * width : (w + 1) * width]
                    found = mine if h + w == 0 else jnp.where(lane_head == h + w, mine, found)
            results.append((r, ((acc_ref[kept + r] * shrink + found) / l).astype(jnp.bfloat16)))
        for r, result in results:
            out_ref[i * block + r] = nt(order, result).astype(jnp.bfloat16)
        return carry

    lax.fori_loop(0, block // unroll, body, 0)


def decode(q, acc, ml, pages, slot, meta, target, targets, part, parts, extra, steps, heads, group):
    requests, lanes, width = q.shape
    count = requests // targets // parts
    block = math.gcd(16, count)
    per_block = count // block

    on_chip = pl.BlockSpec(memory_space=pltpu.VMEM)
    return pl.pallas_call(
        functools.partial(
            decode_kernel,
            extra,
            steps,
            target,
            targets,
            part,
            parts,
            heads,
            group,
            block,
            LOG2E / math.sqrt(width),
        ),
        grid_spec=pltpu.PrefetchScalarGridSpec(
            num_scalar_prefetch=2,
            grid=(per_block,),
            in_specs=[on_chip] * 4,
            out_specs=on_chip,
        ),
        out_shape=pltpu.VMEM((count, lanes, width), jnp.bfloat16),
        compiler_params=params(),
        cost_estimate=pl.CostEstimate(
            flops=10**6, bytes_accessed=10**6, transcendentals=0
        ),
    )(slot, meta, q, acc, ml, pages)


def put(out_ref, source, offset, steps):
    def body(r, carry):
        value = source[r]
        for g in range(source.shape[1] // steps):
            out_ref[offset + r, :, g * 128 : (g + 1) * 128] = value[g * steps : (g + 1) * steps]
        return carry

    lax.fori_loop(0, source.shape[0], body, 0)


def join_kernel(counts, steps, meta_ref, *refs):
    out_ref = refs[-1]
    k = pl.program_id(0)
    targets = len(counts)
    sources = iter(refs)
    for s, count in enumerate(counts):
        parts = [next(sources) for _ in range(count)]

        @pl.when(lax.rem(meta_ref[1] + (targets - s), targets) == k)
        def _():
            for n, source in enumerate(parts):
                put(out_ref, source, n * source.shape[0], steps)


def join_last_kernel(steps, meta_ref, *refs):
    sources, out_ref = refs[:-2], refs[-1]
    for s, source in enumerate(sources):
        @pl.when(pl.program_id(0) == s)
        def _():
            put(out_ref, source, 0, steps)


def join(pieces, meta, steps):
    targets, parts = len(pieces), len(pieces[0])
    count, rows, width = pieces[0][0].shape
    half = rows // steps * width
    early = [pieces[0]] + [p[:-1] for p in pieces[1:]]
    late = [p[-1] for p in pieces[1:]]
    flat = [a for p in early for a in p]
    on_chip = pl.BlockSpec(memory_space=pltpu.VMEM)
    shape = jax.ShapeDtypeStruct((parts * count, steps, half * targets), jnp.bfloat16)
    out = pl.pallas_call(
        functools.partial(join_kernel, [len(p) for p in early], steps),
        grid_spec=pltpu.PrefetchScalarGridSpec(
            num_scalar_prefetch=1,
            grid=(targets,),
            in_specs=[on_chip] * len(flat),
            out_specs=pl.BlockSpec((parts * count, steps, half), lambda k, *_: (0, 0, k)),
        ),
        out_shape=shape,
        compiler_params=params(),
        cost_estimate=pl.CostEstimate(flops=0, bytes_accessed=2 * 10**6, transcendentals=0),
    )(meta, *flat)
    if not late:
        return out
    return pl.pallas_call(
        functools.partial(join_last_kernel, steps),
        grid_spec=pltpu.PrefetchScalarGridSpec(
            num_scalar_prefetch=1,
            grid=(targets - 1,),
            in_specs=[on_chip] * len(late) + [pl.BlockSpec(memory_space=pl.ANY)],
            out_specs=pl.BlockSpec(
                (count, steps, half),
                lambda s, meta: (parts - 1, 0, lax.rem(meta[1] + targets - 1 - s, targets)),
            ),
        ),
        out_shape=shape,
        input_output_aliases={1 + len(late): 0},
        compiler_params=params(),
        cost_estimate=pl.CostEstimate(flops=0, bytes_accessed=10**6, transcendentals=0),
    )(meta, *late, out)


def ring_place(index, size):
    return jnp.where(index % 2 == 0, index // 2, size - 1 - index // 2)


def shards(
    roles,
    ring,
    targets,
    prefill_q,
    prefill_k,
    prefill_v,
    decode_q,
    decode_k,
    decode_v,
    cache_k,
    cache_v,
    cache_len,
    page_list,
):
    tokens, q_heads = prefill_q.shape[1:3]
    heads, width = prefill_k.shape[2:]
    group = q_heads // heads
    own_pages = tokens // PAGE
    requests, steps = decode_q.shape[:2]
    extra = page_list.shape[1]
    role = lax.axis_index("role")
    ctx = lax.axis_index("ctx")
    tp = lax.axis_index("tp")

    order = list(range(0, ring, 2)) + list(range(ring - 1, 0, -2))
    along = [(order[j], order[(j + 1) % ring]) for j in range(ring)]
    flips = [1 << b for b in reversed(range(roles.bit_length() - 1))]

    owner = page_list // own_pages
    place = (ring_place(ctx, ring) - ring_place(owner % ring, ring)) % ring
    slot = ((owner // ring) ^ role) * ring + place
    hot = slot.reshape(-1, 1) == jnp.arange(roles * ring)[None, :]
    pick = jnp.max(jnp.where(hot, (page_list % own_pages).reshape(-1, 1), 0), axis=0)
    meta = jnp.stack([ctx, tp]).astype(jnp.int32)
    scalars = (
        slot.reshape(-1).astype(jnp.int32),
        pick.astype(jnp.int32),
        meta,
    )
    position = jnp.arange(ring)
    where = ring_place(ctx, ring)
    source = (where - position) % ring
    source_ctx = jnp.where(source < (ring + 1) // 2, 2 * source, 2 * (ring - 1 - source) + 1)
    needed = (source_ctx < ctx).astype(jnp.int32)

    raw = [
        a.reshape(requests, -1, width) for a in (decode_q, decode_k, decode_v, cache_k, cache_v)
    ]

    def cache(target):
        lens = cache_len.astype(jnp.int32)
        return cache_part(*raw, lens, meta, target, targets, steps, heads, group)

    gathered = {(0, 0): split_heads(prefill_k, prefill_v)}
    fresh = [(0, 0)]
    for k in range(ring + len(flips) - 1):
        sends = []
        for code, s in fresh:
            for flip in reversed(flips):
                if code == 0 or flip < code & -code:
                    pairs = [(j, j ^ flip) for j in range(roles)]
                    sends.append((flip, (code, s), (code ^ flip, s), "role", pairs))
            if code == 0 and s + 1 < ring:
                sends.append((roles if k else 1.5, (code, s), (0, s + 1), "ctx", along))
        sends.sort(key=lambda a: a[0])
        names = [to for _, _, to, _, _ in sends]
        arrived = [lax.ppermute(gathered[of], axis, pairs) for _, of, _, axis, pairs in sends]
        beside = ()
        if k == 0:
            beside = cache(targets - 1)
        if k == 1:
            beside = scalars, {s: cache(s) for s in range(targets - 1)}
        if k == ring - 2:
            slots = tuple(range(1, ring - 1))
            mine = [gathered[0, s] for s in slots]
            beside = prefill(prefill_q, mine, slots, needed, None)
        if k == ring - 1:
            slots = (0, ring - 1)
            mine = [gathered[0, s] for s in slots]
            beside = prefill(prefill_q, mine, slots, needed, state)
        arrived, beside = lax.optimization_barrier((arrived, beside))
        if k == 0:
            cached = {targets - 1: beside}
        if k == 1:
            scalars, others = beside
            cached.update(others)
        if k == ring - 2:
            state = beside
        if k == ring - 1:
            prefill_out = beside
        gathered.update(zip(names, arrived))
        fresh = names

    blocks = [gathered[r, s] for r in range(roles) for s in range(ring)]
    slot, pick, meta = scalars
    pages, queries = collect(pick, raw[0], blocks)
    pieces = [None] * targets
    for s in reversed(range(targets)):
        parts = math.gcd(2, requests // targets)
        pieces[s] = []
        for part in range(parts):
            if s == 0 and part == parts - 1 and targets > 1:
                sent = [p[0] for p in pieces[1:]]
                cached[0], sent = lax.optimization_barrier((cached[0], sent))
                for p, a in zip(pieces[1:], sent):
                    p[0] = a
            out = decode(
                queries, *cached[s], pages, slot, meta, s, targets, part, parts, extra, steps, heads, group
            )
            if s:
                shift = [(j, (j + s) % targets) for j in range(targets)]
                out = lax.ppermute(out, "tp", shift)
            pieces[s].append(out)
    decode_out = join(pieces, meta, steps)
    return (prefill_out, decode_out)


def solution(mesh):
    body = functools.partial(shards, mesh.shape["role"], mesh.shape["ctx"], mesh.shape["tp"])
    return jax.shard_map(
        body,
        mesh=mesh,
        in_specs=(
            P("role", "ctx", "tp", None),
            P("role", "ctx", "tp", None),
            P("role", "ctx", "tp", None),
            P(("role", "ctx"), None, "tp", None),
            P(("role", "ctx"), None, "tp", None),
            P(("role", "ctx"), None, "tp", None),
            P(("role", "ctx"), None, "tp", None),
            P(("role", "ctx"), None, "tp", None),
            P(("role", "ctx")),
            P(("role", "ctx"), None),
        ),
        out_specs=(P("role", "ctx", "tp", None), P(("role", "ctx", "tp"), None, None)),
        check_vma=False,
    )
```

```python
import functools
import math

import jax
import jax.numpy as jnp
from jax import lax
from jax.experimental import pallas as pl
from jax.experimental.pallas import tpu as pltpu
from jax.sharding import PartitionSpec as P

PAGE = 128
LOG2E = 1.4426950408889634
NEG = -1e30
VMEM_LIMIT = 16 * 1024 * 1024


def nt(a, b):
    return lax.dot_general(a, b, (((1,), (1,)), ((), ())), preferred_element_type=jnp.float32)


def nn(a, b):
    return jnp.dot(a, b, preferred_element_type=jnp.float32)


def in_hbm(*arrays):
    return [pltpu.with_memory_space_constraint(a, pltpu.HBM) for a in arrays]


def params():
    return pltpu.CompilerParams(vmem_limit_bytes=VMEM_LIMIT)


def one_hot(out_rows, in_rows, source):
    row = lax.broadcasted_iota(jnp.int32, (out_rows, in_rows), 0)
    col = lax.broadcasted_iota(jnp.int32, (out_rows, in_rows), 1)
    return jnp.where(col == source(row), 1.0, 0.0).astype(jnp.bfloat16)


def split_kernel(heads, tokens, k_ref, v_ref, out_ref):
    rows = min(tokens * heads, 256)
    step = rows // heads
    pick = one_hot(rows, rows, lambda i: (i % step) * heads + i // step)
    moved, kept = [], []
    for j in range(tokens // step):
        keys = nn(pick, k_ref[pl.ds(j * rows, rows), :]).astype(jnp.bfloat16)
        moved.append(nn(pick, v_ref[pl.ds(j * rows, rows), :]))
        kept.append(keys)
    for h in range(heads):
        keys = jnp.concatenate([a[h * step : (h + 1) * step] for a in kept], axis=0)
        values = jnp.concatenate([a[h * step : (h + 1) * step] for a in moved], axis=0)
        for page in range(tokens // PAGE):
            out_ref[page, h, 0] = keys[page * PAGE : (page + 1) * PAGE]
            out_ref[page, h, 1] = values[page * PAGE : (page + 1) * PAGE].T.astype(jnp.bfloat16)


def split_heads(k, v):
    _, tokens, heads, width = k.shape
    return pl.pallas_call(
        functools.partial(split_kernel, heads, tokens),
        out_specs=pl.BlockSpec(memory_space=pltpu.VMEM),
        out_shape=pltpu.VMEM((tokens // PAGE, heads, 2, PAGE, width), jnp.bfloat16),
        compiler_params=params(),
        cost_estimate=pl.CostEstimate(flops=10**8, bytes_accessed=2 * 10**6, transcendentals=0),
    )(*in_hbm(k.reshape(tokens * heads, width), v.reshape(tokens * heads, width)))


def prefill_kernel(own, count, slots, group, tokens, scale, needed_ref, *refs):
    q_ref = refs[0]
    blocks = refs[1 : 1 + count]
    refs = refs[1 + count :]
    i = pl.program_id(0)
    if own:
        old_acc_ref, old_m_ref, old_l_ref, out_ref, buf, s_ref, acc_ref, m_ref, l_ref, sems = refs
    else:
        acc_ref, m_ref, l_ref, buf, s_ref, sems = refs
        acc_ref, m_ref, l_ref = acc_ref.at[i], m_ref.at[i], l_ref.at[i]
    pages, heads = blocks[0].shape[:2]
    block = q_ref.shape[1]
    rest = range(1 if own else 0, count)
    total = sum(needed_ref[slots[c]] for c in rest)

    def copies():
        found = []
        place = jnp.int32(0)
        for c in rest:
            flag = needed_ref[slots[c]]
            found.append((flag, pltpu.make_async_copy(blocks[c], buf.at[place], sems.at[c])))
            place = place + flag
        return found

    @pl.when(i == 0)
    def _():
        for flag, copy in copies():
            @pl.when(flag == 1)
            def _():
                copy.start()

    rows = block * group
    piece = min(rows, 256)
    parts = [(h, pl.ds(c, piece)) for h in range(heads) for c in range(0, rows, piece)]
    queries = q_ref[0].astype(jnp.float32)
    q = [
        queries[:, h * group : (h + 1) * group, :].reshape(rows, -1).astype(jnp.bfloat16)
        for h in range(heads)
    ]
    q = [q[h][c : c + piece] for h in range(heads) for c in range(0, rows, piece)]

    def fold(a, op):
        return functools.reduce(op, [a[:, j * 128 : (j + 1) * 128] for j in range(a.shape[1] // 128)])

    def keys(ref, h):
        return jnp.concatenate([ref[j, h, 0] for j in range(pages)], axis=0)

    def values(ref, h):
        return jnp.concatenate([ref[j, h, 1] for j in range(pages)], axis=1)

    def weights(place, h, at, m):
        return [
            jnp.exp2((s_ref[place, h, at, pl.ds(j * 128, 128)] - m) * scale)
            for j in range(tokens // 128)
        ]

    last = count - 1
    if own:
        m_ref[...] = old_m_ref[i]
        for j in range(pages):
            @pl.when((i + 1) * block > j * PAGE)
            def _():
                for n, (h, at) in enumerate(parts):
                    row = lax.broadcasted_iota(jnp.int32, (piece, PAGE), 0) + n * piece % rows
                    column = lax.broadcasted_iota(jnp.int32, (piece, PAGE), 1) + j * PAGE
                    s = nt(q[n], blocks[0][j, h, 0])
                    s = jnp.where(column <= row // group + i * block, s, NEG)
                    s_ref[last, h, at, pl.ds(j * PAGE, PAGE)] = s
                    m_ref[h, at] = jnp.maximum(m_ref[h, at], s)
    else:
        m_ref[...] = jnp.full(m_ref.shape, NEG, jnp.float32)

    @pl.when(i == 0)
    def _():
        for flag, copy in copies():
            @pl.when(flag == 1)
            def _():
                copy.wait()

    def sweep(step):
        if len(rest) > 2:
            lax.fori_loop(0, total, step, 0)
            return
        for n in range(1, len(rest) + 1):
            @pl.when(total == n)
            def _():
                for b in range(n):
                    step(b, 0)

    def look(b, carry):
        for n, (h, at) in enumerate(parts):
            s = nt(q[n], keys(buf.at[b], h))
            s_ref[b, h, at] = s
            m_ref[h, at] = jnp.maximum(m_ref[h, at], fold(s, jnp.maximum))
        return carry

    sweep(look)
    for h, at in parts:
        m = m_ref[h, at]
        m = jnp.broadcast_to(jnp.max(m, axis=1, keepdims=True), m.shape)
        m_ref[h, at] = m
        if own:
            share = jnp.exp2((old_m_ref[i, h, at] - m) * scale)
            l_ref[h, at] = old_l_ref[i, h, at] * share
            acc_ref[h, at] = old_acc_ref[i, h, at] * share
        else:
            l_ref[h, at] = jnp.zeros(m.shape, jnp.float32)
            acc_ref[h, at] = jnp.zeros(m.shape, jnp.float32)
    if own:
        for j in range(pages):
            @pl.when((i + 1) * block > j * PAGE)
            def _():
                for h, at in parts:
                    p = s_ref[last, h, at, pl.ds(j * PAGE, PAGE)]
                    p = jnp.exp2((p - m_ref[h, at]) * scale)
                    l_ref[h, at] = l_ref[h, at] + p
                    acc_ref[h, at] = acc_ref[h, at] + nt(p.astype(jnp.bfloat16), blocks[0][j, h, 1])

    def weigh(b, carry):
        for h, at in parts:
            p = weights(b, h, at, m_ref[h, at])
            l_ref[h, at] = l_ref[h, at] + functools.reduce(jnp.add, p)
            p = jnp.concatenate([a.astype(jnp.bfloat16) for a in p], axis=1)
            acc_ref[h, at] = acc_ref[h, at] + nt(p, values(buf.at[b], h))
        return carry

    sweep(weigh)
    if own:
        out = []
        for h in range(heads):
            l = jnp.sum(l_ref[h], axis=1, keepdims=True)
            out.append((acc_ref[h] / l).reshape(block, group, -1))
        out_ref[0] = jnp.concatenate(out, axis=1).astype(out_ref.dtype)


def prefill(q, blocks, slots, needed, state):
    _, tokens, q_heads, width = q.shape
    own = state is not None
    count = len(blocks)
    heads = blocks[0].shape[1]
    group = q_heads // heads
    block = 64
    rows = block * group
    q_spec = pl.BlockSpec((1, block, q_heads, width), lambda i, *_: (0, i, 0, 0))
    own_spec = pl.BlockSpec(blocks[0].shape, lambda i, *_: (0, 0, 0, 0, 0))
    any_spec = pl.BlockSpec(memory_space=pl.ANY)
    on_chip = pl.BlockSpec(memory_space=pltpu.VMEM)
    scratch = [
        pltpu.VMEM((count,) + blocks[0].shape, jnp.bfloat16),
        pltpu.VMEM((count, heads, rows, tokens), jnp.float32),
    ]
    if own:
        in_specs = [q_spec, own_spec] + [any_spec] * (count - 1) + [on_chip] * 3
        out_specs, out_shape = q_spec, jax.ShapeDtypeStruct(q.shape, jnp.bfloat16)
        scratch += [pltpu.VMEM((heads, rows, width), jnp.float32)] * 3
    else:
        in_specs = [q_spec] + [any_spec] * count
        out_specs, state = [on_chip] * 3, ()
        out_shape = [pltpu.VMEM((tokens // block, heads, rows, width), jnp.float32)] * 3
    return pl.pallas_call(
        functools.partial(
            prefill_kernel, own, count, slots, group, tokens, LOG2E / math.sqrt(width)
        ),
        grid_spec=pltpu.PrefetchScalarGridSpec(
            num_scalar_prefetch=1,
            grid=(tokens // block,),
            in_specs=in_specs,
            out_specs=out_specs,
            scratch_shapes=scratch + [pltpu.SemaphoreType.DMA((count,))],
        ),
        out_shape=out_shape,
        compiler_params=params(),
        cost_estimate=pl.CostEstimate(
            flops=16 * q_heads * tokens * tokens * count * width,
            bytes_accessed=12 * 10**6,
            transcendentals=tokens * tokens * count * q_heads,
        ),
    )(needed, *in_hbm(q), *blocks, *state)


def cache_kernel(
    steps, heads, group, target, targets, scale, len_ref, meta_ref, *refs
):
    q_ref, dk_ref, dv_ref, ck_ref, cv_ref, acc_ref, ml_ref = refs
    block, rows, width = q_ref.shape
    cache = ck_ref.shape[1]
    new = dk_ref.shape[1]
    per_step = heads * group

    def mask(columns):
        row = lax.broadcasted_iota(jnp.int32, (rows, columns), 0)
        column = lax.broadcasted_iota(jnp.int32, (rows, columns), 1)
        same = column % heads == row % per_step // group
        return jnp.where(same, column // heads, 1 << 20), row // per_step

    piece = min(cache, 128)
    pieces = range(0, cache, piece)
    place, _ = mask(piece)
    new_place, step = mask(new)
    new_allowed = new_place <= step
    low = lax.broadcasted_iota(jnp.int32, (rows, width), 1) < 4
    i = pl.program_id(0)
    first = (lax.rem(meta_ref[1] + target, targets) * pl.num_programs(0) + i) * block
    unroll = math.gcd(4, block)

    def body(g, carry):
        scores = []
        for u in range(unroll):
            r = g * unroll + u
            q = q_ref[r]
            length = len_ref[first + r]
            old = [
                jnp.where(
                    place < length - c // heads, nt(q, ck_ref[r, pl.ds(c, piece), :]), NEG
                )
                for c in pieces
            ]
            add = jnp.where(new_allowed, nt(q, dk_ref[r]), NEG)
            scores.append((r, old, add))
        weights = []
        for r, old, add in scores:
            top = functools.reduce(jnp.maximum, old)
            m = jnp.maximum(
                jnp.max(top, axis=1, keepdims=True), jnp.max(add, axis=1, keepdims=True)
            )
            old = [jnp.exp2((a - m) * scale) for a in old]
            add = jnp.exp2((add - m) * scale)
            l = jnp.sum(functools.reduce(jnp.add, old), axis=1, keepdims=True)
            l = l + jnp.sum(add, axis=1, keepdims=True)
            ml_ref[i * block + r] = jnp.where(low, m, l).T[:8]
            weights.append((r, [a.astype(jnp.bfloat16) for a in old], add.astype(jnp.bfloat16)))
        for r, old, add in weights:
            acc = nn(add, dv_ref[r])
            for c, p in zip(pieces, old):
                acc = acc + nn(p, cv_ref[r, pl.ds(c, piece), :])
            acc_ref[i * block + r] = acc.T
        return carry

    lax.fori_loop(0, block // unroll, body, 0)


def cache_part(q, dk, dv, ck, cv, lens, meta, target, targets, steps, heads, group):
    requests, rows, width = q.shape
    per_target = requests // targets
    block = math.gcd(8, per_target)
    per_block = per_target // block

    def here(i, lens, meta):
        return (lax.rem(meta[1] + target, targets) * per_block + i, 0, 0)

    spec = [pl.BlockSpec((block,) + a.shape[1:], here) for a in (q, dk, dv, ck, cv)]
    shapes = [(per_target, width, rows), (per_target, 8, rows)]
    return pl.pallas_call(
        functools.partial(
            cache_kernel, steps, heads, group, target, targets, LOG2E / math.sqrt(width)
        ),
        grid_spec=pltpu.PrefetchScalarGridSpec(
            num_scalar_prefetch=2,
            grid=(per_block,),
            in_specs=spec,
            out_specs=[pl.BlockSpec(memory_space=pltpu.VMEM)] * 2,
        ),
        out_shape=[pltpu.VMEM(a, jnp.float32) for a in shapes],
        compiler_params=params(),
        cost_estimate=pl.CostEstimate(
            flops=per_target * rows * ck.shape[1] * width * 16,
            bytes_accessed=7 * 10**6,
            transcendentals=per_target * rows * ck.shape[1],
        ),
    )(lens, meta, *in_hbm(q, dk, dv, ck, cv))


def collect_kernel(pick_ref, q_ref, *refs):
    blocks, (out_ref, q_out_ref, sems) = refs[:-3], refs[-3:]
    copies = [
        pltpu.make_async_copy(block.at[pick_ref[s]], out_ref.at[s], sems.at[s])
        for s, block in enumerate(blocks)
    ]
    copies.append(pltpu.make_async_copy(q_ref, q_out_ref, sems.at[len(blocks)]))
    for copy in copies:
        copy.start()
    for copy in copies:
        copy.wait()


def collect(pick, q, blocks):
    slots = len(blocks)
    return pl.pallas_call(
        collect_kernel,
        grid_spec=pltpu.PrefetchScalarGridSpec(
            num_scalar_prefetch=1,
            grid=(1,),
            in_specs=[pl.BlockSpec(memory_space=pl.ANY)] * (1 + slots),
            out_specs=[pl.BlockSpec(memory_space=pltpu.VMEM)] * 2,
            scratch_shapes=[pltpu.SemaphoreType.DMA((slots + 1,))],
        ),
        out_shape=[
            pltpu.VMEM((slots,) + blocks[0].shape[1:], jnp.bfloat16),
            pltpu.VMEM(q.shape, jnp.bfloat16),
        ],
        compiler_params=params(),
        cost_estimate=pl.CostEstimate(flops=0, bytes_accessed=8 * 10**6, transcendentals=0),
    )(pick, *in_hbm(q), *blocks)


def decode_kernel(
    extra, steps, target, targets, part, parts, heads, group, block, scale, slot_ref, meta_ref, *refs
):
    q_ref, acc_ref, ml_ref, buf, out_ref = refs
    lanes, width = q_ref.shape[1:]
    i = pl.program_id(0)
    kept = (part * pl.num_programs(0) + i) * block
    first = lax.rem(meta_ref[1] + target, targets) * (parts * pl.num_programs(0) * block) + kept

    per_step = heads * group
    row_head = lax.broadcasted_iota(jnp.int32, (lanes, width), 0) % per_step // group
    head_rows = [jnp.where(row_head == h, 1.0, 0.0).astype(jnp.bfloat16) for h in range(heads)]
    lane_head = lax.broadcasted_iota(jnp.int32, (width, lanes), 1) % per_step // group
    order = one_hot(lanes, lanes, lambda r: r % steps * per_step + r // steps)
    unroll = math.gcd(8, block)
    both = math.gcd(2 if target else 1, heads)

    def body(g, carry):
        scores = []
        for u in range(unroll):
            r = g * unroll + u
            q = q_ref[first + r]
            places = [slot_ref[(first + r) * extra + j] for j in range(extra)]
            spread = jnp.concatenate([q * a for a in head_rows], axis=1)
            keys = [
                jnp.concatenate([buf[place, h, 0] for h in range(heads)], axis=1)
                for place in places
            ]
            s = []
            for j in range(0, extra, both):
                pair = jnp.concatenate(keys[j : j + both], axis=0)
                s.append(nt(pair, spread))
            scores.append((r, places, s))
        weights = []
        for r, places, s in scores:
            old = ml_ref[kept + r, 0:1]
            m = jnp.max(functools.reduce(jnp.maximum, s), axis=0, keepdims=True)
            m = jnp.maximum(m, old)
            p = [jnp.exp2((a - m) * scale) for a in s]
            shrink = jnp.exp2((old - m) * scale)
            l = jnp.sum(functools.reduce(jnp.add, p), axis=0, keepdims=True)
            l = ml_ref[kept + r, 4:5] * shrink + l
            p = jnp.concatenate([a.astype(jnp.bfloat16) for a in p], axis=0)
            weights.append((r, places, p, shrink, l))
        results = []
        for r, places, p, shrink, l in weights:
            values = [
                jnp.concatenate([buf[place, h, 1] for place in places], axis=1)
                for h in range(heads)
            ]
            for h in range(0, heads, both):
                pair = nn(jnp.concatenate(values[h : h + both], axis=0), p)
                for w in range(both):
                    mine = pair[w * width : (w + 1) * width]
                    found = mine if h + w == 0 else jnp.where(lane_head == h + w, mine, found)
            results.append((r, ((acc_ref[kept + r] * shrink + found) / l).astype(jnp.bfloat16)))
        for r, result in results:
            out_ref[i * block + r] = nt(order, result).astype(jnp.bfloat16)
        return carry

    lax.fori_loop(0, block // unroll, body, 0)


def decode(q, acc, ml, pages, slot, meta, target, targets, part, parts, extra, steps, heads, group):
    requests, lanes, width = q.shape
    count = requests // targets // parts
    block = math.gcd(16, count)
    per_block = count // block

    on_chip = pl.BlockSpec(memory_space=pltpu.VMEM)
    return pl.pallas_call(
        functools.partial(
            decode_kernel,
            extra,
            steps,
            target,
            targets,
            part,
            parts,
            heads,
            group,
            block,
            LOG2E / math.sqrt(width),
        ),
        grid_spec=pltpu.PrefetchScalarGridSpec(
            num_scalar_prefetch=2,
            grid=(per_block,),
            in_specs=[on_chip] * 4,
            out_specs=on_chip,
        ),
        out_shape=pltpu.VMEM((count, lanes, width), jnp.bfloat16),
        compiler_params=params(),
        cost_estimate=pl.CostEstimate(
            flops=10**6, bytes_accessed=10**6, transcendentals=0
        ),
    )(slot, meta, q, acc, ml, pages)


def put(out_ref, source, offset, steps):
    def body(r, carry):
        value = source[r]
        for g in range(source.shape[1] // steps):
            out_ref[offset + r, :, g * 128 : (g + 1) * 128] = value[g * steps : (g + 1) * steps]
        return carry

    lax.fori_loop(0, source.shape[0], body, 0)


def join_kernel(counts, steps, meta_ref, *refs):
    out_ref = refs[-1]
    k = pl.program_id(0)
    targets = len(counts)
    sources = iter(refs)
    for s, count in enumerate(counts):
        parts = [next(sources) for _ in range(count)]

        @pl.when(lax.rem(meta_ref[1] + (targets - s), targets) == k)
        def _():
            for n, source in enumerate(parts):
                put(out_ref, source, n * source.shape[0], steps)


def join_last_kernel(steps, meta_ref, *refs):
    sources, out_ref = refs[:-2], refs[-1]
    for s, source in enumerate(sources):
        @pl.when(pl.program_id(0) == s)
        def _():
            put(out_ref, source, 0, steps)


def join(pieces, meta, steps):
    targets, parts = len(pieces), len(pieces[0])
    count, rows, width = pieces[0][0].shape
    half = rows // steps * width
    early = [pieces[0]] + [p[:-1] for p in pieces[1:]]
    late = [p[-1] for p in pieces[1:]]
    flat = [a for p in early for a in p]
    on_chip = pl.BlockSpec(memory_space=pltpu.VMEM)
    shape = jax.ShapeDtypeStruct((parts * count, steps, half * targets), jnp.bfloat16)
    out = pl.pallas_call(
        functools.partial(join_kernel, [len(p) for p in early], steps),
        grid_spec=pltpu.PrefetchScalarGridSpec(
            num_scalar_prefetch=1,
            grid=(targets,),
            in_specs=[on_chip] * len(flat),
            out_specs=pl.BlockSpec((parts * count, steps, half), lambda k, *_: (0, 0, k)),
        ),
        out_shape=shape,
        compiler_params=params(),
        cost_estimate=pl.CostEstimate(flops=0, bytes_accessed=2 * 10**6, transcendentals=0),
    )(meta, *flat)
    if not late:
        return out
    return pl.pallas_call(
        functools.partial(join_last_kernel, steps),
        grid_spec=pltpu.PrefetchScalarGridSpec(
            num_scalar_prefetch=1,
            grid=(targets - 1,),
            in_specs=[on_chip] * len(late) + [pl.BlockSpec(memory_space=pl.ANY)],
            out_specs=pl.BlockSpec(
                (count, steps, half),
                lambda s, meta: (parts - 1, 0, lax.rem(meta[1] + targets - 1 - s, targets)),
            ),
        ),
        out_shape=shape,
        input_output_aliases={1 + len(late): 0},
        compiler_params=params(),
        cost_estimate=pl.CostEstimate(flops=0, bytes_accessed=10**6, transcendentals=0),
    )(meta, *late, out)


def ring_place(index, size):
    return jnp.where(index % 2 == 0, index // 2, size - 1 - index // 2)


def shards(
    roles,
    ring,
    targets,
    prefill_q,
    prefill_k,
    prefill_v,
    decode_q,
    decode_k,
    decode_v,
    cache_k,
    cache_v,
    cache_len,
    page_list,
):
    tokens, q_heads = prefill_q.shape[1:3]
    heads, width = prefill_k.shape[2:]
    group = q_heads // heads
    own_pages = tokens // PAGE
    requests, steps = decode_q.shape[:2]
    extra = page_list.shape[1]
    role = lax.axis_index("role")
    ctx = lax.axis_index("ctx")
    tp = lax.axis_index("tp")

    order = list(range(0, ring, 2)) + list(range(ring - 1, 0, -2))
    along = [(order[j], order[(j + 1) % ring]) for j in range(ring)]
    flips = [1 << b for b in reversed(range(roles.bit_length() - 1))]

    owner = page_list // own_pages
    place = (ring_place(ctx, ring) - ring_place(owner % ring, ring)) % ring
    slot = ((owner // ring) ^ role) * ring + place
    hot = slot.reshape(-1, 1) == jnp.arange(roles * ring)[None, :]
    pick = jnp.max(jnp.where(hot, (page_list % own_pages).reshape(-1, 1), 0), axis=0)
    meta = jnp.stack([ctx, tp]).astype(jnp.int32)
    scalars = (
        slot.reshape(-1).astype(jnp.int32),
        pick.astype(jnp.int32),
        meta,
    )
    position = jnp.arange(ring)
    where = ring_place(ctx, ring)
    source = (where - position) % ring
    source_ctx = jnp.where(source < (ring + 1) // 2, 2 * source, 2 * (ring - 1 - source) + 1)
    needed = (source_ctx < ctx).astype(jnp.int32)

    raw = [
        a.reshape(requests, -1, width) for a in (decode_q, decode_k, decode_v, cache_k, cache_v)
    ]

    def cache(target):
        lens = cache_len.astype(jnp.int32)
        return cache_part(*raw, lens, meta, target, targets, steps, heads, group)

    gathered = {(0, 0): split_heads(prefill_k, prefill_v)}
    fresh = [(0, 0)]
    for k in range(ring + len(flips) - 1):
        sends = []
        for code, s in fresh:
            for flip in reversed(flips):
                if code == 0 or flip < code & -code:
                    pairs = [(j, j ^ flip) for j in range(roles)]
                    sends.append((flip, (code, s), (code ^ flip, s), "role", pairs))
            if code == 0 and s + 1 < ring:
                sends.append((roles, (code, s), (0, s + 1), "ctx", along))
        sends.sort(key=lambda a: a[0])
        names = [to for _, _, to, _, _ in sends]
        arrived = [lax.ppermute(gathered[of], axis, pairs) for _, of, _, axis, pairs in sends]
        beside = ()
        if k == 0:
            beside = cache(targets - 1)
        if k == 1:
            beside = scalars, {s: cache(s) for s in range(targets - 1)}
        if k == ring - 2:
            slots = tuple(range(1, ring - 1))
            mine = [gathered[0, s] for s in slots]
            beside = prefill(prefill_q, mine, slots, needed, None)
        if k == ring - 1:
            slots = (0, ring - 1)
            mine = [gathered[0, s] for s in slots]
            beside = prefill(prefill_q, mine, slots, needed, state)
        arrived, beside = lax.optimization_barrier((arrived, beside))
        if k == 0:
            cached = {targets - 1: beside}
        if k == 1:
            scalars, others = beside
            cached.update(others)
        if k == ring - 2:
            state = beside
        if k == ring - 1:
            prefill_out = beside
        gathered.update(zip(names, arrived))
        fresh = names

    blocks = [gathered[r, s] for r in range(roles) for s in range(ring)]
    slot, pick, meta = scalars
    pages, queries = collect(pick, raw[0], blocks)
    pieces = [None] * targets
    for s in reversed(range(targets)):
        parts = math.gcd(2, requests // targets)
        pieces[s] = []
        for part in range(parts):
            if s == 0 and part == parts - 1 and targets > 1:
                sent = [p[0] for p in pieces[1:]]
                cached[0], sent = lax.optimization_barrier((cached[0], sent))
                for p, a in zip(pieces[1:], sent):
                    p[0] = a
            out = decode(
                queries, *cached[s], pages, slot, meta, s, targets, part, parts, extra, steps, heads, group
            )
            if s:
                shift = [(j, (j + s) % targets) for j in range(targets)]
                out = lax.ppermute(out, "tp", shift)
            pieces[s].append(out)
    decode_out = join(pieces, meta, steps)
    return (prefill_out, decode_out)


def solution(mesh):
    body = functools.partial(shards, mesh.shape["role"], mesh.shape["ctx"], mesh.shape["tp"])
    return jax.shard_map(
        body,
        mesh=mesh,
        in_specs=(
            P("role", "ctx", "tp", None),
            P("role", "ctx", "tp", None),
            P("role", "ctx", "tp", None),
            P(("role", "ctx"), None, "tp", None),
            P(("role", "ctx"), None, "tp", None),
            P(("role", "ctx"), None, "tp", None),
            P(("role", "ctx"), None, "tp", None),
            P(("role", "ctx"), None, "tp", None),
            P(("role", "ctx")),
            P(("role", "ctx"), None),
        ),
        out_specs=(P("role", "ctx", "tp", None), P(("role", "ctx", "tp"), None, None)),
        check_vma=False,
    )
```
